32 devices in a mesh: gx: 2 (over core), gy: 4 (over y, x), gz: 4 (over z).
Axes of the slice: x: 2, y: 2, z: 4, core: 2. Of those that a mesh axis runs over, the one named last changes fastest.
Arguments:
- charges: float32 [64, 128, 512], P('gz', 'gx', 'gy'), may hold values from -6 to 6
- widths: float32 [4, 3], replicated, may hold values from 2.5 to 6
- amplitudes: float32 [4, 3], replicated, may hold values from 0.2 to 1
Outputs:
- potential: float32 [64, 128, 512], P('gz', 'gx', 'gy')
The draws below stay inside these ranges and needn't reach their ends.
All inputs are finite; a program needn't handle non-finite values.
Results may differ from the reference program's by a relative error of at most 0.0001.
Values sent between devices are 32-bit elements; how exact they have to be, the bound alone decides.
No kernel may reach another device: no remote copies, remote signals or barrier semaphores. Data moves between devices by JAX's collectives and lax.ppermute only.
A program may use at most 64 MiB of HBM per device.

```python
import math
import jax
import jax.numpy as jnp
from jax import lax

TERMS = 3
RADIUS = 8
NX = 128
NY = 512
NZ = 64


def draw_charges(key, part):
    key = jax.random.fold_in(key, 7)
    grid_shape = (NZ, NX, NY)
    return jax.random.truncated_normal(key, -6.0, 6.0, grid_shape, jnp.float32)


def setup_inputs(seed: int = 0) -> dict:
    key_of = jax.random.split(jax.random.key(seed), 4)
    return {
        "charges": draw_charges(jax.random.fold_in(key_of[3], 71), 0),
        "widths": jnp.clip(jnp.exp(jax.random.uniform(key_of[1], (4, TERMS), jnp.float32, math.log(2.5), math.log(6.0))), 2.5, 6.0),
        "amplitudes": jnp.clip(jnp.exp(jax.random.uniform(key_of[2], (4, TERMS), jnp.float32, math.log(0.2), math.log(1.0))), 0.2, 1.0),
    }


near_weight = 9.0 / 16.0
far_weight = -1.0 / 16.0
highest = lax.Precision.HIGHEST

def bell_taps(widths, level_no):
    offsets = jnp.arange(-RADIUS, RADIUS + 1).astype(jnp.float32)
    spread = widths[level_no][:, None]
    bell_curve = jnp.exp(-offsets[None, :] ** 2 / (2.0 * spread ** 2))
    square_sum = lax.optimization_barrier(jnp.sum(jnp.exp(-offsets[None, :] ** 2 / spread ** 2), axis=1, keepdims=True))
    return bell_curve / jnp.sqrt(square_sum)

def cycle_taps(widths, count_cells):
    steps_away = jnp.arange(count_cells).astype(jnp.float32)
    distance = jnp.minimum(steps_away, count_cells - steps_away)
    spread = widths[3][:, None]
    bell_curve = jnp.exp(-distance[None, :] ** 2 / (2.0 * spread ** 2))
    square_sum = lax.optimization_barrier(jnp.sum(jnp.exp(-distance[None, :] ** 2 / spread ** 2), axis=1, keepdims=True))
    kernel = bell_curve / jnp.sqrt(square_sum)
    cell_ids = jnp.arange(count_cells).astype(jnp.int32)
    lag_ids = (cell_ids[None, :] - cell_ids[:, None]) % count_cells
    picker = (lag_ids[:, :, None] == cell_ids[None, None, :]).astype(jnp.float32)
    return jnp.einsum('td,ijd->tij', kernel, picker, precision=highest)

def top_level(values, widths, amplitudes):
    cycle_depth = cycle_taps(widths, values.shape[0])
    cycle_cross = cycle_taps(widths, values.shape[1])
    cycle_along = cycle_taps(widths, values.shape[2])
    blurred = jnp.einsum('tij,jxy->tixy', cycle_depth, values, precision=highest)
    blurred = jnp.einsum('tij,tzjy->tziy', cycle_cross, blurred, precision=highest)
    blurred = jnp.einsum('tij,tzxj->tzxi', cycle_along, blurred, precision=highest)
    coefficient = amplitudes[3] * 0.25 ** 3
    return lax.optimization_barrier(jnp.sum(coefficient.reshape(-1, 1, 1, 1) * blurred, axis=0))

def conv_pass(values, kernel, axis_no):
    pad_widths = [(RADIUS, RADIUS) if dim_no == axis_no else (0, 0) for dim_no in range(3)]
    padded = jnp.pad(values, pad_widths, mode='wrap')
    window = [1, 1, 1]
    window[axis_no] = 2 * RADIUS + 1
    filter_taps = kernel.reshape(window)[None, None]
    result = lax.conv_general_dilated(padded[None, None], filter_taps, (1, 1, 1), 'VALID', precision=highest)
    return result[0, 0]

def near_level(values, widths, amplitudes, level_no):
    kernel = bell_taps(widths, level_no)
    summed = jnp.zeros(values.shape, jnp.float32)
    for term_no in range(TERMS):
        blurred = conv_pass(values, kernel[term_no], 0)
        blurred = conv_pass(blurred, kernel[term_no], 1)
        blurred = conv_pass(blurred, kernel[term_no], 2)
        summed = summed + amplitudes[level_no, term_no] * 0.25 ** level_no * blurred
    return summed

def restrict_axis(values, axis_no):
    count_cells = values.shape[axis_no]

    def every_other(shift_by):
        return lax.slice_in_dim(jnp.roll(values, -shift_by, axis_no), 0, count_cells, 2, axis_no)
    return every_other(0) + near_weight * (every_other(1) + every_other(-1)) + far_weight * (every_other(3) + every_other(-3))

def restrict_all(values):
    for axis_no in range(3):
        values = restrict_axis(values, axis_no)
    return values

def prolong_axis(values, axis_no):
    odd_cells = near_weight * (values + jnp.roll(values, -1, axis_no)) + far_weight * (jnp.roll(values, 1, axis_no) + jnp.roll(values, -2, axis_no))
    paired = jnp.stack([values, odd_cells], axis=axis_no + 1)
    new_shape = list(values.shape)
    new_shape[axis_no] = 2 * new_shape[axis_no]
    return paired.reshape(new_shape)

def prolong_all(values):
    for axis_no in range(3):
        values = prolong_axis(values, axis_no)
    return values

def reference(charges, widths, amplitudes):
    charges_1 = restrict_all(charges)
    charges_2 = restrict_all(charges_1)
    charges_3 = restrict_all(charges_2)
    top_field = top_level(charges_3, widths, amplitudes)
    level_2 = near_level(charges_2, widths, amplitudes, 2) + prolong_all(top_field)
    level_1 = near_level(charges_1, widths, amplitudes, 1) + prolong_all(level_2)
    return near_level(charges, widths, amplitudes, 0) + prolong_all(level_1)
```

```python
import functools

import jax
import jax.numpy as jnp
import numpy as np
from jax import lax
from jax.experimental import pallas as pl
from jax.experimental.pallas import tpu as pltpu
from jax.sharding import PartitionSpec as P

R = 8
TERMS = 3
LANES = 128
NEAR = 9.0 / 16.0
FAR = -1.0 / 16.0
F32 = jnp.float32
BF16 = jnp.bfloat16
HIGHEST = lax.Precision.HIGHEST
VMEM_LIMIT = 40 * 1024 * 1024


def up8(n):
    return -(-n // 8) * 8


class Sizes:
    def __init__(self, nz, nx, ny, gz, gx, gy):
        self.nz, self.nx, self.ny = nz, nx, ny
        self.gz, self.gx, self.gy = gz, gx, gy
        self.z1, self.x1, self.y1 = nz // 2, nx // 2, ny // 2
        self.z2, self.x2, self.y2 = nz // 4, nx // 4, ny // 4
        self.cz = [nz * gz >> l for l in range(4)]
        self.cx = [nx * gx >> l for l in range(4)]
        self.cy = [ny * gy >> l for l in range(4)]
        self.planes = self.z1 + 3
        self.zrows = up8(self.planes)
        self.rows1 = up8(self.x1 + 3)
        self.rows2 = up8(self.x2 + 5)
        self.wide1 = self.y1 + 3
        self.wide2 = self.y2 + 5
        self.tiles1 = -(-self.planes * self.wide1 // LANES)
        self.tiles2 = -(-self.cz[2] * self.wide2 // LANES)
        self.strip = R + 3
        self.per_tile = LANES // self.strip
        self.tiles_s = -(-TERMS * self.planes // self.per_tile)
        self.fine_tiles = -(-nz // (LANES // R))
        self.ext = nx + 2 * R


def restrict_circle(n):
    m = np.zeros((n // 2, n))
    for i in range(n // 2):
        for d, w in ((0, 1.0), (1, NEAR), (-1, NEAR), (3, FAR), (-3, FAR)):
            m[i, (2 * i + d) % n] += w
    return m


def prolong_circle(n):
    m = np.zeros((2 * n, n))
    for i in range(n):
        m[2 * i, i] += 1.0
        for d, w in ((0, NEAR), (1, NEAR), (-1, FAR), (2, FAR)):
            m[2 * i + 1, (i + d) % n] += w
    return m


def restrict_open(first_in, n_in, first_out, n_out):
    m = np.zeros((n_out, n_in))
    for i in range(n_out):
        for d, w in ((0, 1.0), (1, NEAR), (-1, NEAR), (3, FAR), (-3, FAR)):
            j = 2 * (first_out + i) + d - first_in
            if 0 <= j < n_in:
                m[i, j] = w
    return m


def padded(m, rows, columns):
    out = np.zeros((rows, columns), np.float32)
    out[: m.shape[0], : m.shape[1]] = m
    return out


def constants(s):
    c = {}
    c["ry1"] = padded(restrict_open(0, s.ny, -1, s.wide1).T, s.ny, LANES)
    c["rx1"] = padded(restrict_open(0, s.nx, -1, s.x1 + 3), up8(s.rows1), s.nx)
    c["ry2"] = padded(restrict_open(-1, s.wide1, -2, s.wide2).T, LANES, LANES)
    c["rx2"] = padded(restrict_open(-1, s.x1 + 3, -2, s.x2 + 5), s.rows2, s.rows1)

    def chain(n):
        p1 = prolong_circle(n[1])
        p2 = p1 @ prolong_circle(n[2])
        return p1, p2, p2 @ prolong_circle(n[3])

    x1, x2, x3 = chain(s.cx)
    c["px1"], c["px2"], c["px3"] = (m.astype(np.float32) for m in (x1, x2, x3))
    place = np.zeros((s.cx[2], s.rows2))
    for r in range(s.x2 + 5):
        place[(r - 2) % s.cx[2], r] += 1.0
    c["rx3"] = (restrict_circle(s.cx[2]) @ place).astype(np.float32)
    y1, y2, y3 = chain(s.cy)
    c["py1"], c["py2"], c["py3"] = (
        np.ascontiguousarray(m[: s.ny].T).astype(np.float32) for m in (y1, y2, y3)
    )
    c["ry3"] = np.ascontiguousarray(restrict_circle(s.cy[2]).T).astype(np.float32)
    z2 = prolong_circle(s.cz[2])
    z3 = z2 @ prolong_circle(s.cz[3])
    own = [(o - 1) % s.cz[1] for o in range(s.planes)]
    c["pz2"] = padded(z2[own], s.zrows, s.cz[2])
    c["pz3"] = padded(z3[own], s.zrows, s.cz[3])
    c["rz3"] = padded(restrict_circle(s.cz[2]), s.cz[3], LANES)
    return c


def halves(x):
    high = x.astype(BF16)
    return high, (x - high.astype(F32)).astype(BF16)


def dot(a, b):
    return jnp.dot(a, b, preferred_element_type=F32)


def exact_dot(a, b):
    return jnp.dot(a, b, preferred_element_type=F32, precision=HIGHEST)


def dot3(a, b_high, b_low):
    high, low = halves(a)
    return dot(high, b_high) + dot(low, b_high) + dot(high, b_low)


def lanes_of(shape):
    return lax.broadcasted_iota(jnp.int32, shape, len(shape) - 1)


def turn(x, by):
    by = by % x.shape[-1]
    return x if by == 0 else pltpu.roll(x, by, x.ndim - 1)


def packed(planes, wide, tiles):
    out = [None] * tiles

    def add(t, x):
        out[t] = x if out[t] is None else out[t] + x

    for k, x in enumerate(planes):
        t, at = divmod(k * wide, LANES)
        moved = turn(x, at)
        if at + wide <= LANES:
            add(t, moved)
        else:
            lane = lanes_of(x.shape)
            add(t, jnp.where(lane >= at, moved, 0.0))
            add(t + 1, jnp.where(lane < at, moved, 0.0))
    return out


def unpacked(tile, k, wide, shift):
    t, at = divmod(k * wide, LANES)
    x = tile(t)
    lane = lanes_of(x.shape)
    if at + wide > LANES:
        x = jnp.where(lane >= at, x, tile(t + 1))
    x = turn(x, shift - at)
    if shift + wide <= LANES:
        return jnp.where((lane >= shift) & (lane < shift + wide), x, 0.0)
    return jnp.where((lane >= shift) | (lane < shift + wide - LANES), x, 0.0)


def share_kernel(s, b_ref, ry1_ref, rx1_ref, m_ref, sl_ref, sr_ref, cl_ref, cr_ref, xr_ref):
    b = [b_ref[z] for z in range(s.nz)]
    planes = []
    for k in range(-1, s.z1 + 2):
        out = None
        for d, w in ((0, 1.0), (1, NEAR), (-1, NEAR), (3, FAR), (-3, FAR)):
            if 0 <= 2 * k + d < s.nz:
                term = b[2 * k + d] if d == 0 else b[2 * k + d] * w
                out = term if out is None else out + term
        planes.append(out)
    high, low = halves(jnp.concatenate(planes, axis=0))
    ry1 = ry1_ref[...].astype(BF16)
    rx1 = rx1_ref[...].astype(BF16)
    along = dot(high, ry1) + dot(low, ry1)
    shares = []
    for k in range(s.planes):
        high, low = halves(along[k * s.nx : (k + 1) * s.nx])
        shares.append(dot(rx1, high) + dot(rx1, low))
    for t, x in enumerate(packed(shares, s.wide1, s.tiles1)):
        m_ref[t] = x
    lane = lanes_of((s.nx, LANES))
    group = LANES // R
    for t in range(s.fine_tiles):
        left = right = None
        for g in range(min(group, s.nz - t * group)):
            x = b[t * group + g]
            first = turn(x, R * ((g + 1) % group))
            last = turn(x, R * g + R - s.ny)
            at_first = (lane >= R * ((g + 1) % group)) & (lane < R * ((g + 1) % group) + R)
            at_last = (lane >= R * g) & (lane < R * g + R)
            left = jnp.where(at_first, first, 0.0 if left is None else left)
            right = jnp.where(at_last, last, 0.0 if right is None else right)
        sl_ref[t] = left
        sr_ref[t] = right
        cl_ref[t, 0:R] = left[0:R]
        cl_ref[t, R : 2 * R] = left[s.nx - R :]
        cr_ref[t, 0:R] = right[0:R]
        cr_ref[t, R : 2 * R] = right[s.nx - R :]
    for z in range(s.nz):
        xr_ref[z, 0:R] = b[z][0:R]
        xr_ref[z, R : 2 * R] = b[z][s.nx - R :]


def matrix_kernel(s, w_ref, a_ref, px1, px2, px3, rx3, py1, py2, py3, ry3, pz2, pz3, rz3,
                  tap_ref, z_ref, y0h_ref, y0l_ref, y1h_ref, y1l_ref, y2h_ref, y2l_ref,
                  xah_ref, xal_ref, xbh_ref, xbl_ref):
    def spread(level, t):
        w = jnp.full((8, LANES), w_ref[level, t], F32)
        return (-0.5 / (w * w))[0:1, 0:1]

    def bell(c, d):
        d = jnp.abs(d)
        return jnp.where(d <= R, jnp.exp(c * d * d), 0.0)

    def scale(c, count=None):
        n = lanes_of((1, LANES)).astype(F32)
        if count is None:
            d, valid = n - R, n <= 2 * R
        else:
            d, valid = jnp.minimum(n, count - n), n < count
        return 1.0 / jnp.sqrt(jnp.sum(jnp.where(valid, jnp.exp(2.0 * c * d * d), 0.0), axis=1, keepdims=True))

    coef = [[spread(l, t) for t in range(TERMS)] for l in range(4)]
    unit = [[scale(coef[l][t]) for t in range(TERMS)] for l in range(3)]

    def rows_of(shape):
        return lax.broadcasted_iota(jnp.int32, shape, 0)

    def circle(n, shape, first_row, first_lane, c, u):
        d = ((rows_of(shape) + first_row) - (lanes_of(shape) + first_lane)) & (n - 1)
        d = d.astype(F32)
        return (bell(c, d) + bell(c, n - d)) * u

    def full_circle(n, shape, c, u):
        d = ((rows_of(shape) - lanes_of(shape)) & (n - 1)).astype(F32)
        d = jnp.minimum(d, n - d)
        return jnp.exp(c * d * d) * u

    def put(high_ref, low_ref, at, x):
        high, low = halves(x)
        high_ref[:, at : at + x.shape[1]] = high
        low_ref[:, at : at + x.shape[1]] = low

    def by_term(shape, wide, values):
        t = lanes_of(shape)
        return jnp.where(t < wide, values[0], jnp.where(t < 2 * wide, values[1], values[2]))

    d = lanes_of((1, LANES)).astype(F32)
    for t in range(TERMS):
        g0 = bell(coef[0][t], d) * unit[0][t]
        g1 = bell(coef[1][t], d) * unit[1][t]
        tap_ref[t : t + 1] = g0
        tap_ref[TERMS + t : TERMS + t + 1] = g0 * a_ref[0, t]
        tap_ref[2 * TERMS + t : 2 * TERMS + t + 1] = g1 * (a_ref[1, t] * 0.25)
    for t in range(TERMS):
        shape = (2 * LANES, s.ny)
        i = rows_of(shape)
        cell = jnp.where(i < s.ny, i, jnp.where(i < s.ny + R, i - s.ny - R, i - R))
        g = bell(coef[0][t], (cell - lanes_of(shape)).astype(F32)) * unit[0][t]
        put(y0h_ref, y0l_ref, t * s.ny, jnp.where(i < s.ny + 2 * R, g, 0.0))
    for t in range(TERMS):
        shape = (LANES, s.cy[1])
        g = circle(s.cy[1], shape, -(R + 1), 0, coef[1][t], unit[1][t])
        g = jnp.where(rows_of(shape) < s.y1 + 3 + 2 * R, g, 0.0)
        put(y1h_ref, y1l_ref, t * s.ny, exact_dot(g, py1[...]))
        g = circle(s.cy[2], (s.cy[2], s.cy[2]), 0, 0, coef[2][t], unit[2][t])
        put(y2h_ref, y2l_ref, t * s.ny, exact_dot(g, py2[...]))
        u = scale(coef[3][t], s.cy[3])
        g = full_circle(s.cy[3], (s.cy[3], s.cy[3]), coef[3][t], u)
        put(y2h_ref, y2l_ref, (TERMS + t) * s.ny, exact_dot(exact_dot(ry3[...], g), py3[...]))
    wide = s.rows1
    shape = (s.cx[1], TERMS * wide)
    lane = lanes_of(shape)
    column = lane - jnp.where(lane < wide, 0, jnp.where(lane < 2 * wide, wide, 2 * wide))
    d = ((rows_of(shape) - column + 1) & (s.cx[1] - 1)).astype(F32)
    c = by_term(shape, wide, coef[1])
    g = (bell(c, d) + bell(c, s.cx[1] - d)) * by_term(shape, wide, unit[1])
    put(xah_ref, xal_ref, 0, exact_dot(px1[...], jnp.where(column < s.x1 + 3, g, 0.0)))
    wide = s.rows2
    shape = (s.cx[2], TERMS * wide)
    lane = lanes_of(shape)
    column = lane - jnp.where(lane < wide, 0, jnp.where(lane < 2 * wide, wide, 2 * wide))
    d = ((rows_of(shape) - column + 2) & (s.cx[2] - 1)).astype(F32)
    c = by_term(shape, wide, coef[2])
    g = (bell(c, d) + bell(c, s.cx[2] - d)) * by_term(shape, wide, unit[2])
    put(xbh_ref, xbl_ref, 0, exact_dot(px2[...], jnp.where(column < s.x2 + 5, g, 0.0)))
    for t in range(TERMS):
        u = scale(coef[3][t], s.cx[3])
        g = full_circle(s.cx[3], (s.cx[3], s.cx[3]), coef[3][t], u)
        put(xbh_ref, xbl_ref, (TERMS + t) * wide, exact_dot(px3[...], exact_dot(g, rx3[...])))
    for t in range(TERMS):
        g = circle(s.cz[2], (s.cz[2], LANES), 0, 0, coef[2][t], unit[2][t])
        g = exact_dot(pz2[...], g) * (a_ref[2, t] * 0.0625)
        z_ref[t * s.zrows : (t + 1) * s.zrows] = g
        u = scale(coef[3][t], s.cz[3])
        g = full_circle(s.cz[3], (s.cz[3], s.cz[3]), coef[3][t], u)
        g = exact_dot(exact_dot(pz3[...], g), rz3[...]) * (a_ref[3, t] * 0.015625)
        z_ref[(TERMS + t) * s.zrows : (TERMS + t + 1) * s.zrows] = g


def near_kernel(s, tap_ref, b_ref, xlo_ref, xhi_ref, sl_ref, sr_ref, c_lo_l, c_lo_r, c_hi_l, c_hi_r,
                y0h_ref, y0l_ref, own_ref, down_ref, up_ref, eh_ref, el_ref, u_ref, v_ref):
    ext = s.ext
    group = LANES // R
    lane = lanes_of((ext, LANES))
    for t in range(s.fine_tiles):
        left = jnp.concatenate([c_lo_l[t, R : 2 * R], sl_ref[t], c_hi_l[t, 0:R]], axis=0)
        right = jnp.concatenate([c_lo_r[t, R : 2 * R], sr_ref[t], c_hi_r[t, 0:R]], axis=0)
        for g in range(min(group, s.nz - t * group)):
            z = t * group + g
            strips = jnp.where((lane >= R * g) & (lane < R * g + R), left, right)
            strips = turn(strips, -R * g)
            main = jnp.concatenate([xlo_ref[z, R : 2 * R], b_ref[z], xhi_ref[z, 0:R]], axis=0)
            for at, x in ((0, main), (LANES, strips)):
                high, low = halves(x)
                eh_ref[z * ext : (z + 1) * ext, at : at + LANES] = high
                el_ref[z * ext : (z + 1) * ext, at : at + LANES] = low
    step = 4 * ext
    y0h, y0l = y0h_ref[...], y0l_ref[...]
    for at in range(0, s.nz * ext, step):
        high, low = eh_ref[at : at + step], el_ref[at : at + step]
        u = dot(high, y0h) + dot(low, y0h) + dot(high, y0l)
        for t in range(TERMS):
            for q in range(4):
                u_ref[t, at // ext + q] = u[q * ext : (q + 1) * ext, t * s.ny : (t + 1) * s.ny]

    def cross(z, _):
        for t in range(TERMS):
            v = u_ref[t, z, R : R + s.nx] * tap_ref[t, 0]
            for d in range(1, R + 1):
                v += (u_ref[t, z, R + d : R + d + s.nx] + u_ref[t, z, R - d : R - d + s.nx]) * tap_ref[t, d]
            v_ref[t, z] = v
        return 0

    lax.fori_loop(0, s.nz, cross, 0)

    def depth(r, _):
        rows = pl.ds(pl.multiple_of(r * 8, 8), 8)
        taps = [[tap_ref[TERMS + t, d] for d in range(R + 1)] for t in range(TERMS)]
        for first in range(-R, s.nz + R, R):
            acc = [None] * R
            for t in range(TERMS):
                for z in range(max(0, first - R), min(s.nz, first + 2 * R)):
                    v = v_ref[t, z, rows]
                    for o in range(R):
                        d = abs(first + o - z)
                        if d <= R:
                            term = v * taps[t][d]
                            acc[o] = term if acc[o] is None else acc[o] + term
            for o in range(R):
                if first < 0:
                    down_ref[o, rows] = acc[o]
                elif first >= s.nz:
                    up_ref[o, rows] = acc[o]
                else:
                    own_ref[first + o, rows] = acc[o]
        return 0

    lax.fori_loop(0, s.nx // 8, depth, 0)


def depth_kernel(s, tap_ref, *refs):
    m_refs = refs[: s.gz]
    ry2_ref, rx2_ref, w_ref, down_ref, up_ref, c2_ref, c_ref = refs[s.gz :]
    n = s.cz[1]
    parts = [[] for _ in range(n)]
    for b in range(s.gz):
        for k in range(s.planes):
            parts[(b * s.z1 + k - 1) % n].append((b, k))
    for z in range(n):
        out = None
        for b, k in parts[z]:
            x = unpacked(lambda t, b=b: m_refs[b][t], k, s.wide1, 0)
            out = x if out is None else out + x
        c_ref[z] = out
    lane = lanes_of((s.rows1, LANES))
    down = [jnp.zeros((s.rows1, LANES), F32)] * s.tiles_s
    up = list(down)
    for o in range(s.planes):
        sums = [c_ref[(o - 1) % n]]
        sums += [c_ref[(o - 1 + d) % n] + c_ref[(o - 1 - d) % n] for d in range(1, R + 1)]
        for t in range(TERMS):
            x = sums[0] * tap_ref[2 * TERMS + t, 0]
            for d in range(1, R + 1):
                x += sums[d] * tap_ref[2 * TERMS + t, d]
            k = t * s.planes + o
            w_ref[k] = x
            tile, slot = divmod(k, s.per_tile)
            at = slot * s.strip
            here = (lane >= at) & (lane < at + s.strip)
            down[tile] = jnp.where(here, turn(x, at), down[tile])
            up[tile] = jnp.where(here, turn(x, at - (s.wide1 - s.strip)), up[tile])
    coarse = []
    for j in range(s.cz[2]):
        at = lambda d: c_ref[(2 * j + d) % n]
        coarse.append(at(0) + NEAR * (at(1) + at(-1)) + FAR * (at(3) + at(-3)))
    high, low = halves(jnp.concatenate(coarse, axis=0))
    ry2 = ry2_ref[...].astype(BF16)
    rx2 = rx2_ref[...].astype(BF16)
    along = dot(high, ry2) + dot(low, ry2)
    shares = []
    for j in range(s.cz[2]):
        high, low = halves(along[j * s.rows1 : (j + 1) * s.rows1])
        shares.append(dot(rx2, high) + dot(rx2, low))
    for t in range(s.tiles_s):
        down_ref[t * s.rows1 : (t + 1) * s.rows1] = down[t]
        up_ref[t * s.rows1 : (t + 1) * s.rows1] = up[t]
    base = s.tiles_s * s.rows1
    for t, x in enumerate(packed(shares, s.wide2, s.tiles2)):
        rows = slice(t * s.rows2, (t + 1) * s.rows2)
        c2_ref[rows] = x
        for ref in (down_ref, up_ref):
            ref[base + t * s.rows2 : base + (t + 1) * s.rows2] = x


def along_kernel(s, z_ref, w_ref, *refs):
    c2_refs = refs[: s.gy]
    (y1h_ref, y1l_ref, y2h_ref, y2l_ref, xah_ref, xal_ref, xbh_ref, xbl_ref,
     *g_refs, yb_ref) = refs[s.gy :]
    base = s.tiles_s * s.rows1
    lane = lanes_of((s.rows1, LANES))
    above, below = c2_refs[1], c2_refs[-1]
    end = s.y1 + R
    along = []
    for t in range(TERMS):
        cells = []
        for o in range(s.planes):
            k = t * s.planes + o
            tile, slot = divmod(k, s.per_tile)
            rows = slice(tile * s.rows1, (tile + 1) * s.rows1)
            at = slot * s.strip
            x = turn(w_ref[k], R)
            x += jnp.where(lane < s.strip, turn(below[rows], -at), 0.0)
            x += jnp.where((lane >= end) & (lane < end + s.strip), turn(above[rows], end - at), 0.0)
            cells.append(x)
        columns = slice(t * s.ny, (t + 1) * s.ny)
        along.append(dot3(jnp.concatenate(cells, axis=0), y1h_ref[:, columns], y1l_ref[:, columns]))
    cells = []
    for j in range(s.cz[2]):
        out = None
        for b in range(s.gy):
            first = 0 if b == 0 or c2_refs[b].shape[0] == s.tiles2 * s.rows2 else base
            tile = lambda t, b=b, f=first: c2_refs[b][f + t * s.rows2 : f + (t + 1) * s.rows2]
            x = unpacked(tile, j, s.wide2, (b * s.y2 - 2) % LANES)
            out = x if out is None else out + x
        cells.append(out)
    yb = dot3(jnp.concatenate(cells, axis=0), y2h_ref[...], y2l_ref[...])
    for j in range(s.cz[2]):
        for q in range(2 * TERMS):
            yb_ref[q, j] = yb[j * s.rows2 : (j + 1) * s.rows2, q * s.ny : (q + 1) * s.ny]
    xah, xal, xbh, xbl = xah_ref[...], xal_ref[...], xbh_ref[...], xbl_ref[...]
    for o in range(s.planes):
        rows = slice(o * s.rows1, (o + 1) * s.rows1)
        near_high, near_low = halves(jnp.concatenate([a[rows] for a in along], axis=0))
        far = []
        for q in range(2 * TERMS):
            x = yb_ref[q, 0] * z_ref[q * s.zrows + o, 0]
            for j in range(1, s.cz[2]):
                x += yb_ref[q, j] * z_ref[q * s.zrows + o, j]
            far.append(x)
        far_high, far_low = halves(jnp.concatenate(far, axis=0))
        g = dot(xah, near_high) + dot(xal, near_high) + dot(xah, near_low)
        g += dot(xbh, far_high) + dot(xbl, far_high) + dot(xbh, far_low)
        for shift, ref in enumerate(g_refs):
            ref[o] = g[shift * s.nx : (shift + 1) * s.nx]


def last_kernel(s, own_ref, low_ref, high_ref, *refs):
    g_refs, out_ref = refs[:-1], refs[-1]
    level = []
    for o in range(s.planes):
        x = g_refs[0][o]
        for ref in g_refs[1:]:
            x += ref[o]
        level.append(x)
    for z in range(s.nz):
        m = z // 2 + 1
        if z % 2 == 0:
            x = level[m]
        else:
            x = NEAR * (level[m] + level[m + 1]) + FAR * (level[m - 1] + level[m + 2])
        x += own_ref[z]
        if z < R:
            x += low_ref[z]
        if z >= s.nz - R:
            x += high_ref[z - (s.nz - R)]
        out_ref[z] = x


def call(kernel, name, operands, out_shapes, scalars=(), scratch=(), flops=0):
    def spec(i):
        return pl.BlockSpec(memory_space=pltpu.SMEM if i in scalars else pltpu.VMEM)

    moved = sum(x.size * x.dtype.itemsize for x in operands)
    moved += sum(int(np.prod(x.shape)) * x.dtype.itemsize for x in out_shapes)
    return pl.pallas_call(
        kernel,
        name=name,
        out_shape=out_shapes,
        in_specs=[spec(i) for i in range(len(operands))],
        out_specs=[pl.BlockSpec(memory_space=pltpu.VMEM)] * len(out_shapes),
        scratch_shapes=list(scratch),
        compiler_params=pltpu.CompilerParams(vmem_limit_bytes=VMEM_LIMIT),
        cost_estimate=pl.CostEstimate(flops=flops, bytes_accessed=moved, transcendentals=0),
    )(*operands)


def arrays(*shapes, dtype=F32):
    return [jax.ShapeDtypeStruct(shape, dtype) for shape in shapes]


def fetch(x, **shifts):
    names = tuple(shifts)
    sizes = [lax.axis_size(n) for n in names]
    pairs = []
    for here in np.ndindex(*sizes):
        there = [(h + shifts[n]) % size for h, n, size in zip(here, names, sizes)]
        pairs.append((int(np.ravel_multi_index(there, sizes)), int(np.ravel_multi_index(here, sizes))))
    return lax.ppermute(x, names if len(names) > 1 else names[0], pairs)


def shards(charges, widths, amplitudes):
    s = Sizes(*charges.shape, lax.axis_size("gz"), lax.axis_size("gx"), lax.axis_size("gy"))
    c = {k: jnp.asarray(v) for k, v in constants(s).items()}
    strips = (s.fine_tiles, s.nx, LANES)
    corners = (s.fine_tiles, 2 * R, LANES)
    share, to_low, to_high, corner_low, corner_high, edge_rows = call(
        functools.partial(share_kernel, s), "share",
        [charges, c["ry1"], c["rx1"]],
        arrays((s.tiles1, s.rows1, LANES), strips, strips, corners, corners, (s.nz, 2 * R, s.ny)),
        flops=10**8,
    )
    shares = [share] + [fetch(share, gz=b) for b in range(1, s.gz)]
    left, right = fetch(to_high, gy=-1), fetch(to_low, gy=1)
    x_shifts = (1,) if s.gx == 2 else (-1, 1)
    rows, lefts, rights = [], [], []
    for dx in x_shifts:
        rows.append(fetch(edge_rows, gx=dx))
        lefts.append(fetch(corner_high, gx=dx, gy=-1))
        rights.append(fetch(corner_low, gx=dx, gy=1))

    two = lambda *shape: arrays(shape, shape, dtype=BF16)
    taps, z_taps, y0h, y0l, y1h, y1l, y2h, y2l, xah, xal, xbh, xbl = call(
        functools.partial(matrix_kernel, s), "matrices",
        [widths, amplitudes] + [c[k] for k in "px1 px2 px3 rx3 py1 py2 py3 ry3 pz2 pz3 rz3".split()],
        arrays((16, LANES), (2 * TERMS * s.zrows, LANES))
        + two(2 * LANES, TERMS * s.ny) + two(LANES, TERMS * s.ny) + two(s.cy[2], 2 * TERMS * s.ny)
        + two(s.cx[0], TERMS * s.rows1) + two(s.cx[0], 2 * TERMS * s.rows2),
        scalars=(0, 1), flops=10**8,
    )
    brick = (s.nz, s.nx, s.ny)
    side = (R, s.nx, s.ny)
    near, near_down, near_up = call(
        functools.partial(near_kernel, s), "near",
        [taps, charges, rows[0], rows[-1], left, right, lefts[0], rights[0], lefts[-1], rights[-1], y0h, y0l],
        arrays(brick, side, side), scalars=(0,),
        scratch=[
            pltpu.VMEM((s.nz * s.ext, 2 * LANES), BF16), pltpu.VMEM((s.nz * s.ext, 2 * LANES), BF16),
            pltpu.VMEM((TERMS, s.nz, s.ext, s.ny), F32), pltpu.VMEM((TERMS,) + brick, F32),
        ],
        flops=3 * 10**9,
    )
    base = s.tiles_s * s.rows1
    size2 = s.tiles2 * s.rows2
    waves, to_low, to_high, coarse = call(
        functools.partial(depth_kernel, s), "depth",
        [taps] + shares + [c["ry2"], c["rx2"]],
        arrays((TERMS * s.planes, s.rows1, LANES), (base + size2, LANES), (base + size2, LANES), (size2, LANES)),
        scalars=(0,), scratch=[pltpu.VMEM((s.cz[1], s.rows1, LANES), F32)], flops=10**8,
    )
    coarses = [coarse]
    for b in range(1, s.gy):
        coarses.append(fetch({1: to_low, s.gy - 1: to_high}.get(b, coarse), gy=b))
    near_low, near_high = fetch(near_up, gz=-1), fetch(near_down, gz=1)
    parts = call(
        functools.partial(along_kernel, s), "along",
        [z_taps, waves] + coarses + [y1h, y1l, y2h, y2l, xah, xal, xbh, xbl],
        arrays(*[(s.planes, s.nx, s.ny)] * s.gx), scalars=(0,),
        scratch=[pltpu.VMEM((2 * TERMS, s.cz[2], s.rows2, s.ny), F32)], flops=10**9,
    )
    parts = [parts[0]] + [fetch(parts[dx], gx=-dx) for dx in range(1, s.gx)]
    (out,) = call(
        functools.partial(last_kernel, s), "last",
        [near, near_low, near_high] + list(parts), arrays(brick), flops=10**7,
    )
    return out


def solution(mesh):
    placed = (P("gz", "gx", "gy"), P(), P())
    return jax.shard_map(
        shards, mesh=mesh, in_specs=placed, out_specs=P("gz", "gx", "gy"), check_vma=False
    )
```

```python
import functools

import jax
import jax.numpy as jnp
import numpy as np
from jax import lax
from jax.experimental import pallas as pl
from jax.experimental.pallas import tpu as pltpu
from jax.sharding import PartitionSpec as P

R = 8
TERMS = 3
LANES = 128
NEAR = 9.0 / 16.0
FAR = -1.0 / 16.0
F32 = jnp.float32
BF16 = jnp.bfloat16
HIGHEST = lax.Precision.HIGHEST
VMEM_LIMIT = 40 * 1024 * 1024


def up8(n):
    return -(-n // 8) * 8


class Sizes:
    def __init__(self, nz, nx, ny, gz, gx, gy):
        self.nz, self.nx, self.ny = nz, nx, ny
        self.gz, self.gx, self.gy = gz, gx, gy
        self.z1, self.x1, self.y1 = nz // 2, nx // 2, ny // 2
        self.z2, self.x2, self.y2 = nz // 4, nx // 4, ny // 4
        self.cz = [nz * gz >> l for l in range(4)]
        self.cx = [nx * gx >> l for l in range(4)]
        self.cy = [ny * gy >> l for l in range(4)]
        self.planes = self.z1 + 3
        self.zrows = up8(self.planes)
        self.rows1 = up8(self.x1 + 3)
        self.rows2 = up8(self.x2 + 5)
        self.wide1 = self.y1 + 3
        self.wide2 = self.y2 + 5
        self.tiles1 = -(-self.planes * self.wide1 // LANES)
        self.tiles2 = -(-self.cz[2] * self.wide2 // LANES)
        self.strip = R + 3
        self.per_tile = LANES // self.strip
        self.tiles_s = -(-TERMS * self.planes // self.per_tile)
        self.fine_tiles = -(-nz // (LANES // R))
        self.ext = nx + 2 * R


def restrict_circle(n):
    m = np.zeros((n // 2, n))
    for i in range(n // 2):
        for d, w in ((0, 1.0), (1, NEAR), (-1, NEAR), (3, FAR), (-3, FAR)):
            m[i, (2 * i + d) % n] += w
    return m


def prolong_circle(n):
    m = np.zeros((2 * n, n))
    for i in range(n):
        m[2 * i, i] += 1.0
        for d, w in ((0, NEAR), (1, NEAR), (-1, FAR), (2, FAR)):
            m[2 * i + 1, (i + d) % n] += w
    return m


def restrict_open(first_in, n_in, first_out, n_out):
    m = np.zeros((n_out, n_in))
    for i in range(n_out):
        for d, w in ((0, 1.0), (1, NEAR), (-1, NEAR), (3, FAR), (-3, FAR)):
            j = 2 * (first_out + i) + d - first_in
            if 0 <= j < n_in:
                m[i, j] = w
    return m


def padded(m, rows, columns):
    out = np.zeros((rows, columns), np.float32)
    out[: m.shape[0], : m.shape[1]] = m
    return out


def constants(s):
    c = {}
    c["ry2"] = padded(restrict_open(-1, s.wide1, -2, s.wide2).T, LANES, LANES)
    c["rx2"] = padded(restrict_open(-1, s.x1 + 3, -2, s.x2 + 5), s.rows2, s.rows1)

    def chain(n):
        p1 = prolong_circle(n[1])
        p2 = p1 @ prolong_circle(n[2])
        return p1, p2, p2 @ prolong_circle(n[3])

    x1, x2, x3 = chain(s.cx)
    c["px1"], c["px2"], c["px3"] = (m.astype(np.float32) for m in (x1, x2, x3))
    place = np.zeros((s.cx[2], s.rows2))
    for r in range(s.x2 + 5):
        place[(r - 2) % s.cx[2], r] += 1.0
    c["rx3"] = (restrict_circle(s.cx[2]) @ place).astype(np.float32)
    y1, y2, y3 = chain(s.cy)
    c["py1"], c["py2"], c["py3"] = (
        np.ascontiguousarray(m[: s.ny].T).astype(np.float32) for m in (y1, y2, y3)
    )
    c["ry3"] = np.ascontiguousarray(restrict_circle(s.cy[2]).T).astype(np.float32)
    z2 = prolong_circle(s.cz[2])
    z3 = z2 @ prolong_circle(s.cz[3])
    own = [(o - 1) % s.cz[1] for o in range(s.planes)]
    c["pz2"] = padded(z2[own], s.zrows, s.cz[2])
    c["pz3"] = padded(z3[own], s.zrows, s.cz[3])
    c["rz3"] = padded(restrict_circle(s.cz[2]), s.cz[3], LANES)
    return c


def halves(x):
    high = x.astype(BF16)
    return high, (x - high.astype(F32)).astype(BF16)


def dot(a, b):
    return jnp.dot(a, b, preferred_element_type=F32)


def exact_dot(a, b):
    return jnp.dot(a, b, preferred_element_type=F32, precision=HIGHEST)


def dot3(a, b_high, b_low):
    high, low = halves(a)
    return dot(high, b_high) + dot(low, b_high) + dot(high, b_low)


def lanes_of(shape):
    return lax.broadcasted_iota(jnp.int32, shape, len(shape) - 1)


def turn(x, by):
    by = by % x.shape[-1]
    return x if by == 0 else pltpu.roll(x, by, x.ndim - 1)


def packed(planes, wide, tiles):
    out = [None] * tiles

    def add(t, x):
        out[t] = x if out[t] is None else out[t] + x

    for k, x in enumerate(planes):
        t, at = divmod(k * wide, LANES)
        moved = turn(x, at)
        if at + wide <= LANES:
            add(t, moved)
        else:
            lane = lanes_of(x.shape)
            add(t, jnp.where(lane >= at, moved, 0.0))
            add(t + 1, jnp.where(lane < at, moved, 0.0))
    return out


def unpacked(tile, k, wide, shift):
    t, at = divmod(k * wide, LANES)
    x = tile(t)
    lane = lanes_of(x.shape)
    if at + wide > LANES:
        x = jnp.where(lane >= at, x, tile(t + 1))
    x = turn(x, shift - at)
    if shift + wide <= LANES:
        return jnp.where((lane >= shift) & (lane < shift + wide), x, 0.0)
    return jnp.where((lane >= shift) | (lane < shift + wide - LANES), x, 0.0)


def open_restriction(shape, in_dim, first_out, n_out):
    i = lax.broadcasted_iota(jnp.int32, shape, in_dim)
    o = lax.broadcasted_iota(jnp.int32, shape, 1 - in_dim)
    d = jnp.abs(i - 2 * (o + first_out))
    w = jnp.where(d == 0, 1.0, jnp.where(d == 1, NEAR, jnp.where(d == 3, FAR, 0.0)))
    return jnp.where(o < n_out, w, 0.0).astype(BF16)


def share_kernel(s, b_ref, m_ref, xr_ref):
    b = [b_ref[z] for z in range(s.nz)]
    planes = []
    for k in range(-1, s.z1 + 2):
        out = None
        for d, w in ((0, 1.0), (1, NEAR), (-1, NEAR), (3, FAR), (-3, FAR)):
            if 0 <= 2 * k + d < s.nz:
                term = b[2 * k + d] if d == 0 else b[2 * k + d] * w
                out = term if out is None else out + term
        planes.append(out)
    high, low = halves(jnp.concatenate(planes, axis=0))
    ry1 = open_restriction((s.ny, LANES), 0, -1, s.wide1)
    rx1 = open_restriction((s.rows1, s.nx), 1, -1, s.x1 + 3)
    along = dot(high, ry1) + dot(low, ry1)
    shares = []
    for k in range(s.planes):
        high, low = halves(along[k * s.nx : (k + 1) * s.nx])
        shares.append(dot(rx1, high) + dot(rx1, low))
    for t, x in enumerate(packed(shares, s.wide1, s.tiles1)):
        m_ref[t] = x
    for z in range(s.nz):
        xr_ref[z, 0:R] = b[z][0:R]
        xr_ref[z, R : 2 * R] = b[z][s.nx - R :]


def extended(b_ref, lo_ref, hi_ref, z):
    return jnp.concatenate([lo_ref[z, R : 2 * R], b_ref[z], hi_ref[z, 0:R]], axis=0)


def strip_kernel(s, b_ref, lo_ref, hi_ref, first_ref, last_ref):
    lane = lanes_of((s.ext, LANES))
    group = LANES // R
    for t in range(s.fine_tiles):
        first = last = jnp.zeros((s.ext, LANES), F32)
        for g in range(min(group, s.nz - t * group)):
            x = extended(b_ref, lo_ref, hi_ref, t * group + g)
            at = R * ((g + 1) % group)
            first = jnp.where((lane >= at) & (lane < at + R), turn(x, at), first)
            at = R * g
            last = jnp.where((lane >= at) & (lane < at + R), turn(x, at + R - s.ny), last)
        first_ref[t] = first
        last_ref[t] = last


def rows_of(shape):
    return lax.broadcasted_iota(jnp.int32, shape, 0)


def spread(w_ref, level, t):
    w = jnp.full((8, LANES), w_ref[level, t], F32)
    return (-0.5 / (w * w))[0:1, 0:1]


def bell(c, d):
    d = jnp.abs(d)
    return jnp.where(d <= R, jnp.exp(c * d * d), 0.0)


def scale(c, count=None):
    n = lanes_of((1, LANES)).astype(F32)
    if count is None:
        d, valid = n - R, n <= 2 * R
    else:
        d, valid = jnp.minimum(n, count - n), n < count
    return 1.0 / jnp.sqrt(jnp.sum(jnp.where(valid, jnp.exp(2.0 * c * d * d), 0.0), axis=1, keepdims=True))


def put(high_ref, low_ref, at, x):
    high, low = halves(x)
    high_ref[:, at : at + x.shape[1]] = high
    low_ref[:, at : at + x.shape[1]] = low


def tap_kernel(s, w_ref, a_ref, tap_ref, y0h_ref, y0l_ref):
    coef = [[spread(w_ref, l, t) for t in range(TERMS)] for l in range(2)]
    unit = [[scale(coef[l][t]) for t in range(TERMS)] for l in range(2)]
    d = lanes_of((1, LANES)).astype(F32)
    for t in range(TERMS):
        g0 = bell(coef[0][t], d) * unit[0][t]
        g1 = bell(coef[1][t], d) * unit[1][t]
        tap_ref[t : t + 1] = g0
        tap_ref[TERMS + t : TERMS + t + 1] = g0 * a_ref[0, t]
        tap_ref[2 * TERMS + t : 2 * TERMS + t + 1] = g1 * (a_ref[1, t] * 0.25)
    for t in range(TERMS):
        shape = (2 * LANES, s.ny)
        i = rows_of(shape)
        cell = jnp.where(i < s.ny, i, jnp.where(i < s.ny + R, i - s.ny - R, i - R))
        g = bell(coef[0][t], (cell - lanes_of(shape)).astype(F32)) * unit[0][t]
        put(y0h_ref, y0l_ref, t * s.ny, jnp.where(i < s.ny + 2 * R, g, 0.0))


def matrix_kernel(s, w_ref, a_ref, px1, px2, px3, rx3, py1, py2, py3, ry3, pz2, pz3, rz3, _,
                  z_ref, y1h_ref, y1l_ref, y2h_ref, y2l_ref, xh_ref, xl_ref):
    coef = [[spread(w_ref, l, t) for t in range(TERMS)] for l in range(4)]
    unit = [[scale(coef[l][t]) for t in range(TERMS)] for l in range(3)]

    def circle(n, shape, first_row, first_lane, c, u):
        d = ((rows_of(shape) + first_row) - (lanes_of(shape) + first_lane)) & (n - 1)
        d = d.astype(F32)
        return (bell(c, d) + bell(c, n - d)) * u

    def full_circle(n, shape, c, u):
        d = ((rows_of(shape) - lanes_of(shape)) & (n - 1)).astype(F32)
        d = jnp.minimum(d, n - d)
        return jnp.exp(c * d * d) * u

    def by_term(shape, wide, values):
        t = lanes_of(shape)
        return jnp.where(t < wide, values[0], jnp.where(t < 2 * wide, values[1], values[2]))

    for t in range(TERMS):
        shape = (LANES, s.cy[1])
        g = circle(s.cy[1], shape, -(R + 1), 0, coef[1][t], unit[1][t])
        g = jnp.where(rows_of(shape) < s.y1 + 3 + 2 * R, g, 0.0)
        put(y1h_ref, y1l_ref, t * s.ny, exact_dot(g, py1[...]))
        g = circle(s.cy[2], (s.cy[2], s.cy[2]), 0, 0, coef[2][t], unit[2][t])
        put(y2h_ref, y2l_ref, t * s.ny, exact_dot(g, py2[...]))
        u = scale(coef[3][t], s.cy[3])
        g = full_circle(s.cy[3], (s.cy[3], s.cy[3]), coef[3][t], u)
        put(y2h_ref, y2l_ref, (TERMS + t) * s.ny, exact_dot(exact_dot(ry3[...], g), py3[...]))
    wide = s.rows1
    shape = (s.cx[1], TERMS * wide)
    lane = lanes_of(shape)
    column = lane - jnp.where(lane < wide, 0, jnp.where(lane < 2 * wide, wide, 2 * wide))
    d = ((rows_of(shape) - column + 1) & (s.cx[1] - 1)).astype(F32)
    c = by_term(shape, wide, coef[1])
    g = (bell(c, d) + bell(c, s.cx[1] - d)) * by_term(shape, wide, unit[1])
    put(xh_ref, xl_ref, 0, exact_dot(px1[...], jnp.where(column < s.x1 + 3, g, 0.0)))
    wide = s.rows2
    shape = (s.cx[2], TERMS * wide)
    lane = lanes_of(shape)
    column = lane - jnp.where(lane < wide, 0, jnp.where(lane < 2 * wide, wide, 2 * wide))
    d = ((rows_of(shape) - column + 2) & (s.cx[2] - 1)).astype(F32)
    c = by_term(shape, wide, coef[2])
    g = (bell(c, d) + bell(c, s.cx[2] - d)) * by_term(shape, wide, unit[2])
    put(xh_ref, xl_ref, TERMS * s.rows1, exact_dot(px2[...], jnp.where(column < s.x2 + 5, g, 0.0)))
    for t in range(TERMS):
        u = scale(coef[3][t], s.cx[3])
        g = full_circle(s.cx[3], (s.cx[3], s.cx[3]), coef[3][t], u)
        put(xh_ref, xl_ref, TERMS * s.rows1 + (TERMS + t) * wide, exact_dot(px3[...], exact_dot(g, rx3[...])))
    for t in range(TERMS):
        g = circle(s.cz[2], (s.cz[2], LANES), 0, 0, coef[2][t], unit[2][t])
        g = exact_dot(pz2[...], g) * (a_ref[2, t] * 0.0625)
        z_ref[t * s.zrows : (t + 1) * s.zrows] = g
        u = scale(coef[3][t], s.cz[3])
        g = full_circle(s.cz[3], (s.cz[3], s.cz[3]), coef[3][t], u)
        g = exact_dot(exact_dot(pz3[...], g), rz3[...]) * (a_ref[3, t] * 0.015625)
        z_ref[(TERMS + t) * s.zrows : (TERMS + t + 1) * s.zrows] = g


def near_kernel(s, tap_ref, b_ref, lo_ref, hi_ref, left_ref, right_ref, y0h_ref, y0l_ref,
                own_ref, down_ref, up_ref, eh_ref, el_ref, u_ref, v_ref):
    ext = s.ext
    group = LANES // R
    lane = lanes_of((ext, LANES))
    for z in range(s.nz):
        t, g = divmod(z, group)
        strips = jnp.where((lane >= R * g) & (lane < R * g + R), left_ref[t], right_ref[t])
        for at, x in ((0, extended(b_ref, lo_ref, hi_ref, z)), (LANES, turn(strips, -R * g))):
            high, low = halves(x)
            eh_ref[z * ext : (z + 1) * ext, at : at + LANES] = high
            el_ref[z * ext : (z + 1) * ext, at : at + LANES] = low
    step = 4 * ext
    y0h, y0l = y0h_ref[...], y0l_ref[...]
    for at in range(0, s.nz * ext, step):
        high, low = eh_ref[at : at + step], el_ref[at : at + step]
        u = dot(high, y0h) + dot(low, y0h) + dot(high, y0l)
        for t in range(TERMS):
            for q in range(4):
                u_ref[t, at // ext + q] = u[q * ext : (q + 1) * ext, t * s.ny : (t + 1) * s.ny]

    def cross(z, _):
        for t in range(TERMS):
            v = u_ref[t, z, R : R + s.nx] * tap_ref[t, 0]
            for d in range(1, R + 1):
                v += (u_ref[t, z, R + d : R + d + s.nx] + u_ref[t, z, R - d : R - d + s.nx]) * tap_ref[t, d]
            v_ref[t, z] = v
        return 0

    lax.fori_loop(0, s.nz, cross, 0)

    def depth(r, _):
        rows = pl.ds(pl.multiple_of(r * 8, 8), 8)
        taps = [[tap_ref[TERMS + t, d] for d in range(R + 1)] for t in range(TERMS)]
        for first in range(-R, s.nz + R, R):
            acc = [None] * R
            for t in range(TERMS):
                for z in range(max(0, first - R), min(s.nz, first + 2 * R)):
                    v = v_ref[t, z, rows]
                    for o in range(R):
                        d = abs(first + o - z)
                        if d <= R:
                            term = v * taps[t][d]
                            acc[o] = term if acc[o] is None else acc[o] + term
            for o in range(R):
                if first < 0:
                    down_ref[o, rows] = acc[o]
                elif first >= s.nz:
                    up_ref[o, rows] = acc[o]
                else:
                    own_ref[first + o, rows] = acc[o]
        return 0

    lax.fori_loop(0, s.nx // 8, depth, 0)


def depth_kernel(s, tap_ref, *refs):
    m_refs = refs[: s.gz]
    ry2_ref, rx2_ref, _, w_ref, down_ref, up_ref, c2_ref, c_ref = refs[s.gz :]
    n = s.cz[1]
    parts = [[] for _ in range(n)]
    for b in range(s.gz):
        for k in range(s.planes):
            parts[(b * s.z1 + k - 1) % n].append((b, k))
    for z in range(n):
        out = None
        for b, k in parts[z]:
            x = unpacked(lambda t, b=b: m_refs[b][t], k, s.wide1, 0)
            out = x if out is None else out + x
        c_ref[z] = out
    lane = lanes_of((s.rows1, LANES))
    down = [jnp.zeros((s.rows1, LANES), F32)] * s.tiles_s
    up = list(down)
    for o in range(s.planes):
        sums = [c_ref[(o - 1) % n]]
        sums += [c_ref[(o - 1 + d) % n] + c_ref[(o - 1 - d) % n] for d in range(1, R + 1)]
        for t in range(TERMS):
            x = sums[0] * tap_ref[2 * TERMS + t, 0]
            for d in range(1, R + 1):
                x += sums[d] * tap_ref[2 * TERMS + t, d]
            k = t * s.planes + o
            w_ref[k] = x
            tile, slot = divmod(k, s.per_tile)
            at = slot * s.strip
            here = (lane >= at) & (lane < at + s.strip)
            down[tile] = jnp.where(here, turn(x, at), down[tile])
            up[tile] = jnp.where(here, turn(x, at - (s.wide1 - s.strip)), up[tile])
    coarse = []
    for j in range(s.cz[2]):
        at = lambda d: c_ref[(2 * j + d) % n]
        coarse.append(at(0) + NEAR * (at(1) + at(-1)) + FAR * (at(3) + at(-3)))
    high, low = halves(jnp.concatenate(coarse, axis=0))
    ry2 = ry2_ref[...].astype(BF16)
    rx2 = rx2_ref[...].astype(BF16)
    along = dot(high, ry2) + dot(low, ry2)
    shares = []
    for j in range(s.cz[2]):
        high, low = halves(along[j * s.rows1 : (j + 1) * s.rows1])
        shares.append(dot(rx2, high) + dot(rx2, low))
    for t in range(s.tiles_s):
        down_ref[t * s.rows1 : (t + 1) * s.rows1] = down[t]
        up_ref[t * s.rows1 : (t + 1) * s.rows1] = up[t]
    base = s.tiles_s * s.rows1
    for t, x in enumerate(packed(shares, s.wide2, s.tiles2)):
        rows = slice(t * s.rows2, (t + 1) * s.rows2)
        c2_ref[rows] = x
        for ref in (down_ref, up_ref):
            ref[base + t * s.rows2 : base + (t + 1) * s.rows2] = x


def along_kernel(s, z_ref, w_ref, *refs):
    c2_refs = refs[: s.gy]
    y1h_ref, y1l_ref, y2h_ref, y2l_ref, d_ref, yb_ref = refs[s.gy :]
    base = s.tiles_s * s.rows1
    lane = lanes_of((s.rows1, LANES))
    above, below = c2_refs[1], c2_refs[-1]
    end = s.y1 + R
    for t in range(TERMS):
        cells = []
        for o in range(s.planes):
            k = t * s.planes + o
            tile, slot = divmod(k, s.per_tile)
            rows = slice(tile * s.rows1, (tile + 1) * s.rows1)
            at = slot * s.strip
            x = turn(w_ref[k], R)
            x += jnp.where(lane < s.strip, turn(below[rows], -at), 0.0)
            x += jnp.where((lane >= end) & (lane < end + s.strip), turn(above[rows], end - at), 0.0)
            cells.append(x)
        columns = slice(t * s.ny, (t + 1) * s.ny)
        out = dot3(jnp.concatenate(cells, axis=0), y1h_ref[:, columns], y1l_ref[:, columns])
        for o in range(s.planes):
            d_ref[t * s.rows1 : (t + 1) * s.rows1, o * s.ny : (o + 1) * s.ny] = out[o * s.rows1 : (o + 1) * s.rows1]
    cells = []
    for j in range(s.cz[2]):
        out = None
        for b in range(s.gy):
            first = 0 if b == 0 or c2_refs[b].shape[0] == s.tiles2 * s.rows2 else base
            tile = lambda t, b=b, f=first: c2_refs[b][f + t * s.rows2 : f + (t + 1) * s.rows2]
            x = unpacked(tile, j, s.wide2, (b * s.y2 - 2) % LANES)
            out = x if out is None else out + x
        cells.append(out)
    yb = dot3(jnp.concatenate(cells, axis=0), y2h_ref[...], y2l_ref[...])
    for j in range(s.cz[2]):
        for q in range(2 * TERMS):
            yb_ref[q, j] = yb[j * s.rows2 : (j + 1) * s.rows2, q * s.ny : (q + 1) * s.ny]
    for o in range(s.planes):
        for q in range(2 * TERMS):
            x = yb_ref[q, 0] * z_ref[q * s.zrows + o, 0]
            for j in range(1, s.cz[2]):
                x += yb_ref[q, j] * z_ref[q * s.zrows + o, j]
            at = TERMS * s.rows1 + q * s.rows2
            d_ref[at : at + s.rows2, o * s.ny : (o + 1) * s.ny] = x


def across(s, d_ref, xh_ref, xl_ref, shift):
    rows = slice(shift * s.nx, (shift + 1) * s.nx)
    high, low = halves(d_ref[...])
    return dot(xh_ref[rows], high) + dot(xl_ref[rows], high) + dot(xh_ref[rows], low)


def away_kernel(s, d_ref, xh_ref, xl_ref, *g_refs):
    for shift, ref in enumerate(g_refs):
        ref[...] = across(s, d_ref, xh_ref, xl_ref, shift + 1)


def prolonged(s, level, z):
    m = z // 2 + 1
    if z % 2 == 0:
        return level[m]
    return NEAR * (level[m] + level[m + 1]) + FAR * (level[m - 1] + level[m + 2])


def home_kernel(s, d_ref, xh_ref, xl_ref, own_ref, low_ref, high_ref, out_ref):
    g = across(s, d_ref, xh_ref, xl_ref, 0)
    level = [g[:, o * s.ny : (o + 1) * s.ny] for o in range(s.planes)]
    for z in range(s.nz):
        x = prolonged(s, level, z) + own_ref[z]
        if z < R:
            x += low_ref[z]
        if z >= s.nz - R:
            x += high_ref[z - (s.nz - R)]
        out_ref[z] = x


def last_kernel(s, home_ref, *refs):
    g_refs, out_ref = refs[:-1], refs[-1]
    level = []
    for o in range(s.planes):
        columns = slice(o * s.ny, (o + 1) * s.ny)
        x = g_refs[0][:, columns]
        for ref in g_refs[1:]:
            x += ref[:, columns]
        level.append(x)
    for z in range(s.nz):
        out_ref[z] = home_ref[z] + prolonged(s, level, z)


def call(kernel, name, operands, out_shapes, scalars=(), after=(), scratch=(), flops=0):
    operands = list(operands) + list(after)

    def spec(i):
        if i >= len(operands) - len(after):
            return pl.BlockSpec(memory_space=pl.ANY)
        return pl.BlockSpec(memory_space=pltpu.SMEM if i in scalars else pltpu.VMEM)

    moved = sum(x.size * x.dtype.itemsize for x in operands)
    moved += sum(int(np.prod(x.shape)) * x.dtype.itemsize for x in out_shapes)
    return pl.pallas_call(
        kernel,
        name=name,
        out_shape=out_shapes,
        in_specs=[spec(i) for i in range(len(operands))],
        out_specs=[pl.BlockSpec(memory_space=pltpu.VMEM)] * len(out_shapes),
        scratch_shapes=list(scratch),
        compiler_params=pltpu.CompilerParams(vmem_limit_bytes=VMEM_LIMIT),
        cost_estimate=pl.CostEstimate(flops=flops, bytes_accessed=moved, transcendentals=0),
    )(*operands)


def arrays(*shapes, dtype=F32):
    return [jax.ShapeDtypeStruct(shape, dtype) for shape in shapes]


def fetch(x, **shifts):
    names = tuple(shifts)
    sizes = [lax.axis_size(n) for n in names]
    pairs = []
    for here in np.ndindex(*sizes):
        there = [(h + shifts[n]) % size for h, n, size in zip(here, names, sizes)]
        pairs.append((int(np.ravel_multi_index(there, sizes)), int(np.ravel_multi_index(here, sizes))))
    return lax.ppermute(x, names if len(names) > 1 else names[0], pairs)


def two(*shape):
    return arrays(shape, shape, dtype=BF16)


def shards(charges, widths, amplitudes):
    s = Sizes(*charges.shape, lax.axis_size("gz"), lax.axis_size("gx"), lax.axis_size("gy"))
    c = {k: jnp.asarray(v) for k, v in constants(s).items()}
    brick = (s.nz, s.nx, s.ny)
    side = (R, s.nx, s.ny)
    share, edge_rows = call(
        functools.partial(share_kernel, s), "share", [charges],
        arrays((s.tiles1, s.rows1, LANES), (s.nz, 2 * R, s.ny)), flops=8 * 10**8,
    )
    high_rows = fetch(edge_rows, gx=1)
    low_rows = high_rows if s.gx == 2 else fetch(edge_rows, gx=-1)
    shares = [share] + [fetch(share, gz=b) for b in range(1, s.gz)]
    strips = (s.fine_tiles, s.ext, LANES)
    first_cells, last_cells = call(
        functools.partial(strip_kernel, s), "strips", [charges, low_rows, high_rows],
        arrays(strips, strips), flops=4 * 10**8,
    )
    left, right = fetch(last_cells, gy=-1), fetch(first_cells, gy=1)
    taps, y0h, y0l = call(
        functools.partial(tap_kernel, s), "taps", [widths, amplitudes],
        arrays((16, LANES)) + two(2 * LANES, TERMS * s.ny), scalars=(0, 1), flops=6 * 10**8,
    )
    near, near_down, near_up = call(
        functools.partial(near_kernel, s), "near",
        [taps, charges, low_rows, high_rows, left, right, y0h, y0l],
        arrays(brick, side, side), scalars=(0,),
        scratch=[
            pltpu.VMEM((s.nz * s.ext, 2 * LANES), BF16), pltpu.VMEM((s.nz * s.ext, 2 * LANES), BF16),
            pltpu.VMEM((TERMS, s.nz, s.ext, s.ny), F32), pltpu.VMEM((TERMS,) + brick, F32),
        ],
        flops=6 * 10**9,
    )
    base = s.tiles_s * s.rows1
    size2 = s.tiles2 * s.rows2
    depth = TERMS * (s.rows1 + 2 * s.rows2)
    waves, to_low, to_high, coarse = call(
        functools.partial(depth_kernel, s), "depth",
        [taps] + shares + [c["ry2"], c["rx2"]],
        arrays((TERMS * s.planes, s.rows1, LANES), (base + size2, LANES), (base + size2, LANES), (size2, LANES)),
        scalars=(0,), after=[near], scratch=[pltpu.VMEM((s.cz[1], s.rows1, LANES), F32)], flops=2 * 10**9,
    )
    named = ("px1", "px2", "px3", "rx3", "py1", "py2", "py3", "ry3", "pz2", "pz3", "rz3")
    z_taps, y1h, y1l, y2h, y2l, xh, xl = call(
        functools.partial(matrix_kernel, s), "matrices",
        [widths, amplitudes] + [c[k] for k in named],
        arrays((2 * TERMS * s.zrows, LANES))
        + two(LANES, TERMS * s.ny) + two(s.cy[2], 2 * TERMS * s.ny)
        + two(s.cx[0], depth),
        scalars=(0, 1), after=[coarse], flops=3 * 10**9,
    )
    coarses = [coarse]
    for b in range(1, s.gy):
        coarses.append(fetch({1: to_low, s.gy - 1: to_high}.get(b, coarse), gy=b))
    near_low, near_high = fetch(near_up, gz=-1), fetch(near_down, gz=1)
    (terms,) = call(
        functools.partial(along_kernel, s), "along",
        [z_taps, waves] + coarses + [y1h, y1l, y2h, y2l],
        arrays((depth, s.planes * s.ny)), scalars=(0,),
        scratch=[pltpu.VMEM((2 * TERMS, s.cz[2], s.rows2, s.ny), F32)], flops=3 * 10**9,
    )
    parts = call(
        functools.partial(away_kernel, s), "away", [terms, xh, xl],
        arrays(*[(s.nx, s.planes * s.ny)] * (s.gx - 1)), flops=10**9,
    )
    parts = [fetch(x, gx=-dx) for dx, x in enumerate(parts, 1)]
    (home,) = call(
        functools.partial(home_kernel, s), "home",
        [terms, xh, xl, near, near_low, near_high], arrays(brick), flops=2 * 10**9,
    )
    (out,) = call(
        functools.partial(last_kernel, s), "last", [home] + parts, arrays(brick), flops=10**9,
    )
    return out


def solution(mesh):
    placed = (P("gz", "gx", "gy"), P(), P())
    return jax.shard_map(
        shards, mesh=mesh, in_specs=placed, out_specs=P("gz", "gx", "gy"), check_vma=False
    )
```

```python
import functools

import jax
import jax.numpy as jnp
import numpy as np
from jax import lax
from jax.experimental import pallas as pl
from jax.experimental.pallas import tpu as pltpu
from jax.sharding import PartitionSpec as P

R = 8
TERMS = 3
LANES = 128
NEAR = 9.0 / 16.0
FAR = -1.0 / 16.0
F32 = jnp.float32
BF16 = jnp.bfloat16
HIGHEST = lax.Precision.HIGHEST
VMEM_LIMIT = 40 * 1024 * 1024


def up8(n):
    return -(-n // 8) * 8


class Sizes:
    def __init__(self, nz, nx, ny, gz, gx, gy):
        self.nz, self.nx, self.ny = nz, nx, ny
        self.gz, self.gx, self.gy = gz, gx, gy
        self.z1, self.x1, self.y1 = nz // 2, nx // 2, ny // 2
        self.z2, self.x2, self.y2 = nz // 4, nx // 4, ny // 4
        self.cz = [nz * gz >> l for l in range(4)]
        self.cx = [nx * gx >> l for l in range(4)]
        self.cy = [ny * gy >> l for l in range(4)]
        self.planes = self.z1 + 3
        self.zrows = up8(self.planes)
        self.rows1 = self.x1
        self.rows2 = up8(self.x2 + 3)
        self.wide1 = self.y1 + 3
        self.wide2 = self.y2 + 5
        self.tiles1 = -(-self.planes * self.wide1 // LANES)
        self.tiles2 = -(-self.cz[2] * self.wide2 // LANES)
        self.strip = R + 3
        self.per_tile = LANES // self.strip
        self.tiles_s = -(-TERMS * self.planes // self.per_tile)
        self.fine_tiles = -(-nz // (LANES // R))
        self.ext = nx + 2 * R


def restrict_circle(n):
    m = np.zeros((n // 2, n))
    for i in range(n // 2):
        for d, w in ((0, 1.0), (1, NEAR), (-1, NEAR), (3, FAR), (-3, FAR)):
            m[i, (2 * i + d) % n] += w
    return m


def prolong_circle(n):
    m = np.zeros((2 * n, n))
    for i in range(n):
        m[2 * i, i] += 1.0
        for d, w in ((0, NEAR), (1, NEAR), (-1, FAR), (2, FAR)):
            m[2 * i + 1, (i + d) % n] += w
    return m


def restrict_open(first_in, n_in, first_out, n_out):
    m = np.zeros((n_out, n_in))
    for i in range(n_out):
        for d, w in ((0, 1.0), (1, NEAR), (-1, NEAR), (3, FAR), (-3, FAR)):
            j = 2 * (first_out + i) + d - first_in
            if 0 <= j < n_in:
                m[i, j] = w
    return m


def padded(m, rows, columns):
    out = np.zeros((rows, columns), np.float32)
    out[: m.shape[0], : m.shape[1]] = m
    return out


def constants(s):
    c = {}
    c["ry2"] = padded(restrict_open(-1, s.wide1, -2, s.wide2).T, LANES, LANES)
    c["rx2"] = padded(restrict_open(0, s.x1, -1, s.x2 + 3), s.rows2, s.rows1)

    def chain(n):
        p1 = prolong_circle(n[1])
        p2 = p1 @ prolong_circle(n[2])
        return p1, p2, p2 @ prolong_circle(n[3])

    x1, x2, x3 = chain(s.cx)
    c["px1"], c["px2"], c["px3"] = (m.astype(np.float32) for m in (x1, x2, x3))
    place = np.zeros((s.cx[2], s.rows2))
    for r in range(s.x2 + 3):
        place[(r - 1) % s.cx[2], r] += 1.0
    c["rx3"] = (restrict_circle(s.cx[2]) @ place).astype(np.float32)
    y1, y2, y3 = chain(s.cy)
    c["py1"], c["py2"], c["py3"] = (
        np.ascontiguousarray(m[: s.ny].T).astype(np.float32) for m in (y1, y2, y3)
    )
    c["ry3"] = np.ascontiguousarray(restrict_circle(s.cy[2]).T).astype(np.float32)
    z2 = prolong_circle(s.cz[2])
    z3 = z2 @ prolong_circle(s.cz[3])
    own = [(o - 1) % s.cz[1] for o in range(s.planes)]
    c["pz2"] = padded(z2[own], s.zrows, s.cz[2])
    c["pz3"] = padded(z3[own], s.zrows, s.cz[3])
    c["rz3"] = padded(restrict_circle(s.cz[2]), s.cz[3], LANES)
    return c


def halves(x):
    high = x.astype(BF16)
    return high, (x - high.astype(F32)).astype(BF16)


def dot(a, b):
    return jnp.dot(a, b, preferred_element_type=F32)


def exact_dot(a, b):
    return jnp.dot(a, b, preferred_element_type=F32, precision=HIGHEST)


def dot3(a, b_high, b_low):
    high, low = halves(a)
    return dot(high, b_high) + dot(low, b_high) + dot(high, b_low)


def lanes_of(shape):
    return lax.broadcasted_iota(jnp.int32, shape, len(shape) - 1)


def turn(x, by):
    by = by % x.shape[-1]
    return x if by == 0 else pltpu.roll(x, by, x.ndim - 1)


def packed(planes, wide, tiles):
    out = [None] * tiles

    def add(t, x):
        out[t] = x if out[t] is None else out[t] + x

    for k, x in enumerate(planes):
        t, at = divmod(k * wide, LANES)
        moved = turn(x, at)
        if at + wide <= LANES:
            add(t, moved)
        else:
            lane = lanes_of(x.shape)
            add(t, jnp.where(lane >= at, moved, 0.0))
            add(t + 1, jnp.where(lane < at, moved, 0.0))
    return out


def unpacked(tile, k, wide, shift):
    t, at = divmod(k * wide, LANES)
    x = tile(t)
    lane = lanes_of(x.shape)
    if at + wide > LANES:
        x = jnp.where(lane >= at, x, tile(t + 1))
    x = turn(x, shift - at)
    if shift + wide <= LANES:
        return jnp.where((lane >= shift) & (lane < shift + wide), x, 0.0)
    return jnp.where((lane >= shift) | (lane < shift + wide - LANES), x, 0.0)


def open_restriction(shape, in_dim, first_in, first_out, n_out):
    i = lax.broadcasted_iota(jnp.int32, shape, in_dim) + first_in
    o = lax.broadcasted_iota(jnp.int32, shape, 1 - in_dim)
    d = jnp.abs(i - 2 * (o + first_out))
    w = jnp.where(d == 0, 1.0, jnp.where(d == 1, NEAR, jnp.where(d == 3, FAR, 0.0)))
    return jnp.where(o < n_out, w, 0.0).astype(BF16)


def extended(s, b_ref, lo_ref, hi_ref, z):
    return jnp.concatenate([lo_ref[z, s.nx - R :], b_ref[z], hi_ref[z, 0:R]], axis=0)


def share_kernel(s, b_ref, lo_ref, hi_ref, _, m_ref, first_ref, last_ref):
    b = [extended(s, b_ref, lo_ref, hi_ref, z) for z in range(s.nz)]
    planes = []
    for k in range(-1, s.z1 + 2):
        out = None
        for d, w in ((0, 1.0), (1, NEAR), (-1, NEAR), (3, FAR), (-3, FAR)):
            if 0 <= 2 * k + d < s.nz:
                term = b[2 * k + d] if d == 0 else b[2 * k + d] * w
                out = term if out is None else out + term
        planes.append(out)
    high, low = halves(jnp.concatenate(planes, axis=0))
    ry1 = open_restriction((s.ny, LANES), 0, 0, -1, s.wide1)
    rx1 = open_restriction((s.rows1, s.ext), 1, -R, 0, s.x1)
    along = dot(high, ry1) + dot(low, ry1)
    shares = []
    for k in range(s.planes):
        high, low = halves(along[k * s.ext : (k + 1) * s.ext])
        shares.append(dot(rx1, high) + dot(rx1, low))
    for t, x in enumerate(packed(shares, s.wide1, s.tiles1)):
        m_ref[t] = x
    lane = lanes_of((s.ext, LANES))
    group = LANES // R
    for t in range(s.fine_tiles):
        first = last = jnp.zeros((s.ext, LANES), F32)
        for g in range(min(group, s.nz - t * group)):
            x = b[t * group + g]
            at = R * ((g + 1) % group)
            first = jnp.where((lane >= at) & (lane < at + R), turn(x, at), first)
            at = R * g
            last = jnp.where((lane >= at) & (lane < at + R), turn(x, at + R - s.ny), last)
        first_ref[t] = first
        last_ref[t] = last


def rows_of(shape):
    return lax.broadcasted_iota(jnp.int32, shape, 0)


def spread(w_ref, level, t):
    w = jnp.full((8, LANES), w_ref[level, t], F32)
    return (-0.5 / (w * w))[0:1, 0:1]


def bell(c, d):
    d = jnp.abs(d)
    return jnp.where(d <= R, jnp.exp(c * d * d), 0.0)


def scale(c, count=None):
    n = lanes_of((1, LANES)).astype(F32)
    if count is None:
        d, valid = n - R, n <= 2 * R
    else:
        d, valid = jnp.minimum(n, count - n), n < count
    return 1.0 / jnp.sqrt(jnp.sum(jnp.where(valid, jnp.exp(2.0 * c * d * d), 0.0), axis=1, keepdims=True))


def put(high_ref, low_ref, at, x):
    high, low = halves(x)
    high_ref[:, at : at + x.shape[1]] = high
    low_ref[:, at : at + x.shape[1]] = low


def tap_kernel(s, w_ref, a_ref, tap_ref, y0h_ref, y0l_ref):
    coef = [[spread(w_ref, l, t) for t in range(TERMS)] for l in range(2)]
    unit = [[scale(coef[l][t]) for t in range(TERMS)] for l in range(2)]
    d = lanes_of((1, LANES)).astype(F32)
    for t in range(TERMS):
        g0 = bell(coef[0][t], d) * unit[0][t]
        g1 = bell(coef[1][t], d) * unit[1][t]
        tap_ref[t : t + 1] = g0
        tap_ref[TERMS + t : TERMS + t + 1] = g0 * a_ref[0, t]
        tap_ref[2 * TERMS + t : 2 * TERMS + t + 1] = g1 * (a_ref[1, t] * 0.25)
    for t in range(TERMS):
        shape = (2 * LANES, s.ny)
        i = rows_of(shape)
        cell = jnp.where(i < s.ny, i, jnp.where(i < s.ny + R, i - s.ny - R, i - R))
        g = bell(coef[0][t], (cell - lanes_of(shape)).astype(F32)) * unit[0][t]
        put(y0h_ref, y0l_ref, t * s.ny, jnp.where(i < s.ny + 2 * R, g, 0.0))


def matrix_kernel(s, w_ref, a_ref, px1, px2, px3, rx3, py1, py2, py3, ry3, pz2, pz3, rz3, _,
                  z_ref, y1h_ref, y1l_ref, y2h_ref, y2l_ref, xh_ref, xl_ref):
    coef = [[spread(w_ref, l, t) for t in range(TERMS)] for l in range(4)]
    unit = [[scale(coef[l][t]) for t in range(TERMS)] for l in range(3)]

    def circle(n, shape, first_row, first_lane, c, u):
        d = ((rows_of(shape) + first_row) - (lanes_of(shape) + first_lane)) & (n - 1)
        d = d.astype(F32)
        return (bell(c, d) + bell(c, n - d)) * u

    def full_circle(n, shape, c, u):
        d = ((rows_of(shape) - lanes_of(shape)) & (n - 1)).astype(F32)
        d = jnp.minimum(d, n - d)
        return jnp.exp(c * d * d) * u

    def by_term(shape, wide, values):
        t = lanes_of(shape)
        return jnp.where(t < wide, values[0], jnp.where(t < 2 * wide, values[1], values[2]))

    for t in range(TERMS):
        shape = (LANES, s.cy[1])
        g = circle(s.cy[1], shape, -(R + 1), 0, coef[1][t], unit[1][t])
        g = jnp.where(rows_of(shape) < s.y1 + 3 + 2 * R, g, 0.0)
        put(y1h_ref, y1l_ref, t * s.ny, exact_dot(g, py1[...]))
        g = circle(s.cy[2], (s.cy[2], s.cy[2]), 0, 0, coef[2][t], unit[2][t])
        put(y2h_ref, y2l_ref, t * s.ny, exact_dot(g, py2[...]))
        u = scale(coef[3][t], s.cy[3])
        g = full_circle(s.cy[3], (s.cy[3], s.cy[3]), coef[3][t], u)
        put(y2h_ref, y2l_ref, (TERMS + t) * s.ny, exact_dot(exact_dot(ry3[...], g), py3[...]))
    wide = s.rows1
    shape = (s.cx[1], TERMS * wide)
    lane = lanes_of(shape)
    column = lane - jnp.where(lane < wide, 0, jnp.where(lane < 2 * wide, wide, 2 * wide))
    d = ((rows_of(shape) - column) & (s.cx[1] - 1)).astype(F32)
    c = by_term(shape, wide, coef[1])
    g = (bell(c, d) + bell(c, s.cx[1] - d)) * by_term(shape, wide, unit[1])
    put(xh_ref, xl_ref, 0, exact_dot(px1[...], g))
    wide = s.rows2
    shape = (s.cx[2], TERMS * wide)
    lane = lanes_of(shape)
    column = lane - jnp.where(lane < wide, 0, jnp.where(lane < 2 * wide, wide, 2 * wide))
    d = ((rows_of(shape) - column + 1) & (s.cx[2] - 1)).astype(F32)
    c = by_term(shape, wide, coef[2])
    g = (bell(c, d) + bell(c, s.cx[2] - d)) * by_term(shape, wide, unit[2])
    put(xh_ref, xl_ref, TERMS * s.rows1, exact_dot(px2[...], jnp.where(column < s.x2 + 3, g, 0.0)))
    for t in range(TERMS):
        u = scale(coef[3][t], s.cx[3])
        g = full_circle(s.cx[3], (s.cx[3], s.cx[3]), coef[3][t], u)
        put(xh_ref, xl_ref, TERMS * s.rows1 + (TERMS + t) * wide, exact_dot(px3[...], exact_dot(g, rx3[...])))
    for t in range(TERMS):
        g = circle(s.cz[2], (s.cz[2], LANES), 0, 0, coef[2][t], unit[2][t])
        g = exact_dot(pz2[...], g) * (a_ref[2, t] * 0.0625)
        z_ref[t * s.zrows : (t + 1) * s.zrows] = g
        u = scale(coef[3][t], s.cz[3])
        g = full_circle(s.cz[3], (s.cz[3], s.cz[3]), coef[3][t], u)
        g = exact_dot(exact_dot(pz3[...], g), rz3[...]) * (a_ref[3, t] * 0.015625)
        z_ref[(TERMS + t) * s.zrows : (TERMS + t + 1) * s.zrows] = g


def near_kernel(s, tap_ref, b_ref, lo_ref, hi_ref, left_ref, right_ref, y0h_ref, y0l_ref,
                own_ref, down_ref, up_ref, eh_ref, el_ref, u_ref, v_ref):
    ext = s.ext
    group = LANES // R
    lane = lanes_of((ext, LANES))
    for z in range(s.nz):
        t, g = divmod(z, group)
        strips = jnp.where((lane >= R * g) & (lane < R * g + R), left_ref[t], right_ref[t])
        for at, x in ((0, extended(s, b_ref, lo_ref, hi_ref, z)), (LANES, turn(strips, -R * g))):
            high, low = halves(x)
            eh_ref[z * ext : (z + 1) * ext, at : at + LANES] = high
            el_ref[z * ext : (z + 1) * ext, at : at + LANES] = low
    step = 4 * ext
    y0h, y0l = y0h_ref[...], y0l_ref[...]
    for at in range(0, s.nz * ext, step):
        high, low = eh_ref[at : at + step], el_ref[at : at + step]
        u = dot(high, y0h) + dot(low, y0h) + dot(high, y0l)
        for t in range(TERMS):
            for q in range(4):
                u_ref[t, at // ext + q] = u[q * ext : (q + 1) * ext, t * s.ny : (t + 1) * s.ny]

    def cross(z, _):
        for t in range(TERMS):
            v = u_ref[t, z, R : R + s.nx] * tap_ref[t, 0]
            for d in range(1, R + 1):
                v += (u_ref[t, z, R + d : R + d + s.nx] + u_ref[t, z, R - d : R - d + s.nx]) * tap_ref[t, d]
            v_ref[t, z] = v
        return 0

    lax.fori_loop(0, s.nz, cross, 0)

    def depth(r, _):
        rows = pl.ds(pl.multiple_of(r * 8, 8), 8)
        taps = [[tap_ref[TERMS + t, d] for d in range(R + 1)] for t in range(TERMS)]
        for first in range(-R, s.nz + R, R):
            acc = [None] * R
            for t in range(TERMS):
                for z in range(max(0, first - R), min(s.nz, first + 2 * R)):
                    v = v_ref[t, z, rows]
                    for o in range(R):
                        d = abs(first + o - z)
                        if d <= R:
                            term = v * taps[t][d]
                            acc[o] = term if acc[o] is None else acc[o] + term
            for o in range(R):
                if first < 0:
                    down_ref[o, rows] = acc[o]
                elif first >= s.nz:
                    up_ref[o, rows] = acc[o]
                else:
                    own_ref[first + o, rows] = acc[o]
        return 0

    lax.fori_loop(0, s.nx // 8, depth, 0)


def depth_kernel(s, tap_ref, *refs):
    m_refs = refs[: s.gz]
    ry2_ref, rx2_ref, _, w_ref, down_ref, up_ref, c2_ref, c_ref = refs[s.gz :]
    n = s.cz[1]
    parts = [[] for _ in range(n)]
    for b in range(s.gz):
        for k in range(s.planes):
            parts[(b * s.z1 + k - 1) % n].append((b, k))
    for z in range(n):
        out = None
        for b, k in parts[z]:
            x = unpacked(lambda t, b=b: m_refs[b][t], k, s.wide1, 0)
            out = x if out is None else out + x
        c_ref[z] = out
    lane = lanes_of((s.rows1, LANES))
    down = [jnp.zeros((s.rows1, LANES), F32)] * s.tiles_s
    up = list(down)
    for o in range(s.planes):
        sums = [c_ref[(o - 1) % n]]
        sums += [c_ref[(o - 1 + d) % n] + c_ref[(o - 1 - d) % n] for d in range(1, R + 1)]
        for t in range(TERMS):
            x = sums[0] * tap_ref[2 * TERMS + t, 0]
            for d in range(1, R + 1):
                x += sums[d] * tap_ref[2 * TERMS + t, d]
            k = t * s.planes + o
            w_ref[k] = x
            tile, slot = divmod(k, s.per_tile)
            at = slot * s.strip
            here = (lane >= at) & (lane < at + s.strip)
            down[tile] = jnp.where(here, turn(x, at), down[tile])
            up[tile] = jnp.where(here, turn(x, at - (s.wide1 - s.strip)), up[tile])
    coarse = []
    for j in range(s.cz[2]):
        at = lambda d: c_ref[(2 * j + d) % n]
        coarse.append(at(0) + NEAR * (at(1) + at(-1)) + FAR * (at(3) + at(-3)))
    high, low = halves(jnp.concatenate(coarse, axis=0))
    ry2 = ry2_ref[...].astype(BF16)
    rx2 = rx2_ref[...].astype(BF16)
    along = dot(high, ry2) + dot(low, ry2)
    shares = []
    for j in range(s.cz[2]):
        high, low = halves(along[j * s.rows1 : (j + 1) * s.rows1])
        shares.append(dot(rx2, high) + dot(rx2, low))
    for t in range(s.tiles_s):
        down_ref[t * s.rows1 : (t + 1) * s.rows1] = down[t]
        up_ref[t * s.rows1 : (t + 1) * s.rows1] = up[t]
    base = s.tiles_s * s.rows1
    for t, x in enumerate(packed(shares, s.wide2, s.tiles2)):
        rows = slice(t * s.rows2, (t + 1) * s.rows2)
        c2_ref[rows] = x
        for ref in (down_ref, up_ref):
            ref[base + t * s.rows2 : base + (t + 1) * s.rows2] = x


def along_kernel(s, z_ref, w_ref, *refs):
    c2_refs = refs[: s.gy]
    y1h_ref, y1l_ref, y2h_ref, y2l_ref, d_ref, yb_ref = refs[s.gy :]
    base = s.tiles_s * s.rows1
    lane = lanes_of((s.rows1, LANES))
    above, below = c2_refs[1], c2_refs[-1]
    end = s.y1 + R
    for t in range(TERMS):
        cells = []
        for o in range(s.planes):
            k = t * s.planes + o
            tile, slot = divmod(k, s.per_tile)
            rows = slice(tile * s.rows1, (tile + 1) * s.rows1)
            at = slot * s.strip
            x = turn(w_ref[k], R)
            x += jnp.where(lane < s.strip, turn(below[rows], -at), 0.0)
            x += jnp.where((lane >= end) & (lane < end + s.strip), turn(above[rows], end - at), 0.0)
            cells.append(x)
        columns = slice(t * s.ny, (t + 1) * s.ny)
        out = dot3(jnp.concatenate(cells, axis=0), y1h_ref[:, columns], y1l_ref[:, columns])
        for o in range(s.planes):
            d_ref[t * s.rows1 : (t + 1) * s.rows1, o * s.ny : (o + 1) * s.ny] = out[o * s.rows1 : (o + 1) * s.rows1]
    cells = []
    for j in range(s.cz[2]):
        out = None
        for b in range(s.gy):
            first = 0 if b == 0 or c2_refs[b].shape[0] == s.tiles2 * s.rows2 else base
            tile = lambda t, b=b, f=first: c2_refs[b][f + t * s.rows2 : f + (t + 1) * s.rows2]
            x = unpacked(tile, j, s.wide2, (b * s.y2 - 2) % LANES)
            out = x if out is None else out + x
        cells.append(out)
    yb = dot3(jnp.concatenate(cells, axis=0), y2h_ref[...], y2l_ref[...])
    for j in range(s.cz[2]):
        for q in range(2 * TERMS):
            yb_ref[q, j] = yb[j * s.rows2 : (j + 1) * s.rows2, q * s.ny : (q + 1) * s.ny]
    for o in range(s.planes):
        for q in range(2 * TERMS):
            x = yb_ref[q, 0] * z_ref[q * s.zrows + o, 0]
            for j in range(1, s.cz[2]):
                x += yb_ref[q, j] * z_ref[q * s.zrows + o, j]
            at = TERMS * s.rows1 + q * s.rows2
            d_ref[at : at + s.rows2, o * s.ny : (o + 1) * s.ny] = x


def across(s, d_ref, xh_ref, xl_ref, shift):
    rows = slice(shift * s.nx, (shift + 1) * s.nx)
    high, low = halves(d_ref[...])
    return dot(xh_ref[rows], high) + dot(xl_ref[rows], high) + dot(xh_ref[rows], low)


def away_kernel(s, d_ref, xh_ref, xl_ref, *g_refs):
    for shift, ref in enumerate(g_refs):
        ref[...] = across(s, d_ref, xh_ref, xl_ref, shift + 1)


def prolonged(s, level, z):
    m = z // 2 + 1
    if z % 2 == 0:
        return level[m]
    return NEAR * (level[m] + level[m + 1]) + FAR * (level[m - 1] + level[m + 2])


def home_kernel(s, d_ref, xh_ref, xl_ref, own_ref, low_ref, high_ref, out_ref):
    g = across(s, d_ref, xh_ref, xl_ref, 0)
    level = [g[:, o * s.ny : (o + 1) * s.ny] for o in range(s.planes)]
    for z in range(s.nz):
        x = prolonged(s, level, z) + own_ref[z]
        if z < R:
            x += low_ref[z]
        if z >= s.nz - R:
            x += high_ref[z - (s.nz - R)]
        out_ref[z] = x


def last_kernel(s, home_ref, *refs):
    g_refs, out_ref = refs[:-1], refs[-1]
    level = []
    for o in range(s.planes):
        columns = slice(o * s.ny, (o + 1) * s.ny)
        x = g_refs[0][:, columns]
        for ref in g_refs[1:]:
            x += ref[:, columns]
        level.append(x)
    for z in range(s.nz):
        out_ref[z] = home_ref[z] + prolonged(s, level, z)


def call(kernel, name, operands, out_shapes, scalars=(), after=(), scratch=(), flops=0):
    operands = list(operands) + list(after)

    def spec(i):
        if i >= len(operands) - len(after):
            return pl.BlockSpec(memory_space=pl.ANY)
        return pl.BlockSpec(memory_space=pltpu.SMEM if i in scalars else pltpu.VMEM)

    moved = sum(x.size * x.dtype.itemsize for x in operands)
    moved += sum(int(np.prod(x.shape)) * x.dtype.itemsize for x in out_shapes)
    return pl.pallas_call(
        kernel,
        name=name,
        out_shape=out_shapes,
        in_specs=[spec(i) for i in range(len(operands))],
        out_specs=[pl.BlockSpec(memory_space=pltpu.VMEM)] * len(out_shapes),
        scratch_shapes=list(scratch),
        compiler_params=pltpu.CompilerParams(vmem_limit_bytes=VMEM_LIMIT),
        cost_estimate=pl.CostEstimate(flops=flops, bytes_accessed=moved, transcendentals=0),
    )(*operands)


def arrays(*shapes, dtype=F32):
    return [jax.ShapeDtypeStruct(shape, dtype) for shape in shapes]


def fetch(x, **shifts):
    names = tuple(shifts)
    sizes = [lax.axis_size(n) for n in names]
    pairs = []
    for here in np.ndindex(*sizes):
        there = [(h + shifts[n]) % size for h, n, size in zip(here, names, sizes)]
        pairs.append((int(np.ravel_multi_index(there, sizes)), int(np.ravel_multi_index(here, sizes))))
    return lax.ppermute(x, names if len(names) > 1 else names[0], pairs)


def two(*shape):
    return arrays(shape, shape, dtype=BF16)


def shards(charges, widths, amplitudes):
    s = Sizes(*charges.shape, lax.axis_size("gz"), lax.axis_size("gx"), lax.axis_size("gy"))
    c = {k: jnp.asarray(v) for k, v in constants(s).items()}
    brick = (s.nz, s.nx, s.ny)
    side = (R, s.nx, s.ny)
    taps, y0h, y0l = call(
        functools.partial(tap_kernel, s), "taps", [widths, amplitudes],
        arrays((16, LANES)) + two(2 * LANES, TERMS * s.ny), scalars=(0, 1), flops=6 * 10**8,
    )
    high_rows = fetch(charges, gx=1)
    low_rows = high_rows if s.gx == 2 else fetch(charges, gx=-1)
    strips = (s.fine_tiles, s.ext, LANES)
    share, first_cells, last_cells = call(
        functools.partial(share_kernel, s), "share", [charges, low_rows, high_rows],
        arrays((s.tiles1, s.rows1, LANES), strips, strips), after=[y0h], flops=10**9,
    )
    shares = [share] + [fetch(share, gz=b) for b in range(1, s.gz)]
    left, right = fetch(last_cells, gy=-1), fetch(first_cells, gy=1)
    near, near_down, near_up = call(
        functools.partial(near_kernel, s), "near",
        [taps, charges, low_rows, high_rows, left, right, y0h, y0l],
        arrays(brick, side, side), scalars=(0,),
        scratch=[
            pltpu.VMEM((s.nz * s.ext, 2 * LANES), BF16), pltpu.VMEM((s.nz * s.ext, 2 * LANES), BF16),
            pltpu.VMEM((TERMS, s.nz, s.ext, s.ny), F32), pltpu.VMEM((TERMS,) + brick, F32),
        ],
        flops=6 * 10**9,
    )
    base = s.tiles_s * s.rows1
    size2 = s.tiles2 * s.rows2
    depth = TERMS * (s.rows1 + 2 * s.rows2)
    waves, to_low, to_high, coarse = call(
        functools.partial(depth_kernel, s), "depth",
        [taps] + shares + [c["ry2"], c["rx2"]],
        arrays((TERMS * s.planes, s.rows1, LANES), (base + size2, LANES), (base + size2, LANES), (size2, LANES)),
        scalars=(0,), after=[near], scratch=[pltpu.VMEM((s.cz[1], s.rows1, LANES), F32)], flops=2 * 10**9,
    )
    named = ("px1", "px2", "px3", "rx3", "py1", "py2", "py3", "ry3", "pz2", "pz3", "rz3")
    z_taps, y1h, y1l, y2h, y2l, xh, xl = call(
        functools.partial(matrix_kernel, s), "matrices",
        [widths, amplitudes] + [c[k] for k in named],
        arrays((2 * TERMS * s.zrows, LANES))
        + two(LANES, TERMS * s.ny) + two(s.cy[2], 2 * TERMS * s.ny)
        + two(s.cx[0], depth),
        scalars=(0, 1), after=[coarse], flops=3 * 10**9,
    )
    coarses = [coarse]
    for b in range(1, s.gy):
        coarses.append(fetch({1: to_low, s.gy - 1: to_high}.get(b, coarse), gy=b))
    near_low, near_high = fetch(near_up, gz=-1), fetch(near_down, gz=1)
    (terms,) = call(
        functools.partial(along_kernel, s), "along",
        [z_taps, waves] + coarses + [y1h, y1l, y2h, y2l],
        arrays((depth, s.planes * s.ny)), scalars=(0,),
        scratch=[pltpu.VMEM((2 * TERMS, s.cz[2], s.rows2, s.ny), F32)], flops=3 * 10**9,
    )
    parts = call(
        functools.partial(away_kernel, s), "away", [terms, xh, xl],
        arrays(*[(s.nx, s.planes * s.ny)] * (s.gx - 1)), flops=10**9,
    )
    parts = [fetch(x, gx=-dx) for dx, x in enumerate(parts, 1)]
    (home,) = call(
        functools.partial(home_kernel, s), "home",
        [terms, xh, xl, near, near_low, near_high], arrays(brick), flops=2 * 10**9,
    )
    (out,) = call(
        functools.partial(last_kernel, s), "last", [home] + parts, arrays(brick), flops=10**9,
    )
    return out


def solution(mesh):
    placed = (P("gz", "gx", "gy"), P(), P())
    return jax.shard_map(
        shards, mesh=mesh, in_specs=placed, out_specs=P("gz", "gx", "gy"), check_vma=False
    )
```

```python
import functools

import jax
import jax.numpy as jnp
import numpy as np
from jax import lax
from jax.experimental import pallas as pl
from jax.experimental.pallas import tpu as pltpu
from jax.sharding import PartitionSpec as P

R = 8
TERMS = 3
LANES = 128
NEAR = 9.0 / 16.0
FAR = -1.0 / 16.0
F32 = jnp.float32
BF16 = jnp.bfloat16
HIGHEST = lax.Precision.HIGHEST
VMEM_LIMIT = 40 * 1024 * 1024


def up8(n):
    return -(-n // 8) * 8


class Sizes:
    def __init__(self, nz, nx, ny, gz, gx, gy):
        self.nz, self.nx, self.ny = nz, nx, ny
        self.gz, self.gx, self.gy = gz, gx, gy
        self.z1, self.x1, self.y1 = nz // 2, nx // 2, ny // 2
        self.z2, self.x2, self.y2 = nz // 4, nx // 4, ny // 4
        self.cz = [nz * gz >> l for l in range(4)]
        self.cx = [nx * gx >> l for l in range(4)]
        self.cy = [ny * gy >> l for l in range(4)]
        self.planes = self.z1 + 3
        self.zrows = up8(self.planes)
        self.rows1 = self.x1
        self.rows2 = up8(self.x2 + 3)
        self.wide1 = self.y1 + 3
        self.wide2 = self.y2 + 5
        self.tiles1 = -(-self.planes * self.wide1 // LANES)
        self.tiles2 = -(-self.cz[2] * self.wide2 // LANES)
        self.strip = R + 3
        self.per_tile = LANES // self.strip
        self.tiles_s = -(-TERMS * self.planes // self.per_tile)
        self.fine_tiles = -(-nz // (LANES // R))
        self.ext = nx + 2 * R


def restrict_circle(n):
    m = np.zeros((n // 2, n))
    for i in range(n // 2):
        for d, w in ((0, 1.0), (1, NEAR), (-1, NEAR), (3, FAR), (-3, FAR)):
            m[i, (2 * i + d) % n] += w
    return m


def prolong_circle(n):
    m = np.zeros((2 * n, n))
    for i in range(n):
        m[2 * i, i] += 1.0
        for d, w in ((0, NEAR), (1, NEAR), (-1, FAR), (2, FAR)):
            m[2 * i + 1, (i + d) % n] += w
    return m


def restrict_open(first_in, n_in, first_out, n_out):
    m = np.zeros((n_out, n_in))
    for i in range(n_out):
        for d, w in ((0, 1.0), (1, NEAR), (-1, NEAR), (3, FAR), (-3, FAR)):
            j = 2 * (first_out + i) + d - first_in
            if 0 <= j < n_in:
                m[i, j] = w
    return m


def padded(m, rows, columns):
    out = np.zeros((rows, columns), np.float32)
    out[: m.shape[0], : m.shape[1]] = m
    return out


def constants(s):
    c = {}
    c["ry2"] = padded(restrict_open(-1, s.wide1, -2, s.wide2).T, LANES, LANES)
    c["rx2"] = padded(restrict_open(0, s.x1, -1, s.x2 + 3), s.rows2, s.rows1)

    def chain(n):
        p1 = prolong_circle(n[1])
        p2 = p1 @ prolong_circle(n[2])
        return p1, p2, p2 @ prolong_circle(n[3])

    x1, x2, x3 = chain(s.cx)
    c["px1"], c["px2"], c["px3"] = (m.astype(np.float32) for m in (x1, x2, x3))
    place = np.zeros((s.cx[2], s.rows2))
    for r in range(s.x2 + 3):
        place[(r - 1) % s.cx[2], r] += 1.0
    c["rx3"] = (restrict_circle(s.cx[2]) @ place).astype(np.float32)
    y1, y2, y3 = chain(s.cy)
    c["py1"], c["py2"], c["py3"] = (
        np.ascontiguousarray(m[: s.ny].T).astype(np.float32) for m in (y1, y2, y3)
    )
    c["ry3"] = np.ascontiguousarray(restrict_circle(s.cy[2]).T).astype(np.float32)
    z2 = prolong_circle(s.cz[2])
    z3 = z2 @ prolong_circle(s.cz[3])
    own = [(o - 1) % s.cz[1] for o in range(s.planes)]
    c["pz2"] = padded(z2[own], s.zrows, s.cz[2])
    c["pz3"] = padded(z3[own], s.zrows, s.cz[3])
    c["rz3"] = padded(restrict_circle(s.cz[2]), s.cz[3], LANES)
    return c


def halves(x):
    high = x.astype(BF16)
    return high, (x - high.astype(F32)).astype(BF16)


def dot(a, b):
    return jnp.dot(a, b, preferred_element_type=F32)


def exact_dot(a, b):
    return jnp.dot(a, b, preferred_element_type=F32, precision=HIGHEST)


def dot3(a, b_high, b_low):
    high, low = halves(a)
    return dot(high, b_high) + dot(low, b_high) + dot(high, b_low)


def lanes_of(shape):
    return lax.broadcasted_iota(jnp.int32, shape, len(shape) - 1)


def turn(x, by):
    by = by % x.shape[-1]
    return x if by == 0 else pltpu.roll(x, by, x.ndim - 1)


def packed(planes, wide, tiles):
    out = [None] * tiles

    def add(t, x):
        out[t] = x if out[t] is None else out[t] + x

    for k, x in enumerate(planes):
        t, at = divmod(k * wide, LANES)
        moved = turn(x, at)
        if at + wide <= LANES:
            add(t, moved)
        else:
            lane = lanes_of(x.shape)
            add(t, jnp.where(lane >= at, moved, 0.0))
            add(t + 1, jnp.where(lane < at, moved, 0.0))
    return out


def unpacked(tile, k, wide, shift):
    t, at = divmod(k * wide, LANES)
    x = tile(t)
    lane = lanes_of(x.shape)
    if at + wide > LANES:
        x = jnp.where(lane >= at, x, tile(t + 1))
    x = turn(x, shift - at)
    if shift + wide <= LANES:
        return jnp.where((lane >= shift) & (lane < shift + wide), x, 0.0)
    return jnp.where((lane >= shift) | (lane < shift + wide - LANES), x, 0.0)


def open_restriction(shape, in_dim, first_in, first_out, n_out):
    i = lax.broadcasted_iota(jnp.int32, shape, in_dim) + first_in
    o = lax.broadcasted_iota(jnp.int32, shape, 1 - in_dim)
    d = jnp.abs(i - 2 * (o + first_out))
    w = jnp.where(d == 0, 1.0, jnp.where(d == 1, NEAR, jnp.where(d == 3, FAR, 0.0)))
    return jnp.where(o < n_out, w, 0.0).astype(BF16)


def extended(s, b_ref, lo_ref, hi_ref, z):
    return jnp.concatenate([lo_ref[z, s.nx - R :], b_ref[z], hi_ref[z, 0:R]], axis=0)


def share_kernel(s, b_ref, lo_ref, hi_ref, _, m_ref, first_ref, last_ref):
    b = [extended(s, b_ref, lo_ref, hi_ref, z) for z in range(s.nz)]
    planes = []
    for k in range(-1, s.z1 + 2):
        out = None
        for d, w in ((0, 1.0), (1, NEAR), (-1, NEAR), (3, FAR), (-3, FAR)):
            if 0 <= 2 * k + d < s.nz:
                term = b[2 * k + d] if d == 0 else b[2 * k + d] * w
                out = term if out is None else out + term
        planes.append(out)
    high, low = halves(jnp.concatenate(planes, axis=0))
    ry1 = open_restriction((s.ny, LANES), 0, 0, -1, s.wide1)
    rx1 = open_restriction((s.rows1, s.ext), 1, -R, 0, s.x1)
    along = dot(high, ry1) + dot(low, ry1)
    shares = []
    for k in range(s.planes):
        high, low = halves(along[k * s.ext : (k + 1) * s.ext])
        shares.append(dot(rx1, high) + dot(rx1, low))
    for t, x in enumerate(packed(shares, s.wide1, s.tiles1)):
        m_ref[t] = x
    lane = lanes_of((s.ext, LANES))
    group = LANES // R
    for t in range(s.fine_tiles):
        first = last = jnp.zeros((s.ext, LANES), F32)
        for g in range(min(group, s.nz - t * group)):
            x = b[t * group + g]
            at = R * ((g + 1) % group)
            first = jnp.where((lane >= at) & (lane < at + R), turn(x, at), first)
            at = R * g
            last = jnp.where((lane >= at) & (lane < at + R), turn(x, at + R - s.ny), last)
        first_ref[t] = first
        last_ref[t] = last


def rows_of(shape):
    return lax.broadcasted_iota(jnp.int32, shape, 0)


def spread(w_ref, level, t):
    w = jnp.full((8, LANES), w_ref[level, t], F32)
    return (-0.5 / (w * w))[0:1, 0:1]


def bell(c, d):
    d = jnp.abs(d)
    return jnp.where(d <= R, jnp.exp(c * d * d), 0.0)


def scale(c, count=None):
    n = lanes_of((1, LANES)).astype(F32)
    if count is None:
        d, valid = n - R, n <= 2 * R
    else:
        d, valid = jnp.minimum(n, count - n), n < count
    return 1.0 / jnp.sqrt(jnp.sum(jnp.where(valid, jnp.exp(2.0 * c * d * d), 0.0), axis=1, keepdims=True))


def put(high_ref, low_ref, at, x):
    high, low = halves(x)
    high_ref[:, at : at + x.shape[1]] = high
    low_ref[:, at : at + x.shape[1]] = low


def tap_kernel(s, w_ref, a_ref, tap_ref, y0h_ref, y0l_ref):
    coef = [[spread(w_ref, l, t) for t in range(TERMS)] for l in range(2)]
    unit = [[scale(coef[l][t]) for t in range(TERMS)] for l in range(2)]
    d = lanes_of((1, LANES)).astype(F32)
    for t in range(TERMS):
        g0 = bell(coef[0][t], d) * unit[0][t]
        g1 = bell(coef[1][t], d) * unit[1][t]
        tap_ref[t : t + 1] = g0
        tap_ref[TERMS + t : TERMS + t + 1] = g0 * a_ref[0, t]
        tap_ref[2 * TERMS + t : 2 * TERMS + t + 1] = g1 * (a_ref[1, t] * 0.25)
    for t in range(TERMS):
        shape = (2 * LANES, s.ny)
        i = rows_of(shape)
        cell = jnp.where(i < s.ny, i, jnp.where(i < s.ny + R, i - s.ny - R, i - R))
        g = bell(coef[0][t], (cell - lanes_of(shape)).astype(F32)) * unit[0][t]
        put(y0h_ref, y0l_ref, t * s.ny, jnp.where(i < s.ny + 2 * R, g, 0.0))


def matrix_kernel(s, w_ref, a_ref, px1, px2, px3, rx3, py1, py2, py3, ry3, pz2, pz3, rz3, _,
                  z_ref, y1h_ref, y1l_ref, y2h_ref, y2l_ref, xh_ref, xl_ref):
    coef = [[spread(w_ref, l, t) for t in range(TERMS)] for l in range(4)]
    unit = [[scale(coef[l][t]) for t in range(TERMS)] for l in range(3)]

    def circle(n, shape, first_row, first_lane, c, u):
        d = ((rows_of(shape) + first_row) - (lanes_of(shape) + first_lane)) & (n - 1)
        d = d.astype(F32)
        return (bell(c, d) + bell(c, n - d)) * u

    def full_circle(n, shape, c, u):
        d = ((rows_of(shape) - lanes_of(shape)) & (n - 1)).astype(F32)
        d = jnp.minimum(d, n - d)
        return jnp.exp(c * d * d) * u

    def by_term(shape, wide, values):
        t = lanes_of(shape)
        return jnp.where(t < wide, values[0], jnp.where(t < 2 * wide, values[1], values[2]))

    for t in range(TERMS):
        shape = (LANES, s.cy[1])
        g = circle(s.cy[1], shape, -(R + 1), 0, coef[1][t], unit[1][t])
        g = jnp.where(rows_of(shape) < s.y1 + 3 + 2 * R, g, 0.0)
        put(y1h_ref, y1l_ref, t * s.ny, exact_dot(g, py1[...]))
        g = circle(s.cy[2], (s.cy[2], s.cy[2]), 0, 0, coef[2][t], unit[2][t])
        put(y2h_ref, y2l_ref, t * s.ny, exact_dot(g, py2[...]))
        u = scale(coef[3][t], s.cy[3])
        g = full_circle(s.cy[3], (s.cy[3], s.cy[3]), coef[3][t], u)
        put(y2h_ref, y2l_ref, (TERMS + t) * s.ny, exact_dot(exact_dot(ry3[...], g), py3[...]))
    wide = s.rows1
    shape = (s.cx[1], TERMS * wide)
    lane = lanes_of(shape)
    column = lane - jnp.where(lane < wide, 0, jnp.where(lane < 2 * wide, wide, 2 * wide))
    d = ((rows_of(shape) - column) & (s.cx[1] - 1)).astype(F32)
    c = by_term(shape, wide, coef[1])
    g = (bell(c, d) + bell(c, s.cx[1] - d)) * by_term(shape, wide, unit[1])
    put(xh_ref, xl_ref, 0, exact_dot(px1[...], g))
    wide = s.rows2
    shape = (s.cx[2], TERMS * wide)
    lane = lanes_of(shape)
    column = lane - jnp.where(lane < wide, 0, jnp.where(lane < 2 * wide, wide, 2 * wide))
    d = ((rows_of(shape) - column + 1) & (s.cx[2] - 1)).astype(F32)
    c = by_term(shape, wide, coef[2])
    g = (bell(c, d) + bell(c, s.cx[2] - d)) * by_term(shape, wide, unit[2])
    put(xh_ref, xl_ref, TERMS * s.rows1, exact_dot(px2[...], jnp.where(column < s.x2 + 3, g, 0.0)))
    for t in range(TERMS):
        u = scale(coef[3][t], s.cx[3])
        g = full_circle(s.cx[3], (s.cx[3], s.cx[3]), coef[3][t], u)
        put(xh_ref, xl_ref, TERMS * s.rows1 + (TERMS + t) * wide, exact_dot(px3[...], exact_dot(g, rx3[...])))
    for t in range(TERMS):
        g = circle(s.cz[2], (s.cz[2], LANES), 0, 0, coef[2][t], unit[2][t])
        g = exact_dot(pz2[...], g) * (a_ref[2, t] * 0.0625)
        z_ref[t * s.zrows : (t + 1) * s.zrows] = g
        u = scale(coef[3][t], s.cz[3])
        g = full_circle(s.cz[3], (s.cz[3], s.cz[3]), coef[3][t], u)
        g = exact_dot(exact_dot(pz3[...], g), rz3[...]) * (a_ref[3, t] * 0.015625)
        z_ref[(TERMS + t) * s.zrows : (TERMS + t + 1) * s.zrows] = g


def near_kernel(s, tap_ref, b_ref, lo_ref, hi_ref, left_ref, right_ref, y0h_ref, y0l_ref,
                own_ref, down_ref, up_ref, eh_ref, el_ref, u_ref, v_ref):
    ext = s.ext
    group = LANES // R
    lane = lanes_of((ext, LANES))
    for z in range(s.nz):
        t, g = divmod(z, group)
        strips = jnp.where((lane >= R * g) & (lane < R * g + R), left_ref[t], right_ref[t])
        for at, x in ((0, extended(s, b_ref, lo_ref, hi_ref, z)), (LANES, turn(strips, -R * g))):
            high, low = halves(x)
            eh_ref[z * ext : (z + 1) * ext, at : at + LANES] = high
            el_ref[z * ext : (z + 1) * ext, at : at + LANES] = low
    step = 4 * ext
    y0h, y0l = y0h_ref[...], y0l_ref[...]
    for at in range(0, s.nz * ext, step):
        high, low = eh_ref[at : at + step], el_ref[at : at + step]
        u = dot(high, y0h) + dot(low, y0h) + dot(high, y0l)
        for t in range(TERMS):
            for q in range(4):
                u_ref[t, at // ext + q] = u[q * ext : (q + 1) * ext, t * s.ny : (t + 1) * s.ny]

    def cross(z, _):
        for t in range(TERMS):
            v = u_ref[t, z, R : R + s.nx] * tap_ref[t, 0]
            for d in range(1, R + 1):
                v += (u_ref[t, z, R + d : R + d + s.nx] + u_ref[t, z, R - d : R - d + s.nx]) * tap_ref[t, d]
            v_ref[t, z] = v
        return 0

    lax.fori_loop(0, s.nz, cross, 0)

    def depth(r, _):
        rows = pl.ds(pl.multiple_of(r * 8, 8), 8)
        taps = [[tap_ref[TERMS + t, d] for d in range(R + 1)] for t in range(TERMS)]
        for first in range(-R, s.nz + R, R):
            acc = [None] * R
            for t in range(TERMS):
                for z in range(max(0, first - R), min(s.nz, first + 2 * R)):
                    v = v_ref[t, z, rows]
                    for o in range(R):
                        d = abs(first + o - z)
                        if d <= R:
                            term = v * taps[t][d]
                            acc[o] = term if acc[o] is None else acc[o] + term
            for o in range(R):
                if first < 0:
                    down_ref[o, rows] = acc[o]
                elif first >= s.nz:
                    up_ref[o, rows] = acc[o]
                else:
                    own_ref[first + o, rows] = acc[o]
        return 0

    lax.fori_loop(0, s.nx // 8, depth, 0)


def depth_kernel(s, tap_ref, *refs):
    m_refs = refs[: s.gz]
    ry2_ref, rx2_ref, _, w_ref, send_ref, c_ref = refs[s.gz :]
    n = s.cz[1]
    parts = [[] for _ in range(n)]
    for b in range(s.gz):
        for k in range(s.planes):
            parts[(b * s.z1 + k - 1) % n].append((b, k))
    for z in range(n):
        out = None
        for b, k in parts[z]:
            x = unpacked(lambda t, b=b: m_refs[b][t], k, s.wide1, 0)
            out = x if out is None else out + x
        c_ref[z] = out
    lane = lanes_of((s.rows1, LANES))
    down = [jnp.zeros((s.rows1, LANES), F32)] * s.tiles_s
    up = list(down)
    for o in range(s.planes):
        sums = [c_ref[(o - 1) % n]]
        sums += [c_ref[(o - 1 + d) % n] + c_ref[(o - 1 - d) % n] for d in range(1, R + 1)]
        for t in range(TERMS):
            x = sums[0] * tap_ref[2 * TERMS + t, 0]
            for d in range(1, R + 1):
                x += sums[d] * tap_ref[2 * TERMS + t, d]
            k = t * s.planes + o
            w_ref[k] = x
            tile, slot = divmod(k, s.per_tile)
            at = slot * s.strip
            here = (lane >= at) & (lane < at + s.strip)
            down[tile] = jnp.where(here, turn(x, at), down[tile])
            up[tile] = jnp.where(here, turn(x, at - (s.wide1 - s.strip)), up[tile])
    coarse = []
    for j in range(s.cz[2]):
        at = lambda d: c_ref[(2 * j + d) % n]
        coarse.append(at(0) + NEAR * (at(1) + at(-1)) + FAR * (at(3) + at(-3)))
    high, low = halves(jnp.concatenate(coarse, axis=0))
    ry2 = ry2_ref[...].astype(BF16)
    rx2 = rx2_ref[...].astype(BF16)
    along = dot(high, ry2) + dot(low, ry2)
    shares = []
    for j in range(s.cz[2]):
        high, low = halves(along[j * s.rows1 : (j + 1) * s.rows1])
        shares.append(dot(rx2, high) + dot(rx2, low))
    me = lax.axis_index("gy")
    base = s.tiles_s * s.rows1
    coarse = packed(shares, s.wide2, s.tiles2)
    for shift in range(s.gy):
        slot = lax.rem(me + shift, s.gy)
        strips = {1: up, s.gy - 1: down}.get(shift)
        for t in range(s.tiles_s if strips else 0):
            send_ref[slot, t * s.rows1 : (t + 1) * s.rows1] = strips[t]
        for t, x in enumerate(coarse):
            send_ref[slot, base + t * s.rows2 : base + (t + 1) * s.rows2] = x


def along_kernel(s, z_ref, w_ref, got_ref, y1h_ref, y1l_ref, y2h_ref, y2l_ref, d_ref, yb_ref):
    me = lax.axis_index("gy")
    slots = [lax.rem(me + shift, s.gy) for shift in range(s.gy)]
    base = s.tiles_s * s.rows1
    lane = lanes_of((s.rows1, LANES))
    end = s.y1 + R
    for t in range(TERMS):
        cells = []
        for o in range(s.planes):
            k = t * s.planes + o
            tile, slot = divmod(k, s.per_tile)
            rows = slice(tile * s.rows1, (tile + 1) * s.rows1)
            at = slot * s.strip
            x = turn(w_ref[k], R)
            x += jnp.where(lane < s.strip, turn(got_ref[slots[-1], rows], -at), 0.0)
            x += jnp.where((lane >= end) & (lane < end + s.strip), turn(got_ref[slots[1], rows], end - at), 0.0)
            cells.append(x)
        columns = slice(t * s.ny, (t + 1) * s.ny)
        out = dot3(jnp.concatenate(cells, axis=0), y1h_ref[:, columns], y1l_ref[:, columns])
        for o in range(s.planes):
            d_ref[t * s.rows1 : (t + 1) * s.rows1, o * s.ny : (o + 1) * s.ny] = out[o * s.rows1 : (o + 1) * s.rows1]
    cells = []
    for j in range(s.cz[2]):
        out = None
        for b in range(s.gy):
            tile = lambda t, b=b: got_ref[slots[b], base + t * s.rows2 : base + (t + 1) * s.rows2]
            x = unpacked(tile, j, s.wide2, (b * s.y2 - 2) % LANES)
            out = x if out is None else out + x
        cells.append(out)
    yb = dot3(jnp.concatenate(cells, axis=0), y2h_ref[...], y2l_ref[...])
    for j in range(s.cz[2]):
        for q in range(2 * TERMS):
            yb_ref[q, j] = yb[j * s.rows2 : (j + 1) * s.rows2, q * s.ny : (q + 1) * s.ny]
    for o in range(s.planes):
        for q in range(2 * TERMS):
            x = yb_ref[q, 0] * z_ref[q * s.zrows + o, 0]
            for j in range(1, s.cz[2]):
                x += yb_ref[q, j] * z_ref[q * s.zrows + o, j]
            at = TERMS * s.rows1 + q * s.rows2
            d_ref[at : at + s.rows2, o * s.ny : (o + 1) * s.ny] = x


def across(s, d_ref, xh_ref, xl_ref, shift):
    rows = slice(shift * s.nx, (shift + 1) * s.nx)
    high, low = halves(d_ref[...])
    return dot(xh_ref[rows], high) + dot(xl_ref[rows], high) + dot(xh_ref[rows], low)


def away_kernel(s, d_ref, xh_ref, xl_ref, *g_refs):
    for shift, ref in enumerate(g_refs):
        ref[...] = across(s, d_ref, xh_ref, xl_ref, shift + 1)


def prolonged(s, level, z):
    m = z // 2 + 1
    if z % 2 == 0:
        return level[m]
    return NEAR * (level[m] + level[m + 1]) + FAR * (level[m - 1] + level[m + 2])


def home_kernel(s, d_ref, xh_ref, xl_ref, own_ref, low_ref, high_ref, out_ref):
    g = across(s, d_ref, xh_ref, xl_ref, 0)
    level = [g[:, o * s.ny : (o + 1) * s.ny] for o in range(s.planes)]
    for z in range(s.nz):
        x = prolonged(s, level, z) + own_ref[z]
        if z < R:
            x += low_ref[z]
        if z >= s.nz - R:
            x += high_ref[z - (s.nz - R)]
        out_ref[z] = x


def last_kernel(s, home_ref, *refs):
    g_refs, out_ref = refs[:-1], refs[-1]
    level = []
    for o in range(s.planes):
        columns = slice(o * s.ny, (o + 1) * s.ny)
        x = g_refs[0][:, columns]
        for ref in g_refs[1:]:
            x += ref[:, columns]
        level.append(x)
    for z in range(s.nz):
        out_ref[z] = home_ref[z] + prolonged(s, level, z)


def call(kernel, name, operands, out_shapes, scalars=(), after=(), scratch=(), flops=0):
    operands = list(operands) + list(after)

    def spec(i):
        if i >= len(operands) - len(after):
            return pl.BlockSpec(memory_space=pl.ANY)
        return pl.BlockSpec(memory_space=pltpu.SMEM if i in scalars else pltpu.VMEM)

    moved = sum(x.size * x.dtype.itemsize for x in operands)
    moved += sum(int(np.prod(x.shape)) * x.dtype.itemsize for x in out_shapes)
    return pl.pallas_call(
        kernel,
        name=name,
        out_shape=out_shapes,
        in_specs=[spec(i) for i in range(len(operands))],
        out_specs=[pl.BlockSpec(memory_space=pltpu.VMEM)] * len(out_shapes),
        scratch_shapes=list(scratch),
        compiler_params=pltpu.CompilerParams(vmem_limit_bytes=VMEM_LIMIT),
        cost_estimate=pl.CostEstimate(flops=flops, bytes_accessed=moved, transcendentals=0),
    )(*operands)


def arrays(*shapes, dtype=F32):
    return [jax.ShapeDtypeStruct(shape, dtype) for shape in shapes]


def fetch(x, **shifts):
    names = tuple(shifts)
    sizes = [lax.axis_size(n) for n in names]
    pairs = []
    for here in np.ndindex(*sizes):
        there = [(h + shifts[n]) % size for h, n, size in zip(here, names, sizes)]
        pairs.append((int(np.ravel_multi_index(there, sizes)), int(np.ravel_multi_index(here, sizes))))
    return lax.ppermute(x, names if len(names) > 1 else names[0], pairs)


def two(*shape):
    return arrays(shape, shape, dtype=BF16)


def shards(charges, widths, amplitudes):
    s = Sizes(*charges.shape, lax.axis_size("gz"), lax.axis_size("gx"), lax.axis_size("gy"))
    c = {k: jnp.asarray(v) for k, v in constants(s).items()}
    brick = (s.nz, s.nx, s.ny)
    side = (R, s.nx, s.ny)
    taps, y0h, y0l = call(
        functools.partial(tap_kernel, s), "taps", [widths, amplitudes],
        arrays((16, LANES)) + two(2 * LANES, TERMS * s.ny), scalars=(0, 1), flops=6 * 10**8,
    )
    high_rows = fetch(charges, gx=1)
    low_rows = high_rows if s.gx == 2 else fetch(charges, gx=-1)
    strips = (s.fine_tiles, s.ext, LANES)
    share, first_cells, last_cells = call(
        functools.partial(share_kernel, s), "share", [charges, low_rows, high_rows],
        arrays((s.tiles1, s.rows1, LANES), strips, strips), after=[y0h], flops=10**9,
    )
    shares = [share] + [fetch(share, gz=b) for b in range(1, s.gz)]
    left, right = fetch(last_cells, gy=-1), fetch(first_cells, gy=1)
    near, near_down, near_up = call(
        functools.partial(near_kernel, s), "near",
        [taps, charges, low_rows, high_rows, left, right, y0h, y0l],
        arrays(brick, side, side), scalars=(0,),
        scratch=[
            pltpu.VMEM((s.nz * s.ext, 2 * LANES), BF16), pltpu.VMEM((s.nz * s.ext, 2 * LANES), BF16),
            pltpu.VMEM((TERMS, s.nz, s.ext, s.ny), F32), pltpu.VMEM((TERMS,) + brick, F32),
        ],
        flops=6 * 10**9,
    )
    base = s.tiles_s * s.rows1
    size2 = s.tiles2 * s.rows2
    depth = TERMS * (s.rows1 + 2 * s.rows2)
    waves, send = call(
        functools.partial(depth_kernel, s), "depth",
        [taps] + shares + [c["ry2"], c["rx2"]],
        arrays((TERMS * s.planes, s.rows1, LANES), (s.gy, base + size2, LANES)),
        scalars=(0,), after=[near], scratch=[pltpu.VMEM((s.cz[1], s.rows1, LANES), F32)], flops=2 * 10**9,
    )
    named = ("px1", "px2", "px3", "rx3", "py1", "py2", "py3", "ry3", "pz2", "pz3", "rz3")
    z_taps, y1h, y1l, y2h, y2l, xh, xl = call(
        functools.partial(matrix_kernel, s), "matrices",
        [widths, amplitudes] + [c[k] for k in named],
        arrays((2 * TERMS * s.zrows, LANES))
        + two(LANES, TERMS * s.ny) + two(s.cy[2], 2 * TERMS * s.ny)
        + two(s.cx[0], depth),
        scalars=(0, 1), after=[waves], flops=3 * 10**9,
    )
    got = lax.all_to_all(send, "gy", 0, 0)
    near_low, near_high = fetch(near_up, gz=-1), fetch(near_down, gz=1)
    (terms,) = call(
        functools.partial(along_kernel, s), "along",
        [z_taps, waves, got, y1h, y1l, y2h, y2l],
        arrays((depth, s.planes * s.ny)), scalars=(0,),
        scratch=[pltpu.VMEM((2 * TERMS, s.cz[2], s.rows2, s.ny), F32)], flops=3 * 10**9,
    )
    parts = call(
        functools.partial(away_kernel, s), "away", [terms, xh, xl],
        arrays(*[(s.nx, s.planes * s.ny)] * (s.gx - 1)), flops=10**9,
    )
    parts = [fetch(x, gx=-dx) for dx, x in enumerate(parts, 1)]
    (home,) = call(
        functools.partial(home_kernel, s), "home",
        [terms, xh, xl, near, near_low, near_high], arrays(brick), flops=2 * 10**9,
    )
    (out,) = call(
        functools.partial(last_kernel, s), "last", [home] + parts, arrays(brick), flops=10**9,
    )
    return out


def solution(mesh):
    placed = (P("gz", "gx", "gy"), P(), P())
    return jax.shard_map(
        shards, mesh=mesh, in_specs=placed, out_specs=P("gz", "gx", "gy"), check_vma=False
    )
```

```python
import functools

import jax
import jax.numpy as jnp
import ml_dtypes
import numpy as np
from jax import lax
from jax.experimental import pallas as pl
from jax.experimental.pallas import tpu as pltpu
from jax.sharding import PartitionSpec as P

R = 8
TERMS = 3
LANES = 128
NEAR = 9.0 / 16.0
FAR = -1.0 / 16.0
F32 = jnp.float32
BF16 = jnp.bfloat16
VMEM_LIMIT = 40 * 1024 * 1024


def up8(n):
    return -(-n // 8) * 8


class Sizes:
    def __init__(self, nz, nx, ny, gz, gx, gy):
        self.nz, self.nx, self.ny = nz, nx, ny
        self.gz, self.gx, self.gy = gz, gx, gy
        self.z1, self.x1, self.y1 = nz // 2, nx // 2, ny // 2
        self.z2, self.x2, self.y2 = nz // 4, nx // 4, ny // 4
        self.cz = [nz * gz >> l for l in range(4)]
        self.cx = [nx * gx >> l for l in range(4)]
        self.cy = [ny * gy >> l for l in range(4)]
        self.planes = self.z1 + 3
        self.zrows = up8(self.planes)
        self.rows1 = self.x1
        self.rows2 = up8(self.x2 + 3)
        self.wide1 = self.y1 + 3
        self.wide2 = self.y2 + 5
        self.tiles1 = -(-self.planes * self.wide1 // LANES)
        self.tiles2 = -(-self.cz[2] * self.wide2 // LANES)
        self.strip = R + 3
        self.per_tile = LANES // self.strip
        self.tiles_s = -(-TERMS * self.planes // self.per_tile)
        self.fine_tiles = -(-nz // (LANES // R))
        self.ext = nx + 2 * R
        self.depth = TERMS * (self.rows1 + 2 * self.rows2)
        self.depth_lanes = -(-self.depth // LANES) * LANES


def restrict_circle(n):
    m = np.zeros((n // 2, n))
    for i in range(n // 2):
        for d, w in ((0, 1.0), (1, NEAR), (-1, NEAR), (3, FAR), (-3, FAR)):
            m[i, (2 * i + d) % n] += w
    return m


def prolong_circle(n):
    m = np.zeros((2 * n, n))
    for i in range(n):
        m[2 * i, i] += 1.0
        for d, w in ((0, NEAR), (1, NEAR), (-1, FAR), (2, FAR)):
            m[2 * i + 1, (i + d) % n] += w
    return m


def restrict_open(first_in, n_in, first_out, n_out):
    m = np.zeros((n_out, n_in))
    for i in range(n_out):
        for d, w in ((0, 1.0), (1, NEAR), (-1, NEAR), (3, FAR), (-3, FAR)):
            j = 2 * (first_out + i) + d - first_in
            if 0 <= j < n_in:
                m[i, j] = w
    return m


def padded(m, rows, columns):
    out = np.zeros((rows, columns), np.float32)
    out[: m.shape[0], : m.shape[1]] = m
    return out


def exact(m):
    out = m.astype(ml_dtypes.bfloat16)
    assert np.all(out.astype(np.float64) == m)
    return out


def constants(s):
    c = {}
    c["ry2"] = padded(restrict_open(-1, s.wide1, -2, s.wide2).T, LANES, LANES)
    c["rx2"] = padded(restrict_open(0, s.x1, -1, s.x2 + 3), s.rows2, s.rows1)

    def chain(n):
        p1 = prolong_circle(n[1])
        p2 = p1 @ prolong_circle(n[2])
        return p1, p2, p2 @ prolong_circle(n[3])

    def parts(name, m):
        m = m.astype(np.float32)
        c[name] = m.astype(ml_dtypes.bfloat16)
        c[name + "l"] = (m - c[name].astype(np.float32)).astype(ml_dtypes.bfloat16)

    x1, x2, x3 = chain(s.cx)
    c["px1"], c["px2"] = exact(x1), exact(x2)
    parts("px3", x3)
    place = np.zeros((s.cx[2], s.rows2))
    for r in range(s.x2 + 3):
        place[(r - 1) % s.cx[2], r] += 1.0
    rx3 = np.zeros((TERMS, s.cx[3], s.depth_lanes))
    for t in range(TERMS):
        first = TERMS * s.rows1 + (TERMS + t) * s.rows2
        rx3[t, :, first : first + s.rows2] = restrict_circle(s.cx[2]) @ place
    c["rx3"] = exact(rx3)
    _, y2, y3 = chain(s.cy)
    c["py2"] = exact(y2[: s.ny].T)
    parts("py3", y3[: s.ny].T)
    c["ry3"] = exact(restrict_circle(s.cy[2]).T)
    z2 = prolong_circle(s.cz[2])
    z3 = z2 @ prolong_circle(s.cz[3])
    own = [(o - 1) % s.cz[1] for o in range(s.planes)]
    c["pz2"] = exact(padded(z2[own], s.zrows, s.cz[2]))
    c["pz3"] = exact(padded(z3[own], s.zrows, s.cz[3]))
    c["rz3"] = exact(padded(restrict_circle(s.cz[2]), s.cz[3], LANES))
    return c


def halves(x):
    high = x.astype(BF16)
    return high, (x - high.astype(F32)).astype(BF16)


def dot(a, b):
    return jnp.dot(a, b, preferred_element_type=F32)


def dot2(a, b):
    high, low = halves(a)
    return dot(high, b) + dot(low, b)


def dot3(a, b_high, b_low):
    high, low = halves(a)
    return dot(high, b_high) + dot(low, b_high) + dot(high, b_low)


def lanes_of(shape):
    return lax.broadcasted_iota(jnp.int32, shape, len(shape) - 1)


def turn(x, by):
    by = by % x.shape[-1]
    return x if by == 0 else pltpu.roll(x, by, x.ndim - 1)


def packed(planes, wide, tiles):
    out = [None] * tiles

    def add(t, x):
        out[t] = x if out[t] is None else out[t] + x

    for k, x in enumerate(planes):
        t, at = divmod(k * wide, LANES)
        moved = turn(x, at)
        if at + wide <= LANES:
            add(t, moved)
        else:
            lane = lanes_of(x.shape)
            add(t, jnp.where(lane >= at, moved, 0.0))
            add(t + 1, jnp.where(lane < at, moved, 0.0))
    return out


def unpacked(tile, k, wide, shift):
    t, at = divmod(k * wide, LANES)
    x = tile(t)
    lane = lanes_of(x.shape)
    if at + wide > LANES:
        x = jnp.where(lane >= at, x, tile(t + 1))
    x = turn(x, shift - at)
    if shift + wide <= LANES:
        return jnp.where((lane >= shift) & (lane < shift + wide), x, 0.0)
    return jnp.where((lane >= shift) | (lane < shift + wide - LANES), x, 0.0)


def open_restriction(shape, in_dim, first_in, first_out, n_out):
    i = lax.broadcasted_iota(jnp.int32, shape, in_dim) + first_in
    o = lax.broadcasted_iota(jnp.int32, shape, 1 - in_dim)
    d = jnp.abs(i - 2 * (o + first_out))
    w = jnp.where(d == 0, 1.0, jnp.where(d == 1, NEAR, jnp.where(d == 3, FAR, 0.0)))
    return jnp.where(o < n_out, w, 0.0).astype(BF16)


def extended(s, b_ref, lo_ref, hi_ref, z):
    return jnp.concatenate([lo_ref[z, s.nx - R :], b_ref[z], hi_ref[z, 0:R]], axis=0)


def share_kernel(s, b_ref, lo_ref, hi_ref, m_ref, first_ref, last_ref):
    b = [extended(s, b_ref, lo_ref, hi_ref, z) for z in range(s.nz)]
    planes = []
    for k in range(-1, s.z1 + 2):
        out = None
        for d, w in ((0, 1.0), (1, NEAR), (-1, NEAR), (3, FAR), (-3, FAR)):
            if 0 <= 2 * k + d < s.nz:
                term = b[2 * k + d] if d == 0 else b[2 * k + d] * w
                out = term if out is None else out + term
        planes.append(out)
    high, low = halves(jnp.concatenate(planes, axis=0))
    ry1 = open_restriction((s.ny, LANES), 0, 0, -1, s.wide1)
    rx1 = open_restriction((s.rows1, s.ext), 1, -R, 0, s.x1)
    along = dot(high, ry1) + dot(low, ry1)
    shares = []
    for k in range(s.planes):
        high, low = halves(along[k * s.ext : (k + 1) * s.ext])
        shares.append(dot(rx1, high) + dot(rx1, low))
    for t, x in enumerate(packed(shares, s.wide1, s.tiles1)):
        m_ref[t] = x
    lane = lanes_of((s.ext, LANES))
    group = LANES // R
    for t in range(s.fine_tiles):
        first = last = jnp.zeros((s.ext, LANES), F32)
        for g in range(min(group, s.nz - t * group)):
            x = b[t * group + g]
            at = R * ((g + 1) % group)
            first = jnp.where((lane >= at) & (lane < at + R), turn(x, at), first)
            at = R * g
            last = jnp.where((lane >= at) & (lane < at + R), turn(x, at + R - s.ny), last)
        first_ref[t] = first
        last_ref[t] = last


def rows_of(shape):
    return lax.broadcasted_iota(jnp.int32, shape, 0)


def bell(c, d):
    d = jnp.abs(d)
    return jnp.where(d <= R, jnp.exp(c * d * d), 0.0)


def one(ref, level, t):
    return ref[level : level + 1, t : t + 1]


def spreads(w_ref, levels):
    out = []
    for l in levels:
        w = [one(w_ref, l, t) for t in range(TERMS)]
        out.append([-0.5 / (x * x) for x in w])
    return out


def units(coef, distance, valid):
    shape = (up8(len(coef)), LANES)
    row = rows_of(shape)
    column = jnp.zeros(shape, F32)
    for r, c in enumerate(coef):
        column = jnp.where(row == r, c, column)
    lane = lanes_of(shape)
    d = distance(row, lane).astype(F32)
    total = jnp.sum(jnp.where(valid(row, lane), jnp.exp(2.0 * column * d * d), 0.0), axis=1, keepdims=True)
    unit = 1.0 / jnp.sqrt(total)
    return [unit[r : r + 1] for r in range(len(coef))]


def near_units(coef):
    flat = [c for level in coef for c in level]
    out = units(flat, lambda row, lane: lane - R, lambda row, lane: lane <= 2 * R)
    return [out[i : i + TERMS] for i in range(0, len(out), TERMS)]


def tap_kernel(s, w_ref, a_ref, _, tap_ref, x0_ref, y0_ref):
    coef = spreads(w_ref, (0, 1))
    unit = near_units(coef)
    d = lanes_of((1, LANES)).astype(F32)
    for t in range(TERMS):
        tap_ref[t : t + 1] = bell(coef[0][t], d) * (unit[0][t] * one(a_ref, 0, t))
        tap_ref[TERMS + t : TERMS + t + 1] = bell(coef[1][t], d) * (unit[1][t] * one(a_ref, 1, t) * 0.25)
    shape = (s.nx, 3 * s.ext)
    lane = lanes_of(shape)
    part = jnp.where(lane < s.ext, 0, jnp.where(lane < 2 * s.ext, 1, 2))
    d = (lane - part * s.ext - R - rows_of(shape)).astype(F32)
    for t in range(TERMS):
        high, low = halves(bell(coef[0][t], d) * unit[0][t])
        x0_ref[t * s.nx : (t + 1) * s.nx] = jnp.where(part == 1, low.astype(F32), high.astype(F32)).astype(BF16)
    shape = (s.ny + 2 * R, s.ny)
    i = rows_of(shape)
    cell = jnp.where(i < s.ny, i, jnp.where(i < s.ny + R, i - s.ny - R, i - R))
    d = (cell - lanes_of(shape)).astype(F32)
    for t in range(TERMS):
        high, low = halves(bell(coef[0][t], d) * unit[0][t])
        at = 2 * t * s.ny
        y0_ref[s.ny + 2 * R :, at : at + 2 * s.ny] = jnp.zeros((2 * LANES - s.ny - 2 * R, 2 * s.ny), BF16)
        y0_ref[: s.ny + 2 * R, at : at + s.ny] = high
        y0_ref[: s.ny + 2 * R, at + s.ny : at + 2 * s.ny] = low


def matrix_kernel(s, w_ref, a_ref, px1, px2, px3, px3l, rx3, py2, py3, py3l, ry3, pz2, pz3, rz3, _,
                  z_ref, y1_ref, y2h_ref, y2l_ref, xh_ref, xl_ref):
    coef = spreads(w_ref, range(4))
    unit = near_units(coef[:3])
    sizes = [s.cx[3], s.cy[3], s.cz[3]]

    def per_row(row):
        return jnp.where(row < TERMS, sizes[0], jnp.where(row < 2 * TERMS, sizes[1], sizes[2]))

    top = units(
        coef[3] * 3,
        lambda row, lane: jnp.minimum(lane, per_row(row) - lane),
        lambda row, lane: lane < per_row(row),
    )
    top_x, top_y, top_z = top[:TERMS], top[TERMS : 2 * TERMS], top[2 * TERMS :]

    def circle(n, d, c, u):
        d = (d & (n - 1)).astype(F32)
        return (bell(c, d) + bell(c, n - d)) * u

    def full_circle(n, shape, c, u):
        d = ((rows_of(shape) - lanes_of(shape)) & (n - 1)).astype(F32)
        d = jnp.minimum(d, n - d)
        return jnp.exp(c * d * d) * u

    shape = (LANES, s.ny)
    fine = lanes_of(shape)
    d = (rows_of(shape) - (R + 1) - (fine >> 1)).astype(F32)
    even = (fine & 1) == 0
    known = rows_of(shape) < s.y1 + 3 + 2 * R
    wide = (s.cy[2], s.cy[2])
    for t in range(TERMS):
        c = coef[1][t]
        here = bell(c, d)
        between = NEAR * (here + bell(c, d - 1.0)) + FAR * (bell(c, d + 1.0) + bell(c, d - 2.0))
        high, low = halves(jnp.where(known, jnp.where(even, here, between) * unit[1][t], 0.0))
        y1_ref[:, 2 * t * s.ny : (2 * t + 1) * s.ny] = high
        y1_ref[:, (2 * t + 1) * s.ny : (2 * t + 2) * s.ny] = low
        g = circle(s.cy[2], rows_of(wide) - lanes_of(wide), coef[2][t], unit[2][t])
        high, low = halves(dot2(g, py2[...]))
        y2h_ref[:, t * s.ny : (t + 1) * s.ny] = high
        y2l_ref[:, t * s.ny : (t + 1) * s.ny] = low
        g = full_circle(s.cy[3], (s.cy[3], s.cy[3]), coef[3][t], top_y[t])
        high, low = halves(g)
        g = dot(ry3[...], high) + dot(ry3[...], low)
        high, low = halves(dot3(g, py3[...], py3l[...]))
        at = (TERMS + t) * s.ny
        y2h_ref[:, at : at + s.ny] = high
        y2l_ref[:, at : at + s.ny] = low

    def terms(level, first, rows, valid, shift):
        shape = (s.cx[level], s.depth_lanes)
        lane = lanes_of(shape) - first
        column = lane - jnp.where(lane < rows, 0, jnp.where(lane < 2 * rows, rows, 2 * rows))

        def by_term(v):
            return jnp.where(lane < rows, v[0], jnp.where(lane < 2 * rows, v[1], v[2]))

        g = circle(s.cx[level], rows_of(shape) - column + shift, by_term(coef[level]), by_term(unit[level]))
        high, low = halves(jnp.where((lane >= 0) & (lane < TERMS * rows) & (column < valid), g, 0.0))
        return high, low

    high, low = terms(1, 0, s.rows1, s.rows1, 0)
    x = dot(px1[...], high) + dot(px1[...], low)
    high, low = terms(2, TERMS * s.rows1, s.rows2, s.x2 + 3, 1)
    x += dot(px2[...], high) + dot(px2[...], low)
    g = None
    for t in range(TERMS):
        part = dot2(full_circle(s.cx[3], (s.cx[3], s.cx[3]), coef[3][t], top_x[t]), rx3[t])
        g = part if g is None else g + part
    high, low = halves(g)
    x += dot(px3[...], high) + dot(px3l[...], high) + dot(px3[...], low)
    xh_ref[...], xl_ref[...] = halves(x)
    for t in range(TERMS):
        shape = (s.cz[2], LANES)
        g = circle(s.cz[2], rows_of(shape) - lanes_of(shape), coef[2][t], unit[2][t])
        high, low = halves(g * (one(a_ref, 2, t) * 0.0625))
        z_ref[t * s.zrows : (t + 1) * s.zrows] = dot(pz2[...], high) + dot(pz2[...], low)
        g = full_circle(s.cz[3], (s.cz[3], s.cz[3]), coef[3][t], top_z[t])
        high, low = halves(g * (one(a_ref, 3, t) * 0.015625))
        g = dot2(dot(pz3[...], high) + dot(pz3[...], low), rz3[...])
        z_ref[(TERMS + t) * s.zrows : (TERMS + t + 1) * s.zrows] = g


def near_kernel(s, tap_ref, b_ref, lo_ref, hi_ref, left_ref, right_ref, x0_ref, y0_ref,
                own_ref, down_ref, up_ref, e_ref, u_ref, eh_ref, el_ref, v_ref):
    group = LANES // R
    tiles = [extended(s, b_ref, lo_ref, hi_ref, z) for z in range(s.nz)]
    tiles += [left_ref[t] for t in range(s.fine_tiles)] + [right_ref[t] for t in range(s.fine_tiles)]
    for i, x in enumerate(tiles):
        high, low = halves(x)
        columns = slice(i * LANES, (i + 1) * LANES)
        e_ref[0 : s.ext, columns] = high
        e_ref[s.ext : 2 * s.ext, columns] = high
        e_ref[2 * s.ext :, columns] = low
    x0 = x0_ref[...]
    for at in range(0, len(tiles) * LANES, 2 * LANES):
        columns = slice(at, min(at + 2 * LANES, len(tiles) * LANES))
        u_ref[:, columns] = dot(x0, e_ref[:, columns])
    lane = lanes_of((TERMS * s.nx, LANES))
    for z in range(s.nz):
        t, g = divmod(z, group)
        left = u_ref[:, (s.nz + t) * LANES : (s.nz + t + 1) * LANES]
        right = u_ref[:, (s.nz + s.fine_tiles + t) * LANES : (s.nz + s.fine_tiles + t + 1) * LANES]
        strips = turn(jnp.where((lane >= R * g) & (lane < R * g + R), left, right), -R * g)
        for at, x in ((0, u_ref[:, z * LANES : (z + 1) * LANES]), (LANES, strips)):
            high, low = halves(x)
            for t in range(TERMS):
                rows = slice(t * s.nx, (t + 1) * s.nx)
                eh_ref[t, z * s.nx : (z + 1) * s.nx, at : at + LANES] = high[rows]
                el_ref[t, z * s.nx : (z + 1) * s.nx, at : at + LANES] = low[rows]
    step = 4 * s.nx
    for t in range(TERMS):
        at = 2 * t * s.ny
        y0, y0h = y0_ref[:, at : at + 2 * s.ny], y0_ref[:, at : at + s.ny]
        for first in range(0, s.nz * s.nx, step):
            both = dot(eh_ref[t, first : first + step], y0)
            v = both[:, : s.ny] + both[:, s.ny :] + dot(el_ref[t, first : first + step], y0h)
            for q in range(step // s.nx):
                v_ref[t, first // s.nx + q] = v[q * s.nx : (q + 1) * s.nx]

    def depth(r, _):
        rows = pl.ds(pl.multiple_of(r * 8, 8), 8)
        taps = [[tap_ref[t, d] for d in range(R + 1)] for t in range(TERMS)]
        for first in range(-R, s.nz + R, R):
            acc = [None] * R
            for t in range(TERMS):
                for z in range(max(0, first - R), min(s.nz, first + 2 * R)):
                    v = v_ref[t, z, rows]
                    for o in range(R):
                        d = abs(first + o - z)
                        if d <= R:
                            term = v * taps[t][d]
                            acc[o] = term if acc[o] is None else acc[o] + term
            for o in range(R):
                if first < 0:
                    down_ref[o, rows] = acc[o]
                elif first >= s.nz:
                    up_ref[o, rows] = acc[o]
                else:
                    own_ref[first + o, rows] = acc[o]
        return 0

    lax.fori_loop(0, s.nx // 8, depth, 0)


def depth_kernel(s, tap_ref, *refs):
    m_refs = refs[: s.gz]
    ry2_ref, rx2_ref, _, w_ref, down_ref, up_ref, c2_ref, c_ref = refs[s.gz :]
    n = s.cz[1]
    parts = [[] for _ in range(n)]
    for b in range(s.gz):
        for k in range(s.planes):
            parts[(b * s.z1 + k - 1) % n].append((b, k))
    for z in range(n):
        out = None
        for b, k in parts[z]:
            x = unpacked(lambda t, b=b: m_refs[b][t], k, s.wide1, 0)
            out = x if out is None else out + x
        c_ref[z] = out
    lane = lanes_of((s.rows1, LANES))
    down = [jnp.zeros((s.rows1, LANES), F32)] * s.tiles_s
    up = list(down)
    for o in range(s.planes):
        sums = [c_ref[(o - 1) % n]]
        sums += [c_ref[(o - 1 + d) % n] + c_ref[(o - 1 - d) % n] for d in range(1, R + 1)]
        for t in range(TERMS):
            x = sums[0] * tap_ref[TERMS + t, 0]
            for d in range(1, R + 1):
                x += sums[d] * tap_ref[TERMS + t, d]
            k = t * s.planes + o
            w_ref[k] = x
            tile, slot = divmod(k, s.per_tile)
            at = slot * s.strip
            here = (lane >= at) & (lane < at + s.strip)
            down[tile] = jnp.where(here, turn(x, at), down[tile])
            up[tile] = jnp.where(here, turn(x, at - (s.wide1 - s.strip)), up[tile])
    coarse = []
    for j in range(s.cz[2]):
        at = lambda d: c_ref[(2 * j + d) % n]
        coarse.append(at(0) + NEAR * (at(1) + at(-1)) + FAR * (at(3) + at(-3)))
    high, low = halves(jnp.concatenate(coarse, axis=0))
    ry2 = ry2_ref[...].astype(BF16)
    rx2 = rx2_ref[...].astype(BF16)
    along = dot(high, ry2) + dot(low, ry2)
    shares = []
    for j in range(s.cz[2]):
        high, low = halves(along[j * s.rows1 : (j + 1) * s.rows1])
        shares.append(dot(rx2, high) + dot(rx2, low))
    for t in range(s.tiles_s):
        down_ref[t * s.rows1 : (t + 1) * s.rows1] = down[t]
        up_ref[t * s.rows1 : (t + 1) * s.rows1] = up[t]
    base = s.tiles_s * s.rows1
    for t, x in enumerate(packed(shares, s.wide2, s.tiles2)):
        rows = slice(t * s.rows2, (t + 1) * s.rows2)
        c2_ref[rows] = x
        for ref in (down_ref, up_ref):
            ref[base + t * s.rows2 : base + (t + 1) * s.rows2] = x


def along_kernel(s, z_ref, w_ref, *refs):
    c2_refs = refs[: s.gy]
    y1_ref, y2h_ref, y2l_ref, d_ref, yb_ref = refs[s.gy :]
    base = s.tiles_s * s.rows1
    lane = lanes_of((s.rows1, LANES))
    above, below = c2_refs[1], c2_refs[-1]
    end = s.y1 + R
    for t in range(TERMS):
        cells = []
        for o in range(s.planes):
            k = t * s.planes + o
            tile, slot = divmod(k, s.per_tile)
            rows = slice(tile * s.rows1, (tile + 1) * s.rows1)
            at = slot * s.strip
            x = turn(w_ref[k], R)
            x += jnp.where(lane < s.strip, turn(below[rows], -at), 0.0)
            x += jnp.where((lane >= end) & (lane < end + s.strip), turn(above[rows], end - at), 0.0)
            cells.append(x)
        high, low = halves(jnp.concatenate(cells, axis=0))
        at = 2 * t * s.ny
        both = dot(high, y1_ref[:, at : at + 2 * s.ny])
        out = both[:, : s.ny] + both[:, s.ny :] + dot(low, y1_ref[:, at : at + s.ny])
        for o in range(s.planes):
            d_ref[t * s.rows1 : (t + 1) * s.rows1, o * s.ny : (o + 1) * s.ny] = out[o * s.rows1 : (o + 1) * s.rows1]
    cells = []
    for j in range(s.cz[2]):
        out = None
        for b in range(s.gy):
            first = 0 if b == 0 or c2_refs[b].shape[0] == s.tiles2 * s.rows2 else base
            tile = lambda t, b=b, f=first: c2_refs[b][f + t * s.rows2 : f + (t + 1) * s.rows2]
            x = unpacked(tile, j, s.wide2, (b * s.y2 - 2) % LANES)
            out = x if out is None else out + x
        cells.append(out)
    yb = dot3(jnp.concatenate(cells, axis=0), y2h_ref[...], y2l_ref[...])
    for j in range(s.cz[2]):
        for q in range(2 * TERMS):
            yb_ref[q, j] = yb[j * s.rows2 : (j + 1) * s.rows2, q * s.ny : (q + 1) * s.ny]
    for o in range(s.planes):
        for q in range(2 * TERMS):
            x = yb_ref[q, 0] * z_ref[q * s.zrows + o, 0]
            for j in range(1, s.cz[2]):
                x += yb_ref[q, j] * z_ref[q * s.zrows + o, j]
            at = TERMS * s.rows1 + q * s.rows2
            d_ref[at : at + s.rows2, o * s.ny : (o + 1) * s.ny] = x


def across(s, d_ref, xh_ref, xl_ref, shift):
    rows = slice(shift * s.nx, (shift + 1) * s.nx)
    high, low = halves(d_ref[...])
    xh, xl = xh_ref[rows, : s.depth], xl_ref[rows, : s.depth]
    return dot(xh, high) + dot(xl, high) + dot(xh, low)


def away_kernel(s, d_ref, xh_ref, xl_ref, *g_refs):
    for shift, ref in enumerate(g_refs):
        ref[...] = across(s, d_ref, xh_ref, xl_ref, shift + 1)


def prolonged(s, level, z):
    m = z // 2 + 1
    if z % 2 == 0:
        return level[m]
    return NEAR * (level[m] + level[m + 1]) + FAR * (level[m - 1] + level[m + 2])


def home_kernel(s, d_ref, xh_ref, xl_ref, own_ref, low_ref, high_ref, out_ref):
    g = across(s, d_ref, xh_ref, xl_ref, 0)
    level = [g[:, o * s.ny : (o + 1) * s.ny] for o in range(s.planes)]
    for z in range(s.nz):
        x = prolonged(s, level, z) + own_ref[z]
        if z < R:
            x += low_ref[z]
        if z >= s.nz - R:
            x += high_ref[z - (s.nz - R)]
        out_ref[z] = x


def last_kernel(s, home_ref, *refs):
    g_refs, out_ref = refs[:-1], refs[-1]
    level = []
    for o in range(s.planes):
        columns = slice(o * s.ny, (o + 1) * s.ny)
        x = g_refs[0][:, columns]
        for ref in g_refs[1:]:
            x += ref[:, columns]
        level.append(x)
    for z in range(s.nz):
        out_ref[z] = home_ref[z] + prolonged(s, level, z)


def call(kernel, name, operands, out_shapes, scalars=(), after=(), scratch=(), flops=0):
    operands = list(operands) + list(after)

    def spec(i):
        if i >= len(operands) - len(after):
            return pl.BlockSpec(memory_space=pl.ANY)
        return pl.BlockSpec(memory_space=pltpu.SMEM if i in scalars else pltpu.VMEM)

    moved = sum(x.size * x.dtype.itemsize for x in operands)
    moved += sum(int(np.prod(x.shape)) * x.dtype.itemsize for x in out_shapes)
    return pl.pallas_call(
        kernel,
        name=name,
        out_shape=out_shapes,
        in_specs=[spec(i) for i in range(len(operands))],
        out_specs=[pl.BlockSpec(memory_space=pltpu.VMEM)] * len(out_shapes),
        scratch_shapes=list(scratch),
        compiler_params=pltpu.CompilerParams(vmem_limit_bytes=VMEM_LIMIT),
        cost_estimate=pl.CostEstimate(flops=flops, bytes_accessed=moved, transcendentals=0),
    )(*operands)


def arrays(*shapes, dtype=F32):
    return [jax.ShapeDtypeStruct(shape, dtype) for shape in shapes]


def fetch(x, **shifts):
    names = tuple(shifts)
    sizes = [lax.axis_size(n) for n in names]
    pairs = []
    for here in np.ndindex(*sizes):
        there = [(h + shifts[n]) % size for h, n, size in zip(here, names, sizes)]
        pairs.append((int(np.ravel_multi_index(there, sizes)), int(np.ravel_multi_index(here, sizes))))
    return lax.ppermute(x, names if len(names) > 1 else names[0], pairs)


def two(*shape):
    return arrays(shape, shape, dtype=BF16)


def shards(charges, widths, amplitudes):
    s = Sizes(*charges.shape, lax.axis_size("gz"), lax.axis_size("gx"), lax.axis_size("gy"))
    c = {k: jnp.asarray(v) for k, v in constants(s).items()}
    brick = (s.nz, s.nx, s.ny)
    side = (R, s.nx, s.ny)
    high_rows = fetch(charges, gx=1)
    low_rows = high_rows if s.gx == 2 else fetch(charges, gx=-1)
    strips = (s.fine_tiles, s.ext, LANES)
    share, first_cells, last_cells = call(
        functools.partial(share_kernel, s), "share", [charges, low_rows, high_rows],
        arrays((s.tiles1, s.rows1, LANES), strips, strips), flops=10**9,
    )
    shares = [share] + [fetch(share, gz=b) for b in range(1, s.gz)]
    left, right = fetch(last_cells, gy=-1), fetch(first_cells, gy=1)
    taps, x0, y0 = call(
        functools.partial(tap_kernel, s), "taps", [widths, amplitudes],
        arrays((8, LANES))
        + arrays((TERMS * s.nx, 3 * s.ext), (2 * LANES, 2 * TERMS * s.ny), dtype=BF16),
        after=[share], flops=6 * 10**8,
    )
    tiles = s.nz + 2 * s.fine_tiles
    halved = pltpu.VMEM((TERMS, s.nz * s.nx, 2 * LANES), BF16)
    near, near_down, near_up = call(
        functools.partial(near_kernel, s), "near",
        [taps, charges, low_rows, high_rows, left, right, x0, y0],
        arrays(brick, side, side), scalars=(0,),
        scratch=[
            pltpu.VMEM((3 * s.ext, tiles * LANES), BF16), pltpu.VMEM((TERMS * s.nx, tiles * LANES), F32),
            halved, halved, pltpu.VMEM((TERMS,) + brick, F32),
        ],
        flops=5 * 10**9,
    )
    base = s.tiles_s * s.rows1
    size2 = s.tiles2 * s.rows2
    waves, to_low, to_high, coarse = call(
        functools.partial(depth_kernel, s), "depth",
        [taps] + shares + [c["ry2"], c["rx2"]],
        arrays((TERMS * s.planes, s.rows1, LANES), (base + size2, LANES), (base + size2, LANES), (size2, LANES)),
        scalars=(0,), after=[near], scratch=[pltpu.VMEM((s.cz[1], s.rows1, LANES), F32)], flops=2 * 10**9,
    )
    named = ("px1", "px2", "px3", "px3l", "rx3", "py2", "py3", "py3l", "ry3", "pz2", "pz3", "rz3")
    z_taps, y1, y2h, y2l, xh, xl = call(
        functools.partial(matrix_kernel, s), "matrices",
        [widths, amplitudes] + [c[k] for k in named],
        arrays((2 * TERMS * s.zrows, LANES))
        + arrays((LANES, 2 * TERMS * s.ny), dtype=BF16)
        + two(s.cy[2], 2 * TERMS * s.ny) + two(s.cx[0], s.depth_lanes),
        after=[coarse], flops=2 * 10**9,
    )
    coarses = [coarse]
    for b in range(1, s.gy):
        coarses.append(fetch({1: to_low, s.gy - 1: to_high}.get(b, coarse), gy=b))
    near_low, near_high = fetch(near_up, gz=-1), fetch(near_down, gz=1)
    (terms,) = call(
        functools.partial(along_kernel, s), "along",
        [z_taps, waves] + coarses + [y1, y2h, y2l],
        arrays((s.depth, s.planes * s.ny)), scalars=(0,),
        scratch=[pltpu.VMEM((2 * TERMS, s.cz[2], s.rows2, s.ny), F32)], flops=3 * 10**9,
    )
    parts = call(
        functools.partial(away_kernel, s), "away", [terms, xh, xl],
        arrays(*[(s.nx, s.planes * s.ny)] * (s.gx - 1)), flops=10**9,
    )
    parts = [fetch(x, gx=-dx) for dx, x in enumerate(parts, 1)]
    (home,) = call(
        functools.partial(home_kernel, s), "home",
        [terms, xh, xl, near, near_low, near_high], arrays(brick), flops=2 * 10**9,
    )
    (out,) = call(
        functools.partial(last_kernel, s), "last", [home] + parts, arrays(brick), flops=10**9,
    )
    return out


def solution(mesh):
    placed = (P("gz", "gx", "gy"), P(), P())
    return jax.shard_map(
        shards, mesh=mesh, in_specs=placed, out_specs=P("gz", "gx", "gy"), check_vma=False
    )
```

```python
import functools

import jax
import jax.numpy as jnp
import ml_dtypes
import numpy as np
from jax import lax
from jax.experimental import pallas as pl
from jax.experimental.pallas import tpu as pltpu
from jax.sharding import PartitionSpec as P

R = 8
TERMS = 3
LANES = 128
NEAR = 9.0 / 16.0
FAR = -1.0 / 16.0
F32 = jnp.float32
BF16 = jnp.bfloat16
VMEM_LIMIT = 40 * 1024 * 1024


def up8(n):
    return -(-n // 8) * 8


class Sizes:
    def __init__(self, nz, nx, ny, gz, gx, gy):
        self.nz, self.nx, self.ny = nz, nx, ny
        self.gz, self.gx, self.gy = gz, gx, gy
        self.z1, self.x1, self.y1 = nz // 2, nx // 2, ny // 2
        self.z2, self.x2, self.y2 = nz // 4, nx // 4, ny // 4
        self.cz = [nz * gz >> l for l in range(4)]
        self.cx = [nx * gx >> l for l in range(4)]
        self.cy = [ny * gy >> l for l in range(4)]
        self.planes = self.z1 + 3
        self.zrows = up8(self.planes)
        self.rows1 = self.x1
        self.rows2 = up8(self.x2 + 3)
        self.wide1 = self.y1 + 3
        self.wide2 = self.y2 + 5
        self.tiles1 = -(-self.planes * self.wide1 // LANES)
        self.tiles2 = -(-self.cz[2] * self.wide2 // LANES)
        self.strip = R + 3
        self.per_tile = LANES // self.strip
        self.tiles_s = -(-TERMS * self.planes // self.per_tile)
        self.fine_tiles = -(-nz // (LANES // R))
        self.ext = nx + 2 * R
        self.depth = TERMS * (self.rows1 + 2 * self.rows2)
        self.depth_lanes = -(-self.depth // LANES) * LANES


def restrict_circle(n):
    m = np.zeros((n // 2, n))
    for i in range(n // 2):
        for d, w in ((0, 1.0), (1, NEAR), (-1, NEAR), (3, FAR), (-3, FAR)):
            m[i, (2 * i + d) % n] += w
    return m


def prolong_circle(n):
    m = np.zeros((2 * n, n))
    for i in range(n):
        m[2 * i, i] += 1.0
        for d, w in ((0, NEAR), (1, NEAR), (-1, FAR), (2, FAR)):
            m[2 * i + 1, (i + d) % n] += w
    return m


def restrict_open(first_in, n_in, first_out, n_out):
    m = np.zeros((n_out, n_in))
    for i in range(n_out):
        for d, w in ((0, 1.0), (1, NEAR), (-1, NEAR), (3, FAR), (-3, FAR)):
            j = 2 * (first_out + i) + d - first_in
            if 0 <= j < n_in:
                m[i, j] = w
    return m


def padded(m, rows, columns):
    out = np.zeros((rows, columns), np.float32)
    out[: m.shape[0], : m.shape[1]] = m
    return out


def exact(m):
    out = m.astype(ml_dtypes.bfloat16)
    assert np.all(out.astype(np.float64) == m)
    return out


def constants(s):
    c = {}
    c["ry2"] = padded(restrict_open(-1, s.wide1, -2, s.wide2).T, LANES, LANES)
    c["rx2"] = padded(restrict_open(0, s.x1, -1, s.x2 + 3), s.rows2, s.rows1)

    def chain(n):
        p1 = prolong_circle(n[1])
        p2 = p1 @ prolong_circle(n[2])
        return p1, p2, p2 @ prolong_circle(n[3])

    def parts(name, m):
        m = m.astype(np.float32)
        c[name] = m.astype(ml_dtypes.bfloat16)
        c[name + "l"] = (m - c[name].astype(np.float32)).astype(ml_dtypes.bfloat16)

    x1, x2, x3 = chain(s.cx)
    c["px1"], c["px2"] = exact(x1), exact(x2)
    parts("px3", x3)
    place = np.zeros((s.cx[2], s.rows2))
    for r in range(s.x2 + 3):
        place[(r - 1) % s.cx[2], r] += 1.0
    rx3 = np.zeros((TERMS, s.cx[3], s.depth_lanes))
    for t in range(TERMS):
        first = TERMS * s.rows1 + (TERMS + t) * s.rows2
        rx3[t, :, first : first + s.rows2] = restrict_circle(s.cx[2]) @ place
    c["rx3"] = exact(rx3)
    _, y2, y3 = chain(s.cy)
    c["py2"] = exact(y2[: s.ny].T)
    parts("py3", y3[: s.ny].T)
    c["ry3"] = exact(restrict_circle(s.cy[2]).T)
    z2 = prolong_circle(s.cz[2])
    z3 = z2 @ prolong_circle(s.cz[3])
    own = [(o - 1) % s.cz[1] for o in range(s.planes)]
    c["pz2"] = exact(padded(z2[own], s.zrows, s.cz[2]))
    c["pz3"] = exact(padded(z3[own], s.zrows, s.cz[3]))
    c["rz3"] = exact(padded(restrict_circle(s.cz[2]), s.cz[3], LANES))
    return c


def halves(x):
    high = x.astype(BF16)
    return high, (x - high.astype(F32)).astype(BF16)


def dot(a, b):
    return jnp.dot(a, b, preferred_element_type=F32)


def dot2(a, b):
    high, low = halves(a)
    return dot(high, b) + dot(low, b)


def dot3(a, b_high, b_low):
    high, low = halves(a)
    return dot(high, b_high) + dot(low, b_high) + dot(high, b_low)


def lanes_of(shape):
    return lax.broadcasted_iota(jnp.int32, shape, len(shape) - 1)


def turn(x, by):
    by = by % x.shape[-1]
    return x if by == 0 else pltpu.roll(x, by, x.ndim - 1)


def packed(planes, wide, tiles):
    out = [None] * tiles

    def add(t, x):
        out[t] = x if out[t] is None else out[t] + x

    for k, x in enumerate(planes):
        t, at = divmod(k * wide, LANES)
        moved = turn(x, at)
        if at + wide <= LANES:
            add(t, moved)
        else:
            lane = lanes_of(x.shape)
            add(t, jnp.where(lane >= at, moved, 0.0))
            add(t + 1, jnp.where(lane < at, moved, 0.0))
    return out


def unpacked(tile, k, wide, shift):
    t, at = divmod(k * wide, LANES)
    x = tile(t)
    lane = lanes_of(x.shape)
    if at + wide > LANES:
        x = jnp.where(lane >= at, x, tile(t + 1))
    x = turn(x, shift - at)
    if shift + wide <= LANES:
        return jnp.where((lane >= shift) & (lane < shift + wide), x, 0.0)
    return jnp.where((lane >= shift) | (lane < shift + wide - LANES), x, 0.0)


def open_restriction(shape, in_dim, first_in, first_out, n_out):
    i = lax.broadcasted_iota(jnp.int32, shape, in_dim) + first_in
    o = lax.broadcasted_iota(jnp.int32, shape, 1 - in_dim)
    d = jnp.abs(i - 2 * (o + first_out))
    w = jnp.where(d == 0, 1.0, jnp.where(d == 1, NEAR, jnp.where(d == 3, FAR, 0.0)))
    return jnp.where(o < n_out, w, 0.0).astype(BF16)


def extended(s, b_ref, lo_ref, hi_ref, z):
    return jnp.concatenate([lo_ref[z, s.nx - R :], b_ref[z], hi_ref[z, 0:R]], axis=0)


def share_kernel(s, b_ref, lo_ref, hi_ref, _, m_ref, first_ref, last_ref):
    b = [extended(s, b_ref, lo_ref, hi_ref, z) for z in range(s.nz)]
    planes = []
    for k in range(-1, s.z1 + 2):
        out = None
        for d, w in ((0, 1.0), (1, NEAR), (-1, NEAR), (3, FAR), (-3, FAR)):
            if 0 <= 2 * k + d < s.nz:
                term = b[2 * k + d] if d == 0 else b[2 * k + d] * w
                out = term if out is None else out + term
        planes.append(out)
    high, low = halves(jnp.concatenate(planes, axis=0))
    ry1 = open_restriction((s.ny, LANES), 0, 0, -1, s.wide1)
    rx1 = open_restriction((s.rows1, s.ext), 1, -R, 0, s.x1)
    along = dot(high, ry1) + dot(low, ry1)
    shares = []
    for k in range(s.planes):
        high, low = halves(along[k * s.ext : (k + 1) * s.ext])
        shares.append(dot(rx1, high) + dot(rx1, low))
    for t, x in enumerate(packed(shares, s.wide1, s.tiles1)):
        m_ref[t] = x
    lane = lanes_of((s.ext, LANES))
    group = LANES // R
    for t in range(s.fine_tiles):
        first = last = jnp.zeros((s.ext, LANES), F32)
        for g in range(min(group, s.nz - t * group)):
            x = b[t * group + g]
            at = R * ((g + 1) % group)
            first = jnp.where((lane >= at) & (lane < at + R), turn(x, at), first)
            at = R * g
            last = jnp.where((lane >= at) & (lane < at + R), turn(x, at + R - s.ny), last)
        first_ref[t] = first
        last_ref[t] = last


def rows_of(shape):
    return lax.broadcasted_iota(jnp.int32, shape, 0)


def bell(c, d):
    d = jnp.abs(d)
    return jnp.where(d <= R, jnp.exp(c * d * d), 0.0)


def one(ref, level, t):
    return ref[level : level + 1, t : t + 1]


def spreads(w_ref, levels):
    out = []
    for l in levels:
        w = [one(w_ref, l, t) for t in range(TERMS)]
        out.append([-0.5 / (x * x) for x in w])
    return out


def units(coef, distance, valid):
    shape = (up8(len(coef)), LANES)
    row = rows_of(shape)
    column = jnp.zeros(shape, F32)
    for r, c in enumerate(coef):
        column = jnp.where(row == r, c, column)
    lane = lanes_of(shape)
    d = distance(row, lane).astype(F32)
    total = jnp.sum(jnp.where(valid(row, lane), jnp.exp(2.0 * column * d * d), 0.0), axis=1, keepdims=True)
    unit = 1.0 / jnp.sqrt(total)
    return [unit[r : r + 1] for r in range(len(coef))]


def near_units(coef):
    flat = [c for level in coef for c in level]
    out = units(flat, lambda row, lane: lane - R, lambda row, lane: lane <= 2 * R)
    return [out[i : i + TERMS] for i in range(0, len(out), TERMS)]


def tap_kernel(s, w_ref, a_ref, tap_ref, x0_ref, y0_ref):
    coef = spreads(w_ref, (0, 1))
    unit = near_units(coef)
    d = lanes_of((1, LANES)).astype(F32)
    for t in range(TERMS):
        tap_ref[t : t + 1] = bell(coef[0][t], d) * (unit[0][t] * one(a_ref, 0, t))
        tap_ref[TERMS + t : TERMS + t + 1] = bell(coef[1][t], d) * (unit[1][t] * one(a_ref, 1, t) * 0.25)
    shape = (s.nx, 3 * s.ext)
    lane = lanes_of(shape)
    part = jnp.where(lane < s.ext, 0, jnp.where(lane < 2 * s.ext, 1, 2))
    d = (lane - part * s.ext - R - rows_of(shape)).astype(F32)
    for t in range(TERMS):
        high, low = halves(bell(coef[0][t], d) * unit[0][t])
        x0_ref[t * s.nx : (t + 1) * s.nx] = jnp.where(part == 1, low.astype(F32), high.astype(F32)).astype(BF16)
    shape = (s.ny + 2 * R, s.ny)
    i = rows_of(shape)
    cell = jnp.where(i < s.ny, i, jnp.where(i < s.ny + R, i - s.ny - R, i - R))
    d = (cell - lanes_of(shape)).astype(F32)
    for t in range(TERMS):
        high, low = halves(bell(coef[0][t], d) * unit[0][t])
        at = 2 * t * s.ny
        y0_ref[s.ny + 2 * R :, at : at + 2 * s.ny] = jnp.zeros((2 * LANES - s.ny - 2 * R, 2 * s.ny), BF16)
        y0_ref[: s.ny + 2 * R, at : at + s.ny] = high
        y0_ref[: s.ny + 2 * R, at + s.ny : at + 2 * s.ny] = low


def matrix_kernel(s, w_ref, a_ref, px1, px2, px3, px3l, rx3, py2, py3, py3l, ry3, pz2, pz3, rz3, _,
                  z_ref, y1_ref, y2h_ref, y2l_ref, xh_ref, xl_ref):
    coef = spreads(w_ref, range(4))
    unit = near_units(coef[:3])
    sizes = [s.cx[3], s.cy[3], s.cz[3]]

    def per_row(row):
        return jnp.where(row < TERMS, sizes[0], jnp.where(row < 2 * TERMS, sizes[1], sizes[2]))

    top = units(
        coef[3] * 3,
        lambda row, lane: jnp.minimum(lane, per_row(row) - lane),
        lambda row, lane: lane < per_row(row),
    )
    top_x, top_y, top_z = top[:TERMS], top[TERMS : 2 * TERMS], top[2 * TERMS :]

    def circle(n, d, c, u):
        d = (d & (n - 1)).astype(F32)
        return (bell(c, d) + bell(c, n - d)) * u

    def full_circle(n, shape, c, u):
        d = ((rows_of(shape) - lanes_of(shape)) & (n - 1)).astype(F32)
        d = jnp.minimum(d, n - d)
        return jnp.exp(c * d * d) * u

    shape = (LANES, s.ny)
    fine = lanes_of(shape)
    d = (rows_of(shape) - (R + 1) - (fine >> 1)).astype(F32)
    even = (fine & 1) == 0
    known = rows_of(shape) < s.y1 + 3 + 2 * R
    wide = (s.cy[2], s.cy[2])
    for t in range(TERMS):
        c = coef[1][t]
        here = bell(c, d)
        between = NEAR * (here + bell(c, d - 1.0)) + FAR * (bell(c, d + 1.0) + bell(c, d - 2.0))
        high, low = halves(jnp.where(known, jnp.where(even, here, between) * unit[1][t], 0.0))
        y1_ref[:, 2 * t * s.ny : (2 * t + 1) * s.ny] = high
        y1_ref[:, (2 * t + 1) * s.ny : (2 * t + 2) * s.ny] = low
        g = circle(s.cy[2], rows_of(wide) - lanes_of(wide), coef[2][t], unit[2][t])
        high, low = halves(dot2(g, py2[...]))
        y2h_ref[:, t * s.ny : (t + 1) * s.ny] = high
        y2l_ref[:, t * s.ny : (t + 1) * s.ny] = low
        g = full_circle(s.cy[3], (s.cy[3], s.cy[3]), coef[3][t], top_y[t])
        high, low = halves(g)
        g = dot(ry3[...], high) + dot(ry3[...], low)
        high, low = halves(dot3(g, py3[...], py3l[...]))
        at = (TERMS + t) * s.ny
        y2h_ref[:, at : at + s.ny] = high
        y2l_ref[:, at : at + s.ny] = low

    def terms(level, first, rows, valid, shift):
        shape = (s.cx[level], s.depth_lanes)
        lane = lanes_of(shape) - first
        column = lane - jnp.where(lane < rows, 0, jnp.where(lane < 2 * rows, rows, 2 * rows))

        def by_term(v):
            return jnp.where(lane < rows, v[0], jnp.where(lane < 2 * rows, v[1], v[2]))

        g = circle(s.cx[level], rows_of(shape) - column + shift, by_term(coef[level]), by_term(unit[level]))
        high, low = halves(jnp.where((lane >= 0) & (lane < TERMS * rows) & (column < valid), g, 0.0))
        return high, low

    high, low = terms(1, 0, s.rows1, s.rows1, 0)
    x = dot(px1[...], high) + dot(px1[...], low)
    high, low = terms(2, TERMS * s.rows1, s.rows2, s.x2 + 3, 1)
    x += dot(px2[...], high) + dot(px2[...], low)
    g = None
    for t in range(TERMS):
        part = dot2(full_circle(s.cx[3], (s.cx[3], s.cx[3]), coef[3][t], top_x[t]), rx3[t])
        g = part if g is None else g + part
    high, low = halves(g)
    x += dot(px3[...], high) + dot(px3l[...], high) + dot(px3[...], low)
    xh_ref[...], xl_ref[...] = halves(x)
    for t in range(TERMS):
        shape = (s.cz[2], LANES)
        g = circle(s.cz[2], rows_of(shape) - lanes_of(shape), coef[2][t], unit[2][t])
        high, low = halves(g * (one(a_ref, 2, t) * 0.0625))
        z_ref[t * s.zrows : (t + 1) * s.zrows] = dot(pz2[...], high) + dot(pz2[...], low)
        g = full_circle(s.cz[3], (s.cz[3], s.cz[3]), coef[3][t], top_z[t])
        high, low = halves(g * (one(a_ref, 3, t) * 0.015625))
        g = dot2(dot(pz3[...], high) + dot(pz3[...], low), rz3[...])
        z_ref[(TERMS + t) * s.zrows : (TERMS + t + 1) * s.zrows] = g


def near_kernel(s, tap_ref, b_ref, lo_ref, hi_ref, left_ref, right_ref, x0_ref, y0_ref,
                own_ref, down_ref, up_ref, e_ref, u_ref, eh_ref, el_ref, v_ref):
    group = LANES // R
    tiles = [extended(s, b_ref, lo_ref, hi_ref, z) for z in range(s.nz)]
    tiles += [left_ref[t] for t in range(s.fine_tiles)] + [right_ref[t] for t in range(s.fine_tiles)]
    for i, x in enumerate(tiles):
        high, low = halves(x)
        columns = slice(i * LANES, (i + 1) * LANES)
        e_ref[0 : s.ext, columns] = high
        e_ref[s.ext : 2 * s.ext, columns] = high
        e_ref[2 * s.ext :, columns] = low
    x0 = x0_ref[...]
    for at in range(0, len(tiles) * LANES, 2 * LANES):
        columns = slice(at, min(at + 2 * LANES, len(tiles) * LANES))
        u_ref[:, columns] = dot(x0, e_ref[:, columns])
    lane = lanes_of((TERMS * s.nx, LANES))
    for z in range(s.nz):
        t, g = divmod(z, group)
        left = u_ref[:, (s.nz + t) * LANES : (s.nz + t + 1) * LANES]
        right = u_ref[:, (s.nz + s.fine_tiles + t) * LANES : (s.nz + s.fine_tiles + t + 1) * LANES]
        strips = turn(jnp.where((lane >= R * g) & (lane < R * g + R), left, right), -R * g)
        for at, x in ((0, u_ref[:, z * LANES : (z + 1) * LANES]), (LANES, strips)):
            high, low = halves(x)
            for t in range(TERMS):
                rows = slice(t * s.nx, (t + 1) * s.nx)
                eh_ref[t, z * s.nx : (z + 1) * s.nx, at : at + LANES] = high[rows]
                el_ref[t, z * s.nx : (z + 1) * s.nx, at : at + LANES] = low[rows]
    step = 4 * s.nx
    for t in range(TERMS):
        at = 2 * t * s.ny
        y0, y0h = y0_ref[:, at : at + 2 * s.ny], y0_ref[:, at : at + s.ny]
        for first in range(0, s.nz * s.nx, step):
            both = dot(eh_ref[t, first : first + step], y0)
            v = both[:, : s.ny] + both[:, s.ny :] + dot(el_ref[t, first : first + step], y0h)
            for q in range(step // s.nx):
                v_ref[t, first // s.nx + q] = v[q * s.nx : (q + 1) * s.nx]

    def depth(r, _):
        rows = pl.ds(pl.multiple_of(r * 8, 8), 8)
        taps = [[tap_ref[t, d] for d in range(R + 1)] for t in range(TERMS)]
        for first in range(-R, s.nz + R, R):
            acc = [None] * R
            for t in range(TERMS):
                for z in range(max(0, first - R), min(s.nz, first + 2 * R)):
                    v = v_ref[t, z, rows]
                    for o in range(R):
                        d = abs(first + o - z)
                        if d <= R:
                            term = v * taps[t][d]
                            acc[o] = term if acc[o] is None else acc[o] + term
            for o in range(R):
                if first < 0:
                    down_ref[o, rows] = acc[o]
                elif first >= s.nz:
                    up_ref[o, rows] = acc[o]
                else:
                    own_ref[first + o, rows] = acc[o]
        return 0

    lax.fori_loop(0, s.nx // 8, depth, 0)


def depth_kernel(s, tap_ref, *refs):
    m_refs = refs[: s.gz]
    ry2_ref, rx2_ref, _, w_ref, down_ref, up_ref, c2_ref, c_ref = refs[s.gz :]
    n = s.cz[1]
    parts = [[] for _ in range(n)]
    for b in range(s.gz):
        for k in range(s.planes):
            parts[(b * s.z1 + k - 1) % n].append((b, k))
    for z in range(n):
        out = None
        for b, k in parts[z]:
            x = unpacked(lambda t, b=b: m_refs[b][t], k, s.wide1, 0)
            out = x if out is None else out + x
        c_ref[z] = out
    lane = lanes_of((s.rows1, LANES))
    down = [jnp.zeros((s.rows1, LANES), F32)] * s.tiles_s
    up = list(down)
    for o in range(s.planes):
        sums = [c_ref[(o - 1) % n]]
        sums += [c_ref[(o - 1 + d) % n] + c_ref[(o - 1 - d) % n] for d in range(1, R + 1)]
        for t in range(TERMS):
            x = sums[0] * tap_ref[TERMS + t, 0]
            for d in range(1, R + 1):
                x += sums[d] * tap_ref[TERMS + t, d]
            k = t * s.planes + o
            w_ref[k] = x
            tile, slot = divmod(k, s.per_tile)
            at = slot * s.strip
            here = (lane >= at) & (lane < at + s.strip)
            down[tile] = jnp.where(here, turn(x, at), down[tile])
            up[tile] = jnp.where(here, turn(x, at - (s.wide1 - s.strip)), up[tile])
    coarse = []
    for j in range(s.cz[2]):
        at = lambda d: c_ref[(2 * j + d) % n]
        coarse.append(at(0) + NEAR * (at(1) + at(-1)) + FAR * (at(3) + at(-3)))
    high, low = halves(jnp.concatenate(coarse, axis=0))
    ry2 = ry2_ref[...].astype(BF16)
    rx2 = rx2_ref[...].astype(BF16)
    along = dot(high, ry2) + dot(low, ry2)
    shares = []
    for j in range(s.cz[2]):
        high, low = halves(along[j * s.rows1 : (j + 1) * s.rows1])
        shares.append(dot(rx2, high) + dot(rx2, low))
    for t in range(s.tiles_s):
        down_ref[t * s.rows1 : (t + 1) * s.rows1] = down[t]
        up_ref[t * s.rows1 : (t + 1) * s.rows1] = up[t]
    base = s.tiles_s * s.rows1
    for t, x in enumerate(packed(shares, s.wide2, s.tiles2)):
        rows = slice(t * s.rows2, (t + 1) * s.rows2)
        c2_ref[rows] = x
        for ref in (down_ref, up_ref):
            ref[base + t * s.rows2 : base + (t + 1) * s.rows2] = x


def along_kernel(s, z_ref, w_ref, *refs):
    c2_refs = refs[: s.gy]
    y1_ref, y2h_ref, y2l_ref, d_ref, yb_ref = refs[s.gy :]
    base = s.tiles_s * s.rows1
    lane = lanes_of((s.rows1, LANES))
    above, below = c2_refs[1], c2_refs[-1]
    end = s.y1 + R
    for t in range(TERMS):
        cells = []
        for o in range(s.planes):
            k = t * s.planes + o
            tile, slot = divmod(k, s.per_tile)
            rows = slice(tile * s.rows1, (tile + 1) * s.rows1)
            at = slot * s.strip
            x = turn(w_ref[k], R)
            x += jnp.where(lane < s.strip, turn(below[rows], -at), 0.0)
            x += jnp.where((lane >= end) & (lane < end + s.strip), turn(above[rows], end - at), 0.0)
            cells.append(x)
        high, low = halves(jnp.concatenate(cells, axis=0))
        at = 2 * t * s.ny
        both = dot(high, y1_ref[:, at : at + 2 * s.ny])
        out = both[:, : s.ny] + both[:, s.ny :] + dot(low, y1_ref[:, at : at + s.ny])
        for o in range(s.planes):
            d_ref[t * s.rows1 : (t + 1) * s.rows1, o * s.ny : (o + 1) * s.ny] = out[o * s.rows1 : (o + 1) * s.rows1]
    cells = []
    for j in range(s.cz[2]):
        out = None
        for b in range(s.gy):
            first = 0 if b == 0 or c2_refs[b].shape[0] == s.tiles2 * s.rows2 else base
            tile = lambda t, b=b, f=first: c2_refs[b][f + t * s.rows2 : f + (t + 1) * s.rows2]
            x = unpacked(tile, j, s.wide2, (b * s.y2 - 2) % LANES)
            out = x if out is None else out + x
        cells.append(out)
    yb = dot3(jnp.concatenate(cells, axis=0), y2h_ref[...], y2l_ref[...])
    for j in range(s.cz[2]):
        for q in range(2 * TERMS):
            yb_ref[q, j] = yb[j * s.rows2 : (j + 1) * s.rows2, q * s.ny : (q + 1) * s.ny]
    for o in range(s.planes):
        for q in range(2 * TERMS):
            x = yb_ref[q, 0] * z_ref[q * s.zrows + o, 0]
            for j in range(1, s.cz[2]):
                x += yb_ref[q, j] * z_ref[q * s.zrows + o, j]
            at = TERMS * s.rows1 + q * s.rows2
            d_ref[at : at + s.rows2, o * s.ny : (o + 1) * s.ny] = x


def across(s, d_ref, xh_ref, xl_ref, shift):
    rows = slice(shift * s.nx, (shift + 1) * s.nx)
    high, low = halves(d_ref[...])
    xh, xl = xh_ref[rows, : s.depth], xl_ref[rows, : s.depth]
    return dot(xh, high) + dot(xl, high) + dot(xh, low)


def away_kernel(s, d_ref, xh_ref, xl_ref, *g_refs):
    for shift, ref in enumerate(g_refs):
        ref[...] = across(s, d_ref, xh_ref, xl_ref, shift + 1)


def prolonged(s, level, z):
    m = z // 2 + 1
    if z % 2 == 0:
        return level[m]
    return NEAR * (level[m] + level[m + 1]) + FAR * (level[m - 1] + level[m + 2])


def home_kernel(s, d_ref, xh_ref, xl_ref, own_ref, low_ref, high_ref, out_ref):
    g = across(s, d_ref, xh_ref, xl_ref, 0)
    level = [g[:, o * s.ny : (o + 1) * s.ny] for o in range(s.planes)]
    for z in range(s.nz):
        x = prolonged(s, level, z) + own_ref[z]
        if z < R:
            x += low_ref[z]
        if z >= s.nz - R:
            x += high_ref[z - (s.nz - R)]
        out_ref[z] = x


def last_kernel(s, home_ref, *refs):
    g_refs, out_ref = refs[:-1], refs[-1]
    level = []
    for o in range(s.planes):
        columns = slice(o * s.ny, (o + 1) * s.ny)
        x = g_refs[0][:, columns]
        for ref in g_refs[1:]:
            x += ref[:, columns]
        level.append(x)
    for z in range(s.nz):
        out_ref[z] = home_ref[z] + prolonged(s, level, z)


def call(kernel, name, operands, out_shapes, scalars=(), after=(), scratch=(), flops=0):
    operands = list(operands) + list(after)

    def spec(i):
        if i >= len(operands) - len(after):
            return pl.BlockSpec(memory_space=pl.ANY)
        return pl.BlockSpec(memory_space=pltpu.SMEM if i in scalars else pltpu.VMEM)

    moved = sum(x.size * x.dtype.itemsize for x in operands)
    moved += sum(int(np.prod(x.shape)) * x.dtype.itemsize for x in out_shapes)
    return pl.pallas_call(
        kernel,
        name=name,
        out_shape=out_shapes,
        in_specs=[spec(i) for i in range(len(operands))],
        out_specs=[pl.BlockSpec(memory_space=pltpu.VMEM)] * len(out_shapes),
        scratch_shapes=list(scratch),
        compiler_params=pltpu.CompilerParams(vmem_limit_bytes=VMEM_LIMIT),
        cost_estimate=pl.CostEstimate(flops=flops, bytes_accessed=moved, transcendentals=0),
    )(*operands)


def arrays(*shapes, dtype=F32):
    return [jax.ShapeDtypeStruct(shape, dtype) for shape in shapes]


def fetch(x, **shifts):
    names = tuple(shifts)
    sizes = [lax.axis_size(n) for n in names]
    pairs = []
    for here in np.ndindex(*sizes):
        there = [(h + shifts[n]) % size for h, n, size in zip(here, names, sizes)]
        pairs.append((int(np.ravel_multi_index(there, sizes)), int(np.ravel_multi_index(here, sizes))))
    return lax.ppermute(x, names if len(names) > 1 else names[0], pairs)


def two(*shape):
    return arrays(shape, shape, dtype=BF16)


def shards(charges, widths, amplitudes):
    s = Sizes(*charges.shape, lax.axis_size("gz"), lax.axis_size("gx"), lax.axis_size("gy"))
    c = {k: jnp.asarray(v) for k, v in constants(s).items()}
    brick = (s.nz, s.nx, s.ny)
    side = (R, s.nx, s.ny)
    taps, x0, y0 = call(
        functools.partial(tap_kernel, s), "taps", [widths, amplitudes],
        arrays((8, LANES))
        + arrays((TERMS * s.nx, 3 * s.ext), (2 * LANES, 2 * TERMS * s.ny), dtype=BF16),
        flops=6 * 10**8,
    )
    high_rows = fetch(charges, gx=1)
    low_rows = high_rows if s.gx == 2 else fetch(charges, gx=-1)
    strips = (s.fine_tiles, s.ext, LANES)
    share, first_cells, last_cells = call(
        functools.partial(share_kernel, s), "share", [charges, low_rows, high_rows],
        arrays((s.tiles1, s.rows1, LANES), strips, strips), after=[x0], flops=10**9,
    )
    shares = [share] + [fetch(share, gz=b) for b in range(1, s.gz)]
    left, right = fetch(last_cells, gy=-1), fetch(first_cells, gy=1)
    tiles = s.nz + 2 * s.fine_tiles
    halved = pltpu.VMEM((TERMS, s.nz * s.nx, 2 * LANES), BF16)
    near, near_down, near_up = call(
        functools.partial(near_kernel, s), "near",
        [taps, charges, low_rows, high_rows, left, right, x0, y0],
        arrays(brick, side, side), scalars=(0,),
        scratch=[
            pltpu.VMEM((3 * s.ext, tiles * LANES), BF16), pltpu.VMEM((TERMS * s.nx, tiles * LANES), F32),
            halved, halved, pltpu.VMEM((TERMS,) + brick, F32),
        ],
        flops=5 * 10**9,
    )
    base = s.tiles_s * s.rows1
    size2 = s.tiles2 * s.rows2
    waves, to_low, to_high, coarse = call(
        functools.partial(depth_kernel, s), "depth",
        [taps] + shares + [c["ry2"], c["rx2"]],
        arrays((TERMS * s.planes, s.rows1, LANES), (base + size2, LANES), (base + size2, LANES), (size2, LANES)),
        scalars=(0,), after=[near], scratch=[pltpu.VMEM((s.cz[1], s.rows1, LANES), F32)], flops=2 * 10**9,
    )
    named = ("px1", "px2", "px3", "px3l", "rx3", "py2", "py3", "py3l", "ry3", "pz2", "pz3", "rz3")
    z_taps, y1, y2h, y2l, xh, xl = call(
        functools.partial(matrix_kernel, s), "matrices",
        [widths, amplitudes] + [c[k] for k in named],
        arrays((2 * TERMS * s.zrows, LANES))
        + arrays((LANES, 2 * TERMS * s.ny), dtype=BF16)
        + two(s.cy[2], 2 * TERMS * s.ny) + two(s.cx[0], s.depth_lanes),
        after=[coarse], flops=2 * 10**9,
    )
    coarses = [coarse]
    for b in range(1, s.gy):
        coarses.append(fetch({1: to_low, s.gy - 1: to_high}.get(b, coarse), gy=b))
    near_low, near_high = fetch(near_up, gz=-1), fetch(near_down, gz=1)
    (terms,) = call(
        functools.partial(along_kernel, s), "along",
        [z_taps, waves] + coarses + [y1, y2h, y2l],
        arrays((s.depth, s.planes * s.ny)), scalars=(0,),
        scratch=[pltpu.VMEM((2 * TERMS, s.cz[2], s.rows2, s.ny), F32)], flops=3 * 10**9,
    )
    parts = call(
        functools.partial(away_kernel, s), "away", [terms, xh, xl],
        arrays(*[(s.nx, s.planes * s.ny)] * (s.gx - 1)), flops=10**9,
    )
    parts = [fetch(x, gx=-dx) for dx, x in enumerate(parts, 1)]
    (home,) = call(
        functools.partial(home_kernel, s), "home",
        [terms, xh, xl, near, near_low, near_high], arrays(brick), flops=2 * 10**9,
    )
    (out,) = call(
        functools.partial(last_kernel, s), "last", [home] + parts, arrays(brick), flops=10**9,
    )
    return out


def solution(mesh):
    placed = (P("gz", "gx", "gy"), P(), P())
    return jax.shard_map(
        shards, mesh=mesh, in_specs=placed, out_specs=P("gz", "gx", "gy"), check_vma=False
    )
```

```python
import functools

import jax
import jax.numpy as jnp
import ml_dtypes
import numpy as np
from jax import lax
from jax.experimental import pallas as pl
from jax.experimental.pallas import tpu as pltpu
from jax.sharding import PartitionSpec as P

R = 8
TERMS = 3
LANES = 128
NEAR = 9.0 / 16.0
FAR = -1.0 / 16.0
F32 = jnp.float32
BF16 = jnp.bfloat16
VMEM_LIMIT = 40 * 1024 * 1024


def up8(n):
    return -(-n // 8) * 8


class Sizes:
    def __init__(self, nz, nx, ny, gz, gx, gy):
        self.nz, self.nx, self.ny = nz, nx, ny
        self.gz, self.gx, self.gy = gz, gx, gy
        self.z1, self.x1, self.y1 = nz // 2, nx // 2, ny // 2
        self.z2, self.x2, self.y2 = nz // 4, nx // 4, ny // 4
        self.cz = [nz * gz >> l for l in range(4)]
        self.cx = [nx * gx >> l for l in range(4)]
        self.cy = [ny * gy >> l for l in range(4)]
        self.planes = self.z1 + 3
        self.zrows = up8(self.planes)
        self.rows1 = self.x1
        self.rows2 = up8(self.x2 + 3)
        self.wide1 = self.y1 + 3
        self.wide2 = self.y2 + 5
        self.tiles1 = -(-self.planes * self.wide1 // LANES)
        self.tiles2 = -(-self.cz[2] * self.wide2 // LANES)
        self.strip = R + 3
        self.per_tile = LANES // self.strip
        self.tiles_s = -(-TERMS * self.planes // self.per_tile)
        self.fine_tiles = -(-nz // (LANES // R))
        self.ext = nx + 2 * R
        self.depth = TERMS * (self.rows1 + 2 * self.rows2)
        self.depth_lanes = -(-self.depth // LANES) * LANES


def restrict_circle(n):
    m = np.zeros((n // 2, n))
    for i in range(n // 2):
        for d, w in ((0, 1.0), (1, NEAR), (-1, NEAR), (3, FAR), (-3, FAR)):
            m[i, (2 * i + d) % n] += w
    return m


def prolong_circle(n):
    m = np.zeros((2 * n, n))
    for i in range(n):
        m[2 * i, i] += 1.0
        for d, w in ((0, NEAR), (1, NEAR), (-1, FAR), (2, FAR)):
            m[2 * i + 1, (i + d) % n] += w
    return m


def restrict_open(first_in, n_in, first_out, n_out):
    m = np.zeros((n_out, n_in))
    for i in range(n_out):
        for d, w in ((0, 1.0), (1, NEAR), (-1, NEAR), (3, FAR), (-3, FAR)):
            j = 2 * (first_out + i) + d - first_in
            if 0 <= j < n_in:
                m[i, j] = w
    return m


def padded(m, rows, columns):
    out = np.zeros((rows, columns), np.float32)
    out[: m.shape[0], : m.shape[1]] = m
    return out


def exact(m):
    out = m.astype(ml_dtypes.bfloat16)
    assert np.all(out.astype(np.float64) == m)
    return out


def constants(s):
    c = {}
    c["ry2"] = padded(restrict_open(-1, s.wide1, -2, s.wide2).T, LANES, LANES)
    c["rx2"] = padded(restrict_open(0, s.x1, -1, s.x2 + 3), s.rows2, s.rows1)

    def chain(n):
        p1 = prolong_circle(n[1])
        p2 = p1 @ prolong_circle(n[2])
        return p1, p2, p2 @ prolong_circle(n[3])

    def parts(name, m):
        m = m.astype(np.float32)
        c[name] = m.astype(ml_dtypes.bfloat16)
        c[name + "l"] = (m - c[name].astype(np.float32)).astype(ml_dtypes.bfloat16)

    x1, x2, x3 = chain(s.cx)
    c["px1"], c["px2"] = exact(x1), exact(x2)
    parts("px3", x3)
    place = np.zeros((s.cx[2], s.rows2))
    for r in range(s.x2 + 3):
        place[(r - 1) % s.cx[2], r] += 1.0
    rx3 = np.zeros((TERMS, s.cx[3], s.depth_lanes))
    for t in range(TERMS):
        first = TERMS * s.rows1 + (TERMS + t) * s.rows2
        rx3[t, :, first : first + s.rows2] = restrict_circle(s.cx[2]) @ place
    c["rx3"] = exact(rx3)
    _, y2, y3 = chain(s.cy)
    c["py2"] = exact(y2[: s.ny].T)
    parts("py3", y3[: s.ny].T)
    c["ry3"] = exact(restrict_circle(s.cy[2]).T)
    z2 = prolong_circle(s.cz[2])
    z3 = z2 @ prolong_circle(s.cz[3])
    own = [(o - 1) % s.cz[1] for o in range(s.planes)]
    c["pz2"] = exact(padded(z2[own], s.zrows, s.cz[2]))
    c["pz3"] = exact(padded(z3[own], s.zrows, s.cz[3]))
    c["rz3"] = exact(padded(restrict_circle(s.cz[2]), s.cz[3], LANES))
    return c


def halves(x):
    high = x.astype(BF16)
    return high, (x - high.astype(F32)).astype(BF16)


def dot(a, b):
    return jnp.dot(a, b, preferred_element_type=F32)


def dot2(a, b):
    high, low = halves(a)
    return dot(high, b) + dot(low, b)


def dot3(a, b_high, b_low):
    high, low = halves(a)
    return dot(high, b_high) + dot(low, b_high) + dot(high, b_low)


def lanes_of(shape):
    return lax.broadcasted_iota(jnp.int32, shape, len(shape) - 1)


def turn(x, by):
    by = by % x.shape[-1]
    return x if by == 0 else pltpu.roll(x, by, x.ndim - 1)


def packed(planes, wide, tiles):
    out = [None] * tiles

    def add(t, x):
        out[t] = x if out[t] is None else out[t] + x

    for k, x in enumerate(planes):
        t, at = divmod(k * wide, LANES)
        moved = turn(x, at)
        if at + wide <= LANES:
            add(t, moved)
        else:
            lane = lanes_of(x.shape)
            add(t, jnp.where(lane >= at, moved, 0.0))
            add(t + 1, jnp.where(lane < at, moved, 0.0))
    return out


def unpacked(tile, k, wide, shift):
    t, at = divmod(k * wide, LANES)
    x = tile(t)
    lane = lanes_of(x.shape)
    if at + wide > LANES:
        x = jnp.where(lane >= at, x, tile(t + 1))
    x = turn(x, shift - at)
    if shift + wide <= LANES:
        return jnp.where((lane >= shift) & (lane < shift + wide), x, 0.0)
    return jnp.where((lane >= shift) | (lane < shift + wide - LANES), x, 0.0)


def open_restriction(shape, in_dim, first_in, first_out, n_out):
    i = lax.broadcasted_iota(jnp.int32, shape, in_dim) + first_in
    o = lax.broadcasted_iota(jnp.int32, shape, 1 - in_dim)
    d = jnp.abs(i - 2 * (o + first_out))
    w = jnp.where(d == 0, 1.0, jnp.where(d == 1, NEAR, jnp.where(d == 3, FAR, 0.0)))
    return jnp.where(o < n_out, w, 0.0).astype(BF16)


def extended(s, b_ref, lo_ref, hi_ref, z):
    return jnp.concatenate([lo_ref[z, s.nx - R :], b_ref[z], hi_ref[z, 0:R]], axis=0)


def share_kernel(s, b_ref, lo_ref, hi_ref, _, m_ref, first_ref, last_ref):
    b = [extended(s, b_ref, lo_ref, hi_ref, z) for z in range(s.nz)]
    planes = []
    for k in range(-1, s.z1 + 2):
        out = None
        for d, w in ((0, 1.0), (1, NEAR), (-1, NEAR), (3, FAR), (-3, FAR)):
            if 0 <= 2 * k + d < s.nz:
                term = b[2 * k + d] if d == 0 else b[2 * k + d] * w
                out = term if out is None else out + term
        planes.append(out)
    high, low = halves(jnp.concatenate(planes, axis=0))
    ry1 = open_restriction((s.ny, LANES), 0, 0, -1, s.wide1)
    rx1 = open_restriction((s.rows1, s.ext), 1, -R, 0, s.x1)
    along = dot(high, ry1) + dot(low, ry1)
    shares = []
    for k in range(s.planes):
        high, low = halves(along[k * s.ext : (k + 1) * s.ext])
        shares.append(dot(rx1, high) + dot(rx1, low))
    for t, x in enumerate(packed(shares, s.wide1, s.tiles1)):
        m_ref[t] = x
    lane = lanes_of((s.ext, LANES))
    group = LANES // R
    for t in range(s.fine_tiles):
        first = last = jnp.zeros((s.ext, LANES), F32)
        for g in range(min(group, s.nz - t * group)):
            x = b[t * group + g]
            at = R * ((g + 1) % group)
            first = jnp.where((lane >= at) & (lane < at + R), turn(x, at), first)
            at = R * g
            last = jnp.where((lane >= at) & (lane < at + R), turn(x, at + R - s.ny), last)
        first_ref[t] = first
        last_ref[t] = last


def rows_of(shape):
    return lax.broadcasted_iota(jnp.int32, shape, 0)


def bell(c, d):
    d = jnp.abs(d)
    return jnp.where(d <= R, jnp.exp(c * d * d), 0.0)


def one(ref, level, t):
    return ref[level : level + 1, t : t + 1]


def spreads(w_ref, levels):
    out = []
    for l in levels:
        w = [one(w_ref, l, t) for t in range(TERMS)]
        out.append([-0.5 / (x * x) for x in w])
    return out


def units(coef, distance, valid):
    shape = (up8(len(coef)), LANES)
    row = rows_of(shape)
    column = jnp.zeros(shape, F32)
    for r, c in enumerate(coef):
        column = jnp.where(row == r, c, column)
    lane = lanes_of(shape)
    d = distance(row, lane).astype(F32)
    total = jnp.sum(jnp.where(valid(row, lane), jnp.exp(2.0 * column * d * d), 0.0), axis=1, keepdims=True)
    unit = 1.0 / jnp.sqrt(total)
    return [unit[r : r + 1] for r in range(len(coef))]


def near_units(coef):
    flat = [c for level in coef for c in level]
    out = units(flat, lambda row, lane: lane - R, lambda row, lane: lane <= 2 * R)
    return [out[i : i + TERMS] for i in range(0, len(out), TERMS)]


def tap_kernel(s, w_ref, a_ref, tap_ref, x0_ref):
    coef = spreads(w_ref, (0, 1))
    unit = near_units(coef)
    d = lanes_of((1, LANES)).astype(F32)
    for t in range(TERMS):
        tap_ref[t : t + 1] = bell(coef[0][t], d) * (unit[0][t] * one(a_ref, 0, t))
        tap_ref[TERMS + t : TERMS + t + 1] = bell(coef[1][t], d) * (unit[1][t] * one(a_ref, 1, t) * 0.25)
    shape = (s.nx, 3 * s.ext)
    lane = lanes_of(shape)
    part = jnp.where(lane < s.ext, 0, jnp.where(lane < 2 * s.ext, 1, 2))
    d = (lane - part * s.ext - R - rows_of(shape)).astype(F32)
    for t in range(TERMS):
        high, low = halves(bell(coef[0][t], d) * unit[0][t])
        x0_ref[t * s.nx : (t + 1) * s.nx] = jnp.where(part == 1, low.astype(F32), high.astype(F32)).astype(BF16)


def along_matrix_kernel(s, w_ref, _, y0_ref):
    coef = spreads(w_ref, (0,))
    unit = near_units(coef)
    shape = (s.ny + 2 * R, s.ny)
    i = rows_of(shape)
    cell = jnp.where(i < s.ny, i, jnp.where(i < s.ny + R, i - s.ny - R, i - R))
    d = (cell - lanes_of(shape)).astype(F32)
    for t in range(TERMS):
        high, low = halves(bell(coef[0][t], d) * unit[0][t])
        at = 2 * t * s.ny
        y0_ref[s.ny + 2 * R :, at : at + 2 * s.ny] = jnp.zeros((2 * LANES - s.ny - 2 * R, 2 * s.ny), BF16)
        y0_ref[: s.ny + 2 * R, at : at + s.ny] = high
        y0_ref[: s.ny + 2 * R, at + s.ny : at + 2 * s.ny] = low


def matrix_kernel(s, w_ref, a_ref, px1, px2, px3, px3l, rx3, py2, py3, py3l, ry3, pz2, pz3, rz3, _,
                  z_ref, y1_ref, y2h_ref, y2l_ref, xh_ref, xl_ref):
    coef = spreads(w_ref, range(4))
    unit = near_units(coef[:3])
    sizes = [s.cx[3], s.cy[3], s.cz[3]]

    def per_row(row):
        return jnp.where(row < TERMS, sizes[0], jnp.where(row < 2 * TERMS, sizes[1], sizes[2]))

    top = units(
        coef[3] * 3,
        lambda row, lane: jnp.minimum(lane, per_row(row) - lane),
        lambda row, lane: lane < per_row(row),
    )
    top_x, top_y, top_z = top[:TERMS], top[TERMS : 2 * TERMS], top[2 * TERMS :]

    def circle(n, d, c, u):
        d = (d & (n - 1)).astype(F32)
        return (bell(c, d) + bell(c, n - d)) * u

    def full_circle(n, shape, c, u):
        d = ((rows_of(shape) - lanes_of(shape)) & (n - 1)).astype(F32)
        d = jnp.minimum(d, n - d)
        return jnp.exp(c * d * d) * u

    shape = (LANES, s.ny)
    fine = lanes_of(shape)
    d = (rows_of(shape) - (R + 1) - (fine >> 1)).astype(F32)
    even = (fine & 1) == 0
    known = rows_of(shape) < s.y1 + 3 + 2 * R
    wide = (s.cy[2], s.cy[2])
    for t in range(TERMS):
        c = coef[1][t]
        here = bell(c, d)
        between = NEAR * (here + bell(c, d - 1.0)) + FAR * (bell(c, d + 1.0) + bell(c, d - 2.0))
        high, low = halves(jnp.where(known, jnp.where(even, here, between) * unit[1][t], 0.0))
        y1_ref[:, 2 * t * s.ny : (2 * t + 1) * s.ny] = high
        y1_ref[:, (2 * t + 1) * s.ny : (2 * t + 2) * s.ny] = low
        g = circle(s.cy[2], rows_of(wide) - lanes_of(wide), coef[2][t], unit[2][t])
        high, low = halves(dot2(g, py2[...]))
        y2h_ref[:, t * s.ny : (t + 1) * s.ny] = high
        y2l_ref[:, t * s.ny : (t + 1) * s.ny] = low
        g = full_circle(s.cy[3], (s.cy[3], s.cy[3]), coef[3][t], top_y[t])
        high, low = halves(g)
        g = dot(ry3[...], high) + dot(ry3[...], low)
        high, low = halves(dot3(g, py3[...], py3l[...]))
        at = (TERMS + t) * s.ny
        y2h_ref[:, at : at + s.ny] = high
        y2l_ref[:, at : at + s.ny] = low

    def terms(level, first, rows, valid, shift):
        shape = (s.cx[level], s.depth_lanes)
        lane = lanes_of(shape) - first
        column = lane - jnp.where(lane < rows, 0, jnp.where(lane < 2 * rows, rows, 2 * rows))

        def by_term(v):
            return jnp.where(lane < rows, v[0], jnp.where(lane < 2 * rows, v[1], v[2]))

        g = circle(s.cx[level], rows_of(shape) - column + shift, by_term(coef[level]), by_term(unit[level]))
        high, low = halves(jnp.where((lane >= 0) & (lane < TERMS * rows) & (column < valid), g, 0.0))
        return high, low

    high, low = terms(1, 0, s.rows1, s.rows1, 0)
    x = dot(px1[...], high) + dot(px1[...], low)
    high, low = terms(2, TERMS * s.rows1, s.rows2, s.x2 + 3, 1)
    x += dot(px2[...], high) + dot(px2[...], low)
    g = None
    for t in range(TERMS):
        part = dot2(full_circle(s.cx[3], (s.cx[3], s.cx[3]), coef[3][t], top_x[t]), rx3[t])
        g = part if g is None else g + part
    high, low = halves(g)
    x += dot(px3[...], high) + dot(px3l[...], high) + dot(px3[...], low)
    xh_ref[...], xl_ref[...] = halves(x)
    for t in range(TERMS):
        shape = (s.cz[2], LANES)
        g = circle(s.cz[2], rows_of(shape) - lanes_of(shape), coef[2][t], unit[2][t])
        high, low = halves(g * (one(a_ref, 2, t) * 0.0625))
        z_ref[t * s.zrows : (t + 1) * s.zrows] = dot(pz2[...], high) + dot(pz2[...], low)
        g = full_circle(s.cz[3], (s.cz[3], s.cz[3]), coef[3][t], top_z[t])
        high, low = halves(g * (one(a_ref, 3, t) * 0.015625))
        g = dot2(dot(pz3[...], high) + dot(pz3[...], low), rz3[...])
        z_ref[(TERMS + t) * s.zrows : (TERMS + t + 1) * s.zrows] = g


def near_kernel(s, tap_ref, b_ref, lo_ref, hi_ref, left_ref, right_ref, x0_ref, y0_ref,
                own_ref, down_ref, up_ref, e_ref, u_ref, eh_ref, el_ref, v_ref):
    group = LANES // R
    tiles = [extended(s, b_ref, lo_ref, hi_ref, z) for z in range(s.nz)]
    tiles += [left_ref[t] for t in range(s.fine_tiles)] + [right_ref[t] for t in range(s.fine_tiles)]
    for i, x in enumerate(tiles):
        high, low = halves(x)
        columns = slice(i * LANES, (i + 1) * LANES)
        e_ref[0 : s.ext, columns] = high
        e_ref[s.ext : 2 * s.ext, columns] = high
        e_ref[2 * s.ext :, columns] = low
    x0 = x0_ref[...]
    for at in range(0, len(tiles) * LANES, 2 * LANES):
        columns = slice(at, min(at + 2 * LANES, len(tiles) * LANES))
        u_ref[:, columns] = dot(x0, e_ref[:, columns])
    lane = lanes_of((TERMS * s.nx, LANES))
    for z in range(s.nz):
        t, g = divmod(z, group)
        left = u_ref[:, (s.nz + t) * LANES : (s.nz + t + 1) * LANES]
        right = u_ref[:, (s.nz + s.fine_tiles + t) * LANES : (s.nz + s.fine_tiles + t + 1) * LANES]
        strips = turn(jnp.where((lane >= R * g) & (lane < R * g + R), left, right), -R * g)
        for at, x in ((0, u_ref[:, z * LANES : (z + 1) * LANES]), (LANES, strips)):
            high, low = halves(x)
            for t in range(TERMS):
                rows = slice(t * s.nx, (t + 1) * s.nx)
                eh_ref[t, z * s.nx : (z + 1) * s.nx, at : at + LANES] = high[rows]
                el_ref[t, z * s.nx : (z + 1) * s.nx, at : at + LANES] = low[rows]
    step = 4 * s.nx
    for t in range(TERMS):
        at = 2 * t * s.ny
        y0, y0h = y0_ref[:, at : at + 2 * s.ny], y0_ref[:, at : at + s.ny]
        for first in range(0, s.nz * s.nx, step):
            both = dot(eh_ref[t, first : first + step], y0)
            v = both[:, : s.ny] + both[:, s.ny :] + dot(el_ref[t, first : first + step], y0h)
            for q in range(step // s.nx):
                v_ref[t, first // s.nx + q] = v[q * s.nx : (q + 1) * s.nx]

    def depth(r, _):
        rows = pl.ds(pl.multiple_of(r * 8, 8), 8)
        taps = [[tap_ref[t, d] for d in range(R + 1)] for t in range(TERMS)]
        for first in range(-R, s.nz + R, R):
            acc = [None] * R
            for t in range(TERMS):
                for z in range(max(0, first - R), min(s.nz, first + 2 * R)):
                    v = v_ref[t, z, rows]
                    for o in range(R):
                        d = abs(first + o - z)
                        if d <= R:
                            term = v * taps[t][d]
                            acc[o] = term if acc[o] is None else acc[o] + term
            for o in range(R):
                if first < 0:
                    down_ref[o, rows] = acc[o]
                elif first >= s.nz:
                    up_ref[o, rows] = acc[o]
                else:
                    own_ref[first + o, rows] = acc[o]
        return 0

    lax.fori_loop(0, s.nx // 8, depth, 0)


def depth_kernel(s, tap_ref, *refs):
    m_refs = refs[: s.gz]
    ry2_ref, rx2_ref, _, _, w_ref, down_ref, up_ref, c2_ref, _, _, c_ref = refs[s.gz :]
    n = s.cz[1]
    parts = [[] for _ in range(n)]
    for b in range(s.gz):
        for k in range(s.planes):
            parts[(b * s.z1 + k - 1) % n].append((b, k))
    for z in range(n):
        out = None
        for b, k in parts[z]:
            x = unpacked(lambda t, b=b: m_refs[b][t], k, s.wide1, 0)
            out = x if out is None else out + x
        c_ref[z] = out
    lane = lanes_of((s.rows1, LANES))
    down = [jnp.zeros((s.rows1, LANES), F32)] * s.tiles_s
    up = list(down)
    for o in range(s.planes):
        sums = [c_ref[(o - 1) % n]]
        sums += [c_ref[(o - 1 + d) % n] + c_ref[(o - 1 - d) % n] for d in range(1, R + 1)]
        for t in range(TERMS):
            x = sums[0] * tap_ref[TERMS + t, 0]
            for d in range(1, R + 1):
                x += sums[d] * tap_ref[TERMS + t, d]
            k = t * s.planes + o
            w_ref[k] = x
            tile, slot = divmod(k, s.per_tile)
            at = slot * s.strip
            here = (lane >= at) & (lane < at + s.strip)
            down[tile] = jnp.where(here, turn(x, at), down[tile])
            up[tile] = jnp.where(here, turn(x, at - (s.wide1 - s.strip)), up[tile])
    coarse = []
    for j in range(s.cz[2]):
        at = lambda d: c_ref[(2 * j + d) % n]
        coarse.append(at(0) + NEAR * (at(1) + at(-1)) + FAR * (at(3) + at(-3)))
    high, low = halves(jnp.concatenate(coarse, axis=0))
    ry2 = ry2_ref[...].astype(BF16)
    rx2 = rx2_ref[...].astype(BF16)
    along = dot(high, ry2) + dot(low, ry2)
    shares = []
    for j in range(s.cz[2]):
        high, low = halves(along[j * s.rows1 : (j + 1) * s.rows1])
        shares.append(dot(rx2, high) + dot(rx2, low))
    for t in range(s.tiles_s):
        down_ref[t * s.rows1 : (t + 1) * s.rows1] = down[t]
        up_ref[t * s.rows1 : (t + 1) * s.rows1] = up[t]
    base = s.tiles_s * s.rows1
    for t, x in enumerate(packed(shares, s.wide2, s.tiles2)):
        rows = slice(t * s.rows2, (t + 1) * s.rows2)
        c2_ref[rows] = x
        for ref in (down_ref, up_ref):
            ref[base + t * s.rows2 : base + (t + 1) * s.rows2] = x


def along_kernel(s, z_ref, w_ref, *refs):
    c2_refs = refs[: s.gy]
    y1_ref, y2h_ref, y2l_ref, d_ref, yb_ref = refs[s.gy :]
    base = s.tiles_s * s.rows1
    lane = lanes_of((s.rows1, LANES))
    above, below = c2_refs[1], c2_refs[-1]
    end = s.y1 + R
    for t in range(TERMS):
        cells = []
        for o in range(s.planes):
            k = t * s.planes + o
            tile, slot = divmod(k, s.per_tile)
            rows = slice(tile * s.rows1, (tile + 1) * s.rows1)
            at = slot * s.strip
            x = turn(w_ref[k], R)
            x += jnp.where(lane < s.strip, turn(below[rows], -at), 0.0)
            x += jnp.where((lane >= end) & (lane < end + s.strip), turn(above[rows], end - at), 0.0)
            cells.append(x)
        high, low = halves(jnp.concatenate(cells, axis=0))
        at = 2 * t * s.ny
        both = dot(high, y1_ref[:, at : at + 2 * s.ny])
        out = both[:, : s.ny] + both[:, s.ny :] + dot(low, y1_ref[:, at : at + s.ny])
        for o in range(s.planes):
            d_ref[t * s.rows1 : (t + 1) * s.rows1, o * s.ny : (o + 1) * s.ny] = out[o * s.rows1 : (o + 1) * s.rows1]
    cells = []
    for j in range(s.cz[2]):
        out = None
        for b in range(s.gy):
            first = 0 if b == 0 or c2_refs[b].shape[0] == s.tiles2 * s.rows2 else base
            tile = lambda t, b=b, f=first: c2_refs[b][f + t * s.rows2 : f + (t + 1) * s.rows2]
            x = unpacked(tile, j, s.wide2, (b * s.y2 - 2) % LANES)
            out = x if out is None else out + x
        cells.append(out)
    yb = dot3(jnp.concatenate(cells, axis=0), y2h_ref[...], y2l_ref[...])
    for j in range(s.cz[2]):
        for q in range(2 * TERMS):
            yb_ref[q, j] = yb[j * s.rows2 : (j + 1) * s.rows2, q * s.ny : (q + 1) * s.ny]
    for o in range(s.planes):
        for q in range(2 * TERMS):
            x = yb_ref[q, 0] * z_ref[q * s.zrows + o, 0]
            for j in range(1, s.cz[2]):
                x += yb_ref[q, j] * z_ref[q * s.zrows + o, j]
            at = TERMS * s.rows1 + q * s.rows2
            d_ref[at : at + s.rows2, o * s.ny : (o + 1) * s.ny] = x


def across(s, d_ref, xh_ref, xl_ref, shift):
    rows = slice(shift * s.nx, (shift + 1) * s.nx)
    high, low = halves(d_ref[...])
    xh, xl = xh_ref[rows, : s.depth], xl_ref[rows, : s.depth]
    return dot(xh, high) + dot(xl, high) + dot(xh, low)


def away_kernel(s, d_ref, xh_ref, xl_ref, *g_refs):
    for shift, ref in enumerate(g_refs):
        ref[...] = across(s, d_ref, xh_ref, xl_ref, shift + 1)


def prolonged(s, level, z):
    m = z // 2 + 1
    if z % 2 == 0:
        return level[m]
    return NEAR * (level[m] + level[m + 1]) + FAR * (level[m - 1] + level[m + 2])


def home_kernel(s, d_ref, xh_ref, xl_ref, own_ref, low_ref, high_ref, out_ref):
    g = across(s, d_ref, xh_ref, xl_ref, 0)
    level = [g[:, o * s.ny : (o + 1) * s.ny] for o in range(s.planes)]
    for z in range(s.nz):
        x = prolonged(s, level, z) + own_ref[z]
        if z < R:
            x += low_ref[z]
        if z >= s.nz - R:
            x += high_ref[z - (s.nz - R)]
        out_ref[z] = x


def last_kernel(s, home_ref, *refs):
    g_refs, out_ref = refs[:-1], refs[-1]
    level = []
    for o in range(s.planes):
        columns = slice(o * s.ny, (o + 1) * s.ny)
        x = g_refs[0][:, columns]
        for ref in g_refs[1:]:
            x += ref[:, columns]
        level.append(x)
    for z in range(s.nz):
        out_ref[z] = home_ref[z] + prolonged(s, level, z)


def call(kernel, name, operands, out_shapes, scalars=(), after=(), through=(), scratch=(), flops=0):
    read, given = len(operands), len(out_shapes)
    operands = list(operands) + list(after) + list(through)
    first = len(operands) - len(through)
    out_shapes = list(out_shapes) + [jax.ShapeDtypeStruct(x.shape, x.dtype) for x in through]

    def spec(i):
        if i >= read:
            return pl.BlockSpec(memory_space=pl.ANY)
        return pl.BlockSpec(memory_space=pltpu.SMEM if i in scalars else pltpu.VMEM)

    moved = sum(x.size * x.dtype.itemsize for x in operands)
    moved += sum(int(np.prod(x.shape)) * x.dtype.itemsize for x in out_shapes)
    return pl.pallas_call(
        kernel,
        name=name,
        out_shape=out_shapes,
        in_specs=[spec(i) for i in range(len(operands))],
        out_specs=[pl.BlockSpec(memory_space=pltpu.VMEM)] * given
        + [pl.BlockSpec(memory_space=pl.ANY)] * len(through),
        input_output_aliases={first + i: given + i for i in range(len(through))},
        scratch_shapes=list(scratch),
        compiler_params=pltpu.CompilerParams(vmem_limit_bytes=VMEM_LIMIT),
        cost_estimate=pl.CostEstimate(flops=flops, bytes_accessed=moved, transcendentals=0),
    )(*operands)


def arrays(*shapes, dtype=F32):
    return [jax.ShapeDtypeStruct(shape, dtype) for shape in shapes]


def fetch(x, **shifts):
    names = tuple(shifts)
    sizes = [lax.axis_size(n) for n in names]
    pairs = []
    for here in np.ndindex(*sizes):
        there = [(h + shifts[n]) % size for h, n, size in zip(here, names, sizes)]
        pairs.append((int(np.ravel_multi_index(there, sizes)), int(np.ravel_multi_index(here, sizes))))
    return lax.ppermute(x, names if len(names) > 1 else names[0], pairs)


def two(*shape):
    return arrays(shape, shape, dtype=BF16)


def shards(charges, widths, amplitudes):
    s = Sizes(*charges.shape, lax.axis_size("gz"), lax.axis_size("gx"), lax.axis_size("gy"))
    c = {k: jnp.asarray(v) for k, v in constants(s).items()}
    brick = (s.nz, s.nx, s.ny)
    side = (R, s.nx, s.ny)
    taps, x0 = call(
        functools.partial(tap_kernel, s), "taps", [widths, amplitudes],
        arrays((8, LANES)) + arrays((TERMS * s.nx, 3 * s.ext), dtype=BF16), flops=6 * 10**8,
    )
    high_rows = fetch(charges, gx=1)
    low_rows = high_rows if s.gx == 2 else fetch(charges, gx=-1)
    strips = (s.fine_tiles, s.ext, LANES)
    share, first_cells, last_cells = call(
        functools.partial(share_kernel, s), "share", [charges, low_rows, high_rows],
        arrays((s.tiles1, s.rows1, LANES), strips, strips), after=[x0], flops=10**9,
    )
    shares = [share] + [fetch(share, gz=b) for b in range(1, s.gz)]
    left, right = fetch(last_cells, gy=-1), fetch(first_cells, gy=1)
    (y0,) = call(
        functools.partial(along_matrix_kernel, s), "taps_y", [widths],
        arrays((2 * LANES, 2 * TERMS * s.ny), dtype=BF16), after=[share], flops=6 * 10**8,
    )
    tiles = s.nz + 2 * s.fine_tiles
    halved = pltpu.VMEM((TERMS, s.nz * s.nx, 2 * LANES), BF16)
    near, near_down, near_up = call(
        functools.partial(near_kernel, s), "near",
        [taps, charges, low_rows, high_rows, left, right, x0, y0],
        arrays(brick, side, side), scalars=(0,),
        scratch=[
            pltpu.VMEM((3 * s.ext, tiles * LANES), BF16), pltpu.VMEM((TERMS * s.nx, tiles * LANES), F32),
            halved, halved, pltpu.VMEM((TERMS,) + brick, F32),
        ],
        flops=5 * 10**9,
    )
    base = s.tiles_s * s.rows1
    size2 = s.tiles2 * s.rows2
    waves, to_low, to_high, coarse, near_down, near_up = call(
        functools.partial(depth_kernel, s), "depth",
        [taps] + shares + [c["ry2"], c["rx2"]],
        arrays((TERMS * s.planes, s.rows1, LANES), (base + size2, LANES), (base + size2, LANES), (size2, LANES)),
        scalars=(0,), through=[near_down, near_up], scratch=[pltpu.VMEM((s.cz[1], s.rows1, LANES), F32)], flops=2 * 10**9,
    )
    named = ("px1", "px2", "px3", "px3l", "rx3", "py2", "py3", "py3l", "ry3", "pz2", "pz3", "rz3")
    z_taps, y1, y2h, y2l, xh, xl = call(
        functools.partial(matrix_kernel, s), "matrices",
        [widths, amplitudes] + [c[k] for k in named],
        arrays((2 * TERMS * s.zrows, LANES))
        + arrays((LANES, 2 * TERMS * s.ny), dtype=BF16)
        + two(s.cy[2], 2 * TERMS * s.ny) + two(s.cx[0], s.depth_lanes),
        after=[coarse], flops=2 * 10**9,
    )
    coarses = [coarse]
    for b in range(1, s.gy):
        coarses.append(fetch({1: to_low, s.gy - 1: to_high}.get(b, coarse), gy=b))
    near_low, near_high = fetch(near_up, gz=-1), fetch(near_down, gz=1)
    (terms,) = call(
        functools.partial(along_kernel, s), "along",
        [z_taps, waves] + coarses + [y1, y2h, y2l],
        arrays((s.depth, s.planes * s.ny)), scalars=(0,),
        scratch=[pltpu.VMEM((2 * TERMS, s.cz[2], s.rows2, s.ny), F32)], flops=3 * 10**9,
    )
    parts = call(
        functools.partial(away_kernel, s), "away", [terms, xh, xl],
        arrays(*[(s.nx, s.planes * s.ny)] * (s.gx - 1)), flops=10**9,
    )
    parts = [fetch(x, gx=-dx) for dx, x in enumerate(parts, 1)]
    (home,) = call(
        functools.partial(home_kernel, s), "home",
        [terms, xh, xl, near, near_low, near_high], arrays(brick), flops=2 * 10**9,
    )
    (out,) = call(
        functools.partial(last_kernel, s), "last", [home] + parts, arrays(brick), flops=10**9,
    )
    return out


def solution(mesh):
    placed = (P("gz", "gx", "gy"), P(), P())
    return jax.shard_map(
        shards, mesh=mesh, in_specs=placed, out_specs=P("gz", "gx", "gy"), check_vma=False
    )
```

```python
import functools

import jax
import jax.numpy as jnp
import ml_dtypes
import numpy as np
from jax import lax
from jax.experimental import pallas as pl
from jax.experimental.pallas import tpu as pltpu
from jax.sharding import PartitionSpec as P

R = 8
TERMS = 3
LANES = 128
NEAR = 9.0 / 16.0
FAR = -1.0 / 16.0
F32 = jnp.float32
BF16 = jnp.bfloat16
VMEM_LIMIT = 40 * 1024 * 1024


def up8(n):
    return -(-n // 8) * 8


class Sizes:
    def __init__(self, nz, nx, ny, gz, gx, gy):
        self.nz, self.nx, self.ny = nz, nx, ny
        self.gz, self.gx, self.gy = gz, gx, gy
        self.z1, self.x1, self.y1 = nz // 2, nx // 2, ny // 2
        self.z2, self.x2, self.y2 = nz // 4, nx // 4, ny // 4
        self.cz = [nz * gz >> l for l in range(4)]
        self.cx = [nx * gx >> l for l in range(4)]
        self.cy = [ny * gy >> l for l in range(4)]
        self.planes = self.z1 + 3
        self.zrows = up8(self.planes)
        self.rows1 = self.x1
        self.rows2 = up8(self.x2 + 3)
        self.wide1 = self.y1 + 3
        self.wide2 = self.y2 + 5
        self.tiles1 = -(-self.planes * self.wide1 // LANES)
        self.tiles2 = -(-self.cz[2] * self.wide2 // LANES)
        self.strip = R + 3
        self.per_tile = LANES // self.strip
        self.tiles_s = -(-TERMS * self.planes // self.per_tile)
        self.fine_tiles = -(-nz // (LANES // R))
        self.ext = nx + 2 * R
        self.depth = TERMS * (self.rows1 + 2 * self.rows2)
        self.depth_lanes = -(-self.depth // LANES) * LANES


def restrict_circle(n):
    m = np.zeros((n // 2, n))
    for i in range(n // 2):
        for d, w in ((0, 1.0), (1, NEAR), (-1, NEAR), (3, FAR), (-3, FAR)):
            m[i, (2 * i + d) % n] += w
    return m


def prolong_circle(n):
    m = np.zeros((2 * n, n))
    for i in range(n):
        m[2 * i, i] += 1.0
        for d, w in ((0, NEAR), (1, NEAR), (-1, FAR), (2, FAR)):
            m[2 * i + 1, (i + d) % n] += w
    return m


def restrict_open(first_in, n_in, first_out, n_out):
    m = np.zeros((n_out, n_in))
    for i in range(n_out):
        for d, w in ((0, 1.0), (1, NEAR), (-1, NEAR), (3, FAR), (-3, FAR)):
            j = 2 * (first_out + i) + d - first_in
            if 0 <= j < n_in:
                m[i, j] = w
    return m


def padded(m, rows, columns):
    out = np.zeros((rows, columns), np.float32)
    out[: m.shape[0], : m.shape[1]] = m
    return out


def exact(m):
    out = m.astype(ml_dtypes.bfloat16)
    assert np.all(out.astype(np.float64) == m)
    return out


def constants(s):
    c = {}
    c["ry2"] = padded(restrict_open(-1, s.wide1, -2, s.wide2).T, LANES, LANES)
    c["rx2"] = padded(restrict_open(0, s.x1, -1, s.x2 + 3), s.rows2, s.rows1)

    def chain(n):
        p1 = prolong_circle(n[1])
        p2 = p1 @ prolong_circle(n[2])
        return p1, p2, p2 @ prolong_circle(n[3])

    def parts(name, m):
        m = m.astype(np.float32)
        c[name] = m.astype(ml_dtypes.bfloat16)
        c[name + "l"] = (m - c[name].astype(np.float32)).astype(ml_dtypes.bfloat16)

    x1, x2, x3 = chain(s.cx)
    c["px1"], c["px2"] = exact(x1), exact(x2)
    parts("px3", x3)
    place = np.zeros((s.cx[2], s.rows2))
    for r in range(s.x2 + 3):
        place[(r - 1) % s.cx[2], r] += 1.0
    rx3 = np.zeros((TERMS, s.cx[3], s.depth_lanes))
    for t in range(TERMS):
        first = TERMS * s.rows1 + (TERMS + t) * s.rows2
        rx3[t, :, first : first + s.rows2] = restrict_circle(s.cx[2]) @ place
    c["rx3"] = exact(rx3)
    _, y2, y3 = chain(s.cy)
    c["py2"] = exact(y2[: s.ny].T)
    parts("py3", y3[: s.ny].T)
    c["ry3"] = exact(restrict_circle(s.cy[2]).T)
    z2 = prolong_circle(s.cz[2])
    z3 = z2 @ prolong_circle(s.cz[3])
    own = [(o - 1) % s.cz[1] for o in range(s.planes)]
    c["pz2"] = exact(padded(z2[own], s.zrows, s.cz[2]))
    c["pz3"] = exact(padded(z3[own], s.zrows, s.cz[3]))
    c["rz3"] = exact(padded(restrict_circle(s.cz[2]), s.cz[3], LANES))
    return c


def halves(x):
    high = x.astype(BF16)
    return high, (x - high.astype(F32)).astype(BF16)


def dot(a, b):
    return jnp.dot(a, b, preferred_element_type=F32)


def dot2(a, b):
    high, low = halves(a)
    return dot(high, b) + dot(low, b)


def dot3(a, b_high, b_low):
    high, low = halves(a)
    return dot(high, b_high) + dot(low, b_high) + dot(high, b_low)


def lanes_of(shape):
    return lax.broadcasted_iota(jnp.int32, shape, len(shape) - 1)


def turn(x, by):
    by = by % x.shape[-1]
    return x if by == 0 else pltpu.roll(x, by, x.ndim - 1)


def packed(planes, wide, tiles):
    out = [None] * tiles

    def add(t, x):
        out[t] = x if out[t] is None else out[t] + x

    for k, x in enumerate(planes):
        t, at = divmod(k * wide, LANES)
        moved = turn(x, at)
        if at + wide <= LANES:
            add(t, moved)
        else:
            lane = lanes_of(x.shape)
            add(t, jnp.where(lane >= at, moved, 0.0))
            add(t + 1, jnp.where(lane < at, moved, 0.0))
    return out


def unpacked(tile, k, wide, shift):
    t, at = divmod(k * wide, LANES)
    x = tile(t)
    lane = lanes_of(x.shape)
    if at + wide > LANES:
        x = jnp.where(lane >= at, x, tile(t + 1))
    x = turn(x, shift - at)
    if shift + wide <= LANES:
        return jnp.where((lane >= shift) & (lane < shift + wide), x, 0.0)
    return jnp.where((lane >= shift) | (lane < shift + wide - LANES), x, 0.0)


def open_restriction(shape, in_dim, first_in, first_out, n_out):
    i = lax.broadcasted_iota(jnp.int32, shape, in_dim) + first_in
    o = lax.broadcasted_iota(jnp.int32, shape, 1 - in_dim)
    d = jnp.abs(i - 2 * (o + first_out))
    w = jnp.where(d == 0, 1.0, jnp.where(d == 1, NEAR, jnp.where(d == 3, FAR, 0.0)))
    return jnp.where(o < n_out, w, 0.0).astype(BF16)


def extended(s, b_ref, lo_ref, hi_ref, z):
    return jnp.concatenate([lo_ref[z, s.nx - R :], b_ref[z], hi_ref[z, 0:R]], axis=0)


def share_kernel(s, b_ref, lo_ref, hi_ref, _, m_ref, first_ref, last_ref):
    b = [extended(s, b_ref, lo_ref, hi_ref, z) for z in range(s.nz)]
    planes = []
    for k in range(-1, s.z1 + 2):
        out = None
        for d, w in ((0, 1.0), (1, NEAR), (-1, NEAR), (3, FAR), (-3, FAR)):
            if 0 <= 2 * k + d < s.nz:
                term = b[2 * k + d] if d == 0 else b[2 * k + d] * w
                out = term if out is None else out + term
        planes.append(out)
    high, low = halves(jnp.concatenate(planes, axis=0))
    ry1 = open_restriction((s.ny, LANES), 0, 0, -1, s.wide1)
    rx1 = open_restriction((s.rows1, s.ext), 1, -R, 0, s.x1)
    along = dot(high, ry1) + dot(low, ry1)
    shares = []
    for k in range(s.planes):
        high, low = halves(along[k * s.ext : (k + 1) * s.ext])
        shares.append(dot(rx1, high) + dot(rx1, low))
    for t, x in enumerate(packed(shares, s.wide1, s.tiles1)):
        m_ref[t] = x
    lane = lanes_of((s.ext, LANES))
    group = LANES // R
    for t in range(s.fine_tiles):
        first = last = jnp.zeros((s.ext, LANES), F32)
        for g in range(min(group, s.nz - t * group)):
            x = b[t * group + g]
            at = R * ((g + 1) % group)
            first = jnp.where((lane >= at) & (lane < at + R), turn(x, at), first)
            at = R * g
            last = jnp.where((lane >= at) & (lane < at + R), turn(x, at + R - s.ny), last)
        first_ref[t] = first
        last_ref[t] = last


def rows_of(shape):
    return lax.broadcasted_iota(jnp.int32, shape, 0)


def bell(c, d):
    d = jnp.abs(d)
    return jnp.where(d <= R, jnp.exp(c * d * d), 0.0)


def one(ref, level, t):
    return ref[level : level + 1, t : t + 1]


def spreads(w_ref, levels):
    out = []
    for l in levels:
        w = [one(w_ref, l, t) for t in range(TERMS)]
        out.append([-0.5 / (x * x) for x in w])
    return out


def units(coef, distance, valid):
    shape = (up8(len(coef)), LANES)
    row = rows_of(shape)
    column = jnp.zeros(shape, F32)
    for r, c in enumerate(coef):
        column = jnp.where(row == r, c, column)
    lane = lanes_of(shape)
    d = distance(row, lane).astype(F32)
    total = jnp.sum(jnp.where(valid(row, lane), jnp.exp(2.0 * column * d * d), 0.0), axis=1, keepdims=True)
    unit = 1.0 / jnp.sqrt(total)
    return [unit[r : r + 1] for r in range(len(coef))]


def near_units(coef):
    flat = [c for level in coef for c in level]
    out = units(flat, lambda row, lane: lane - R, lambda row, lane: lane <= 2 * R)
    return [out[i : i + TERMS] for i in range(0, len(out), TERMS)]


def tap_kernel(s, w_ref, a_ref, tap_ref, x0_ref, y0_ref):
    coef = spreads(w_ref, (0, 1))
    unit = near_units(coef)
    d = lanes_of((1, LANES)).astype(F32)
    for t in range(TERMS):
        tap_ref[t : t + 1] = bell(coef[0][t], d) * (unit[0][t] * one(a_ref, 0, t))
        tap_ref[TERMS + t : TERMS + t + 1] = bell(coef[1][t], d) * (unit[1][t] * one(a_ref, 1, t) * 0.25)
    shape = (s.nx, 3 * s.ext)
    lane = lanes_of(shape)
    part = jnp.where(lane < s.ext, 0, jnp.where(lane < 2 * s.ext, 1, 2))
    d = (lane - part * s.ext - R - rows_of(shape)).astype(F32)
    for t in range(TERMS):
        high, low = halves(bell(coef[0][t], d) * unit[0][t])
        x0_ref[t * s.nx : (t + 1) * s.nx] = jnp.where(part == 1, low.astype(F32), high.astype(F32)).astype(BF16)
    shape = (s.ny + 2 * R, s.ny)
    i = rows_of(shape)
    cell = jnp.where(i < s.ny, i, jnp.where(i < s.ny + R, i - s.ny - R, i - R))
    d = (cell - lanes_of(shape)).astype(F32)
    for t in range(TERMS):
        high, low = halves(bell(coef[0][t], d) * unit[0][t])
        at = 2 * t * s.ny
        y0_ref[s.ny + 2 * R :, at : at + 2 * s.ny] = jnp.zeros((2 * LANES - s.ny - 2 * R, 2 * s.ny), BF16)
        y0_ref[: s.ny + 2 * R, at : at + s.ny] = high
        y0_ref[: s.ny + 2 * R, at + s.ny : at + 2 * s.ny] = low


def matrix_kernel(s, w_ref, a_ref, px1, px2, px3, px3l, rx3, py2, py3, py3l, ry3, pz2, pz3, rz3, _,
                  z_ref, y1_ref, y2h_ref, y2l_ref, xh_ref, xl_ref):
    coef = spreads(w_ref, range(4))
    unit = near_units(coef[:3])
    sizes = [s.cx[3], s.cy[3], s.cz[3]]

    def per_row(row):
        return jnp.where(row < TERMS, sizes[0], jnp.where(row < 2 * TERMS, sizes[1], sizes[2]))

    top = units(
        coef[3] * 3,
        lambda row, lane: jnp.minimum(lane, per_row(row) - lane),
        lambda row, lane: lane < per_row(row),
    )
    top_x, top_y, top_z = top[:TERMS], top[TERMS : 2 * TERMS], top[2 * TERMS :]

    def circle(n, d, c, u):
        d = (d & (n - 1)).astype(F32)
        return (bell(c, d) + bell(c, n - d)) * u

    def full_circle(n, shape, c, u):
        d = ((rows_of(shape) - lanes_of(shape)) & (n - 1)).astype(F32)
        d = jnp.minimum(d, n - d)
        return jnp.exp(c * d * d) * u

    shape = (LANES, s.ny)
    fine = lanes_of(shape)
    d = (rows_of(shape) - (R + 1) - (fine >> 1)).astype(F32)
    even = (fine & 1) == 0
    known = rows_of(shape) < s.y1 + 3 + 2 * R
    wide = (s.cy[2], s.cy[2])
    for t in range(TERMS):
        c = coef[1][t]
        here = bell(c, d)
        between = NEAR * (here + bell(c, d - 1.0)) + FAR * (bell(c, d + 1.0) + bell(c, d - 2.0))
        high, low = halves(jnp.where(known, jnp.where(even, here, between) * unit[1][t], 0.0))
        y1_ref[:, 2 * t * s.ny : (2 * t + 1) * s.ny] = high
        y1_ref[:, (2 * t + 1) * s.ny : (2 * t + 2) * s.ny] = low
        g = circle(s.cy[2], rows_of(wide) - lanes_of(wide), coef[2][t], unit[2][t])
        high, low = halves(dot2(g, py2[...]))
        y2h_ref[:, t * s.ny : (t + 1) * s.ny] = high
        y2l_ref[:, t * s.ny : (t + 1) * s.ny] = low
        g = full_circle(s.cy[3], (s.cy[3], s.cy[3]), coef[3][t], top_y[t])
        high, low = halves(g)
        g = dot(ry3[...], high) + dot(ry3[...], low)
        high, low = halves(dot3(g, py3[...], py3l[...]))
        at = (TERMS + t) * s.ny
        y2h_ref[:, at : at + s.ny] = high
        y2l_ref[:, at : at + s.ny] = low

    def terms(level, first, rows, valid, shift):
        shape = (s.cx[level], s.depth_lanes)
        lane = lanes_of(shape) - first
        column = lane - jnp.where(lane < rows, 0, jnp.where(lane < 2 * rows, rows, 2 * rows))

        def by_term(v):
            return jnp.where(lane < rows, v[0], jnp.where(lane < 2 * rows, v[1], v[2]))

        g = circle(s.cx[level], rows_of(shape) - column + shift, by_term(coef[level]), by_term(unit[level]))
        high, low = halves(jnp.where((lane >= 0) & (lane < TERMS * rows) & (column < valid), g, 0.0))
        return high, low

    high, low = terms(1, 0, s.rows1, s.rows1, 0)
    x = dot(px1[...], high) + dot(px1[...], low)
    high, low = terms(2, TERMS * s.rows1, s.rows2, s.x2 + 3, 1)
    x += dot(px2[...], high) + dot(px2[...], low)
    g = None
    for t in range(TERMS):
        part = dot2(full_circle(s.cx[3], (s.cx[3], s.cx[3]), coef[3][t], top_x[t]), rx3[t])
        g = part if g is None else g + part
    high, low = halves(g)
    x += dot(px3[...], high) + dot(px3l[...], high) + dot(px3[...], low)
    xh_ref[...], xl_ref[...] = halves(x)
    for t in range(TERMS):
        shape = (s.cz[2], LANES)
        g = circle(s.cz[2], rows_of(shape) - lanes_of(shape), coef[2][t], unit[2][t])
        high, low = halves(g * (one(a_ref, 2, t) * 0.0625))
        z_ref[t * s.zrows : (t + 1) * s.zrows] = dot(pz2[...], high) + dot(pz2[...], low)
        g = full_circle(s.cz[3], (s.cz[3], s.cz[3]), coef[3][t], top_z[t])
        high, low = halves(g * (one(a_ref, 3, t) * 0.015625))
        g = dot2(dot(pz3[...], high) + dot(pz3[...], low), rz3[...])
        z_ref[(TERMS + t) * s.zrows : (TERMS + t + 1) * s.zrows] = g


def near_kernel(s, tap_ref, b_ref, lo_ref, hi_ref, left_ref, right_ref, x0_ref, y0_ref,
                own_ref, down_ref, up_ref, e_ref, u_ref, eh_ref, el_ref, v_ref):
    group = LANES // R
    tiles = [extended(s, b_ref, lo_ref, hi_ref, z) for z in range(s.nz)]
    tiles += [left_ref[t] for t in range(s.fine_tiles)] + [right_ref[t] for t in range(s.fine_tiles)]
    for i, x in enumerate(tiles):
        high, low = halves(x)
        columns = slice(i * LANES, (i + 1) * LANES)
        e_ref[0 : s.ext, columns] = high
        e_ref[s.ext : 2 * s.ext, columns] = high
        e_ref[2 * s.ext :, columns] = low
    x0 = x0_ref[...]
    for at in range(0, len(tiles) * LANES, 2 * LANES):
        columns = slice(at, min(at + 2 * LANES, len(tiles) * LANES))
        u_ref[:, columns] = dot(x0, e_ref[:, columns])
    lane = lanes_of((TERMS * s.nx, LANES))
    for z in range(s.nz):
        t, g = divmod(z, group)
        left = u_ref[:, (s.nz + t) * LANES : (s.nz + t + 1) * LANES]
        right = u_ref[:, (s.nz + s.fine_tiles + t) * LANES : (s.nz + s.fine_tiles + t + 1) * LANES]
        strips = turn(jnp.where((lane >= R * g) & (lane < R * g + R), left, right), -R * g)
        for at, x in ((0, u_ref[:, z * LANES : (z + 1) * LANES]), (LANES, strips)):
            high, low = halves(x)
            for t in range(TERMS):
                rows = slice(t * s.nx, (t + 1) * s.nx)
                eh_ref[t, z * s.nx : (z + 1) * s.nx, at : at + LANES] = high[rows]
                el_ref[t, z * s.nx : (z + 1) * s.nx, at : at + LANES] = low[rows]
    step = 4 * s.nx
    for t in range(TERMS):
        at = 2 * t * s.ny
        y0, y0h = y0_ref[:, at : at + 2 * s.ny], y0_ref[:, at : at + s.ny]
        for first in range(0, s.nz * s.nx, step):
            both = dot(eh_ref[t, first : first + step], y0)
            v = both[:, : s.ny] + both[:, s.ny :] + dot(el_ref[t, first : first + step], y0h)
            for q in range(step // s.nx):
                v_ref[t, first // s.nx + q] = v[q * s.nx : (q + 1) * s.nx]

    def depth(r, _):
        rows = pl.ds(pl.multiple_of(r * 8, 8), 8)
        taps = [[tap_ref[t, d] for d in range(R + 1)] for t in range(TERMS)]
        for first in range(-R, s.nz + R, R):
            acc = [None] * R
            for t in range(TERMS):
                for z in range(max(0, first - R), min(s.nz, first + 2 * R)):
                    v = v_ref[t, z, rows]
                    for o in range(R):
                        d = abs(first + o - z)
                        if d <= R:
                            term = v * taps[t][d]
                            acc[o] = term if acc[o] is None else acc[o] + term
            for o in range(R):
                if first < 0:
                    down_ref[o, rows] = acc[o]
                elif first >= s.nz:
                    up_ref[o, rows] = acc[o]
                else:
                    own_ref[first + o, rows] = acc[o]
        return 0

    lax.fori_loop(0, s.nx // 8, depth, 0)


def depth_kernel(s, tap_ref, m_ref, all_ref, ry2_ref, rx2_ref, _,
                 w_ref, down_ref, up_ref, c2_ref, c_ref):
    me = lax.axis_index("gz")
    m_refs = [m_ref] + [all_ref.at[lax.rem(me + b, s.gz)] for b in range(1, s.gz)]
    n = s.cz[1]
    parts = [[] for _ in range(n)]
    for b in range(s.gz):
        for k in range(s.planes):
            parts[(b * s.z1 + k - 1) % n].append((b, k))
    for z in range(n):
        out = None
        for b, k in parts[z]:
            x = unpacked(lambda t, b=b: m_refs[b][t], k, s.wide1, 0)
            out = x if out is None else out + x
        c_ref[z] = out
    lane = lanes_of((s.rows1, LANES))
    down = [jnp.zeros((s.rows1, LANES), F32)] * s.tiles_s
    up = list(down)
    for o in range(s.planes):
        sums = [c_ref[(o - 1) % n]]
        sums += [c_ref[(o - 1 + d) % n] + c_ref[(o - 1 - d) % n] for d in range(1, R + 1)]
        for t in range(TERMS):
            x = sums[0] * tap_ref[TERMS + t, 0]
            for d in range(1, R + 1):
                x += sums[d] * tap_ref[TERMS + t, d]
            k = t * s.planes + o
            w_ref[k] = x
            tile, slot = divmod(k, s.per_tile)
            at = slot * s.strip
            here = (lane >= at) & (lane < at + s.strip)
            down[tile] = jnp.where(here, turn(x, at), down[tile])
            up[tile] = jnp.where(here, turn(x, at - (s.wide1 - s.strip)), up[tile])
    coarse = []
    for j in range(s.cz[2]):
        at = lambda d: c_ref[(2 * j + d) % n]
        coarse.append(at(0) + NEAR * (at(1) + at(-1)) + FAR * (at(3) + at(-3)))
    high, low = halves(jnp.concatenate(coarse, axis=0))
    ry2 = ry2_ref[...].astype(BF16)
    rx2 = rx2_ref[...].astype(BF16)
    along = dot(high, ry2) + dot(low, ry2)
    shares = []
    for j in range(s.cz[2]):
        high, low = halves(along[j * s.rows1 : (j + 1) * s.rows1])
        shares.append(dot(rx2, high) + dot(rx2, low))
    for t in range(s.tiles_s):
        down_ref[t * s.rows1 : (t + 1) * s.rows1] = down[t]
        up_ref[t * s.rows1 : (t + 1) * s.rows1] = up[t]
    base = s.tiles_s * s.rows1
    for t, x in enumerate(packed(shares, s.wide2, s.tiles2)):
        rows = slice(t * s.rows2, (t + 1) * s.rows2)
        c2_ref[rows] = x
        for ref in (down_ref, up_ref):
            ref[base + t * s.rows2 : base + (t + 1) * s.rows2] = x


def along_kernel(s, z_ref, w_ref, *refs):
    c2_refs = refs[: s.gy]
    y1_ref, y2h_ref, y2l_ref, d_ref, yb_ref = refs[s.gy :]
    base = s.tiles_s * s.rows1
    lane = lanes_of((s.rows1, LANES))
    above, below = c2_refs[1], c2_refs[-1]
    end = s.y1 + R
    for t in range(TERMS):
        cells = []
        for o in range(s.planes):
            k = t * s.planes + o
            tile, slot = divmod(k, s.per_tile)
            rows = slice(tile * s.rows1, (tile + 1) * s.rows1)
            at = slot * s.strip
            x = turn(w_ref[k], R)
            x += jnp.where(lane < s.strip, turn(below[rows], -at), 0.0)
            x += jnp.where((lane >= end) & (lane < end + s.strip), turn(above[rows], end - at), 0.0)
            cells.append(x)
        high, low = halves(jnp.concatenate(cells, axis=0))
        at = 2 * t * s.ny
        both = dot(high, y1_ref[:, at : at + 2 * s.ny])
        out = both[:, : s.ny] + both[:, s.ny :] + dot(low, y1_ref[:, at : at + s.ny])
        for o in range(s.planes):
            d_ref[t * s.rows1 : (t + 1) * s.rows1, o * s.ny : (o + 1) * s.ny] = out[o * s.rows1 : (o + 1) * s.rows1]
    cells = []
    for j in range(s.cz[2]):
        out = None
        for b in range(s.gy):
            first = 0 if b == 0 or c2_refs[b].shape[0] == s.tiles2 * s.rows2 else base
            tile = lambda t, b=b, f=first: c2_refs[b][f + t * s.rows2 : f + (t + 1) * s.rows2]
            x = unpacked(tile, j, s.wide2, (b * s.y2 - 2) % LANES)
            out = x if out is None else out + x
        cells.append(out)
    yb = dot3(jnp.concatenate(cells, axis=0), y2h_ref[...], y2l_ref[...])
    for j in range(s.cz[2]):
        for q in range(2 * TERMS):
            yb_ref[q, j] = yb[j * s.rows2 : (j + 1) * s.rows2, q * s.ny : (q + 1) * s.ny]
    for o in range(s.planes):
        for q in range(2 * TERMS):
            x = yb_ref[q, 0] * z_ref[q * s.zrows + o, 0]
            for j in range(1, s.cz[2]):
                x += yb_ref[q, j] * z_ref[q * s.zrows + o, j]
            at = TERMS * s.rows1 + q * s.rows2
            d_ref[at : at + s.rows2, o * s.ny : (o + 1) * s.ny] = x


def across(s, d_ref, xh_ref, xl_ref, shift):
    rows = slice(shift * s.nx, (shift + 1) * s.nx)
    high, low = halves(d_ref[...])
    xh, xl = xh_ref[rows, : s.depth], xl_ref[rows, : s.depth]
    return dot(xh, high) + dot(xl, high) + dot(xh, low)


def away_kernel(s, d_ref, xh_ref, xl_ref, *g_refs):
    for shift, ref in enumerate(g_refs):
        ref[...] = across(s, d_ref, xh_ref, xl_ref, shift + 1)


def prolonged(s, level, z):
    m = z // 2 + 1
    if z % 2 == 0:
        return level[m]
    return NEAR * (level[m] + level[m + 1]) + FAR * (level[m - 1] + level[m + 2])


def home_kernel(s, d_ref, xh_ref, xl_ref, own_ref, low_ref, high_ref, out_ref):
    g = across(s, d_ref, xh_ref, xl_ref, 0)
    level = [g[:, o * s.ny : (o + 1) * s.ny] for o in range(s.planes)]
    for z in range(s.nz):
        x = prolonged(s, level, z) + own_ref[z]
        if z < R:
            x += low_ref[z]
        if z >= s.nz - R:
            x += high_ref[z - (s.nz - R)]
        out_ref[z] = x


def last_kernel(s, home_ref, *refs):
    g_refs, out_ref = refs[:-1], refs[-1]
    level = []
    for o in range(s.planes):
        columns = slice(o * s.ny, (o + 1) * s.ny)
        x = g_refs[0][:, columns]
        for ref in g_refs[1:]:
            x += ref[:, columns]
        level.append(x)
    for z in range(s.nz):
        out_ref[z] = home_ref[z] + prolonged(s, level, z)


def call(kernel, name, operands, out_shapes, scalars=(), after=(), scratch=(), flops=0):
    operands = list(operands) + list(after)

    def spec(i):
        if i >= len(operands) - len(after):
            return pl.BlockSpec(memory_space=pl.ANY)
        return pl.BlockSpec(memory_space=pltpu.SMEM if i in scalars else pltpu.VMEM)

    moved = sum(x.size * x.dtype.itemsize for x in operands)
    moved += sum(int(np.prod(x.shape)) * x.dtype.itemsize for x in out_shapes)
    return pl.pallas_call(
        kernel,
        name=name,
        out_shape=out_shapes,
        in_specs=[spec(i) for i in range(len(operands))],
        out_specs=[pl.BlockSpec(memory_space=pltpu.VMEM)] * len(out_shapes),
        scratch_shapes=list(scratch),
        compiler_params=pltpu.CompilerParams(vmem_limit_bytes=VMEM_LIMIT),
        cost_estimate=pl.CostEstimate(flops=flops, bytes_accessed=moved, transcendentals=0),
    )(*operands)


def arrays(*shapes, dtype=F32):
    return [jax.ShapeDtypeStruct(shape, dtype) for shape in shapes]


def fetch(x, **shifts):
    names = tuple(shifts)
    sizes = [lax.axis_size(n) for n in names]
    pairs = []
    for here in np.ndindex(*sizes):
        there = [(h + shifts[n]) % size for h, n, size in zip(here, names, sizes)]
        pairs.append((int(np.ravel_multi_index(there, sizes)), int(np.ravel_multi_index(here, sizes))))
    return lax.ppermute(x, names if len(names) > 1 else names[0], pairs)


def two(*shape):
    return arrays(shape, shape, dtype=BF16)


def shards(charges, widths, amplitudes):
    s = Sizes(*charges.shape, lax.axis_size("gz"), lax.axis_size("gx"), lax.axis_size("gy"))
    c = {k: jnp.asarray(v) for k, v in constants(s).items()}
    brick = (s.nz, s.nx, s.ny)
    side = (R, s.nx, s.ny)
    taps, x0, y0 = call(
        functools.partial(tap_kernel, s), "taps", [widths, amplitudes],
        arrays((8, LANES))
        + arrays((TERMS * s.nx, 3 * s.ext), (2 * LANES, 2 * TERMS * s.ny), dtype=BF16),
        flops=6 * 10**8,
    )
    high_rows = fetch(charges, gx=1)
    low_rows = high_rows if s.gx == 2 else fetch(charges, gx=-1)
    strips = (s.fine_tiles, s.ext, LANES)
    share, first_cells, last_cells = call(
        functools.partial(share_kernel, s), "share", [charges, low_rows, high_rows],
        arrays((s.tiles1, s.rows1, LANES), strips, strips), after=[x0], flops=10**9,
    )
    shares = lax.all_gather(share, "gz")
    left, right = fetch(last_cells, gy=-1), fetch(first_cells, gy=1)
    tiles = s.nz + 2 * s.fine_tiles
    halved = pltpu.VMEM((TERMS, s.nz * s.nx, 2 * LANES), BF16)
    near, near_down, near_up = call(
        functools.partial(near_kernel, s), "near",
        [taps, charges, low_rows, high_rows, left, right, x0, y0],
        arrays(brick, side, side), scalars=(0,),
        scratch=[
            pltpu.VMEM((3 * s.ext, tiles * LANES), BF16), pltpu.VMEM((TERMS * s.nx, tiles * LANES), F32),
            halved, halved, pltpu.VMEM((TERMS,) + brick, F32),
        ],
        flops=5 * 10**9,
    )
    base = s.tiles_s * s.rows1
    size2 = s.tiles2 * s.rows2
    waves, to_low, to_high, coarse = call(
        functools.partial(depth_kernel, s), "depth",
        [taps, share, shares, c["ry2"], c["rx2"]],
        arrays((TERMS * s.planes, s.rows1, LANES), (base + size2, LANES), (base + size2, LANES), (size2, LANES)),
        scalars=(0,), after=[near], scratch=[pltpu.VMEM((s.cz[1], s.rows1, LANES), F32)], flops=2 * 10**9,
    )
    named = ("px1", "px2", "px3", "px3l", "rx3", "py2", "py3", "py3l", "ry3", "pz2", "pz3", "rz3")
    z_taps, y1, y2h, y2l, xh, xl = call(
        functools.partial(matrix_kernel, s), "matrices",
        [widths, amplitudes] + [c[k] for k in named],
        arrays((2 * TERMS * s.zrows, LANES))
        + arrays((LANES, 2 * TERMS * s.ny), dtype=BF16)
        + two(s.cy[2], 2 * TERMS * s.ny) + two(s.cx[0], s.depth_lanes),
        after=[coarse], flops=2 * 10**9,
    )
    coarses = [coarse]
    for b in range(1, s.gy):
        coarses.append(fetch({1: to_low, s.gy - 1: to_high}.get(b, coarse), gy=b))
    near_low, near_high = fetch(near_up, gz=-1), fetch(near_down, gz=1)
    (terms,) = call(
        functools.partial(along_kernel, s), "along",
        [z_taps, waves] + coarses + [y1, y2h, y2l],
        arrays((s.depth, s.planes * s.ny)), scalars=(0,),
        scratch=[pltpu.VMEM((2 * TERMS, s.cz[2], s.rows2, s.ny), F32)], flops=3 * 10**9,
    )
    parts = call(
        functools.partial(away_kernel, s), "away", [terms, xh, xl],
        arrays(*[(s.nx, s.planes * s.ny)] * (s.gx - 1)), flops=10**9,
    )
    parts = [fetch(x, gx=-dx) for dx, x in enumerate(parts, 1)]
    (home,) = call(
        functools.partial(home_kernel, s), "home",
        [terms, xh, xl, near, near_low, near_high], arrays(brick), flops=2 * 10**9,
    )
    (out,) = call(
        functools.partial(last_kernel, s), "last", [home] + parts, arrays(brick), flops=10**9,
    )
    return out


def solution(mesh):
    placed = (P("gz", "gx", "gy"), P(), P())
    return jax.shard_map(
        shards, mesh=mesh, in_specs=placed, out_specs=P("gz", "gx", "gy"), check_vma=False
    )
```

```python
import functools

import jax
import jax.numpy as jnp
import ml_dtypes
import numpy as np
from jax import lax
from jax.experimental import pallas as pl
from jax.experimental.pallas import tpu as pltpu
from jax.sharding import PartitionSpec as P

R = 8
TERMS = 3
LANES = 128
NEAR = 9.0 / 16.0
FAR = -1.0 / 16.0
F32 = jnp.float32
BF16 = jnp.bfloat16
VMEM_LIMIT = 40 * 1024 * 1024


def up8(n):
    return -(-n // 8) * 8


class Sizes:
    def __init__(self, nz, nx, ny, gz, gx, gy):
        self.nz, self.nx, self.ny = nz, nx, ny
        self.gz, self.gx, self.gy = gz, gx, gy
        self.z1, self.x1, self.y1 = nz // 2, nx // 2, ny // 2
        self.z2, self.x2, self.y2 = nz // 4, nx // 4, ny // 4
        self.cz = [nz * gz >> l for l in range(4)]
        self.cx = [nx * gx >> l for l in range(4)]
        self.cy = [ny * gy >> l for l in range(4)]
        self.planes = self.z1 + 3
        self.zrows = up8(self.planes)
        self.rows1 = self.x1
        self.rows2 = up8(self.x2 + 3)
        self.wide1 = self.y1 + 3
        self.wide2 = self.y2 + 5
        self.tiles1 = -(-self.planes * self.wide1 // LANES)
        self.tiles2 = -(-self.cz[2] * self.wide2 // LANES)
        self.strip = R + 3
        self.per_tile = LANES // self.strip
        self.tiles_s = -(-TERMS * self.planes // self.per_tile)
        self.fine_tiles = -(-nz // (LANES // R))
        self.ext = nx + 2 * R
        self.depth = TERMS * (self.rows1 + 2 * self.rows2)
        self.depth_lanes = -(-self.depth // LANES) * LANES


def restrict_circle(n):
    m = np.zeros((n // 2, n))
    for i in range(n // 2):
        for d, w in ((0, 1.0), (1, NEAR), (-1, NEAR), (3, FAR), (-3, FAR)):
            m[i, (2 * i + d) % n] += w
    return m


def prolong_circle(n):
    m = np.zeros((2 * n, n))
    for i in range(n):
        m[2 * i, i] += 1.0
        for d, w in ((0, NEAR), (1, NEAR), (-1, FAR), (2, FAR)):
            m[2 * i + 1, (i + d) % n] += w
    return m


def restrict_open(first_in, n_in, first_out, n_out):
    m = np.zeros((n_out, n_in))
    for i in range(n_out):
        for d, w in ((0, 1.0), (1, NEAR), (-1, NEAR), (3, FAR), (-3, FAR)):
            j = 2 * (first_out + i) + d - first_in
            if 0 <= j < n_in:
                m[i, j] = w
    return m


def padded(m, rows, columns):
    out = np.zeros((rows, columns), np.float32)
    out[: m.shape[0], : m.shape[1]] = m
    return out


def exact(m):
    out = m.astype(ml_dtypes.bfloat16)
    assert np.all(out.astype(np.float64) == m)
    return out


def constants(s):
    c = {}
    c["ry2"] = padded(restrict_open(-1, s.wide1, -2, s.wide2).T, LANES, LANES)
    c["rx2"] = padded(restrict_open(0, s.x1, -1, s.x2 + 3), s.rows2, s.rows1)

    def chain(n):
        p1 = prolong_circle(n[1])
        p2 = p1 @ prolong_circle(n[2])
        return p1, p2, p2 @ prolong_circle(n[3])

    def parts(name, m):
        m = m.astype(np.float32)
        c[name] = m.astype(ml_dtypes.bfloat16)
        c[name + "l"] = (m - c[name].astype(np.float32)).astype(ml_dtypes.bfloat16)

    x1, x2, x3 = chain(s.cx)
    c["px1"], c["px2"] = exact(x1), exact(x2)
    parts("px3", x3)
    place = np.zeros((s.cx[2], s.rows2))
    for r in range(s.x2 + 3):
        place[(r - 1) % s.cx[2], r] += 1.0
    rx3 = np.zeros((TERMS, s.cx[3], s.depth_lanes))
    for t in range(TERMS):
        first = TERMS * s.rows1 + (TERMS + t) * s.rows2
        rx3[t, :, first : first + s.rows2] = restrict_circle(s.cx[2]) @ place
    c["rx3"] = exact(rx3)
    _, y2, y3 = chain(s.cy)
    c["py2"] = exact(y2[: s.ny].T)
    parts("py3", y3[: s.ny].T)
    c["ry3"] = exact(restrict_circle(s.cy[2]).T)
    z2 = prolong_circle(s.cz[2])
    z3 = z2 @ prolong_circle(s.cz[3])
    own = [(o - 1) % s.cz[1] for o in range(s.planes)]
    c["pz2"] = exact(padded(z2[own], s.zrows, s.cz[2]))
    c["pz3"] = exact(padded(z3[own], s.zrows, s.cz[3]))
    c["rz3"] = exact(padded(restrict_circle(s.cz[2]), s.cz[3], LANES))
    return c


def halves(x):
    high = x.astype(BF16)
    return high, (x - high.astype(F32)).astype(BF16)


def dot(a, b):
    return jnp.dot(a, b, preferred_element_type=F32)


def dot2(a, b):
    high, low = halves(a)
    return dot(high, b) + dot(low, b)


def dot3(a, b_high, b_low):
    high, low = halves(a)
    return dot(high, b_high) + dot(low, b_high) + dot(high, b_low)


def lanes_of(shape):
    return lax.broadcasted_iota(jnp.int32, shape, len(shape) - 1)


def turn(x, by):
    by = by % x.shape[-1]
    return x if by == 0 else pltpu.roll(x, by, x.ndim - 1)


def packed(planes, wide, tiles):
    out = [None] * tiles

    def add(t, x):
        out[t] = x if out[t] is None else out[t] + x

    for k, x in enumerate(planes):
        t, at = divmod(k * wide, LANES)
        moved = turn(x, at)
        if at + wide <= LANES:
            add(t, moved)
        else:
            lane = lanes_of(x.shape)
            add(t, jnp.where(lane >= at, moved, 0.0))
            add(t + 1, jnp.where(lane < at, moved, 0.0))
    return out


def unpacked(tile, k, wide, shift):
    t, at = divmod(k * wide, LANES)
    x = tile(t)
    lane = lanes_of(x.shape)
    if at + wide > LANES:
        x = jnp.where(lane >= at, x, tile(t + 1))
    x = turn(x, shift - at)
    if shift + wide <= LANES:
        return jnp.where((lane >= shift) & (lane < shift + wide), x, 0.0)
    return jnp.where((lane >= shift) | (lane < shift + wide - LANES), x, 0.0)


def open_restriction(shape, in_dim, first_in, first_out, n_out):
    i = lax.broadcasted_iota(jnp.int32, shape, in_dim) + first_in
    o = lax.broadcasted_iota(jnp.int32, shape, 1 - in_dim)
    d = jnp.abs(i - 2 * (o + first_out))
    w = jnp.where(d == 0, 1.0, jnp.where(d == 1, NEAR, jnp.where(d == 3, FAR, 0.0)))
    return jnp.where(o < n_out, w, 0.0).astype(BF16)


def extended(s, b_ref, lo_ref, hi_ref, z):
    return jnp.concatenate([lo_ref[z, s.nx - R :], b_ref[z], hi_ref[z, 0:R]], axis=0)


def strips(s, rows):
    lane = lanes_of(rows[0].shape)
    group = LANES // R
    first, last = [], []
    for t in range(s.fine_tiles):
        f = l = jnp.zeros(rows[0].shape, F32)
        for g in range(min(group, s.nz - t * group)):
            x = rows[t * group + g]
            at = R * ((g + 1) % group)
            f = jnp.where((lane >= at) & (lane < at + R), turn(x, at), f)
            at = R * g
            l = jnp.where((lane >= at) & (lane < at + R), turn(x, at + R - s.ny), l)
        first.append(f)
        last.append(l)
    return first, last


def share_kernel(s, b_ref, lo_ref, hi_ref, _, m_ref, *strip_refs):
    b = [extended(s, b_ref, lo_ref, hi_ref, z) for z in range(s.nz)]
    planes = []
    for k in range(-1, s.z1 + 2):
        out = None
        for d, w in ((0, 1.0), (1, NEAR), (-1, NEAR), (3, FAR), (-3, FAR)):
            if 0 <= 2 * k + d < s.nz:
                term = b[2 * k + d] if d == 0 else b[2 * k + d] * w
                out = term if out is None else out + term
        planes.append(out)
    high, low = halves(jnp.concatenate(planes, axis=0))
    ry1 = open_restriction((s.ny, LANES), 0, 0, -1, s.wide1)
    rx1 = open_restriction((s.rows1, s.ext), 1, -R, 0, s.x1)
    along = dot(high, ry1) + dot(low, ry1)
    shares = []
    for k in range(s.planes):
        high, low = halves(along[k * s.ext : (k + 1) * s.ext])
        shares.append(dot(rx1, high) + dot(rx1, low))
    for t, x in enumerate(packed(shares, s.wide1, s.tiles1)):
        m_ref[t] = x
    if s.gx == 2:
        low_slab = lax.axis_index("gx") == 0
        own, other = strips(s, [b_ref[z] for z in range(s.nz)]), strips(s, [hi_ref[z] for z in range(s.nz)])
        for t in range(s.fine_tiles):
            strip_refs[0][t, : s.nx] = jnp.where(low_slab, own[1][t], other[0][t])
            strip_refs[0][t, s.nx :] = jnp.where(low_slab, other[1][t], own[0][t])
        return
    for ref, x in zip(strip_refs, strips(s, b)):
        for t in range(s.fine_tiles):
            ref[t] = x[t]


def rows_of(shape):
    return lax.broadcasted_iota(jnp.int32, shape, 0)


def bell(c, d):
    d = jnp.abs(d)
    return jnp.where(d <= R, jnp.exp(c * d * d), 0.0)


def one(ref, level, t):
    return ref[level : level + 1, t : t + 1]


def spreads(w_ref, levels):
    out = []
    for l in levels:
        w = [one(w_ref, l, t) for t in range(TERMS)]
        out.append([-0.5 / (x * x) for x in w])
    return out


def units(coef, distance, valid):
    shape = (up8(len(coef)), LANES)
    row = rows_of(shape)
    column = jnp.zeros(shape, F32)
    for r, c in enumerate(coef):
        column = jnp.where(row == r, c, column)
    lane = lanes_of(shape)
    d = distance(row, lane).astype(F32)
    total = jnp.sum(jnp.where(valid(row, lane), jnp.exp(2.0 * column * d * d), 0.0), axis=1, keepdims=True)
    unit = 1.0 / jnp.sqrt(total)
    return [unit[r : r + 1] for r in range(len(coef))]


def near_units(coef):
    flat = [c for level in coef for c in level]
    out = units(flat, lambda row, lane: lane - R, lambda row, lane: lane <= 2 * R)
    return [out[i : i + TERMS] for i in range(0, len(out), TERMS)]


def tap_kernel(s, w_ref, a_ref, tap_ref, x0_ref):
    coef = spreads(w_ref, (0, 1))
    unit = near_units(coef)
    d = lanes_of((1, LANES)).astype(F32)
    for t in range(TERMS):
        tap_ref[t : t + 1] = bell(coef[0][t], d) * (unit[0][t] * one(a_ref, 0, t))
        tap_ref[TERMS + t : TERMS + t + 1] = bell(coef[1][t], d) * (unit[1][t] * one(a_ref, 1, t) * 0.25)
    shape = (s.nx, 3 * s.ext)
    lane = lanes_of(shape)
    part = jnp.where(lane < s.ext, 0, jnp.where(lane < 2 * s.ext, 1, 2))
    d = (lane - part * s.ext - R - rows_of(shape)).astype(F32)
    for t in range(TERMS):
        high, low = halves(bell(coef[0][t], d) * unit[0][t])
        x0_ref[t * s.nx : (t + 1) * s.nx] = jnp.where(part == 1, low.astype(F32), high.astype(F32)).astype(BF16)


def along_matrix_kernel(s, w_ref, _, y0_ref, _out):
    coef = spreads(w_ref, (0,))
    unit = near_units(coef)
    shape = (s.ny + 2 * R, s.ny)
    i = rows_of(shape)
    cell = jnp.where(i < s.ny, i, jnp.where(i < s.ny + R, i - s.ny - R, i - R))
    d = (cell - lanes_of(shape)).astype(F32)
    for t in range(TERMS):
        high, low = halves(bell(coef[0][t], d) * unit[0][t])
        at = 2 * t * s.ny
        y0_ref[s.ny + 2 * R :, at : at + 2 * s.ny] = jnp.zeros((2 * LANES - s.ny - 2 * R, 2 * s.ny), BF16)
        y0_ref[: s.ny + 2 * R, at : at + s.ny] = high
        y0_ref[: s.ny + 2 * R, at + s.ny : at + 2 * s.ny] = low


def matrix_kernel(s, w_ref, a_ref, px1, px2, px3, px3l, rx3, py2, py3, py3l, ry3, pz2, pz3, rz3, _,
                  z_ref, y1_ref, y2h_ref, y2l_ref, xh_ref, xl_ref):
    coef = spreads(w_ref, range(4))
    unit = near_units(coef[:3])
    sizes = [s.cx[3], s.cy[3], s.cz[3]]

    def per_row(row):
        return jnp.where(row < TERMS, sizes[0], jnp.where(row < 2 * TERMS, sizes[1], sizes[2]))

    top = units(
        coef[3] * 3,
        lambda row, lane: jnp.minimum(lane, per_row(row) - lane),
        lambda row, lane: lane < per_row(row),
    )
    top_x, top_y, top_z = top[:TERMS], top[TERMS : 2 * TERMS], top[2 * TERMS :]

    def circle(n, d, c, u):
        d = (d & (n - 1)).astype(F32)
        return (bell(c, d) + bell(c, n - d)) * u

    def full_circle(n, shape, c, u):
        d = ((rows_of(shape) - lanes_of(shape)) & (n - 1)).astype(F32)
        d = jnp.minimum(d, n - d)
        return jnp.exp(c * d * d) * u

    shape = (LANES, s.ny)
    fine = lanes_of(shape)
    d = (rows_of(shape) - (R + 1) - (fine >> 1)).astype(F32)
    even = (fine & 1) == 0
    known = rows_of(shape) < s.y1 + 3 + 2 * R
    wide = (s.cy[2], s.cy[2])
    for t in range(TERMS):
        c = coef[1][t]
        here = bell(c, d)
        between = NEAR * (here + bell(c, d - 1.0)) + FAR * (bell(c, d + 1.0) + bell(c, d - 2.0))
        high, low = halves(jnp.where(known, jnp.where(even, here, between) * unit[1][t], 0.0))
        y1_ref[:, 2 * t * s.ny : (2 * t + 1) * s.ny] = high
        y1_ref[:, (2 * t + 1) * s.ny : (2 * t + 2) * s.ny] = low
        g = circle(s.cy[2], rows_of(wide) - lanes_of(wide), coef[2][t], unit[2][t])
        high, low = halves(dot2(g, py2[...]))
        y2h_ref[:, t * s.ny : (t + 1) * s.ny] = high
        y2l_ref[:, t * s.ny : (t + 1) * s.ny] = low
        g = full_circle(s.cy[3], (s.cy[3], s.cy[3]), coef[3][t], top_y[t])
        high, low = halves(g)
        g = dot(ry3[...], high) + dot(ry3[...], low)
        high, low = halves(dot3(g, py3[...], py3l[...]))
        at = (TERMS + t) * s.ny
        y2h_ref[:, at : at + s.ny] = high
        y2l_ref[:, at : at + s.ny] = low

    def terms(level, first, rows, valid, shift):
        shape = (s.cx[level], s.depth_lanes)
        lane = lanes_of(shape) - first
        column = lane - jnp.where(lane < rows, 0, jnp.where(lane < 2 * rows, rows, 2 * rows))

        def by_term(v):
            return jnp.where(lane < rows, v[0], jnp.where(lane < 2 * rows, v[1], v[2]))

        g = circle(s.cx[level], rows_of(shape) - column + shift, by_term(coef[level]), by_term(unit[level]))
        high, low = halves(jnp.where((lane >= 0) & (lane < TERMS * rows) & (column < valid), g, 0.0))
        return high, low

    high, low = terms(1, 0, s.rows1, s.rows1, 0)
    x = dot(px1[...], high) + dot(px1[...], low)
    high, low = terms(2, TERMS * s.rows1, s.rows2, s.x2 + 3, 1)
    x += dot(px2[...], high) + dot(px2[...], low)
    g = None
    for t in range(TERMS):
        part = dot2(full_circle(s.cx[3], (s.cx[3], s.cx[3]), coef[3][t], top_x[t]), rx3[t])
        g = part if g is None else g + part
    high, low = halves(g)
    x += dot(px3[...], high) + dot(px3l[...], high) + dot(px3[...], low)
    xh_ref[...], xl_ref[...] = halves(x)
    for t in range(TERMS):
        shape = (s.cz[2], LANES)
        g = circle(s.cz[2], rows_of(shape) - lanes_of(shape), coef[2][t], unit[2][t])
        high, low = halves(g * (one(a_ref, 2, t) * 0.0625))
        z_ref[t * s.zrows : (t + 1) * s.zrows] = dot(pz2[...], high) + dot(pz2[...], low)
        g = full_circle(s.cz[3], (s.cz[3], s.cz[3]), coef[3][t], top_z[t])
        high, low = halves(g * (one(a_ref, 3, t) * 0.015625))
        g = dot2(dot(pz3[...], high) + dot(pz3[...], low), rz3[...])
        z_ref[(TERMS + t) * s.zrows : (TERMS + t + 1) * s.zrows] = g


def near_kernel(s, tap_ref, b_ref, lo_ref, hi_ref, left_ref, right_ref, x0_ref, y0_ref,
                own_ref, down_ref, up_ref, e_ref, u_ref, eh_ref, el_ref, v_ref):
    group = LANES // R
    tiles = [extended(s, b_ref, lo_ref, hi_ref, z) for z in range(s.nz)]
    if s.gx == 2:
        low_slab = lax.axis_index("gx") == 0

        def side(x, y):
            out = []
            for t in range(s.fine_tiles):
                x0, x1 = (jnp.where(low_slab, x[t, r], y[t, r]) for r in (slice(0, s.nx), slice(s.nx, 2 * s.nx)))
                own, other = jnp.where(low_slab, x0, x1), jnp.where(low_slab, x1, x0)
                out.append(jnp.concatenate([other[s.nx - R :], own, other[0:R]], axis=0))
            return out

        tiles += side(left_ref, right_ref) + side(right_ref, left_ref)
    else:
        tiles += [ref[t] for ref in (left_ref, right_ref) for t in range(s.fine_tiles)]
    for i, x in enumerate(tiles):
        high, low = halves(x)
        columns = slice(i * LANES, (i + 1) * LANES)
        e_ref[0 : s.ext, columns] = high
        e_ref[s.ext : 2 * s.ext, columns] = high
        e_ref[2 * s.ext :, columns] = low
    x0 = x0_ref[...]
    for at in range(0, len(tiles) * LANES, 2 * LANES):
        columns = slice(at, min(at + 2 * LANES, len(tiles) * LANES))
        u_ref[:, columns] = dot(x0, e_ref[:, columns])
    lane = lanes_of((TERMS * s.nx, LANES))
    for z in range(s.nz):
        t, g = divmod(z, group)
        left = u_ref[:, (s.nz + t) * LANES : (s.nz + t + 1) * LANES]
        right = u_ref[:, (s.nz + s.fine_tiles + t) * LANES : (s.nz + s.fine_tiles + t + 1) * LANES]
        strips = turn(jnp.where((lane >= R * g) & (lane < R * g + R), left, right), -R * g)
        for at, x in ((0, u_ref[:, z * LANES : (z + 1) * LANES]), (LANES, strips)):
            high, low = halves(x)
            for t in range(TERMS):
                rows = slice(t * s.nx, (t + 1) * s.nx)
                eh_ref[t, z * s.nx : (z + 1) * s.nx, at : at + LANES] = high[rows]
                el_ref[t, z * s.nx : (z + 1) * s.nx, at : at + LANES] = low[rows]
    step = 4 * s.nx
    for t in range(TERMS):
        at = 2 * t * s.ny
        y0, y0h = y0_ref[:, at : at + 2 * s.ny], y0_ref[:, at : at + s.ny]
        for first in range(0, s.nz * s.nx, step):
            both = dot(eh_ref[t, first : first + step], y0)
            v = both[:, : s.ny] + both[:, s.ny :] + dot(el_ref[t, first : first + step], y0h)
            for q in range(step // s.nx):
                v_ref[t, first // s.nx + q] = v[q * s.nx : (q + 1) * s.nx]

    def depth(r, _):
        rows = pl.ds(pl.multiple_of(r * 8, 8), 8)
        taps = [[tap_ref[t, d] for d in range(R + 1)] for t in range(TERMS)]
        for first in range(-R, s.nz + R, R):
            acc = [None] * R
            for t in range(TERMS):
                for z in range(max(0, first - R), min(s.nz, first + 2 * R)):
                    v = v_ref[t, z, rows]
                    for o in range(R):
                        d = abs(first + o - z)
                        if d <= R:
                            term = v * taps[t][d]
                            acc[o] = term if acc[o] is None else acc[o] + term
            for o in range(R):
                if first < 0:
                    down_ref[o, rows] = acc[o]
                elif first >= s.nz:
                    up_ref[o, rows] = acc[o]
                else:
                    own_ref[first + o, rows] = acc[o]
        return 0

    lax.fori_loop(0, s.nx // 8, depth, 0)


def depth_kernel(s, tap_ref, *refs):
    m_refs = refs[: s.gz]
    ry2_ref, rx2_ref, _, w_ref, down_ref, up_ref, c2_ref, c_ref = refs[s.gz :]
    n = s.cz[1]
    parts = [[] for _ in range(n)]
    for b in range(s.gz):
        for k in range(s.planes):
            parts[(b * s.z1 + k - 1) % n].append((b, k))
    for z in range(n):
        out = None
        for b, k in parts[z]:
            x = unpacked(lambda t, b=b: m_refs[b][t], k, s.wide1, 0)
            out = x if out is None else out + x
        c_ref[z] = out
    lane = lanes_of((s.rows1, LANES))
    down = [jnp.zeros((s.rows1, LANES), F32)] * s.tiles_s
    up = list(down)
    for o in range(s.planes):
        sums = [c_ref[(o - 1) % n]]
        sums += [c_ref[(o - 1 + d) % n] + c_ref[(o - 1 - d) % n] for d in range(1, R + 1)]
        for t in range(TERMS):
            x = sums[0] * tap_ref[TERMS + t, 0]
            for d in range(1, R + 1):
                x += sums[d] * tap_ref[TERMS + t, d]
            k = t * s.planes + o
            w_ref[k] = x
            tile, slot = divmod(k, s.per_tile)
            at = slot * s.strip
            here = (lane >= at) & (lane < at + s.strip)
            down[tile] = jnp.where(here, turn(x, at), down[tile])
            up[tile] = jnp.where(here, turn(x, at - (s.wide1 - s.strip)), up[tile])
    coarse = []
    for j in range(s.cz[2]):
        at = lambda d: c_ref[(2 * j + d) % n]
        coarse.append(at(0) + NEAR * (at(1) + at(-1)) + FAR * (at(3) + at(-3)))
    high, low = halves(jnp.concatenate(coarse, axis=0))
    ry2 = ry2_ref[...].astype(BF16)
    rx2 = rx2_ref[...].astype(BF16)
    along = dot(high, ry2) + dot(low, ry2)
    shares = []
    for j in range(s.cz[2]):
        high, low = halves(along[j * s.rows1 : (j + 1) * s.rows1])
        shares.append(dot(rx2, high) + dot(rx2, low))
    for t in range(s.tiles_s):
        down_ref[t * s.rows1 : (t + 1) * s.rows1] = down[t]
        up_ref[t * s.rows1 : (t + 1) * s.rows1] = up[t]
    base = s.tiles_s * s.rows1
    for t, x in enumerate(packed(shares, s.wide2, s.tiles2)):
        rows = slice(t * s.rows2, (t + 1) * s.rows2)
        c2_ref[rows] = x
        for ref in (down_ref, up_ref):
            ref[base + t * s.rows2 : base + (t + 1) * s.rows2] = x


def along_kernel(s, z_ref, w_ref, *refs):
    c2_refs = refs[: s.gy]
    y1_ref, y2h_ref, y2l_ref, d_ref, yb_ref = refs[s.gy :]
    base = s.tiles_s * s.rows1
    lane = lanes_of((s.rows1, LANES))
    above, below = c2_refs[1], c2_refs[-1]
    end = s.y1 + R
    for t in range(TERMS):
        cells = []
        for o in range(s.planes):
            k = t * s.planes + o
            tile, slot = divmod(k, s.per_tile)
            rows = slice(tile * s.rows1, (tile + 1) * s.rows1)
            at = slot * s.strip
            x = turn(w_ref[k], R)
            x += jnp.where(lane < s.strip, turn(below[rows], -at), 0.0)
            x += jnp.where((lane >= end) & (lane < end + s.strip), turn(above[rows], end - at), 0.0)
            cells.append(x)
        high, low = halves(jnp.concatenate(cells, axis=0))
        at = 2 * t * s.ny
        both = dot(high, y1_ref[:, at : at + 2 * s.ny])
        out = both[:, : s.ny] + both[:, s.ny :] + dot(low, y1_ref[:, at : at + s.ny])
        for o in range(s.planes):
            d_ref[t * s.rows1 : (t + 1) * s.rows1, o * s.ny : (o + 1) * s.ny] = out[o * s.rows1 : (o + 1) * s.rows1]
    cells = []
    for j in range(s.cz[2]):
        out = None
        for b in range(s.gy):
            first = 0 if b == 0 or c2_refs[b].shape[0] == s.tiles2 * s.rows2 else base
            tile = lambda t, b=b, f=first: c2_refs[b][f + t * s.rows2 : f + (t + 1) * s.rows2]
            x = unpacked(tile, j, s.wide2, (b * s.y2 - 2) % LANES)
            out = x if out is None else out + x
        cells.append(out)
    yb = dot3(jnp.concatenate(cells, axis=0), y2h_ref[...], y2l_ref[...])
    for j in range(s.cz[2]):
        for q in range(2 * TERMS):
            yb_ref[q, j] = yb[j * s.rows2 : (j + 1) * s.rows2, q * s.ny : (q + 1) * s.ny]
    for o in range(s.planes):
        for q in range(2 * TERMS):
            x = yb_ref[q, 0] * z_ref[q * s.zrows + o, 0]
            for j in range(1, s.cz[2]):
                x += yb_ref[q, j] * z_ref[q * s.zrows + o, j]
            at = TERMS * s.rows1 + q * s.rows2
            d_ref[at : at + s.rows2, o * s.ny : (o + 1) * s.ny] = x


def across(s, d_ref, xh_ref, xl_ref, shift):
    rows = slice(shift * s.nx, (shift + 1) * s.nx)
    high, low = halves(d_ref[...])
    xh, xl = xh_ref[rows, : s.depth], xl_ref[rows, : s.depth]
    return dot(xh, high) + dot(xl, high) + dot(xh, low)


def away_kernel(s, d_ref, xh_ref, xl_ref, *g_refs):
    for shift, ref in enumerate(g_refs):
        ref[...] = across(s, d_ref, xh_ref, xl_ref, shift + 1)


def prolonged(s, level, z):
    m = z // 2 + 1
    if z % 2 == 0:
        return level[m]
    return NEAR * (level[m] + level[m + 1]) + FAR * (level[m - 1] + level[m + 2])


def home_kernel(s, d_ref, xh_ref, xl_ref, own_ref, low_ref, high_ref, out_ref):
    g = across(s, d_ref, xh_ref, xl_ref, 0)
    level = [g[:, o * s.ny : (o + 1) * s.ny] for o in range(s.planes)]
    for z in range(s.nz):
        x = prolonged(s, level, z) + own_ref[z]
        if z < R:
            x += low_ref[z]
        if z >= s.nz - R:
            x += high_ref[z - (s.nz - R)]
        out_ref[z] = x


def last_kernel(s, home_ref, *refs):
    g_refs, out_ref = refs[:-1], refs[-1]
    level = []
    for o in range(s.planes):
        columns = slice(o * s.ny, (o + 1) * s.ny)
        x = g_refs[0][:, columns]
        for ref in g_refs[1:]:
            x += ref[:, columns]
        level.append(x)
    for z in range(s.nz):
        out_ref[z] = home_ref[z] + prolonged(s, level, z)


def call(kernel, name, operands, out_shapes, scalars=(), after=(), through=(), scratch=(), flops=0):
    read, given = len(operands), len(out_shapes)
    operands = list(operands) + list(after) + list(through)
    first = len(operands) - len(through)
    out_shapes = list(out_shapes) + [jax.ShapeDtypeStruct(x.shape, x.dtype) for x in through]

    def spec(i):
        if i >= read:
            return pl.BlockSpec(memory_space=pl.ANY)
        return pl.BlockSpec(memory_space=pltpu.SMEM if i in scalars else pltpu.VMEM)

    moved = sum(x.size * x.dtype.itemsize for x in operands)
    moved += sum(int(np.prod(x.shape)) * x.dtype.itemsize for x in out_shapes)
    moved = moved if flops else 0
    return pl.pallas_call(
        kernel,
        name=name,
        out_shape=out_shapes,
        in_specs=[spec(i) for i in range(len(operands))],
        out_specs=[pl.BlockSpec(memory_space=pltpu.VMEM)] * given
        + [pl.BlockSpec(memory_space=pl.ANY)] * len(through),
        input_output_aliases={first + i: given + i for i in range(len(through))},
        scratch_shapes=list(scratch),
        compiler_params=pltpu.CompilerParams(vmem_limit_bytes=VMEM_LIMIT),
        cost_estimate=pl.CostEstimate(flops=flops, bytes_accessed=moved, transcendentals=0),
    )(*operands)


def arrays(*shapes, dtype=F32):
    return [jax.ShapeDtypeStruct(shape, dtype) for shape in shapes]


def fetch(x, **shifts):
    names = tuple(shifts)
    sizes = [lax.axis_size(n) for n in names]
    pairs = []
    for here in np.ndindex(*sizes):
        there = [(h + shifts[n]) % size for h, n, size in zip(here, names, sizes)]
        pairs.append((int(np.ravel_multi_index(there, sizes)), int(np.ravel_multi_index(here, sizes))))
    return lax.ppermute(x, names if len(names) > 1 else names[0], pairs)


def two(*shape):
    return arrays(shape, shape, dtype=BF16)


def shards(charges, widths, amplitudes):
    s = Sizes(*charges.shape, lax.axis_size("gz"), lax.axis_size("gx"), lax.axis_size("gy"))
    c = {k: jnp.asarray(v) for k, v in constants(s).items()}
    brick = (s.nz, s.nx, s.ny)
    side = (R, s.nx, s.ny)
    taps, x0 = call(
        functools.partial(tap_kernel, s), "taps", [widths, amplitudes],
        arrays((8, LANES)) + arrays((TERMS * s.nx, 3 * s.ext), dtype=BF16), flops=6 * 10**8,
    )
    high_rows = fetch(charges, gx=1)
    low_rows = high_rows if s.gx == 2 else fetch(charges, gx=-1)
    paired = s.gx == 2
    strip = (s.fine_tiles, 2 * s.nx if paired else s.ext, LANES)
    share, *cells = call(
        functools.partial(share_kernel, s), "share", [charges, low_rows, high_rows],
        arrays((s.tiles1, s.rows1, LANES), *[strip] * (1 if paired else 2)), after=[x0], flops=10**9,
    )
    if paired:
        pairs = []
        for y in range(s.gy):
            pairs.append((y, (y + 1) % s.gy))
            pairs.append((s.gy + y, s.gy + (y - 1) % s.gy))
        left = lax.ppermute(cells[0], ("gx", "gy"), pairs)
    else:
        left, right = fetch(cells[1], gy=-1), fetch(cells[0], gy=1)
    y0, left = call(
        functools.partial(along_matrix_kernel, s), "taps_y", [widths],
        arrays((2 * LANES, 2 * TERMS * s.ny), dtype=BF16), through=[left], flops=3 * 10**8,
    )
    if paired:
        right = fetch(left, gx=1)
    shares = [share] + [fetch(share, gz=b) for b in range(1, s.gz)]
    tiles = s.nz + 2 * s.fine_tiles
    halved = pltpu.VMEM((TERMS, s.nz * s.nx, 2 * LANES), BF16)
    near, near_down, near_up = call(
        functools.partial(near_kernel, s), "near",
        [taps, charges, low_rows, high_rows, left, right, x0, y0],
        arrays(brick, side, side), scalars=(0,),
        scratch=[
            pltpu.VMEM((3 * s.ext, tiles * LANES), BF16), pltpu.VMEM((TERMS * s.nx, tiles * LANES), F32),
            halved, halved, pltpu.VMEM((TERMS,) + brick, F32),
        ],
        flops=0,
    )
    base = s.tiles_s * s.rows1
    size2 = s.tiles2 * s.rows2
    waves, to_low, to_high, coarse = call(
        functools.partial(depth_kernel, s), "depth",
        [taps] + shares + [c["ry2"], c["rx2"]],
        arrays((TERMS * s.planes, s.rows1, LANES), (base + size2, LANES), (base + size2, LANES), (size2, LANES)),
        scalars=(0,), after=[near], scratch=[pltpu.VMEM((s.cz[1], s.rows1, LANES), F32)], flops=2 * 10**9,
    )
    named = ("px1", "px2", "px3", "px3l", "rx3", "py2", "py3", "py3l", "ry3", "pz2", "pz3", "rz3")
    z_taps, y1, y2h, y2l, xh, xl = call(
        functools.partial(matrix_kernel, s), "matrices",
        [widths, amplitudes] + [c[k] for k in named],
        arrays((2 * TERMS * s.zrows, LANES))
        + arrays((LANES, 2 * TERMS * s.ny), dtype=BF16)
        + two(s.cy[2], 2 * TERMS * s.ny) + two(s.cx[0], s.depth_lanes),
        after=[coarse], flops=2 * 10**9,
    )
    coarses = [coarse]
    for b in range(1, s.gy):
        coarses.append(fetch({1: to_low, s.gy - 1: to_high}.get(b, coarse), gy=b))
    near_low, near_high = fetch(near_up, gz=-1), fetch(near_down, gz=1)
    (terms,) = call(
        functools.partial(along_kernel, s), "along",
        [z_taps, waves] + coarses + [y1, y2h, y2l],
        arrays((s.depth, s.planes * s.ny)), scalars=(0,),
        scratch=[pltpu.VMEM((2 * TERMS, s.cz[2], s.rows2, s.ny), F32)], flops=3 * 10**9,
    )
    parts = call(
        functools.partial(away_kernel, s), "away", [terms, xh, xl],
        arrays(*[(s.nx, s.planes * s.ny)] * (s.gx - 1)), flops=10**9,
    )
    parts = [fetch(x, gx=-dx) for dx, x in enumerate(parts, 1)]
    (home,) = call(
        functools.partial(home_kernel, s), "home",
        [terms, xh, xl, near, near_low, near_high], arrays(brick), flops=2 * 10**9,
    )
    (out,) = call(
        functools.partial(last_kernel, s), "last", [home] + parts, arrays(brick), flops=10**9,
    )
    return out


def solution(mesh):
    placed = (P("gz", "gx", "gy"), P(), P())
    return jax.shard_map(
        shards, mesh=mesh, in_specs=placed, out_specs=P("gz", "gx", "gy"), check_vma=False
    )
```

```python
import functools

import jax
import jax.numpy as jnp
import ml_dtypes
import numpy as np
from jax import lax
from jax.experimental import pallas as pl
from jax.experimental.pallas import tpu as pltpu
from jax.sharding import PartitionSpec as P

R = 8
TERMS = 3
LANES = 128
NEAR = 9.0 / 16.0
FAR = -1.0 / 16.0
F32 = jnp.float32
BF16 = jnp.bfloat16
VMEM_LIMIT = 40 * 1024 * 1024


def up8(n):
    return -(-n // 8) * 8


class Sizes:
    def __init__(self, nz, nx, ny, gz, gx, gy):
        self.nz, self.nx, self.ny = nz, nx, ny
        self.gz, self.gx, self.gy = gz, gx, gy
        self.z1, self.x1, self.y1 = nz // 2, nx // 2, ny // 2
        self.z2, self.x2, self.y2 = nz // 4, nx // 4, ny // 4
        self.cz = [nz * gz >> l for l in range(4)]
        self.cx = [nx * gx >> l for l in range(4)]
        self.cy = [ny * gy >> l for l in range(4)]
        self.planes = self.z1 + 3
        self.zrows = up8(self.planes)
        self.rows1 = self.x1
        self.rows2 = up8(self.x2 + 3)
        self.wide1 = self.y1 + 3
        self.wide2 = self.y2 + 5
        self.tiles1 = -(-self.planes * self.wide1 // LANES)
        self.x3, self.y3 = nx // 8, ny // 8
        self.rows3 = up8(self.x3 + 5)
        self.wide3 = self.y3 + 5
        self.tiles3 = -(-self.cz[3] * self.wide3 // LANES)
        self.strip2 = R + 5
        self.per_tile2 = LANES // self.strip2
        self.tiles_s2 = -(-self.cz[2] // self.per_tile2)
        self.strip = R + 3
        self.per_tile = LANES // self.strip
        self.tiles_s = -(-TERMS * self.planes // self.per_tile)
        self.fine_tiles = -(-nz // (LANES // R))
        self.ext = nx + 2 * R
        self.depth = TERMS * (self.rows1 + self.rows2 + self.rows3)
        self.base2 = self.tiles_s * self.rows1
        self.base3 = self.base2 + self.tiles_s2 * self.rows2
        self.depth_lanes = -(-self.depth // LANES) * LANES


def restrict_circle(n):
    m = np.zeros((n // 2, n))
    for i in range(n // 2):
        for d, w in ((0, 1.0), (1, NEAR), (-1, NEAR), (3, FAR), (-3, FAR)):
            m[i, (2 * i + d) % n] += w
    return m


def prolong_circle(n):
    m = np.zeros((2 * n, n))
    for i in range(n):
        m[2 * i, i] += 1.0
        for d, w in ((0, NEAR), (1, NEAR), (-1, FAR), (2, FAR)):
            m[2 * i + 1, (i + d) % n] += w
    return m


def restrict_open(first_in, n_in, first_out, n_out):
    m = np.zeros((n_out, n_in))
    for i in range(n_out):
        for d, w in ((0, 1.0), (1, NEAR), (-1, NEAR), (3, FAR), (-3, FAR)):
            j = 2 * (first_out + i) + d - first_in
            if 0 <= j < n_in:
                m[i, j] = w
    return m


def padded(m, rows, columns):
    out = np.zeros((rows, columns), np.float32)
    out[: m.shape[0], : m.shape[1]] = m
    return out


def exact(m):
    out = m.astype(ml_dtypes.bfloat16)
    assert np.all(out.astype(np.float64) == m)
    return out


def constants(s):
    c = {}
    c["ry2"] = padded(restrict_open(-1, s.wide1, -2, s.wide2).T, LANES, LANES)
    c["rx2"] = padded(restrict_open(0, s.x1, -1, s.x2 + 3), s.rows2, s.rows1)

    def chain(n):
        p1 = prolong_circle(n[1])
        p2 = p1 @ prolong_circle(n[2])
        return p1, p2, p2 @ prolong_circle(n[3])

    def parts(name, m):
        m = m.astype(np.float32)
        c[name] = m.astype(ml_dtypes.bfloat16)
        c[name + "l"] = (m - c[name].astype(np.float32)).astype(ml_dtypes.bfloat16)

    x1, x2, x3 = chain(s.cx)
    c["px1"], c["px2"] = exact(x1), exact(x2)
    parts("px3", x3)
    _, y2, y3 = chain(s.cy)
    c["py2"] = exact(y2[: s.ny].T)
    parts("py3", y3[: s.ny].T)
    z2 = prolong_circle(s.cz[2])
    z3 = z2 @ prolong_circle(s.cz[3])
    own = [(o - 1) % s.cz[1] for o in range(s.planes)]
    c["pz2"] = exact(padded(z2[own], s.zrows, s.cz[2]))
    c["pz3"] = exact(padded(z3[own], s.zrows, s.cz[3]))
    c["ry3"] = padded(restrict_open(-2, s.wide2, -2, s.wide3).T, LANES, LANES)
    c["rx3"] = padded(restrict_open(-1, s.x2 + 3, -2, s.x3 + 5), s.rows3, s.rows2)
    return c


def halves(x):
    high = x.astype(BF16)
    return high, (x - high.astype(F32)).astype(BF16)


def dot(a, b):
    return jnp.dot(a, b, preferred_element_type=F32)


def dot2(a, b):
    high, low = halves(a)
    return dot(high, b) + dot(low, b)


def dot3(a, b_high, b_low):
    high, low = halves(a)
    return dot(high, b_high) + dot(low, b_high) + dot(high, b_low)


def lanes_of(shape):
    return lax.broadcasted_iota(jnp.int32, shape, len(shape) - 1)


def turn(x, by):
    by = by % x.shape[-1]
    return x if by == 0 else pltpu.roll(x, by, x.ndim - 1)


def packed(planes, wide, tiles):
    out = [None] * tiles

    def add(t, x):
        out[t] = x if out[t] is None else out[t] + x

    for k, x in enumerate(planes):
        t, at = divmod(k * wide, LANES)
        moved = turn(x, at)
        if at + wide <= LANES:
            add(t, moved)
        else:
            lane = lanes_of(x.shape)
            add(t, jnp.where(lane >= at, moved, 0.0))
            add(t + 1, jnp.where(lane < at, moved, 0.0))
    return out


def unpacked(tile, k, wide, shift):
    t, at = divmod(k * wide, LANES)
    x = tile(t)
    lane = lanes_of(x.shape)
    if at + wide > LANES:
        x = jnp.where(lane >= at, x, tile(t + 1))
    x = turn(x, shift - at)
    if shift + wide <= LANES:
        return jnp.where((lane >= shift) & (lane < shift + wide), x, 0.0)
    return jnp.where((lane >= shift) | (lane < shift + wide - LANES), x, 0.0)


def open_restriction(shape, in_dim, first_in, first_out, n_out):
    i = lax.broadcasted_iota(jnp.int32, shape, in_dim) + first_in
    o = lax.broadcasted_iota(jnp.int32, shape, 1 - in_dim)
    d = jnp.abs(i - 2 * (o + first_out))
    w = jnp.where(d == 0, 1.0, jnp.where(d == 1, NEAR, jnp.where(d == 3, FAR, 0.0)))
    return jnp.where(o < n_out, w, 0.0).astype(BF16)


def extended(s, b_ref, lo_ref, hi_ref, z):
    return jnp.concatenate([lo_ref[z, s.nx - R :], b_ref[z], hi_ref[z, 0:R]], axis=0)


def share_kernel(s, b_ref, lo_ref, hi_ref, _, m_ref, first_ref, last_ref):
    b = [extended(s, b_ref, lo_ref, hi_ref, z) for z in range(s.nz)]
    planes = []
    for k in range(-1, s.z1 + 2):
        out = None
        for d, w in ((0, 1.0), (1, NEAR), (-1, NEAR), (3, FAR), (-3, FAR)):
            if 0 <= 2 * k + d < s.nz:
                term = b[2 * k + d] if d == 0 else b[2 * k + d] * w
                out = term if out is None else out + term
        planes.append(out)
    high, low = halves(jnp.concatenate(planes, axis=0))
    ry1 = open_restriction((s.ny, LANES), 0, 0, -1, s.wide1)
    rx1 = open_restriction((s.rows1, s.ext), 1, -R, 0, s.x1)
    along = dot(high, ry1) + dot(low, ry1)
    shares = []
    for k in range(s.planes):
        high, low = halves(along[k * s.ext : (k + 1) * s.ext])
        shares.append(dot(rx1, high) + dot(rx1, low))
    for t, x in enumerate(packed(shares, s.wide1, s.tiles1)):
        m_ref[t] = x
    lane = lanes_of((s.ext, LANES))
    group = LANES // R
    for t in range(s.fine_tiles):
        first = last = jnp.zeros((s.ext, LANES), F32)
        for g in range(min(group, s.nz - t * group)):
            x = b[t * group + g]
            at = R * ((g + 1) % group)
            first = jnp.where((lane >= at) & (lane < at + R), turn(x, at), first)
            at = R * g
            last = jnp.where((lane >= at) & (lane < at + R), turn(x, at + R - s.ny), last)
        first_ref[t] = first
        last_ref[t] = last


def rows_of(shape):
    return lax.broadcasted_iota(jnp.int32, shape, 0)


def bell(c, d):
    d = jnp.abs(d)
    return jnp.where(d <= R, jnp.exp(c * d * d), 0.0)


def one(ref, level, t):
    return ref[level : level + 1, t : t + 1]


def spreads(w_ref, levels):
    out = []
    for l in levels:
        w = [one(w_ref, l, t) for t in range(TERMS)]
        out.append([-0.5 / (x * x) for x in w])
    return out


def units(coef, distance, valid):
    shape = (up8(len(coef)), LANES)
    row = rows_of(shape)
    column = jnp.zeros(shape, F32)
    for r, c in enumerate(coef):
        column = jnp.where(row == r, c, column)
    lane = lanes_of(shape)
    d = distance(row, lane).astype(F32)
    total = jnp.sum(jnp.where(valid(row, lane), jnp.exp(2.0 * column * d * d), 0.0), axis=1, keepdims=True)
    unit = 1.0 / jnp.sqrt(total)
    return [unit[r : r + 1] for r in range(len(coef))]


def near_units(coef):
    flat = [c for level in coef for c in level]
    out = units(flat, lambda row, lane: lane - R, lambda row, lane: lane <= 2 * R)
    return [out[i : i + TERMS] for i in range(0, len(out), TERMS)]


def tap_kernel(s, w_ref, a_ref, tap_ref, x0_ref, y0_ref):
    coef = spreads(w_ref, (0, 1))
    unit = near_units(coef)
    d = lanes_of((1, LANES)).astype(F32)
    for t in range(TERMS):
        tap_ref[t : t + 1] = bell(coef[0][t], d) * (unit[0][t] * one(a_ref, 0, t))
        tap_ref[TERMS + t : TERMS + t + 1] = bell(coef[1][t], d) * (unit[1][t] * one(a_ref, 1, t) * 0.25)
    shape = (s.nx, 3 * s.ext)
    lane = lanes_of(shape)
    part = jnp.where(lane < s.ext, 0, jnp.where(lane < 2 * s.ext, 1, 2))
    d = (lane - part * s.ext - R - rows_of(shape)).astype(F32)
    for t in range(TERMS):
        high, low = halves(bell(coef[0][t], d) * unit[0][t])
        x0_ref[t * s.nx : (t + 1) * s.nx] = jnp.where(part == 1, low.astype(F32), high.astype(F32)).astype(BF16)
    shape = (s.ny + 2 * R, s.ny)
    i = rows_of(shape)
    cell = jnp.where(i < s.ny, i, jnp.where(i < s.ny + R, i - s.ny - R, i - R))
    d = (cell - lanes_of(shape)).astype(F32)
    for t in range(TERMS):
        high, low = halves(bell(coef[0][t], d) * unit[0][t])
        at = 2 * t * s.ny
        y0_ref[s.ny + 2 * R :, at : at + 2 * s.ny] = jnp.zeros((2 * LANES - s.ny - 2 * R, 2 * s.ny), BF16)
        y0_ref[: s.ny + 2 * R, at : at + s.ny] = high
        y0_ref[: s.ny + 2 * R, at + s.ny : at + 2 * s.ny] = low


def matrix_kernel(s, w_ref, a_ref, px1, px2, px3, px3l, py2, py3, py3l, pz2, pz3, _,
                  z_ref, y1_ref, y2h_ref, y2l_ref, xh_ref, xl_ref):
    coef = spreads(w_ref, range(4))
    unit = near_units(coef[:3])
    sizes = [s.cx[3], s.cy[3], s.cz[3]]

    def per_row(row):
        return jnp.where(row < TERMS, sizes[0], jnp.where(row < 2 * TERMS, sizes[1], sizes[2]))

    top = units(
        coef[3] * 3,
        lambda row, lane: jnp.minimum(lane, per_row(row) - lane),
        lambda row, lane: lane < per_row(row),
    )
    top_x, top_y, top_z = top[:TERMS], top[TERMS : 2 * TERMS], top[2 * TERMS :]

    def circle(n, d, c, u):
        d = (d & (n - 1)).astype(F32)
        return (bell(c, d) + bell(c, n - d)) * u

    def full_circle(n, d, c, u):
        d = (d & (n - 1)).astype(F32)
        d = jnp.minimum(d, n - d)
        return jnp.exp(c * d * d) * u

    shape = (LANES, s.ny)
    fine = lanes_of(shape)
    d = (rows_of(shape) - (R + 1) - (fine >> 1)).astype(F32)
    even = (fine & 1) == 0
    known = rows_of(shape) < s.y1 + 3 + 2 * R
    two, three = (LANES, s.cy[2]), (LANES, s.cy[3])
    known2 = rows_of(two) < s.y2 + 5 + 2 * R
    known3 = rows_of(three) < (s.gy - 1) * s.y3 + s.wide3
    for t in range(TERMS):
        c = coef[1][t]
        here = bell(c, d)
        between = NEAR * (here + bell(c, d - 1.0)) + FAR * (bell(c, d + 1.0) + bell(c, d - 2.0))
        high, low = halves(jnp.where(known, jnp.where(even, here, between) * unit[1][t], 0.0))
        y1_ref[:, 2 * t * s.ny : (2 * t + 1) * s.ny] = high
        y1_ref[:, (2 * t + 1) * s.ny : (2 * t + 2) * s.ny] = low
        g = circle(s.cy[2], rows_of(two) - (R + 2) - lanes_of(two), coef[2][t], unit[2][t])
        high, low = halves(dot2(jnp.where(known2, g, 0.0), py2[...]))
        y2h_ref[:, t * s.ny : (t + 1) * s.ny] = high
        y2l_ref[:, t * s.ny : (t + 1) * s.ny] = low
        g = full_circle(s.cy[3], rows_of(three) - 2 - lanes_of(three), coef[3][t], top_y[t])
        high, low = halves(dot3(jnp.where(known3, g, 0.0), py3[...], py3l[...]))
        at = (TERMS + t) * s.ny
        y2h_ref[:, at : at + s.ny] = high
        y2l_ref[:, at : at + s.ny] = low

    def terms(level, first, rows, valid, shift, around, u):
        shape = (s.cx[level], s.depth_lanes)
        lane = lanes_of(shape) - first
        column = lane - jnp.where(lane < rows, 0, jnp.where(lane < 2 * rows, rows, 2 * rows))

        def by_term(v):
            return jnp.where(lane < rows, v[0], jnp.where(lane < 2 * rows, v[1], v[2]))

        g = around(s.cx[level], rows_of(shape) - column + shift, by_term(coef[level]), by_term(u))
        high, low = halves(jnp.where((lane >= 0) & (lane < TERMS * rows) & (column < valid), g, 0.0))
        return high, low

    high, low = terms(1, 0, s.rows1, s.rows1, 0, circle, unit[1])
    x = dot(px1[...], high) + dot(px1[...], low)
    high, low = terms(2, TERMS * s.rows1, s.rows2, s.x2 + 3, 1, circle, unit[2])
    x += dot(px2[...], high) + dot(px2[...], low)
    high, low = terms(3, TERMS * (s.rows1 + s.rows2), s.rows3, s.x3 + 5, 2, full_circle, top_x)
    x += dot(px3[...], high) + dot(px3l[...], high) + dot(px3[...], low)
    xh_ref[...], xl_ref[...] = halves(x)
    for t in range(TERMS):
        shape = (s.cz[2], LANES)
        g = circle(s.cz[2], rows_of(shape) - lanes_of(shape), coef[2][t], unit[2][t])
        high, low = halves(g * (one(a_ref, 2, t) * 0.0625))
        z_ref[t * s.zrows : (t + 1) * s.zrows] = dot(pz2[...], high) + dot(pz2[...], low)
        shape = (s.cz[3], LANES)
        g = full_circle(s.cz[3], rows_of(shape) - lanes_of(shape), coef[3][t], top_z[t])
        high, low = halves(g * (one(a_ref, 3, t) * 0.015625))
        z_ref[(TERMS + t) * s.zrows : (TERMS + t + 1) * s.zrows] = dot(pz3[...], high) + dot(pz3[...], low)


def near_kernel(s, tap_ref, b_ref, lo_ref, hi_ref, left_ref, right_ref, x0_ref, y0_ref,
                own_ref, down_ref, up_ref, e_ref, u_ref, eh_ref, el_ref, v_ref):
    group = LANES // R
    tiles = [extended(s, b_ref, lo_ref, hi_ref, z) for z in range(s.nz)]
    tiles += [left_ref[t] for t in range(s.fine_tiles)] + [right_ref[t] for t in range(s.fine_tiles)]
    for i, x in enumerate(tiles):
        high, low = halves(x)
        columns = slice(i * LANES, (i + 1) * LANES)
        e_ref[0 : s.ext, columns] = high
        e_ref[s.ext : 2 * s.ext, columns] = high
        e_ref[2 * s.ext :, columns] = low
    x0 = x0_ref[...]
    for at in range(0, len(tiles) * LANES, 2 * LANES):
        columns = slice(at, min(at + 2 * LANES, len(tiles) * LANES))
        u_ref[:, columns] = dot(x0, e_ref[:, columns])
    lane = lanes_of((TERMS * s.nx, LANES))
    for z in range(s.nz):
        t, g = divmod(z, group)
        left = u_ref[:, (s.nz + t) * LANES : (s.nz + t + 1) * LANES]
        right = u_ref[:, (s.nz + s.fine_tiles + t) * LANES : (s.nz + s.fine_tiles + t + 1) * LANES]
        strips = turn(jnp.where((lane >= R * g) & (lane < R * g + R), left, right), -R * g)
        for at, x in ((0, u_ref[:, z * LANES : (z + 1) * LANES]), (LANES, strips)):
            high, low = halves(x)
            for t in range(TERMS):
                rows = slice(t * s.nx, (t + 1) * s.nx)
                eh_ref[t, z * s.nx : (z + 1) * s.nx, at : at + LANES] = high[rows]
                el_ref[t, z * s.nx : (z + 1) * s.nx, at : at + LANES] = low[rows]
    step = 4 * s.nx
    for t in range(TERMS):
        at = 2 * t * s.ny
        y0, y0h = y0_ref[:, at : at + 2 * s.ny], y0_ref[:, at : at + s.ny]
        for first in range(0, s.nz * s.nx, step):
            both = dot(eh_ref[t, first : first + step], y0)
            v = both[:, : s.ny] + both[:, s.ny :] + dot(el_ref[t, first : first + step], y0h)
            for q in range(step // s.nx):
                v_ref[t, first // s.nx + q] = v[q * s.nx : (q + 1) * s.nx]

    def depth(r, _):
        rows = pl.ds(pl.multiple_of(r * 8, 8), 8)
        taps = [[tap_ref[t, d] for d in range(R + 1)] for t in range(TERMS)]
        for first in range(-R, s.nz + R, R):
            acc = [None] * R
            for t in range(TERMS):
                for z in range(max(0, first - R), min(s.nz, first + 2 * R)):
                    v = v_ref[t, z, rows]
                    for o in range(R):
                        d = abs(first + o - z)
                        if d <= R:
                            term = v * taps[t][d]
                            acc[o] = term if acc[o] is None else acc[o] + term
            for o in range(R):
                if first < 0:
                    down_ref[o, rows] = acc[o]
                elif first >= s.nz:
                    up_ref[o, rows] = acc[o]
                else:
                    own_ref[first + o, rows] = acc[o]
        return 0

    lax.fori_loop(0, s.nx // 8, depth, 0)


def depth_kernel(s, tap_ref, *refs):
    m_refs = refs[: s.gz]
    ry2_ref, rx2_ref, ry3_ref, rx3_ref, _, w_ref, down_ref, up_ref, c2_ref, c3_ref, c_ref = refs[s.gz :]
    n = s.cz[1]
    parts = [[] for _ in range(n)]
    for b in range(s.gz):
        for k in range(s.planes):
            parts[(b * s.z1 + k - 1) % n].append((b, k))
    for z in range(n):
        out = None
        for b, k in parts[z]:
            x = unpacked(lambda t, b=b: m_refs[b][t], k, s.wide1, 0)
            out = x if out is None else out + x
        c_ref[z] = out
    lane = lanes_of((s.rows1, LANES))
    down = [jnp.zeros((s.rows1, LANES), F32)] * s.tiles_s
    up = list(down)
    for o in range(s.planes):
        sums = [c_ref[(o - 1) % n]]
        sums += [c_ref[(o - 1 + d) % n] + c_ref[(o - 1 - d) % n] for d in range(1, R + 1)]
        for t in range(TERMS):
            x = sums[0] * tap_ref[TERMS + t, 0]
            for d in range(1, R + 1):
                x += sums[d] * tap_ref[TERMS + t, d]
            k = t * s.planes + o
            w_ref[k] = x
            tile, slot = divmod(k, s.per_tile)
            at = slot * s.strip
            here = (lane >= at) & (lane < at + s.strip)
            down[tile] = jnp.where(here, turn(x, at), down[tile])
            up[tile] = jnp.where(here, turn(x, at - (s.wide1 - s.strip)), up[tile])

    def restricted(planes, y_ref, x_ref):
        n, rows = len(planes), planes[0].shape[0]
        coarse = []
        for j in range(n // 2):
            at = lambda d: planes[(2 * j + d) % n]
            coarse.append(at(0) + NEAR * (at(1) + at(-1)) + FAR * (at(3) + at(-3)))
        along = dot2(jnp.concatenate(coarse, axis=0), y_ref[...].astype(BF16))
        x = x_ref[...].astype(BF16)
        out = []
        for j in range(n // 2):
            high, low = halves(along[j * rows : (j + 1) * rows])
            out.append(dot(x, high) + dot(x, low))
        return out

    level2 = restricted([c_ref[z] for z in range(n)], ry2_ref, rx2_ref)
    level3 = restricted(level2, ry3_ref, rx3_ref)
    for t in range(s.tiles_s):
        down_ref[t * s.rows1 : (t + 1) * s.rows1] = down[t]
        up_ref[t * s.rows1 : (t + 1) * s.rows1] = up[t]
    lane = lanes_of((s.rows2, LANES))
    down = [jnp.zeros((s.rows2, LANES), F32)] * s.tiles_s2
    up = list(down)
    for j, x in enumerate(level2):
        c2_ref[j] = x
        tile, slot = divmod(j, s.per_tile2)
        at = slot * s.strip2
        here = (lane >= at) & (lane < at + s.strip2)
        down[tile] = jnp.where(here, turn(x, at), down[tile])
        up[tile] = jnp.where(here, turn(x, at - (s.wide2 - s.strip2)), up[tile])
    for t in range(s.tiles_s2):
        rows = slice(s.base2 + t * s.rows2, s.base2 + (t + 1) * s.rows2)
        down_ref[rows] = down[t]
        up_ref[rows] = up[t]
    for t, x in enumerate(packed(level3, s.wide3, s.tiles3)):
        c3_ref[t * s.rows3 : (t + 1) * s.rows3] = x
        for ref in (down_ref, up_ref):
            ref[s.base3 + t * s.rows3 : s.base3 + (t + 1) * s.rows3] = x


def along_kernel(s, z_ref, w_ref, c2_ref, *refs):
    c3_refs = refs[: s.gy]
    y1_ref, y2h_ref, y2l_ref, d_ref, y2_ref, y3_ref = refs[s.gy :]
    lane = lanes_of((s.rows1, LANES))
    above, below = c3_refs[1], c3_refs[-1]
    end = s.y1 + R
    for t in range(TERMS):
        cells = []
        for o in range(s.planes):
            k = t * s.planes + o
            tile, slot = divmod(k, s.per_tile)
            rows = slice(tile * s.rows1, (tile + 1) * s.rows1)
            at = slot * s.strip
            x = turn(w_ref[k], R)
            x += jnp.where(lane < s.strip, turn(below[rows], -at), 0.0)
            x += jnp.where((lane >= end) & (lane < end + s.strip), turn(above[rows], end - at), 0.0)
            cells.append(x)
        high, low = halves(jnp.concatenate(cells, axis=0))
        at = 2 * t * s.ny
        both = dot(high, y1_ref[:, at : at + 2 * s.ny])
        out = both[:, : s.ny] + both[:, s.ny :] + dot(low, y1_ref[:, at : at + s.ny])
        for o in range(s.planes):
            d_ref[t * s.rows1 : (t + 1) * s.rows1, o * s.ny : (o + 1) * s.ny] = out[o * s.rows1 : (o + 1) * s.rows1]
    lane = lanes_of((s.rows2, LANES))
    end = s.y2 + R
    cells = []
    for j in range(s.cz[2]):
        tile, slot = divmod(j, s.per_tile2)
        rows = slice(s.base2 + tile * s.rows2, s.base2 + (tile + 1) * s.rows2)
        at = slot * s.strip2
        x = turn(c2_ref[j], R)
        x += jnp.where(lane < s.strip2, turn(below[rows], -at), 0.0)
        x += jnp.where((lane >= end) & (lane < end + s.strip2), turn(above[rows], end - at), 0.0)
        cells.append(x)
    cells3 = []
    for j in range(s.cz[3]):
        out = None
        for b in range(s.gy):
            first = s.base3 if c3_refs[b].shape[0] > s.tiles3 * s.rows3 else 0
            tile = lambda t, b=b, f=first: c3_refs[b][f + t * s.rows3 : f + (t + 1) * s.rows3]
            x = unpacked(tile, j, s.wide3, b * s.y3)
            out = x if out is None else out + x
        cells3.append(out)
    at = TERMS * s.rows1
    for q, (x, rows, ref) in enumerate(((cells, s.rows2, y2_ref), (cells3, s.rows3, y3_ref))):
        columns = slice(q * TERMS * s.ny, (q + 1) * TERMS * s.ny)
        y = dot3(jnp.concatenate(x, axis=0), y2h_ref[:, columns], y2l_ref[:, columns])
        for t in range(TERMS):
            for j in range(len(x)):
                ref[t, j] = y[j * rows : (j + 1) * rows, t * s.ny : (t + 1) * s.ny]
        for o in range(s.planes):
            for t in range(TERMS):
                scale = [z_ref[(q * TERMS + t) * s.zrows + o, j] for j in range(len(x))]
                out = ref[t, 0] * scale[0]
                for j in range(1, len(x)):
                    out += ref[t, j] * scale[j]
                d_ref[at + t * rows : at + (t + 1) * rows, o * s.ny : (o + 1) * s.ny] = out
        at += TERMS * rows


def across(s, d_ref, xh_ref, xl_ref, shift):
    rows = slice(shift * s.nx, (shift + 1) * s.nx)
    high, low = halves(d_ref[...])
    xh, xl = xh_ref[rows, : s.depth], xl_ref[rows, : s.depth]
    return dot(xh, high) + dot(xl, high) + dot(xh, low)


def away_kernel(s, d_ref, xh_ref, xl_ref, *g_refs):
    for shift, ref in enumerate(g_refs):
        ref[...] = across(s, d_ref, xh_ref, xl_ref, shift + 1)


def prolonged(s, level, z):
    m = z // 2 + 1
    if z % 2 == 0:
        return level[m]
    return NEAR * (level[m] + level[m + 1]) + FAR * (level[m - 1] + level[m + 2])


def home_kernel(s, d_ref, xh_ref, xl_ref, own_ref, low_ref, high_ref, out_ref):
    g = across(s, d_ref, xh_ref, xl_ref, 0)
    level = [g[:, o * s.ny : (o + 1) * s.ny] for o in range(s.planes)]
    for z in range(s.nz):
        x = prolonged(s, level, z) + own_ref[z]
        if z < R:
            x += low_ref[z]
        if z >= s.nz - R:
            x += high_ref[z - (s.nz - R)]
        out_ref[z] = x


def last_kernel(s, home_ref, *refs):
    g_refs, out_ref = refs[:-1], refs[-1]
    level = []
    for o in range(s.planes):
        columns = slice(o * s.ny, (o + 1) * s.ny)
        x = g_refs[0][:, columns]
        for ref in g_refs[1:]:
            x += ref[:, columns]
        level.append(x)
    for z in range(s.nz):
        out_ref[z] = home_ref[z] + prolonged(s, level, z)


def call(kernel, name, operands, out_shapes, scalars=(), after=(), scratch=(), flops=0):
    operands = list(operands) + list(after)

    def spec(i):
        if i >= len(operands) - len(after):
            return pl.BlockSpec(memory_space=pl.ANY)
        return pl.BlockSpec(memory_space=pltpu.SMEM if i in scalars else pltpu.VMEM)

    moved = sum(x.size * x.dtype.itemsize for x in operands)
    moved += sum(int(np.prod(x.shape)) * x.dtype.itemsize for x in out_shapes)
    return pl.pallas_call(
        kernel,
        name=name,
        out_shape=out_shapes,
        in_specs=[spec(i) for i in range(len(operands))],
        out_specs=[pl.BlockSpec(memory_space=pltpu.VMEM)] * len(out_shapes),
        scratch_shapes=list(scratch),
        compiler_params=pltpu.CompilerParams(vmem_limit_bytes=VMEM_LIMIT),
        cost_estimate=pl.CostEstimate(flops=flops, bytes_accessed=moved, transcendentals=0),
    )(*operands)


def arrays(*shapes, dtype=F32):
    return [jax.ShapeDtypeStruct(shape, dtype) for shape in shapes]


def fetch(x, **shifts):
    names = tuple(shifts)
    sizes = [lax.axis_size(n) for n in names]
    pairs = []
    for here in np.ndindex(*sizes):
        there = [(h + shifts[n]) % size for h, n, size in zip(here, names, sizes)]
        pairs.append((int(np.ravel_multi_index(there, sizes)), int(np.ravel_multi_index(here, sizes))))
    return lax.ppermute(x, names if len(names) > 1 else names[0], pairs)


def two(*shape):
    return arrays(shape, shape, dtype=BF16)


def shards(charges, widths, amplitudes):
    s = Sizes(*charges.shape, lax.axis_size("gz"), lax.axis_size("gx"), lax.axis_size("gy"))
    c = {k: jnp.asarray(v) for k, v in constants(s).items()}
    brick = (s.nz, s.nx, s.ny)
    side = (R, s.nx, s.ny)
    taps, x0, y0 = call(
        functools.partial(tap_kernel, s), "taps", [widths, amplitudes],
        arrays((8, LANES))
        + arrays((TERMS * s.nx, 3 * s.ext), (2 * LANES, 2 * TERMS * s.ny), dtype=BF16),
        flops=6 * 10**8,
    )
    high_rows = fetch(charges, gx=1)
    low_rows = high_rows if s.gx == 2 else fetch(charges, gx=-1)
    strips = (s.fine_tiles, s.ext, LANES)
    share, first_cells, last_cells = call(
        functools.partial(share_kernel, s), "share", [charges, low_rows, high_rows],
        arrays((s.tiles1, s.rows1, LANES), strips, strips), after=[x0], flops=10**9,
    )
    shares = [share] + [fetch(share, gz=b) for b in range(1, s.gz)]
    left, right = fetch(last_cells, gy=-1), fetch(first_cells, gy=1)
    tiles = s.nz + 2 * s.fine_tiles
    halved = pltpu.VMEM((TERMS, s.nz * s.nx, 2 * LANES), BF16)
    near, near_down, near_up = call(
        functools.partial(near_kernel, s), "near",
        [taps, charges, low_rows, high_rows, left, right, x0, y0],
        arrays(brick, side, side), scalars=(0,),
        scratch=[
            pltpu.VMEM((3 * s.ext, tiles * LANES), BF16), pltpu.VMEM((TERMS * s.nx, tiles * LANES), F32),
            halved, halved, pltpu.VMEM((TERMS,) + brick, F32),
        ],
        flops=5 * 10**9,
    )
    size3 = s.tiles3 * s.rows3
    message = (s.base3 + size3, LANES)
    waves, to_low, to_high, level2, coarse = call(
        functools.partial(depth_kernel, s), "depth",
        [taps] + shares + [c[k] for k in ("ry2", "rx2", "ry3", "rx3")],
        arrays((TERMS * s.planes, s.rows1, LANES), message, message, (s.cz[2], s.rows2, LANES), (size3, LANES)),
        scalars=(0,), after=[near], scratch=[pltpu.VMEM((s.cz[1], s.rows1, LANES), F32)], flops=2 * 10**9,
    )
    named = ("px1", "px2", "px3", "px3l", "py2", "py3", "py3l", "pz2", "pz3")
    z_taps, y1, y2h, y2l, xh, xl = call(
        functools.partial(matrix_kernel, s), "matrices",
        [widths, amplitudes] + [c[k] for k in named],
        arrays((2 * TERMS * s.zrows, LANES))
        + arrays((LANES, 2 * TERMS * s.ny), dtype=BF16)
        + two(LANES, 2 * TERMS * s.ny) + two(s.cx[0], s.depth_lanes),
        after=[coarse], flops=2 * 10**9,
    )
    coarses = [coarse]
    for b in range(1, s.gy):
        coarses.append(fetch({1: to_low, s.gy - 1: to_high}.get(b, coarse), gy=b))
    near_low, near_high = fetch(near_up, gz=-1), fetch(near_down, gz=1)
    (terms,) = call(
        functools.partial(along_kernel, s), "along",
        [z_taps, waves, level2] + coarses + [y1, y2h, y2l],
        arrays((s.depth, s.planes * s.ny)), scalars=(0,),
        scratch=[
            pltpu.VMEM((TERMS, s.cz[2], s.rows2, s.ny), F32), pltpu.VMEM((TERMS, s.cz[3], s.rows3, s.ny), F32)
        ], flops=3 * 10**9,
    )
    parts = call(
        functools.partial(away_kernel, s), "away", [terms, xh, xl],
        arrays(*[(s.nx, s.planes * s.ny)] * (s.gx - 1)), flops=10**9,
    )
    parts = [fetch(x, gx=-dx) for dx, x in enumerate(parts, 1)]
    (home,) = call(
        functools.partial(home_kernel, s), "home",
        [terms, xh, xl, near, near_low, near_high], arrays(brick), flops=2 * 10**9,
    )
    (out,) = call(
        functools.partial(last_kernel, s), "last", [home] + parts, arrays(brick), flops=10**9,
    )
    return out


def solution(mesh):
    placed = (P("gz", "gx", "gy"), P(), P())
    return jax.shard_map(
        shards, mesh=mesh, in_specs=placed, out_specs=P("gz", "gx", "gy"), check_vma=False
    )
```

```python
import functools

import jax
import jax.numpy as jnp
import ml_dtypes
import numpy as np
from jax import lax
from jax.experimental import pallas as pl
from jax.experimental.pallas import tpu as pltpu
from jax.sharding import PartitionSpec as P

R = 8
TERMS = 3
LANES = 128
NEAR = 9.0 / 16.0
FAR = -1.0 / 16.0
F32 = jnp.float32
BF16 = jnp.bfloat16
VMEM_LIMIT = 40 * 1024 * 1024


def up8(n):
    return -(-n // 8) * 8


class Sizes:
    def __init__(self, nz, nx, ny, gz, gx, gy):
        self.nz, self.nx, self.ny = nz, nx, ny
        self.gz, self.gx, self.gy = gz, gx, gy
        self.z1, self.x1, self.y1 = nz // 2, nx // 2, ny // 2
        self.z2, self.x2, self.y2 = nz // 4, nx // 4, ny // 4
        self.cz = [nz * gz >> l for l in range(4)]
        self.cx = [nx * gx >> l for l in range(4)]
        self.cy = [ny * gy >> l for l in range(4)]
        self.planes = self.z1 + 3
        self.zrows = up8(self.planes)
        self.rows1 = self.x1
        self.rows2 = up8(self.x2 + 3)
        self.wide1 = self.y1 + 3
        self.wide2 = self.y2 + 5
        self.tiles1 = -(-self.planes * self.wide1 // LANES)
        self.x3, self.y3 = nx // 8, ny // 8
        self.rows3 = up8(self.x3 + 5)
        self.wide3 = self.y3 + 5
        self.tiles3 = -(-self.cz[3] * self.wide3 // LANES)
        self.strip2 = R + 5
        self.per_tile2 = LANES // self.strip2
        self.tiles_s2 = -(-self.cz[2] // self.per_tile2)
        self.strip = R + 3
        self.per_tile = LANES // self.strip
        self.tiles_s = -(-TERMS * self.planes // self.per_tile)
        self.fine_tiles = -(-nz // (LANES // R))
        self.ext = nx + 2 * R
        self.depth = TERMS * (self.rows1 + self.rows2 + self.rows3)
        self.base2 = self.tiles_s * self.rows1
        self.base3 = self.base2 + self.tiles_s2 * self.rows2
        self.depth_lanes = -(-self.depth // LANES) * LANES


def restrict_circle(n):
    m = np.zeros((n // 2, n))
    for i in range(n // 2):
        for d, w in ((0, 1.0), (1, NEAR), (-1, NEAR), (3, FAR), (-3, FAR)):
            m[i, (2 * i + d) % n] += w
    return m


def prolong_circle(n):
    m = np.zeros((2 * n, n))
    for i in range(n):
        m[2 * i, i] += 1.0
        for d, w in ((0, NEAR), (1, NEAR), (-1, FAR), (2, FAR)):
            m[2 * i + 1, (i + d) % n] += w
    return m


def restrict_open(first_in, n_in, first_out, n_out):
    m = np.zeros((n_out, n_in))
    for i in range(n_out):
        for d, w in ((0, 1.0), (1, NEAR), (-1, NEAR), (3, FAR), (-3, FAR)):
            j = 2 * (first_out + i) + d - first_in
            if 0 <= j < n_in:
                m[i, j] = w
    return m


def padded(m, rows, columns):
    out = np.zeros((rows, columns), np.float32)
    out[: m.shape[0], : m.shape[1]] = m
    return out


def exact(m):
    out = m.astype(ml_dtypes.bfloat16)
    assert np.all(out.astype(np.float64) == m)
    return out


def constants(s):
    c = {}
    c["ry2"] = padded(restrict_open(-1, s.wide1, -2, s.wide2).T, LANES, LANES)
    c["rx2"] = padded(restrict_open(0, s.x1, -1, s.x2 + 3), s.rows2, s.rows1)

    def chain(n):
        p1 = prolong_circle(n[1])
        p2 = p1 @ prolong_circle(n[2])
        return p1, p2, p2 @ prolong_circle(n[3])

    def parts(name, m):
        m = m.astype(np.float32)
        c[name] = m.astype(ml_dtypes.bfloat16)
        c[name + "l"] = (m - c[name].astype(np.float32)).astype(ml_dtypes.bfloat16)

    x1, x2, x3 = chain(s.cx)
    c["px1"], c["px2"] = exact(x1), exact(x2)
    parts("px3", x3)
    _, y2, y3 = chain(s.cy)
    c["py2"] = exact(y2[: s.ny].T)
    parts("py3", y3[: s.ny].T)
    z2 = prolong_circle(s.cz[2])
    z3 = z2 @ prolong_circle(s.cz[3])
    own = [(o - 1) % s.cz[1] for o in range(s.planes)]
    c["pz2"] = exact(padded(z2[own], s.zrows, s.cz[2]))
    c["pz3"] = exact(padded(z3[own], s.zrows, s.cz[3]))
    c["ry3"] = padded(restrict_open(-2, s.wide2, -2, s.wide3).T, LANES, LANES)
    c["rx3"] = padded(restrict_open(-1, s.x2 + 3, -2, s.x3 + 5), s.rows3, s.rows2)
    return c


def halves(x):
    high = x.astype(BF16)
    return high, (x - high.astype(F32)).astype(BF16)


def dot(a, b):
    return jnp.dot(a, b, preferred_element_type=F32)


def dot2(a, b):
    high, low = halves(a)
    return dot(high, b) + dot(low, b)


def dot3(a, b_high, b_low):
    high, low = halves(a)
    return dot(high, b_high) + dot(low, b_high) + dot(high, b_low)


def lanes_of(shape):
    return lax.broadcasted_iota(jnp.int32, shape, len(shape) - 1)


def turn(x, by):
    by = by % x.shape[-1]
    return x if by == 0 else pltpu.roll(x, by, x.ndim - 1)


def packed(planes, wide, tiles):
    out = [None] * tiles

    def add(t, x):
        out[t] = x if out[t] is None else out[t] + x

    for k, x in enumerate(planes):
        t, at = divmod(k * wide, LANES)
        moved = turn(x, at)
        if at + wide <= LANES:
            add(t, moved)
        else:
            lane = lanes_of(x.shape)
            add(t, jnp.where(lane >= at, moved, 0.0))
            add(t + 1, jnp.where(lane < at, moved, 0.0))
    return out


def unpacked(tile, k, wide, shift):
    t, at = divmod(k * wide, LANES)
    x = tile(t)
    lane = lanes_of(x.shape)
    if at + wide > LANES:
        x = jnp.where(lane >= at, x, tile(t + 1))
    x = turn(x, shift - at)
    if shift + wide <= LANES:
        return jnp.where((lane >= shift) & (lane < shift + wide), x, 0.0)
    return jnp.where((lane >= shift) | (lane < shift + wide - LANES), x, 0.0)


def open_restriction(shape, in_dim, first_in, first_out, n_out):
    i = lax.broadcasted_iota(jnp.int32, shape, in_dim) + first_in
    o = lax.broadcasted_iota(jnp.int32, shape, 1 - in_dim)
    d = jnp.abs(i - 2 * (o + first_out))
    w = jnp.where(d == 0, 1.0, jnp.where(d == 1, NEAR, jnp.where(d == 3, FAR, 0.0)))
    return jnp.where(o < n_out, w, 0.0).astype(BF16)


def extended(s, b_ref, lo_ref, hi_ref, z):
    return jnp.concatenate([lo_ref[z, s.nx - R :], b_ref[z], hi_ref[z, 0:R]], axis=0)


def share_kernel(s, b_ref, lo_ref, hi_ref, _, m_ref, first_ref, last_ref):
    b = [extended(s, b_ref, lo_ref, hi_ref, z) for z in range(s.nz)]
    planes = []
    for k in range(-1, s.z1 + 2):
        out = None
        for d, w in ((0, 1.0), (1, NEAR), (-1, NEAR), (3, FAR), (-3, FAR)):
            if 0 <= 2 * k + d < s.nz:
                term = b[2 * k + d] if d == 0 else b[2 * k + d] * w
                out = term if out is None else out + term
        planes.append(out)
    high, low = halves(jnp.concatenate(planes, axis=0))
    ry1 = open_restriction((s.ny, LANES), 0, 0, -1, s.wide1)
    rx1 = open_restriction((s.rows1, s.ext), 1, -R, 0, s.x1)
    along = dot(high, ry1) + dot(low, ry1)
    shares = []
    for k in range(s.planes):
        high, low = halves(along[k * s.ext : (k + 1) * s.ext])
        shares.append(dot(rx1, high) + dot(rx1, low))
    for t, x in enumerate(packed(shares, s.wide1, s.tiles1)):
        m_ref[t] = x
    lane = lanes_of((s.ext, LANES))
    group = LANES // R
    for t in range(s.fine_tiles):
        first = last = jnp.zeros((s.ext, LANES), F32)
        for g in range(min(group, s.nz - t * group)):
            x = b[t * group + g]
            at = R * ((g + 1) % group)
            first = jnp.where((lane >= at) & (lane < at + R), turn(x, at), first)
            at = R * g
            last = jnp.where((lane >= at) & (lane < at + R), turn(x, at + R - s.ny), last)
        first_ref[t] = first
        last_ref[t] = last


def rows_of(shape):
    return lax.broadcasted_iota(jnp.int32, shape, 0)


def bell(c, d):
    d = jnp.abs(d)
    return jnp.where(d <= R, jnp.exp(c * d * d), 0.0)


def one(ref, level, t):
    return ref[level : level + 1, t : t + 1]


def spreads(w_ref, levels):
    out = []
    for l in levels:
        w = [one(w_ref, l, t) for t in range(TERMS)]
        out.append([-0.5 / (x * x) for x in w])
    return out


def units(coef, distance, valid):
    shape = (up8(len(coef)), LANES)
    row = rows_of(shape)
    column = jnp.zeros(shape, F32)
    for r, c in enumerate(coef):
        column = jnp.where(row == r, c, column)
    lane = lanes_of(shape)
    d = distance(row, lane).astype(F32)
    total = jnp.sum(jnp.where(valid(row, lane), jnp.exp(2.0 * column * d * d), 0.0), axis=1, keepdims=True)
    unit = 1.0 / jnp.sqrt(total)
    return [unit[r : r + 1] for r in range(len(coef))]


def near_units(coef):
    flat = [c for level in coef for c in level]
    out = units(flat, lambda row, lane: lane - R, lambda row, lane: lane <= 2 * R)
    return [out[i : i + TERMS] for i in range(0, len(out), TERMS)]


def tap_kernel(s, w_ref, a_ref, tap_ref, x0_ref, y0_ref):
    coef = spreads(w_ref, (0, 1))
    unit = near_units(coef)
    d = lanes_of((1, LANES)).astype(F32)
    for t in range(TERMS):
        tap_ref[t : t + 1] = bell(coef[0][t], d) * (unit[0][t] * one(a_ref, 0, t))
        tap_ref[TERMS + t : TERMS + t + 1] = bell(coef[1][t], d) * (unit[1][t] * one(a_ref, 1, t) * 0.25)
    shape = (s.nx, 3 * s.ext)
    lane = lanes_of(shape)
    part = jnp.where(lane < s.ext, 0, jnp.where(lane < 2 * s.ext, 1, 2))
    d = (lane - part * s.ext - R - rows_of(shape)).astype(F32)
    for t in range(TERMS):
        high, low = halves(bell(coef[0][t], d) * unit[0][t])
        x0_ref[t * s.nx : (t + 1) * s.nx] = jnp.where(part == 1, low.astype(F32), high.astype(F32)).astype(BF16)
    shape = (s.ny + 2 * R, s.ny)
    i = rows_of(shape)
    cell = jnp.where(i < s.ny, i, jnp.where(i < s.ny + R, i - s.ny - R, i - R))
    d = (cell - lanes_of(shape)).astype(F32)
    for t in range(TERMS):
        high, low = halves(bell(coef[0][t], d) * unit[0][t])
        at = 2 * t * s.ny
        y0_ref[s.ny + 2 * R :, at : at + 2 * s.ny] = jnp.zeros((2 * LANES - s.ny - 2 * R, 2 * s.ny), BF16)
        y0_ref[: s.ny + 2 * R, at : at + s.ny] = high
        y0_ref[: s.ny + 2 * R, at + s.ny : at + 2 * s.ny] = low


def matrix_kernel(s, w_ref, a_ref, px1, px2, px3, px3l, py2, py3, py3l, pz2, pz3, _,
                  z_ref, y1_ref, y2h_ref, y2l_ref, xh_ref, xl_ref):
    coef = spreads(w_ref, range(4))
    unit = near_units(coef[:3])
    sizes = [s.cx[3], s.cy[3], s.cz[3]]

    def per_row(row):
        return jnp.where(row < TERMS, sizes[0], jnp.where(row < 2 * TERMS, sizes[1], sizes[2]))

    top = units(
        coef[3] * 3,
        lambda row, lane: jnp.minimum(lane, per_row(row) - lane),
        lambda row, lane: lane < per_row(row),
    )
    top_x, top_y, top_z = top[:TERMS], top[TERMS : 2 * TERMS], top[2 * TERMS :]

    def circle(n, d, c, u):
        d = (d & (n - 1)).astype(F32)
        return (bell(c, d) + bell(c, n - d)) * u

    def full_circle(n, d, c, u):
        d = (d & (n - 1)).astype(F32)
        d = jnp.minimum(d, n - d)
        return jnp.exp(c * d * d) * u

    shape = (LANES, s.ny)
    fine = lanes_of(shape)
    d = (rows_of(shape) - (R + 1) - (fine >> 1)).astype(F32)
    even = (fine & 1) == 0
    known = rows_of(shape) < s.y1 + 3 + 2 * R
    two, three = (LANES, s.cy[2]), (LANES, s.cy[3])
    known2 = rows_of(two) < s.y2 + 5 + 2 * R
    known3 = rows_of(three) < (s.gy - 1) * s.y3 + s.wide3
    for t in range(TERMS):
        c = coef[1][t]
        here = bell(c, d)
        between = NEAR * (here + bell(c, d - 1.0)) + FAR * (bell(c, d + 1.0) + bell(c, d - 2.0))
        high, low = halves(jnp.where(known, jnp.where(even, here, between) * unit[1][t], 0.0))
        y1_ref[:, 2 * t * s.ny : (2 * t + 1) * s.ny] = high
        y1_ref[:, (2 * t + 1) * s.ny : (2 * t + 2) * s.ny] = low
        g = circle(s.cy[2], rows_of(two) - (R + 2) - lanes_of(two), coef[2][t], unit[2][t])
        high, low = halves(dot2(jnp.where(known2, g, 0.0), py2[...]))
        y2h_ref[:, t * s.ny : (t + 1) * s.ny] = high
        y2l_ref[:, t * s.ny : (t + 1) * s.ny] = low
        g = full_circle(s.cy[3], rows_of(three) - 2 - lanes_of(three), coef[3][t], top_y[t])
        high, low = halves(dot3(jnp.where(known3, g, 0.0), py3[...], py3l[...]))
        at = (TERMS + t) * s.ny
        y2h_ref[:, at : at + s.ny] = high
        y2l_ref[:, at : at + s.ny] = low

    def terms(level, first, rows, valid, shift, around, u):
        shape = (s.cx[level], s.depth_lanes)
        lane = lanes_of(shape) - first
        column = lane - jnp.where(lane < rows, 0, jnp.where(lane < 2 * rows, rows, 2 * rows))

        def by_term(v):
            return jnp.where(lane < rows, v[0], jnp.where(lane < 2 * rows, v[1], v[2]))

        g = around(s.cx[level], rows_of(shape) - column + shift, by_term(coef[level]), by_term(u))
        high, low = halves(jnp.where((lane >= 0) & (lane < TERMS * rows) & (column < valid), g, 0.0))
        return high, low

    high, low = terms(1, 0, s.rows1, s.rows1, 0, circle, unit[1])
    x = dot(px1[...], high) + dot(px1[...], low)
    high, low = terms(2, TERMS * s.rows1, s.rows2, s.x2 + 3, 1, circle, unit[2])
    x += dot(px2[...], high) + dot(px2[...], low)
    high, low = terms(3, TERMS * (s.rows1 + s.rows2), s.rows3, s.x3 + 5, 2, full_circle, top_x)
    x += dot(px3[...], high) + dot(px3l[...], high) + dot(px3[...], low)
    xh_ref[...], xl_ref[...] = halves(x)
    for t in range(TERMS):
        shape = (s.cz[2], LANES)
        g = circle(s.cz[2], rows_of(shape) - lanes_of(shape), coef[2][t], unit[2][t])
        high, low = halves(g * (one(a_ref, 2, t) * 0.0625))
        z_ref[t * s.zrows : (t + 1) * s.zrows] = dot(pz2[...], high) + dot(pz2[...], low)
        shape = (s.cz[3], LANES)
        g = full_circle(s.cz[3], rows_of(shape) - lanes_of(shape), coef[3][t], top_z[t])
        high, low = halves(g * (one(a_ref, 3, t) * 0.015625))
        z_ref[(TERMS + t) * s.zrows : (TERMS + t + 1) * s.zrows] = dot(pz3[...], high) + dot(pz3[...], low)


def near_kernel(s, tap_ref, b_ref, lo_ref, hi_ref, left_ref, right_ref, x0_ref, y0_ref,
                v_ref, down_ref, up_ref, e_ref, u_ref, eh_ref, el_ref):
    group = LANES // R
    tiles = [extended(s, b_ref, lo_ref, hi_ref, z) for z in range(s.nz)]
    tiles += [left_ref[t] for t in range(s.fine_tiles)] + [right_ref[t] for t in range(s.fine_tiles)]
    for i, x in enumerate(tiles):
        high, low = halves(x)
        columns = slice(i * LANES, (i + 1) * LANES)
        e_ref[0 : s.ext, columns] = high
        e_ref[s.ext : 2 * s.ext, columns] = high
        e_ref[2 * s.ext :, columns] = low
    x0 = x0_ref[...]
    for at in range(0, len(tiles) * LANES, 2 * LANES):
        columns = slice(at, min(at + 2 * LANES, len(tiles) * LANES))
        u_ref[:, columns] = dot(x0, e_ref[:, columns])
    lane = lanes_of((TERMS * s.nx, LANES))
    for z in range(s.nz):
        t, g = divmod(z, group)
        left = u_ref[:, (s.nz + t) * LANES : (s.nz + t + 1) * LANES]
        right = u_ref[:, (s.nz + s.fine_tiles + t) * LANES : (s.nz + s.fine_tiles + t + 1) * LANES]
        strips = turn(jnp.where((lane >= R * g) & (lane < R * g + R), left, right), -R * g)
        for at, x in ((0, u_ref[:, z * LANES : (z + 1) * LANES]), (LANES, strips)):
            high, low = halves(x)
            for t in range(TERMS):
                rows = slice(t * s.nx, (t + 1) * s.nx)
                eh_ref[t, z * s.nx : (z + 1) * s.nx, at : at + LANES] = high[rows]
                el_ref[t, z * s.nx : (z + 1) * s.nx, at : at + LANES] = low[rows]
    step = 4 * s.nx
    for t in range(TERMS):
        at = 2 * t * s.ny
        y0, y0h = y0_ref[:, at : at + 2 * s.ny], y0_ref[:, at : at + s.ny]
        for first in range(0, s.nz * s.nx, step):
            both = dot(eh_ref[t, first : first + step], y0)
            v = both[:, : s.ny] + both[:, s.ny :] + dot(el_ref[t, first : first + step], y0h)
            for q in range(step // s.nx):
                v_ref[t, first // s.nx + q] = v[q * s.nx : (q + 1) * s.nx]

    near_depth(s, tap_ref, v_ref, {-R: down_ref, s.nz: up_ref})


def near_depth(s, tap_ref, v_ref, out_refs):
    def depth(r, _):
        rows = pl.ds(pl.multiple_of(r * 8, 8), 8)
        taps = [[tap_ref[t, d] for d in range(R + 1)] for t in range(TERMS)]
        for first, ref in out_refs.items():
            acc = [None] * R
            for t in range(TERMS):
                for z in range(max(0, first - R), min(s.nz, first + 2 * R)):
                    v = v_ref[t, z, rows]
                    for o in range(R):
                        d = abs(first + o - z)
                        if d <= R:
                            term = v * taps[t][d]
                            acc[o] = term if acc[o] is None else acc[o] + term
            for o in range(R):
                ref[o, rows] = acc[o]
        return 0

    lax.fori_loop(0, s.nx // 8, depth, 0)


def own_kernel(s, tap_ref, v_ref, _, own_ref):
    near_depth(s, tap_ref, v_ref, {z: own_ref.at[z : z + R] for z in range(0, s.nz, R)})


def depth_kernel(s, tap_ref, *refs):
    m_refs = refs[: s.gz]
    ry2_ref, rx2_ref, ry3_ref, rx3_ref, _, w_ref, down_ref, up_ref, c2_ref, c3_ref, c_ref = refs[s.gz :]
    n = s.cz[1]
    parts = [[] for _ in range(n)]
    for b in range(s.gz):
        for k in range(s.planes):
            parts[(b * s.z1 + k - 1) % n].append((b, k))
    for z in range(n):
        out = None
        for b, k in parts[z]:
            x = unpacked(lambda t, b=b: m_refs[b][t], k, s.wide1, 0)
            out = x if out is None else out + x
        c_ref[z] = out
    lane = lanes_of((s.rows1, LANES))
    down = [jnp.zeros((s.rows1, LANES), F32)] * s.tiles_s
    up = list(down)
    for o in range(s.planes):
        sums = [c_ref[(o - 1) % n]]
        sums += [c_ref[(o - 1 + d) % n] + c_ref[(o - 1 - d) % n] for d in range(1, R + 1)]
        for t in range(TERMS):
            x = sums[0] * tap_ref[TERMS + t, 0]
            for d in range(1, R + 1):
                x += sums[d] * tap_ref[TERMS + t, d]
            k = t * s.planes + o
            w_ref[k] = x
            tile, slot = divmod(k, s.per_tile)
            at = slot * s.strip
            here = (lane >= at) & (lane < at + s.strip)
            down[tile] = jnp.where(here, turn(x, at), down[tile])
            up[tile] = jnp.where(here, turn(x, at - (s.wide1 - s.strip)), up[tile])

    def restricted(planes, y_ref, x_ref):
        n, rows = len(planes), planes[0].shape[0]
        coarse = []
        for j in range(n // 2):
            at = lambda d: planes[(2 * j + d) % n]
            coarse.append(at(0) + NEAR * (at(1) + at(-1)) + FAR * (at(3) + at(-3)))
        along = dot2(jnp.concatenate(coarse, axis=0), y_ref[...].astype(BF16))
        x = x_ref[...].astype(BF16)
        out = []
        for j in range(n // 2):
            high, low = halves(along[j * rows : (j + 1) * rows])
            out.append(dot(x, high) + dot(x, low))
        return out

    level2 = restricted([c_ref[z] for z in range(n)], ry2_ref, rx2_ref)
    level3 = restricted(level2, ry3_ref, rx3_ref)
    for t in range(s.tiles_s):
        down_ref[t * s.rows1 : (t + 1) * s.rows1] = down[t]
        up_ref[t * s.rows1 : (t + 1) * s.rows1] = up[t]
    lane = lanes_of((s.rows2, LANES))
    down = [jnp.zeros((s.rows2, LANES), F32)] * s.tiles_s2
    up = list(down)
    for j, x in enumerate(level2):
        c2_ref[j] = x
        tile, slot = divmod(j, s.per_tile2)
        at = slot * s.strip2
        here = (lane >= at) & (lane < at + s.strip2)
        down[tile] = jnp.where(here, turn(x, at), down[tile])
        up[tile] = jnp.where(here, turn(x, at - (s.wide2 - s.strip2)), up[tile])
    for t in range(s.tiles_s2):
        rows = slice(s.base2 + t * s.rows2, s.base2 + (t + 1) * s.rows2)
        down_ref[rows] = down[t]
        up_ref[rows] = up[t]
    for t, x in enumerate(packed(level3, s.wide3, s.tiles3)):
        c3_ref[t * s.rows3 : (t + 1) * s.rows3] = x
        for ref in (down_ref, up_ref):
            ref[s.base3 + t * s.rows3 : s.base3 + (t + 1) * s.rows3] = x


def along_kernel(s, z_ref, w_ref, c2_ref, *refs):
    c3_refs = refs[: s.gy]
    y1_ref, y2h_ref, y2l_ref, _, d_ref, y2_ref, y3_ref = refs[s.gy :]
    lane = lanes_of((s.rows1, LANES))
    above, below = c3_refs[1], c3_refs[-1]
    end = s.y1 + R
    for t in range(TERMS):
        cells = []
        for o in range(s.planes):
            k = t * s.planes + o
            tile, slot = divmod(k, s.per_tile)
            rows = slice(tile * s.rows1, (tile + 1) * s.rows1)
            at = slot * s.strip
            x = turn(w_ref[k], R)
            x += jnp.where(lane < s.strip, turn(below[rows], -at), 0.0)
            x += jnp.where((lane >= end) & (lane < end + s.strip), turn(above[rows], end - at), 0.0)
            cells.append(x)
        high, low = halves(jnp.concatenate(cells, axis=0))
        at = 2 * t * s.ny
        both = dot(high, y1_ref[:, at : at + 2 * s.ny])
        out = both[:, : s.ny] + both[:, s.ny :] + dot(low, y1_ref[:, at : at + s.ny])
        for o in range(s.planes):
            d_ref[t * s.rows1 : (t + 1) * s.rows1, o * s.ny : (o + 1) * s.ny] = out[o * s.rows1 : (o + 1) * s.rows1]
    lane = lanes_of((s.rows2, LANES))
    end = s.y2 + R
    cells = []
    for j in range(s.cz[2]):
        tile, slot = divmod(j, s.per_tile2)
        rows = slice(s.base2 + tile * s.rows2, s.base2 + (tile + 1) * s.rows2)
        at = slot * s.strip2
        x = turn(c2_ref[j], R)
        x += jnp.where(lane < s.strip2, turn(below[rows], -at), 0.0)
        x += jnp.where((lane >= end) & (lane < end + s.strip2), turn(above[rows], end - at), 0.0)
        cells.append(x)
    cells3 = []
    for j in range(s.cz[3]):
        out = None
        for b in range(s.gy):
            first = s.base3 if c3_refs[b].shape[0] > s.tiles3 * s.rows3 else 0
            tile = lambda t, b=b, f=first: c3_refs[b][f + t * s.rows3 : f + (t + 1) * s.rows3]
            x = unpacked(tile, j, s.wide3, b * s.y3)
            out = x if out is None else out + x
        cells3.append(out)
    at = TERMS * s.rows1
    for q, (x, rows, ref) in enumerate(((cells, s.rows2, y2_ref), (cells3, s.rows3, y3_ref))):
        columns = slice(q * TERMS * s.ny, (q + 1) * TERMS * s.ny)
        y = dot3(jnp.concatenate(x, axis=0), y2h_ref[:, columns], y2l_ref[:, columns])
        for t in range(TERMS):
            for j in range(len(x)):
                ref[t, j] = y[j * rows : (j + 1) * rows, t * s.ny : (t + 1) * s.ny]
        for o in range(s.planes):
            for t in range(TERMS):
                scale = [z_ref[(q * TERMS + t) * s.zrows + o, j] for j in range(len(x))]
                out = ref[t, 0] * scale[0]
                for j in range(1, len(x)):
                    out += ref[t, j] * scale[j]
                d_ref[at + t * rows : at + (t + 1) * rows, o * s.ny : (o + 1) * s.ny] = out
        at += TERMS * rows


def across(s, d_ref, xh_ref, xl_ref, shift):
    rows = slice(shift * s.nx, (shift + 1) * s.nx)
    high, low = halves(d_ref[...])
    xh, xl = xh_ref[rows, : s.depth], xl_ref[rows, : s.depth]
    return dot(xh, high) + dot(xl, high) + dot(xh, low)


def away_kernel(s, d_ref, xh_ref, xl_ref, *g_refs):
    for shift, ref in enumerate(g_refs):
        ref[...] = across(s, d_ref, xh_ref, xl_ref, shift + 1)


def prolonged(s, level, z):
    m = z // 2 + 1
    if z % 2 == 0:
        return level[m]
    return NEAR * (level[m] + level[m + 1]) + FAR * (level[m - 1] + level[m + 2])


def home_kernel(s, d_ref, xh_ref, xl_ref, own_ref, low_ref, high_ref, out_ref):
    g = across(s, d_ref, xh_ref, xl_ref, 0)
    level = [g[:, o * s.ny : (o + 1) * s.ny] for o in range(s.planes)]
    for z in range(s.nz):
        x = prolonged(s, level, z) + own_ref[z]
        if z < R:
            x += low_ref[z]
        if z >= s.nz - R:
            x += high_ref[z - (s.nz - R)]
        out_ref[z] = x


def last_kernel(s, home_ref, *refs):
    g_refs, out_ref = refs[:-1], refs[-1]
    level = []
    for o in range(s.planes):
        columns = slice(o * s.ny, (o + 1) * s.ny)
        x = g_refs[0][:, columns]
        for ref in g_refs[1:]:
            x += ref[:, columns]
        level.append(x)
    for z in range(s.nz):
        out_ref[z] = home_ref[z] + prolonged(s, level, z)


def call(kernel, name, operands, out_shapes, scalars=(), after=(), scratch=(), flops=0):
    operands = list(operands) + list(after)

    def spec(i):
        if i >= len(operands) - len(after):
            return pl.BlockSpec(memory_space=pl.ANY)
        return pl.BlockSpec(memory_space=pltpu.SMEM if i in scalars else pltpu.VMEM)

    moved = sum(x.size * x.dtype.itemsize for x in operands)
    moved += sum(int(np.prod(x.shape)) * x.dtype.itemsize for x in out_shapes)
    return pl.pallas_call(
        kernel,
        name=name,
        out_shape=out_shapes,
        in_specs=[spec(i) for i in range(len(operands))],
        out_specs=[pl.BlockSpec(memory_space=pltpu.VMEM)] * len(out_shapes),
        scratch_shapes=list(scratch),
        compiler_params=pltpu.CompilerParams(vmem_limit_bytes=VMEM_LIMIT),
        cost_estimate=pl.CostEstimate(flops=flops, bytes_accessed=moved, transcendentals=0),
    )(*operands)


def arrays(*shapes, dtype=F32):
    return [jax.ShapeDtypeStruct(shape, dtype) for shape in shapes]


def fetch(x, **shifts):
    names = tuple(shifts)
    sizes = [lax.axis_size(n) for n in names]
    pairs = []
    for here in np.ndindex(*sizes):
        there = [(h + shifts[n]) % size for h, n, size in zip(here, names, sizes)]
        pairs.append((int(np.ravel_multi_index(there, sizes)), int(np.ravel_multi_index(here, sizes))))
    return lax.ppermute(x, names if len(names) > 1 else names[0], pairs)


def two(*shape):
    return arrays(shape, shape, dtype=BF16)


def shards(charges, widths, amplitudes):
    s = Sizes(*charges.shape, lax.axis_size("gz"), lax.axis_size("gx"), lax.axis_size("gy"))
    c = {k: jnp.asarray(v) for k, v in constants(s).items()}
    brick = (s.nz, s.nx, s.ny)
    side = (R, s.nx, s.ny)
    taps, x0, y0 = call(
        functools.partial(tap_kernel, s), "taps", [widths, amplitudes],
        arrays((8, LANES))
        + arrays((TERMS * s.nx, 3 * s.ext), (2 * LANES, 2 * TERMS * s.ny), dtype=BF16),
        flops=6 * 10**8,
    )
    high_rows = fetch(charges, gx=1)
    low_rows = high_rows if s.gx == 2 else fetch(charges, gx=-1)
    strips = (s.fine_tiles, s.ext, LANES)
    share, first_cells, last_cells = call(
        functools.partial(share_kernel, s), "share", [charges, low_rows, high_rows],
        arrays((s.tiles1, s.rows1, LANES), strips, strips), after=[x0], flops=10**9,
    )
    shares = [share] + [fetch(share, gz=b) for b in range(1, s.gz)]
    left, right = fetch(last_cells, gy=-1), fetch(first_cells, gy=1)
    tiles = s.nz + 2 * s.fine_tiles
    halved = pltpu.VMEM((TERMS, s.nz * s.nx, 2 * LANES), BF16)
    crossed, near_down, near_up = call(
        functools.partial(near_kernel, s), "near",
        [taps, charges, low_rows, high_rows, left, right, x0, y0],
        arrays((TERMS,) + brick, side, side), scalars=(0,),
        scratch=[
            pltpu.VMEM((3 * s.ext, tiles * LANES), BF16), pltpu.VMEM((TERMS * s.nx, tiles * LANES), F32),
            halved, halved,
        ],
        flops=5 * 10**9,
    )
    size3 = s.tiles3 * s.rows3
    message = (s.base3 + size3, LANES)
    waves, to_low, to_high, level2, coarse = call(
        functools.partial(depth_kernel, s), "depth",
        [taps] + shares + [c[k] for k in ("ry2", "rx2", "ry3", "rx3")],
        arrays((TERMS * s.planes, s.rows1, LANES), message, message, (s.cz[2], s.rows2, LANES), (size3, LANES)),
        scalars=(0,), after=[near_up], scratch=[pltpu.VMEM((s.cz[1], s.rows1, LANES), F32)], flops=2 * 10**9,
    )
    named = ("px1", "px2", "px3", "px3l", "py2", "py3", "py3l", "pz2", "pz3")
    z_taps, y1, y2h, y2l, xh, xl = call(
        functools.partial(matrix_kernel, s), "matrices",
        [widths, amplitudes] + [c[k] for k in named],
        arrays((2 * TERMS * s.zrows, LANES))
        + arrays((LANES, 2 * TERMS * s.ny), dtype=BF16)
        + two(LANES, 2 * TERMS * s.ny) + two(s.cx[0], s.depth_lanes),
        after=[coarse], flops=2 * 10**9,
    )
    (near,) = call(
        functools.partial(own_kernel, s), "own", [taps, crossed], arrays(brick),
        scalars=(0,), after=[z_taps], flops=10**8,
    )
    coarses = [coarse]
    for b in range(1, s.gy):
        coarses.append(fetch({1: to_low, s.gy - 1: to_high}.get(b, coarse), gy=b))
    near_low, near_high = fetch(near_up, gz=-1), fetch(near_down, gz=1)
    (terms,) = call(
        functools.partial(along_kernel, s), "along",
        [z_taps, waves, level2] + coarses + [y1, y2h, y2l],
        arrays((s.depth, s.planes * s.ny)), scalars=(0,), after=[near],
        scratch=[
            pltpu.VMEM((TERMS, s.cz[2], s.rows2, s.ny), F32), pltpu.VMEM((TERMS, s.cz[3], s.rows3, s.ny), F32)
        ], flops=3 * 10**9,
    )
    parts = call(
        functools.partial(away_kernel, s), "away", [terms, xh, xl],
        arrays(*[(s.nx, s.planes * s.ny)] * (s.gx - 1)), flops=10**9,
    )
    parts = [fetch(x, gx=-dx) for dx, x in enumerate(parts, 1)]
    (home,) = call(
        functools.partial(home_kernel, s), "home",
        [terms, xh, xl, near, near_low, near_high], arrays(brick), flops=2 * 10**9,
    )
    (out,) = call(
        functools.partial(last_kernel, s), "last", [home] + parts, arrays(brick), flops=10**9,
    )
    return out


def solution(mesh):
    placed = (P("gz", "gx", "gy"), P(), P())
    return jax.shard_map(
        shards, mesh=mesh, in_specs=placed, out_specs=P("gz", "gx", "gy"), check_vma=False
    )
```

```python
import functools

import jax
import jax.numpy as jnp
import ml_dtypes
import numpy as np
from jax import lax
from jax.experimental import pallas as pl
from jax.experimental.pallas import tpu as pltpu
from jax.sharding import PartitionSpec as P

R = 8
TERMS = 3
LANES = 128
NEAR = 9.0 / 16.0
FAR = -1.0 / 16.0
F32 = jnp.float32
BF16 = jnp.bfloat16
VMEM_LIMIT = 40 * 1024 * 1024


def up8(n):
    return -(-n // 8) * 8


class Sizes:
    def __init__(self, nz, nx, ny, gz, gx, gy):
        self.nz, self.nx, self.ny = nz, nx, ny
        self.gz, self.gx, self.gy = gz, gx, gy
        self.z1, self.x1, self.y1 = nz // 2, nx // 2, ny // 2
        self.z2, self.x2, self.y2 = nz // 4, nx // 4, ny // 4
        self.cz = [nz * gz >> l for l in range(4)]
        self.cx = [nx * gx >> l for l in range(4)]
        self.cy = [ny * gy >> l for l in range(4)]
        self.planes = self.z1 + 3
        self.zrows = up8(self.planes)
        self.rows1 = self.x1
        self.rows2 = up8(self.x2 + 3)
        self.wide1 = self.y1 + 3
        self.wide2 = self.y2 + 5
        self.tiles1 = -(-self.planes * self.wide1 // LANES)
        self.x3, self.y3 = nx // 8, ny // 8
        self.rows3 = up8(self.x3 + 5)
        self.wide3 = self.y3 + 5
        self.tiles3 = -(-self.cz[3] * self.wide3 // LANES)
        self.strip2 = R + 5
        self.per_tile2 = LANES // self.strip2
        self.tiles_s2 = -(-self.cz[2] // self.per_tile2)
        self.strip = R + 3
        self.per_tile = LANES // self.strip
        self.tiles_s = -(-TERMS * self.planes // self.per_tile)
        self.fine_tiles = -(-nz // (LANES // R))
        self.ext = nx + 2 * R
        self.depth = TERMS * (self.rows1 + self.rows2 + self.rows3)
        self.base2 = self.tiles_s * self.rows1
        self.base3 = self.base2 + self.tiles_s2 * self.rows2
        self.depth_lanes = -(-self.depth // LANES) * LANES


def restrict_circle(n):
    m = np.zeros((n // 2, n))
    for i in range(n // 2):
        for d, w in ((0, 1.0), (1, NEAR), (-1, NEAR), (3, FAR), (-3, FAR)):
            m[i, (2 * i + d) % n] += w
    return m


def prolong_circle(n):
    m = np.zeros((2 * n, n))
    for i in range(n):
        m[2 * i, i] += 1.0
        for d, w in ((0, NEAR), (1, NEAR), (-1, FAR), (2, FAR)):
            m[2 * i + 1, (i + d) % n] += w
    return m


def restrict_open(first_in, n_in, first_out, n_out):
    m = np.zeros((n_out, n_in))
    for i in range(n_out):
        for d, w in ((0, 1.0), (1, NEAR), (-1, NEAR), (3, FAR), (-3, FAR)):
            j = 2 * (first_out + i) + d - first_in
            if 0 <= j < n_in:
                m[i, j] = w
    return m


def padded(m, rows, columns):
    out = np.zeros((rows, columns), np.float32)
    out[: m.shape[0], : m.shape[1]] = m
    return out


def exact(m):
    out = m.astype(ml_dtypes.bfloat16)
    assert np.all(out.astype(np.float64) == m)
    return out


def constants(s):
    c = {}
    c["ry2"] = padded(restrict_open(-1, s.wide1, -2, s.wide2).T, LANES, LANES)
    c["rx2"] = padded(restrict_open(0, s.x1, -1, s.x2 + 3), s.rows2, s.rows1)

    def chain(n):
        p1 = prolong_circle(n[1])
        p2 = p1 @ prolong_circle(n[2])
        return p1, p2, p2 @ prolong_circle(n[3])

    def parts(name, m):
        m = m.astype(np.float32)
        c[name] = m.astype(ml_dtypes.bfloat16)
        c[name + "l"] = (m - c[name].astype(np.float32)).astype(ml_dtypes.bfloat16)

    x1, x2, x3 = chain(s.cx)
    c["px1"], c["px2"] = exact(x1), exact(x2)
    parts("px3", x3)
    _, y2, y3 = chain(s.cy)
    c["py2"] = exact(y2[: s.ny].T)
    parts("py3", y3[: s.ny].T)
    z2 = prolong_circle(s.cz[2])
    z3 = z2 @ prolong_circle(s.cz[3])
    own = [(o - 1) % s.cz[1] for o in range(s.planes)]
    c["pz2"] = exact(padded(z2[own], s.zrows, s.cz[2]))
    c["pz3"] = exact(padded(z3[own], s.zrows, s.cz[3]))
    c["ry3"] = padded(restrict_open(-2, s.wide2, -2, s.wide3).T, LANES, LANES)
    c["rx3"] = padded(restrict_open(-1, s.x2 + 3, -2, s.x3 + 5), s.rows3, s.rows2)
    return c


def halves(x):
    high = x.astype(BF16)
    return high, (x - high.astype(F32)).astype(BF16)


def dot(a, b):
    return jnp.dot(a, b, preferred_element_type=F32)


def dot2(a, b):
    high, low = halves(a)
    return dot(high, b) + dot(low, b)


def dot3(a, b_high, b_low):
    high, low = halves(a)
    return dot(high, b_high) + dot(low, b_high) + dot(high, b_low)


def lanes_of(shape):
    return lax.broadcasted_iota(jnp.int32, shape, len(shape) - 1)


def turn(x, by):
    by = by % x.shape[-1]
    return x if by == 0 else pltpu.roll(x, by, x.ndim - 1)


def packed(planes, wide, tiles):
    out = [None] * tiles

    def add(t, x):
        out[t] = x if out[t] is None else out[t] + x

    for k, x in enumerate(planes):
        t, at = divmod(k * wide, LANES)
        moved = turn(x, at)
        if at + wide <= LANES:
            add(t, moved)
        else:
            lane = lanes_of(x.shape)
            add(t, jnp.where(lane >= at, moved, 0.0))
            add(t + 1, jnp.where(lane < at, moved, 0.0))
    return out


def unpacked(tile, k, wide, shift):
    t, at = divmod(k * wide, LANES)
    x = tile(t)
    lane = lanes_of(x.shape)
    if at + wide > LANES:
        x = jnp.where(lane >= at, x, tile(t + 1))
    x = turn(x, shift - at)
    if shift + wide <= LANES:
        return jnp.where((lane >= shift) & (lane < shift + wide), x, 0.0)
    return jnp.where((lane >= shift) | (lane < shift + wide - LANES), x, 0.0)


def open_restriction(shape, in_dim, first_in, first_out, n_out):
    i = lax.broadcasted_iota(jnp.int32, shape, in_dim) + first_in
    o = lax.broadcasted_iota(jnp.int32, shape, 1 - in_dim)
    d = jnp.abs(i - 2 * (o + first_out))
    w = jnp.where(d == 0, 1.0, jnp.where(d == 1, NEAR, jnp.where(d == 3, FAR, 0.0)))
    return jnp.where(o < n_out, w, 0.0).astype(BF16)


def extended(s, b_ref, lo_ref, hi_ref, z):
    return jnp.concatenate([lo_ref[z, s.nx - R :], b_ref[z], hi_ref[z, 0:R]], axis=0)


def share_kernel(s, b_ref, lo_ref, hi_ref, _, m_ref, first_ref, last_ref):
    b = [extended(s, b_ref, lo_ref, hi_ref, z) for z in range(s.nz)]
    planes = []
    for k in range(-1, s.z1 + 2):
        out = None
        for d, w in ((0, 1.0), (1, NEAR), (-1, NEAR), (3, FAR), (-3, FAR)):
            if 0 <= 2 * k + d < s.nz:
                term = b[2 * k + d] if d == 0 else b[2 * k + d] * w
                out = term if out is None else out + term
        planes.append(out)
    high, low = halves(jnp.concatenate(planes, axis=0))
    ry1 = open_restriction((s.ny, LANES), 0, 0, -1, s.wide1)
    rx1 = open_restriction((s.rows1, s.ext), 1, -R, 0, s.x1)
    along = dot(high, ry1) + dot(low, ry1)
    shares = []
    for k in range(s.planes):
        high, low = halves(along[k * s.ext : (k + 1) * s.ext])
        shares.append(dot(rx1, high) + dot(rx1, low))
    for t, x in enumerate(packed(shares, s.wide1, s.tiles1)):
        m_ref[t] = x
    lane = lanes_of((s.ext, LANES))
    group = LANES // R
    for t in range(s.fine_tiles):
        first = last = jnp.zeros((s.ext, LANES), F32)
        for g in range(min(group, s.nz - t * group)):
            x = b[t * group + g]
            at = R * ((g + 1) % group)
            first = jnp.where((lane >= at) & (lane < at + R), turn(x, at), first)
            at = R * g
            last = jnp.where((lane >= at) & (lane < at + R), turn(x, at + R - s.ny), last)
        first_ref[t] = first
        last_ref[t] = last


def rows_of(shape):
    return lax.broadcasted_iota(jnp.int32, shape, 0)


def bell(c, d):
    d = jnp.abs(d)
    return jnp.where(d <= R, jnp.exp(c * d * d), 0.0)


def one(ref, level, t):
    return ref[level : level + 1, t : t + 1]


def spreads(w_ref, levels):
    out = []
    for l in levels:
        w = [one(w_ref, l, t) for t in range(TERMS)]
        out.append([-0.5 / (x * x) for x in w])
    return out


def units(coef, distance, valid):
    shape = (up8(len(coef)), LANES)
    row = rows_of(shape)
    column = jnp.zeros(shape, F32)
    for r, c in enumerate(coef):
        column = jnp.where(row == r, c, column)
    lane = lanes_of(shape)
    d = distance(row, lane).astype(F32)
    total = jnp.sum(jnp.where(valid(row, lane), jnp.exp(2.0 * column * d * d), 0.0), axis=1, keepdims=True)
    unit = 1.0 / jnp.sqrt(total)
    return [unit[r : r + 1] for r in range(len(coef))]


def near_units(coef):
    flat = [c for level in coef for c in level]
    out = units(flat, lambda row, lane: lane - R, lambda row, lane: lane <= 2 * R)
    return [out[i : i + TERMS] for i in range(0, len(out), TERMS)]


def tap_kernel(s, w_ref, a_ref, tap_ref, x0_ref, y0_ref):
    coef = spreads(w_ref, (0, 1))
    unit = near_units(coef)
    d = lanes_of((1, LANES)).astype(F32)
    for t in range(TERMS):
        tap_ref[t : t + 1] = bell(coef[0][t], d) * (unit[0][t] * one(a_ref, 0, t))
        tap_ref[TERMS + t : TERMS + t + 1] = bell(coef[1][t], d) * (unit[1][t] * one(a_ref, 1, t) * 0.25)
    shape = (s.nx, 3 * s.ext)
    lane = lanes_of(shape)
    part = jnp.where(lane < s.ext, 0, jnp.where(lane < 2 * s.ext, 1, 2))
    d = (lane - part * s.ext - R - rows_of(shape)).astype(F32)
    for t in range(TERMS):
        high, low = halves(bell(coef[0][t], d) * unit[0][t])
        x0_ref[t * s.nx : (t + 1) * s.nx] = jnp.where(part == 1, low.astype(F32), high.astype(F32)).astype(BF16)
    shape = (s.ny + 2 * R, s.ny)
    i = rows_of(shape)
    cell = jnp.where(i < s.ny, i, jnp.where(i < s.ny + R, i - s.ny - R, i - R))
    d = (cell - lanes_of(shape)).astype(F32)
    for t in range(TERMS):
        high, low = halves(bell(coef[0][t], d) * unit[0][t])
        at = 2 * t * s.ny
        y0_ref[s.ny + 2 * R :, at : at + 2 * s.ny] = jnp.zeros((2 * LANES - s.ny - 2 * R, 2 * s.ny), BF16)
        y0_ref[: s.ny + 2 * R, at : at + s.ny] = high
        y0_ref[: s.ny + 2 * R, at + s.ny : at + 2 * s.ny] = low


def matrix_kernel(s, w_ref, a_ref, px1, px2, px3, px3l, py2, py3, py3l, pz2, pz3, _,
                  z_ref, y1_ref, y2h_ref, y2l_ref, xh_ref, xl_ref):
    coef = spreads(w_ref, range(4))
    unit = near_units(coef[:3])
    sizes = [s.cx[3], s.cy[3], s.cz[3]]

    def per_row(row):
        return jnp.where(row < TERMS, sizes[0], jnp.where(row < 2 * TERMS, sizes[1], sizes[2]))

    top = units(
        coef[3] * 3,
        lambda row, lane: jnp.minimum(lane, per_row(row) - lane),
        lambda row, lane: lane < per_row(row),
    )
    top_x, top_y, top_z = top[:TERMS], top[TERMS : 2 * TERMS], top[2 * TERMS :]

    def circle(n, d, c, u):
        d = (d & (n - 1)).astype(F32)
        return (bell(c, d) + bell(c, n - d)) * u

    def full_circle(n, d, c, u):
        d = (d & (n - 1)).astype(F32)
        d = jnp.minimum(d, n - d)
        return jnp.exp(c * d * d) * u

    shape = (LANES, s.ny)
    fine = lanes_of(shape)
    d = (rows_of(shape) - (R + 1) - (fine >> 1)).astype(F32)
    even = (fine & 1) == 0
    known = rows_of(shape) < s.y1 + 3 + 2 * R
    two, three = (LANES, s.cy[2]), (LANES, s.cy[3])
    known2 = rows_of(two) < s.y2 + 5 + 2 * R
    known3 = rows_of(three) < (s.gy - 1) * s.y3 + s.wide3
    for t in range(TERMS):
        c = coef[1][t]
        here = bell(c, d)
        between = NEAR * (here + bell(c, d - 1.0)) + FAR * (bell(c, d + 1.0) + bell(c, d - 2.0))
        high, low = halves(jnp.where(known, jnp.where(even, here, between) * unit[1][t], 0.0))
        y1_ref[:, 2 * t * s.ny : (2 * t + 1) * s.ny] = high
        y1_ref[:, (2 * t + 1) * s.ny : (2 * t + 2) * s.ny] = low
        g = circle(s.cy[2], rows_of(two) - (R + 2) - lanes_of(two), coef[2][t], unit[2][t])
        high, low = halves(dot2(jnp.where(known2, g, 0.0), py2[...]))
        y2h_ref[:, t * s.ny : (t + 1) * s.ny] = high
        y2l_ref[:, t * s.ny : (t + 1) * s.ny] = low
        g = full_circle(s.cy[3], rows_of(three) - 2 - lanes_of(three), coef[3][t], top_y[t])
        high, low = halves(dot3(jnp.where(known3, g, 0.0), py3[...], py3l[...]))
        at = (TERMS + t) * s.ny
        y2h_ref[:, at : at + s.ny] = high
        y2l_ref[:, at : at + s.ny] = low

    def terms(level, first, rows, valid, shift, around, u):
        shape = (s.cx[level], s.depth_lanes)
        lane = lanes_of(shape) - first
        column = lane - jnp.where(lane < rows, 0, jnp.where(lane < 2 * rows, rows, 2 * rows))

        def by_term(v):
            return jnp.where(lane < rows, v[0], jnp.where(lane < 2 * rows, v[1], v[2]))

        g = around(s.cx[level], rows_of(shape) - column + shift, by_term(coef[level]), by_term(u))
        high, low = halves(jnp.where((lane >= 0) & (lane < TERMS * rows) & (column < valid), g, 0.0))
        return high, low

    high, low = terms(1, 0, s.rows1, s.rows1, 0, circle, unit[1])
    x = dot(px1[...], high) + dot(px1[...], low)
    high, low = terms(2, TERMS * s.rows1, s.rows2, s.x2 + 3, 1, circle, unit[2])
    x += dot(px2[...], high) + dot(px2[...], low)
    high, low = terms(3, TERMS * (s.rows1 + s.rows2), s.rows3, s.x3 + 5, 2, full_circle, top_x)
    x += dot(px3[...], high) + dot(px3l[...], high) + dot(px3[...], low)
    xh_ref[...], xl_ref[...] = halves(x)
    for t in range(TERMS):
        shape = (s.cz[2], LANES)
        g = circle(s.cz[2], rows_of(shape) - lanes_of(shape), coef[2][t], unit[2][t])
        high, low = halves(g * (one(a_ref, 2, t) * 0.0625))
        z_ref[t * s.zrows : (t + 1) * s.zrows] = dot(pz2[...], high) + dot(pz2[...], low)
        shape = (s.cz[3], LANES)
        g = full_circle(s.cz[3], rows_of(shape) - lanes_of(shape), coef[3][t], top_z[t])
        high, low = halves(g * (one(a_ref, 3, t) * 0.015625))
        z_ref[(TERMS + t) * s.zrows : (TERMS + t + 1) * s.zrows] = dot(pz3[...], high) + dot(pz3[...], low)


def near_kernel(s, tap_ref, b_ref, lo_ref, hi_ref, left_ref, right_ref, x0_ref, y0_ref,
                v_ref, down_ref, up_ref, e_ref, u_ref, eh_ref, el_ref):
    group = LANES // R
    tiles = [extended(s, b_ref, lo_ref, hi_ref, z) for z in range(s.nz)]
    tiles += [left_ref[t] for t in range(s.fine_tiles)] + [right_ref[t] for t in range(s.fine_tiles)]
    for i, x in enumerate(tiles):
        high, low = halves(x)
        columns = slice(i * LANES, (i + 1) * LANES)
        e_ref[0 : s.ext, columns] = high
        e_ref[s.ext : 2 * s.ext, columns] = high
        e_ref[2 * s.ext :, columns] = low
    x0 = x0_ref[...]
    for at in range(0, len(tiles) * LANES, 2 * LANES):
        columns = slice(at, min(at + 2 * LANES, len(tiles) * LANES))
        u_ref[:, columns] = dot(x0, e_ref[:, columns])
    lane = lanes_of((TERMS * s.nx, LANES))
    for z in range(s.nz):
        t, g = divmod(z, group)
        left = u_ref[:, (s.nz + t) * LANES : (s.nz + t + 1) * LANES]
        right = u_ref[:, (s.nz + s.fine_tiles + t) * LANES : (s.nz + s.fine_tiles + t + 1) * LANES]
        strips = turn(jnp.where((lane >= R * g) & (lane < R * g + R), left, right), -R * g)
        for at, x in ((0, u_ref[:, z * LANES : (z + 1) * LANES]), (LANES, strips)):
            high, low = halves(x)
            for t in range(TERMS):
                rows = slice(t * s.nx, (t + 1) * s.nx)
                eh_ref[t, z * s.nx : (z + 1) * s.nx, at : at + LANES] = high[rows]
                el_ref[t, z * s.nx : (z + 1) * s.nx, at : at + LANES] = low[rows]
    step = 4 * s.nx
    for t in range(TERMS):
        at = 2 * t * s.ny
        y0, y0h = y0_ref[:, at : at + 2 * s.ny], y0_ref[:, at : at + s.ny]
        for first in range(0, s.nz * s.nx, step):
            both = dot(eh_ref[t, first : first + step], y0)
            v = both[:, : s.ny] + both[:, s.ny :] + dot(el_ref[t, first : first + step], y0h)
            for q in range(step // s.nx):
                v_ref[t, first // s.nx + q] = v[q * s.nx : (q + 1) * s.nx]

    near_depth(s, tap_ref, v_ref, {-R: down_ref, s.nz: up_ref})


def near_depth(s, tap_ref, v_ref, out_refs):
    def depth(r, _):
        rows = pl.ds(pl.multiple_of(r * 8, 8), 8)
        taps = [[tap_ref[t, d] for d in range(R + 1)] for t in range(TERMS)]
        for first, ref in out_refs.items():
            acc = [None] * R
            for t in range(TERMS):
                for z in range(max(0, first - R), min(s.nz, first + 2 * R)):
                    v = v_ref[t, z, rows]
                    for o in range(R):
                        d = abs(first + o - z)
                        if d <= R:
                            term = v * taps[t][d]
                            acc[o] = term if acc[o] is None else acc[o] + term
            for o in range(R):
                ref[o, rows] = acc[o]
        return 0

    lax.fori_loop(0, s.nx // 8, depth, 0)


def gate_kernel(*refs):
    pass


def own_kernel(s, tap_ref, v_ref, _, own_ref):
    near_depth(s, tap_ref, v_ref, {z: own_ref.at[z : z + R] for z in range(0, s.nz, R)})


def depth_kernel(s, tap_ref, *refs):
    m_refs = refs[: s.gz]
    ry2_ref, rx2_ref, ry3_ref, rx3_ref, _, w_ref, down_ref, up_ref, c2_ref, c3_ref, c_ref = refs[s.gz :]
    n = s.cz[1]
    parts = [[] for _ in range(n)]
    for b in range(s.gz):
        for k in range(s.planes):
            parts[(b * s.z1 + k - 1) % n].append((b, k))
    for z in range(n):
        out = None
        for b, k in parts[z]:
            x = unpacked(lambda t, b=b: m_refs[b][t], k, s.wide1, 0)
            out = x if out is None else out + x
        c_ref[z] = out
    lane = lanes_of((s.rows1, LANES))
    down = [jnp.zeros((s.rows1, LANES), F32)] * s.tiles_s
    up = list(down)
    for o in range(s.planes):
        sums = [c_ref[(o - 1) % n]]
        sums += [c_ref[(o - 1 + d) % n] + c_ref[(o - 1 - d) % n] for d in range(1, R + 1)]
        for t in range(TERMS):
            x = sums[0] * tap_ref[TERMS + t, 0]
            for d in range(1, R + 1):
                x += sums[d] * tap_ref[TERMS + t, d]
            k = t * s.planes + o
            w_ref[k] = x
            tile, slot = divmod(k, s.per_tile)
            at = slot * s.strip
            here = (lane >= at) & (lane < at + s.strip)
            down[tile] = jnp.where(here, turn(x, at), down[tile])
            up[tile] = jnp.where(here, turn(x, at - (s.wide1 - s.strip)), up[tile])

    def restricted(planes, y_ref, x_ref):
        n, rows = len(planes), planes[0].shape[0]
        coarse = []
        for j in range(n // 2):
            at = lambda d: planes[(2 * j + d) % n]
            coarse.append(at(0) + NEAR * (at(1) + at(-1)) + FAR * (at(3) + at(-3)))
        along = dot2(jnp.concatenate(coarse, axis=0), y_ref[...].astype(BF16))
        x = x_ref[...].astype(BF16)
        out = []
        for j in range(n // 2):
            high, low = halves(along[j * rows : (j + 1) * rows])
            out.append(dot(x, high) + dot(x, low))
        return out

    level2 = restricted([c_ref[z] for z in range(n)], ry2_ref, rx2_ref)
    level3 = restricted(level2, ry3_ref, rx3_ref)
    for t in range(s.tiles_s):
        down_ref[t * s.rows1 : (t + 1) * s.rows1] = down[t]
        up_ref[t * s.rows1 : (t + 1) * s.rows1] = up[t]
    lane = lanes_of((s.rows2, LANES))
    down = [jnp.zeros((s.rows2, LANES), F32)] * s.tiles_s2
    up = list(down)
    for j, x in enumerate(level2):
        c2_ref[j] = x
        tile, slot = divmod(j, s.per_tile2)
        at = slot * s.strip2
        here = (lane >= at) & (lane < at + s.strip2)
        down[tile] = jnp.where(here, turn(x, at), down[tile])
        up[tile] = jnp.where(here, turn(x, at - (s.wide2 - s.strip2)), up[tile])
    for t in range(s.tiles_s2):
        rows = slice(s.base2 + t * s.rows2, s.base2 + (t + 1) * s.rows2)
        down_ref[rows] = down[t]
        up_ref[rows] = up[t]
    for t, x in enumerate(packed(level3, s.wide3, s.tiles3)):
        c3_ref[t * s.rows3 : (t + 1) * s.rows3] = x
        for ref in (down_ref, up_ref):
            ref[s.base3 + t * s.rows3 : s.base3 + (t + 1) * s.rows3] = x


def along_kernel(s, z_ref, w_ref, c2_ref, *refs):
    c3_refs = refs[: s.gy]
    y1_ref, y2h_ref, y2l_ref, _, d_ref, y2_ref, y3_ref = refs[s.gy :]
    lane = lanes_of((s.rows1, LANES))
    above, below = c3_refs[1], c3_refs[-1]
    end = s.y1 + R
    for t in range(TERMS):
        cells = []
        for o in range(s.planes):
            k = t * s.planes + o
            tile, slot = divmod(k, s.per_tile)
            rows = slice(tile * s.rows1, (tile + 1) * s.rows1)
            at = slot * s.strip
            x = turn(w_ref[k], R)
            x += jnp.where(lane < s.strip, turn(below[rows], -at), 0.0)
            x += jnp.where((lane >= end) & (lane < end + s.strip), turn(above[rows], end - at), 0.0)
            cells.append(x)
        high, low = halves(jnp.concatenate(cells, axis=0))
        at = 2 * t * s.ny
        both = dot(high, y1_ref[:, at : at + 2 * s.ny])
        out = both[:, : s.ny] + both[:, s.ny :] + dot(low, y1_ref[:, at : at + s.ny])
        for o in range(s.planes):
            d_ref[t * s.rows1 : (t + 1) * s.rows1, o * s.ny : (o + 1) * s.ny] = out[o * s.rows1 : (o + 1) * s.rows1]
    lane = lanes_of((s.rows2, LANES))
    end = s.y2 + R
    cells = []
    for j in range(s.cz[2]):
        tile, slot = divmod(j, s.per_tile2)
        rows = slice(s.base2 + tile * s.rows2, s.base2 + (tile + 1) * s.rows2)
        at = slot * s.strip2
        x = turn(c2_ref[j], R)
        x += jnp.where(lane < s.strip2, turn(below[rows], -at), 0.0)
        x += jnp.where((lane >= end) & (lane < end + s.strip2), turn(above[rows], end - at), 0.0)
        cells.append(x)
    cells3 = []
    for j in range(s.cz[3]):
        out = None
        for b in range(s.gy):
            first = s.base3 if c3_refs[b].shape[0] > s.tiles3 * s.rows3 else 0
            tile = lambda t, b=b, f=first: c3_refs[b][f + t * s.rows3 : f + (t + 1) * s.rows3]
            x = unpacked(tile, j, s.wide3, b * s.y3)
            out = x if out is None else out + x
        cells3.append(out)
    at = TERMS * s.rows1
    for q, (x, rows, ref) in enumerate(((cells, s.rows2, y2_ref), (cells3, s.rows3, y3_ref))):
        columns = slice(q * TERMS * s.ny, (q + 1) * TERMS * s.ny)
        y = dot3(jnp.concatenate(x, axis=0), y2h_ref[:, columns], y2l_ref[:, columns])
        for t in range(TERMS):
            for j in range(len(x)):
                ref[t, j] = y[j * rows : (j + 1) * rows, t * s.ny : (t + 1) * s.ny]
        for o in range(s.planes):
            for t in range(TERMS):
                scale = [z_ref[(q * TERMS + t) * s.zrows + o, j] for j in range(len(x))]
                out = ref[t, 0] * scale[0]
                for j in range(1, len(x)):
                    out += ref[t, j] * scale[j]
                d_ref[at + t * rows : at + (t + 1) * rows, o * s.ny : (o + 1) * s.ny] = out
        at += TERMS * rows


def across(s, d_ref, xh_ref, xl_ref, shift):
    rows = slice(shift * s.nx, (shift + 1) * s.nx)
    high, low = halves(d_ref[...])
    xh, xl = xh_ref[rows, : s.depth], xl_ref[rows, : s.depth]
    return dot(xh, high) + dot(xl, high) + dot(xh, low)


def away_kernel(s, d_ref, xh_ref, xl_ref, *g_refs):
    for shift, ref in enumerate(g_refs):
        ref[...] = across(s, d_ref, xh_ref, xl_ref, shift + 1)


def prolonged(s, level, z):
    m = z // 2 + 1
    if z % 2 == 0:
        return level[m]
    return NEAR * (level[m] + level[m + 1]) + FAR * (level[m - 1] + level[m + 2])


def home_kernel(s, d_ref, xh_ref, xl_ref, own_ref, low_ref, high_ref, out_ref):
    g = across(s, d_ref, xh_ref, xl_ref, 0)
    level = [g[:, o * s.ny : (o + 1) * s.ny] for o in range(s.planes)]
    for z in range(s.nz):
        x = prolonged(s, level, z) + own_ref[z]
        if z < R:
            x += low_ref[z]
        if z >= s.nz - R:
            x += high_ref[z - (s.nz - R)]
        out_ref[z] = x


def last_kernel(s, home_ref, *refs):
    g_refs, out_ref = refs[:-1], refs[-1]
    level = []
    for o in range(s.planes):
        columns = slice(o * s.ny, (o + 1) * s.ny)
        x = g_refs[0][:, columns]
        for ref in g_refs[1:]:
            x += ref[:, columns]
        level.append(x)
    for z in range(s.nz):
        out_ref[z] = home_ref[z] + prolonged(s, level, z)


def call(kernel, name, operands, out_shapes, scalars=(), after=(), through=(), scratch=(), flops=0):
    read, given = len(operands), len(out_shapes)
    operands = list(operands) + list(after) + list(through)
    first = len(operands) - len(through)
    out_shapes = list(out_shapes) + [jax.ShapeDtypeStruct(x.shape, x.dtype) for x in through]

    def spec(i):
        if i >= read:
            return pl.BlockSpec(memory_space=pl.ANY)
        return pl.BlockSpec(memory_space=pltpu.SMEM if i in scalars else pltpu.VMEM)

    moved = sum(x.size * x.dtype.itemsize for x in operands)
    moved += sum(int(np.prod(x.shape)) * x.dtype.itemsize for x in out_shapes)
    return pl.pallas_call(
        kernel,
        name=name,
        out_shape=out_shapes,
        in_specs=[spec(i) for i in range(len(operands))],
        out_specs=[pl.BlockSpec(memory_space=pltpu.VMEM)] * given
        + [pl.BlockSpec(memory_space=pl.ANY)] * len(through),
        input_output_aliases={first + i: given + i for i in range(len(through))},
        scratch_shapes=list(scratch),
        compiler_params=pltpu.CompilerParams(vmem_limit_bytes=VMEM_LIMIT),
        cost_estimate=pl.CostEstimate(flops=flops, bytes_accessed=moved, transcendentals=0),
    )(*operands)


def arrays(*shapes, dtype=F32):
    return [jax.ShapeDtypeStruct(shape, dtype) for shape in shapes]


def fetch(x, **shifts):
    names = tuple(shifts)
    sizes = [lax.axis_size(n) for n in names]
    pairs = []
    for here in np.ndindex(*sizes):
        there = [(h + shifts[n]) % size for h, n, size in zip(here, names, sizes)]
        pairs.append((int(np.ravel_multi_index(there, sizes)), int(np.ravel_multi_index(here, sizes))))
    return lax.ppermute(x, names if len(names) > 1 else names[0], pairs)


def two(*shape):
    return arrays(shape, shape, dtype=BF16)


def shards(charges, widths, amplitudes):
    s = Sizes(*charges.shape, lax.axis_size("gz"), lax.axis_size("gx"), lax.axis_size("gy"))
    c = {k: jnp.asarray(v) for k, v in constants(s).items()}
    brick = (s.nz, s.nx, s.ny)
    side = (R, s.nx, s.ny)
    taps, x0, y0 = call(
        functools.partial(tap_kernel, s), "taps", [widths, amplitudes],
        arrays((8, LANES))
        + arrays((TERMS * s.nx, 3 * s.ext), (2 * LANES, 2 * TERMS * s.ny), dtype=BF16),
        flops=6 * 10**8,
    )
    high_rows = fetch(charges, gx=1)
    low_rows = high_rows if s.gx == 2 else fetch(charges, gx=-1)
    strips = (s.fine_tiles, s.ext, LANES)
    share, first_cells, last_cells = call(
        functools.partial(share_kernel, s), "share", [charges, low_rows, high_rows],
        arrays((s.tiles1, s.rows1, LANES), strips, strips), after=[x0], flops=10**9,
    )
    shares = [share] + [fetch(share, gz=b) for b in range(1, s.gz)]
    left, right = fetch(last_cells, gy=-1), fetch(first_cells, gy=1)
    tiles = s.nz + 2 * s.fine_tiles
    halved = pltpu.VMEM((TERMS, s.nz * s.nx, 2 * LANES), BF16)
    crossed, near_down, near_up = call(
        functools.partial(near_kernel, s), "near",
        [taps, charges, low_rows, high_rows, left, right, x0, y0],
        arrays((TERMS,) + brick, side, side), scalars=(0,),
        scratch=[
            pltpu.VMEM((3 * s.ext, tiles * LANES), BF16), pltpu.VMEM((TERMS * s.nx, tiles * LANES), F32),
            halved, halved,
        ],
        flops=5 * 10**9,
    )
    near_down, near_up = call(
        gate_kernel, "gate", [], [], after=shares[1:], through=[near_down, near_up], flops=10**6,
    )
    size3 = s.tiles3 * s.rows3
    message = (s.base3 + size3, LANES)
    waves, to_low, to_high, level2, coarse = call(
        functools.partial(depth_kernel, s), "depth",
        [taps] + shares + [c[k] for k in ("ry2", "rx2", "ry3", "rx3")],
        arrays((TERMS * s.planes, s.rows1, LANES), message, message, (s.cz[2], s.rows2, LANES), (size3, LANES)),
        scalars=(0,), after=[near_up], scratch=[pltpu.VMEM((s.cz[1], s.rows1, LANES), F32)], flops=2 * 10**9,
    )
    named = ("px1", "px2", "px3", "px3l", "py2", "py3", "py3l", "pz2", "pz3")
    z_taps, y1, y2h, y2l, xh, xl = call(
        functools.partial(matrix_kernel, s), "matrices",
        [widths, amplitudes] + [c[k] for k in named],
        arrays((2 * TERMS * s.zrows, LANES))
        + arrays((LANES, 2 * TERMS * s.ny), dtype=BF16)
        + two(LANES, 2 * TERMS * s.ny) + two(s.cx[0], s.depth_lanes),
        after=[coarse], flops=2 * 10**9,
    )
    (near,) = call(
        functools.partial(own_kernel, s), "own", [taps, crossed], arrays(brick),
        scalars=(0,), after=[z_taps], flops=10**8,
    )
    coarses = [coarse]
    for b in range(1, s.gy):
        coarses.append(fetch({1: to_low, s.gy - 1: to_high}.get(b, coarse), gy=b))
    near_low, near_high = fetch(near_up, gz=-1), fetch(near_down, gz=1)
    (terms,) = call(
        functools.partial(along_kernel, s), "along",
        [z_taps, waves, level2] + coarses + [y1, y2h, y2l],
        arrays((s.depth, s.planes * s.ny)), scalars=(0,), after=[near],
        scratch=[
            pltpu.VMEM((TERMS, s.cz[2], s.rows2, s.ny), F32), pltpu.VMEM((TERMS, s.cz[3], s.rows3, s.ny), F32)
        ], flops=3 * 10**9,
    )
    parts = call(
        functools.partial(away_kernel, s), "away", [terms, xh, xl],
        arrays(*[(s.nx, s.planes * s.ny)] * (s.gx - 1)), flops=10**9,
    )
    parts = [fetch(x, gx=-dx) for dx, x in enumerate(parts, 1)]
    (home,) = call(
        functools.partial(home_kernel, s), "home",
        [terms, xh, xl, near, near_low, near_high], arrays(brick), flops=2 * 10**9,
    )
    (out,) = call(
        functools.partial(last_kernel, s), "last", [home] + parts, arrays(brick), flops=10**9,
    )
    return out


def solution(mesh):
    placed = (P("gz", "gx", "gy"), P(), P())
    return jax.shard_map(
        shards, mesh=mesh, in_specs=placed, out_specs=P("gz", "gx", "gy"), check_vma=False
    )
```

```python
import functools

import jax
import jax.numpy as jnp
import ml_dtypes
import numpy as np
from jax import lax
from jax.experimental import pallas as pl
from jax.experimental.pallas import tpu as pltpu
from jax.sharding import PartitionSpec as P

R = 8
TERMS = 3
LANES = 128
NEAR = 9.0 / 16.0
FAR = -1.0 / 16.0
F32 = jnp.float32
BF16 = jnp.bfloat16
VMEM_LIMIT = 40 * 1024 * 1024


def up8(n):
    return -(-n // 8) * 8


class Sizes:
    def __init__(self, nz, nx, ny, gz, gx, gy):
        self.nz, self.nx, self.ny = nz, nx, ny
        self.gz, self.gx, self.gy = gz, gx, gy
        self.z1, self.x1, self.y1 = nz // 2, nx // 2, ny // 2
        self.z2, self.x2, self.y2 = nz // 4, nx // 4, ny // 4
        self.cz = [nz * gz >> l for l in range(4)]
        self.cx = [nx * gx >> l for l in range(4)]
        self.cy = [ny * gy >> l for l in range(4)]
        self.planes = self.z1 + 3
        self.zrows = up8(self.planes)
        self.rows1 = self.x1
        self.rows2 = up8(self.x2 + 3)
        self.wide1 = self.y1 + 3
        self.wide2 = self.y2 + 5
        self.tiles1 = -(-self.planes * self.wide1 // LANES)
        self.x3, self.y3 = nx // 8, ny // 8
        self.rows3 = up8(self.x3 + 5)
        self.wide3 = self.y3 + 5
        self.tiles3 = -(-self.cz[3] * self.wide3 // LANES)
        self.strip2 = R + 5
        self.per_tile2 = LANES // self.strip2
        self.tiles_s2 = -(-self.cz[2] // self.per_tile2)
        self.strip = R + 3
        self.per_tile = LANES // self.strip
        self.tiles_s = -(-TERMS * self.planes // self.per_tile)
        self.fine_tiles = -(-nz // (LANES // R))
        self.ext = nx + 2 * R
        self.depth = TERMS * (self.rows1 + self.rows2 + self.rows3)
        self.base2 = self.tiles_s * self.rows1
        self.base3 = self.base2 + self.tiles_s2 * self.rows2
        self.depth_lanes = -(-self.depth // LANES) * LANES


def restrict_circle(n):
    m = np.zeros((n // 2, n))
    for i in range(n // 2):
        for d, w in ((0, 1.0), (1, NEAR), (-1, NEAR), (3, FAR), (-3, FAR)):
            m[i, (2 * i + d) % n] += w
    return m


def prolong_circle(n):
    m = np.zeros((2 * n, n))
    for i in range(n):
        m[2 * i, i] += 1.0
        for d, w in ((0, NEAR), (1, NEAR), (-1, FAR), (2, FAR)):
            m[2 * i + 1, (i + d) % n] += w
    return m


def restrict_open(first_in, n_in, first_out, n_out):
    m = np.zeros((n_out, n_in))
    for i in range(n_out):
        for d, w in ((0, 1.0), (1, NEAR), (-1, NEAR), (3, FAR), (-3, FAR)):
            j = 2 * (first_out + i) + d - first_in
            if 0 <= j < n_in:
                m[i, j] = w
    return m


def padded(m, rows, columns):
    out = np.zeros((rows, columns), np.float32)
    out[: m.shape[0], : m.shape[1]] = m
    return out


def exact(m):
    out = m.astype(ml_dtypes.bfloat16)
    assert np.all(out.astype(np.float64) == m)
    return out


def constants(s):
    c = {}
    c["ry2"] = padded(restrict_open(-1, s.wide1, -2, s.wide2).T, LANES, LANES)
    c["rx2"] = padded(restrict_open(0, s.x1, -1, s.x2 + 3), s.rows2, s.rows1)

    def chain(n):
        p1 = prolong_circle(n[1])
        p2 = p1 @ prolong_circle(n[2])
        return p1, p2, p2 @ prolong_circle(n[3])

    def parts(name, m):
        m = m.astype(np.float32)
        c[name] = m.astype(ml_dtypes.bfloat16)
        c[name + "l"] = (m - c[name].astype(np.float32)).astype(ml_dtypes.bfloat16)

    x1, x2, x3 = chain(s.cx)
    c["px1"], c["px2"] = exact(x1), exact(x2)
    parts("px3", x3)
    _, y2, y3 = chain(s.cy)
    c["py2"] = exact(y2[: s.ny].T)
    parts("py3", y3[: s.ny].T)
    z2 = prolong_circle(s.cz[2])
    z3 = z2 @ prolong_circle(s.cz[3])
    own = [(o - 1) % s.cz[1] for o in range(s.planes)]
    c["pz2"] = exact(padded(z2[own], s.zrows, s.cz[2]))
    c["pz3"] = exact(padded(z3[own], s.zrows, s.cz[3]))
    c["ry3"] = padded(restrict_open(-2, s.wide2, -2, s.wide3).T, LANES, LANES)
    c["rx3"] = padded(restrict_open(-1, s.x2 + 3, -2, s.x3 + 5), s.rows3, s.rows2)
    return c


def halves(x):
    high = x.astype(BF16)
    return high, (x - high.astype(F32)).astype(BF16)


def dot(a, b):
    return jnp.dot(a, b, preferred_element_type=F32)


def dot2(a, b):
    high, low = halves(a)
    return dot(high, b) + dot(low, b)


def dot3(a, b_high, b_low):
    high, low = halves(a)
    return dot(high, b_high) + dot(low, b_high) + dot(high, b_low)


def lanes_of(shape):
    return lax.broadcasted_iota(jnp.int32, shape, len(shape) - 1)


def turn(x, by):
    by = by % x.shape[-1]
    return x if by == 0 else pltpu.roll(x, by, x.ndim - 1)


def packed(planes, wide, tiles):
    out = [None] * tiles

    def add(t, x):
        out[t] = x if out[t] is None else out[t] + x

    for k, x in enumerate(planes):
        t, at = divmod(k * wide, LANES)
        moved = turn(x, at)
        if at + wide <= LANES:
            add(t, moved)
        else:
            lane = lanes_of(x.shape)
            add(t, jnp.where(lane >= at, moved, 0.0))
            add(t + 1, jnp.where(lane < at, moved, 0.0))
    return out


def unpacked(tile, k, wide, shift):
    t, at = divmod(k * wide, LANES)
    x = tile(t)
    lane = lanes_of(x.shape)
    if at + wide > LANES:
        x = jnp.where(lane >= at, x, tile(t + 1))
    x = turn(x, shift - at)
    if shift + wide <= LANES:
        return jnp.where((lane >= shift) & (lane < shift + wide), x, 0.0)
    return jnp.where((lane >= shift) | (lane < shift + wide - LANES), x, 0.0)


def open_restriction(shape, in_dim, first_in, first_out, n_out):
    i = lax.broadcasted_iota(jnp.int32, shape, in_dim) + first_in
    o = lax.broadcasted_iota(jnp.int32, shape, 1 - in_dim)
    d = jnp.abs(i - 2 * (o + first_out))
    w = jnp.where(d == 0, 1.0, jnp.where(d == 1, NEAR, jnp.where(d == 3, FAR, 0.0)))
    return jnp.where(o < n_out, w, 0.0).astype(BF16)


def extended(s, b_ref, lo_ref, hi_ref, z):
    return jnp.concatenate([lo_ref[z, s.nx - R :], b_ref[z], hi_ref[z, 0:R]], axis=0)


def share_kernel(s, b_ref, lo_ref, hi_ref, _, m_ref, first_ref, last_ref):
    b = [extended(s, b_ref, lo_ref, hi_ref, z) for z in range(s.nz)]
    planes = []
    for k in range(-1, s.z1 + 2):
        out = None
        for d, w in ((0, 1.0), (1, NEAR), (-1, NEAR), (3, FAR), (-3, FAR)):
            if 0 <= 2 * k + d < s.nz:
                term = b[2 * k + d] if d == 0 else b[2 * k + d] * w
                out = term if out is None else out + term
        planes.append(out)
    high, low = halves(jnp.concatenate(planes, axis=0))
    ry1 = open_restriction((s.ny, LANES), 0, 0, -1, s.wide1)
    rx1 = open_restriction((s.rows1, s.ext), 1, -R, 0, s.x1)
    along = dot(high, ry1) + dot(low, ry1)
    shares = []
    for k in range(s.planes):
        high, low = halves(along[k * s.ext : (k + 1) * s.ext])
        shares.append(dot(rx1, high) + dot(rx1, low))
    for t, x in enumerate(packed(shares, s.wide1, s.tiles1)):
        m_ref[t] = x
    lane = lanes_of((s.ext, LANES))
    group = LANES // R
    for t in range(s.fine_tiles):
        first = last = jnp.zeros((s.ext, LANES), F32)
        for g in range(min(group, s.nz - t * group)):
            x = b[t * group + g]
            at = R * ((g + 1) % group)
            first = jnp.where((lane >= at) & (lane < at + R), turn(x, at), first)
            at = R * g
            last = jnp.where((lane >= at) & (lane < at + R), turn(x, at + R - s.ny), last)
        first_ref[t] = first
        last_ref[t] = last


def rows_of(shape):
    return lax.broadcasted_iota(jnp.int32, shape, 0)


def bell(c, d):
    d = jnp.abs(d)
    return jnp.where(d <= R, jnp.exp(c * d * d), 0.0)


def one(ref, level, t):
    return ref[level : level + 1, t : t + 1]


def spreads(w_ref, levels):
    out = []
    for l in levels:
        w = [one(w_ref, l, t) for t in range(TERMS)]
        out.append([-0.5 / (x * x) for x in w])
    return out


def units(coef, distance, valid):
    shape = (up8(len(coef)), LANES)
    row = rows_of(shape)
    column = jnp.zeros(shape, F32)
    for r, c in enumerate(coef):
        column = jnp.where(row == r, c, column)
    lane = lanes_of(shape)
    d = distance(row, lane).astype(F32)
    total = jnp.sum(jnp.where(valid(row, lane), jnp.exp(2.0 * column * d * d), 0.0), axis=1, keepdims=True)
    unit = 1.0 / jnp.sqrt(total)
    return [unit[r : r + 1] for r in range(len(coef))]


def near_units(coef):
    flat = [c for level in coef for c in level]
    out = units(flat, lambda row, lane: lane - R, lambda row, lane: lane <= 2 * R)
    return [out[i : i + TERMS] for i in range(0, len(out), TERMS)]


def tap_kernel(s, w_ref, a_ref, tap_ref, x0_ref, y0_ref):
    coef = spreads(w_ref, (0, 1))
    unit = near_units(coef)
    d = lanes_of((1, LANES)).astype(F32)
    for t in range(TERMS):
        tap_ref[t : t + 1] = bell(coef[0][t], d) * (unit[0][t] * one(a_ref, 0, t))
        tap_ref[TERMS + t : TERMS + t + 1] = bell(coef[1][t], d) * (unit[1][t] * one(a_ref, 1, t) * 0.25)
    shape = (s.nx, 3 * s.ext)
    lane = lanes_of(shape)
    part = jnp.where(lane < s.ext, 0, jnp.where(lane < 2 * s.ext, 1, 2))
    d = (lane - part * s.ext - R - rows_of(shape)).astype(F32)
    for t in range(TERMS):
        high, low = halves(bell(coef[0][t], d) * unit[0][t])
        x0_ref[t * s.nx : (t + 1) * s.nx] = jnp.where(part == 1, low.astype(F32), high.astype(F32)).astype(BF16)
    shape = (s.ny + 2 * R, s.ny)
    i = rows_of(shape)
    cell = jnp.where(i < s.ny, i, jnp.where(i < s.ny + R, i - s.ny - R, i - R))
    d = (cell - lanes_of(shape)).astype(F32)
    for t in range(TERMS):
        high, low = halves(bell(coef[0][t], d) * unit[0][t])
        at = 2 * t * s.ny
        y0_ref[s.ny + 2 * R :, at : at + 2 * s.ny] = jnp.zeros((2 * LANES - s.ny - 2 * R, 2 * s.ny), BF16)
        y0_ref[: s.ny + 2 * R, at : at + s.ny] = high
        y0_ref[: s.ny + 2 * R, at + s.ny : at + 2 * s.ny] = low


def matrix_kernel(s, w_ref, a_ref, px1, px2, px3, px3l, py2, py3, py3l, pz2, pz3, _,
                  z_ref, y1_ref, y2h_ref, y2l_ref, xh_ref, xl_ref):
    coef = spreads(w_ref, range(4))
    unit = near_units(coef[:3])
    sizes = [s.cx[3], s.cy[3], s.cz[3]]

    def per_row(row):
        return jnp.where(row < TERMS, sizes[0], jnp.where(row < 2 * TERMS, sizes[1], sizes[2]))

    top = units(
        coef[3] * 3,
        lambda row, lane: jnp.minimum(lane, per_row(row) - lane),
        lambda row, lane: lane < per_row(row),
    )
    top_x, top_y, top_z = top[:TERMS], top[TERMS : 2 * TERMS], top[2 * TERMS :]

    def circle(n, d, c, u):
        d = (d & (n - 1)).astype(F32)
        return (bell(c, d) + bell(c, n - d)) * u

    def full_circle(n, d, c, u):
        d = (d & (n - 1)).astype(F32)
        d = jnp.minimum(d, n - d)
        return jnp.exp(c * d * d) * u

    shape = (LANES, s.ny)
    fine = lanes_of(shape)
    d = (rows_of(shape) - (R + 1) - (fine >> 1)).astype(F32)
    even = (fine & 1) == 0
    known = rows_of(shape) < s.y1 + 3 + 2 * R
    two, three = (LANES, s.cy[2]), (LANES, s.cy[3])
    known2 = rows_of(two) < s.y2 + 5 + 2 * R
    known3 = rows_of(three) < (s.gy - 1) * s.y3 + s.wide3
    for t in range(TERMS):
        c = coef[1][t]
        here = bell(c, d)
        between = NEAR * (here + bell(c, d - 1.0)) + FAR * (bell(c, d + 1.0) + bell(c, d - 2.0))
        high, low = halves(jnp.where(known, jnp.where(even, here, between) * unit[1][t], 0.0))
        y1_ref[:, 2 * t * s.ny : (2 * t + 1) * s.ny] = high
        y1_ref[:, (2 * t + 1) * s.ny : (2 * t + 2) * s.ny] = low
        g = circle(s.cy[2], rows_of(two) - (R + 2) - lanes_of(two), coef[2][t], unit[2][t])
        high, low = halves(dot2(jnp.where(known2, g, 0.0), py2[...]))
        y2h_ref[:, t * s.ny : (t + 1) * s.ny] = high
        y2l_ref[:, t * s.ny : (t + 1) * s.ny] = low
        g = full_circle(s.cy[3], rows_of(three) - 2 - lanes_of(three), coef[3][t], top_y[t])
        high, low = halves(dot3(jnp.where(known3, g, 0.0), py3[...], py3l[...]))
        at = (TERMS + t) * s.ny
        y2h_ref[:, at : at + s.ny] = high
        y2l_ref[:, at : at + s.ny] = low

    def terms(level, first, rows, valid, shift, around, u):
        shape = (s.cx[level], s.depth_lanes)
        lane = lanes_of(shape) - first
        column = lane - jnp.where(lane < rows, 0, jnp.where(lane < 2 * rows, rows, 2 * rows))

        def by_term(v):
            return jnp.where(lane < rows, v[0], jnp.where(lane < 2 * rows, v[1], v[2]))

        g = around(s.cx[level], rows_of(shape) - column + shift, by_term(coef[level]), by_term(u))
        high, low = halves(jnp.where((lane >= 0) & (lane < TERMS * rows) & (column < valid), g, 0.0))
        return high, low

    high, low = terms(1, 0, s.rows1, s.rows1, 0, circle, unit[1])
    x = dot(px1[...], high) + dot(px1[...], low)
    high, low = terms(2, TERMS * s.rows1, s.rows2, s.x2 + 3, 1, circle, unit[2])
    x += dot(px2[...], high) + dot(px2[...], low)
    high, low = terms(3, TERMS * (s.rows1 + s.rows2), s.rows3, s.x3 + 5, 2, full_circle, top_x)
    x += dot(px3[...], high) + dot(px3l[...], high) + dot(px3[...], low)
    xh_ref[...], xl_ref[...] = halves(x)
    for t in range(TERMS):
        shape = (s.cz[2], LANES)
        g = circle(s.cz[2], rows_of(shape) - lanes_of(shape), coef[2][t], unit[2][t])
        high, low = halves(g * (one(a_ref, 2, t) * 0.0625))
        z_ref[t * s.zrows : (t + 1) * s.zrows] = dot(pz2[...], high) + dot(pz2[...], low)
        shape = (s.cz[3], LANES)
        g = full_circle(s.cz[3], rows_of(shape) - lanes_of(shape), coef[3][t], top_z[t])
        high, low = halves(g * (one(a_ref, 3, t) * 0.015625))
        z_ref[(TERMS + t) * s.zrows : (TERMS + t + 1) * s.zrows] = dot(pz3[...], high) + dot(pz3[...], low)


def near_kernel(s, tap_ref, b_ref, lo_ref, hi_ref, left_ref, right_ref, x0_ref, y0_ref,
                own_ref, down_ref, up_ref, e_ref, u_ref, eh_ref, el_ref, v_ref):
    group = LANES // R
    tiles = [extended(s, b_ref, lo_ref, hi_ref, z) for z in range(s.nz)]
    tiles += [left_ref[t] for t in range(s.fine_tiles)] + [right_ref[t] for t in range(s.fine_tiles)]
    for i, x in enumerate(tiles):
        high, low = halves(x)
        columns = slice(i * LANES, (i + 1) * LANES)
        e_ref[0 : s.ext, columns] = high
        e_ref[s.ext : 2 * s.ext, columns] = high
        e_ref[2 * s.ext :, columns] = low
    x0 = x0_ref[...]
    for at in range(0, len(tiles) * LANES, 2 * LANES):
        columns = slice(at, min(at + 2 * LANES, len(tiles) * LANES))
        u_ref[:, columns] = dot(x0, e_ref[:, columns])
    lane = lanes_of((TERMS * s.nx, LANES))
    for z in range(s.nz):
        t, g = divmod(z, group)
        left = u_ref[:, (s.nz + t) * LANES : (s.nz + t + 1) * LANES]
        right = u_ref[:, (s.nz + s.fine_tiles + t) * LANES : (s.nz + s.fine_tiles + t + 1) * LANES]
        strips = turn(jnp.where((lane >= R * g) & (lane < R * g + R), left, right), -R * g)
        for at, x in ((0, u_ref[:, z * LANES : (z + 1) * LANES]), (LANES, strips)):
            high, low = halves(x)
            for t in range(TERMS):
                rows = slice(t * s.nx, (t + 1) * s.nx)
                eh_ref[t, z * s.nx : (z + 1) * s.nx, at : at + LANES] = high[rows]
                el_ref[t, z * s.nx : (z + 1) * s.nx, at : at + LANES] = low[rows]
    step = 4 * s.nx
    for t in range(TERMS):
        at = 2 * t * s.ny
        y0, y0h = y0_ref[:, at : at + 2 * s.ny], y0_ref[:, at : at + s.ny]
        for first in range(0, s.nz * s.nx, step):
            both = dot(eh_ref[t, first : first + step], y0)
            v = both[:, : s.ny] + both[:, s.ny :] + dot(el_ref[t, first : first + step], y0h)
            for q in range(step // s.nx):
                v_ref[t, first // s.nx + q] = v[q * s.nx : (q + 1) * s.nx]

    def depth(r, _):
        rows = pl.ds(pl.multiple_of(r * 8, 8), 8)
        taps = [[tap_ref[t, d] for d in range(R + 1)] for t in range(TERMS)]
        for first in range(-R, s.nz + R, R):
            acc = [None] * R
            for t in range(TERMS):
                for z in range(max(0, first - R), min(s.nz, first + 2 * R)):
                    v = v_ref[t, z, rows]
                    for o in range(R):
                        d = abs(first + o - z)
                        if d <= R:
                            term = v * taps[t][d]
                            acc[o] = term if acc[o] is None else acc[o] + term
            for o in range(R):
                if first < 0:
                    down_ref[o, rows] = acc[o]
                elif first >= s.nz:
                    up_ref[o, rows] = acc[o]
                else:
                    own_ref[first + o, rows] = acc[o]
        return 0

    lax.fori_loop(0, s.nx // 8, depth, 0)


def depth_kernel(s, tap_ref, *refs):
    m_refs = refs[: s.gz]
    ry2_ref, rx2_ref, ry3_ref, rx3_ref, _, w_ref, down_ref, up_ref, c2_ref, c3_ref, c_ref = refs[s.gz :]
    n = s.cz[1]
    parts = [[] for _ in range(n)]
    for b in range(s.gz):
        for k in range(s.planes):
            parts[(b * s.z1 + k - 1) % n].append((b, k))
    for z in range(n):
        out = None
        for b, k in parts[z]:
            x = unpacked(lambda t, b=b: m_refs[b][t], k, s.wide1, 0)
            out = x if out is None else out + x
        c_ref[z] = out
    lane = lanes_of((s.rows1, LANES))
    down = [jnp.zeros((s.rows1, LANES), F32)] * s.tiles_s
    up = list(down)
    for o in range(s.planes):
        sums = [c_ref[(o - 1) % n]]
        sums += [c_ref[(o - 1 + d) % n] + c_ref[(o - 1 - d) % n] for d in range(1, R + 1)]
        for t in range(TERMS):
            x = sums[0] * tap_ref[TERMS + t, 0]
            for d in range(1, R + 1):
                x += sums[d] * tap_ref[TERMS + t, d]
            k = t * s.planes + o
            w_ref[k] = x
            tile, slot = divmod(k, s.per_tile)
            at = slot * s.strip
            here = (lane >= at) & (lane < at + s.strip)
            down[tile] = jnp.where(here, turn(x, at), down[tile])
            up[tile] = jnp.where(here, turn(x, at - (s.wide1 - s.strip)), up[tile])

    def restricted(planes, y_ref, x_ref):
        n, rows = len(planes), planes[0].shape[0]
        coarse = []
        for j in range(n // 2):
            at = lambda d: planes[(2 * j + d) % n]
            coarse.append(at(0) + NEAR * (at(1) + at(-1)) + FAR * (at(3) + at(-3)))
        along = dot2(jnp.concatenate(coarse, axis=0), y_ref[...].astype(BF16))
        x = x_ref[...].astype(BF16)
        out = []
        for j in range(n // 2):
            high, low = halves(along[j * rows : (j + 1) * rows])
            out.append(dot(x, high) + dot(x, low))
        return out

    level2 = restricted([c_ref[z] for z in range(n)], ry2_ref, rx2_ref)
    level3 = restricted(level2, ry3_ref, rx3_ref)
    for t in range(s.tiles_s):
        down_ref[t * s.rows1 : (t + 1) * s.rows1] = down[t]
        up_ref[t * s.rows1 : (t + 1) * s.rows1] = up[t]
    lane = lanes_of((s.rows2, LANES))
    down = [jnp.zeros((s.rows2, LANES), F32)] * s.tiles_s2
    up = list(down)
    for j, x in enumerate(level2):
        c2_ref[j] = x
        tile, slot = divmod(j, s.per_tile2)
        at = slot * s.strip2
        here = (lane >= at) & (lane < at + s.strip2)
        down[tile] = jnp.where(here, turn(x, at), down[tile])
        up[tile] = jnp.where(here, turn(x, at - (s.wide2 - s.strip2)), up[tile])
    for t in range(s.tiles_s2):
        rows = slice(s.base2 + t * s.rows2, s.base2 + (t + 1) * s.rows2)
        down_ref[rows] = down[t]
        up_ref[rows] = up[t]
    for t, x in enumerate(packed(level3, s.wide3, s.tiles3)):
        c3_ref[t * s.rows3 : (t + 1) * s.rows3] = x
        for ref in (down_ref, up_ref):
            ref[s.base3 + t * s.rows3 : s.base3 + (t + 1) * s.rows3] = x


def along_kernel(s, z_ref, w_ref, c2_ref, *refs):
    c3_refs = refs[: s.gy]
    y1_ref, y2h_ref, y2l_ref, d_ref, y2_ref, y3_ref = refs[s.gy :]
    lane = lanes_of((s.rows1, LANES))
    above, below = c3_refs[1], c3_refs[-1]
    end = s.y1 + R
    for t in range(TERMS):
        cells = []
        for o in range(s.planes):
            k = t * s.planes + o
            tile, slot = divmod(k, s.per_tile)
            rows = slice(tile * s.rows1, (tile + 1) * s.rows1)
            at = slot * s.strip
            x = turn(w_ref[k], R)
            x += jnp.where(lane < s.strip, turn(below[rows], -at), 0.0)
            x += jnp.where((lane >= end) & (lane < end + s.strip), turn(above[rows], end - at), 0.0)
            cells.append(x)
        high, low = halves(jnp.concatenate(cells, axis=0))
        at = 2 * t * s.ny
        both = dot(high, y1_ref[:, at : at + 2 * s.ny])
        out = both[:, : s.ny] + both[:, s.ny :] + dot(low, y1_ref[:, at : at + s.ny])
        for o in range(s.planes):
            d_ref[t * s.rows1 : (t + 1) * s.rows1, o * s.ny : (o + 1) * s.ny] = out[o * s.rows1 : (o + 1) * s.rows1]
    lane = lanes_of((s.rows2, LANES))
    end = s.y2 + R
    cells = []
    for j in range(s.cz[2]):
        tile, slot = divmod(j, s.per_tile2)
        rows = slice(s.base2 + tile * s.rows2, s.base2 + (tile + 1) * s.rows2)
        at = slot * s.strip2
        x = turn(c2_ref[j], R)
        x += jnp.where(lane < s.strip2, turn(below[rows], -at), 0.0)
        x += jnp.where((lane >= end) & (lane < end + s.strip2), turn(above[rows], end - at), 0.0)
        cells.append(x)
    cells3 = []
    for j in range(s.cz[3]):
        out = None
        for b in range(s.gy):
            first = s.base3 if c3_refs[b].shape[0] > s.tiles3 * s.rows3 else 0
            tile = lambda t, b=b, f=first: c3_refs[b][f + t * s.rows3 : f + (t + 1) * s.rows3]
            x = unpacked(tile, j, s.wide3, b * s.y3)
            out = x if out is None else out + x
        cells3.append(out)
    at = TERMS * s.rows1
    for q, (x, rows, ref) in enumerate(((cells, s.rows2, y2_ref), (cells3, s.rows3, y3_ref))):
        columns = slice(q * TERMS * s.ny, (q + 1) * TERMS * s.ny)
        y = dot3(jnp.concatenate(x, axis=0), y2h_ref[:, columns], y2l_ref[:, columns])
        for t in range(TERMS):
            for j in range(len(x)):
                ref[t, j] = y[j * rows : (j + 1) * rows, t * s.ny : (t + 1) * s.ny]
        for o in range(s.planes):
            for t in range(TERMS):
                scale = [z_ref[(q * TERMS + t) * s.zrows + o, j] for j in range(len(x))]
                out = ref[t, 0] * scale[0]
                for j in range(1, len(x)):
                    out += ref[t, j] * scale[j]
                d_ref[at + t * rows : at + (t + 1) * rows, o * s.ny : (o + 1) * s.ny] = out
        at += TERMS * rows


def across(s, d_ref, xh_ref, xl_ref, shift):
    rows = slice(shift * s.nx, (shift + 1) * s.nx)
    high, low = halves(d_ref[...])
    xh, xl = xh_ref[rows, : s.depth], xl_ref[rows, : s.depth]
    return dot(xh, high) + dot(xl, high) + dot(xh, low)


def away_kernel(s, d_ref, xh_ref, xl_ref, *g_refs):
    for shift, ref in enumerate(g_refs):
        ref[...] = across(s, d_ref, xh_ref, xl_ref, shift + 1)


def prolonged(s, level, z):
    m = z // 2 + 1
    if z % 2 == 0:
        return level[m]
    return NEAR * (level[m] + level[m + 1]) + FAR * (level[m - 1] + level[m + 2])


def home_kernel(s, d_ref, xh_ref, xl_ref, own_ref, low_ref, high_ref, out_ref):
    g = across(s, d_ref, xh_ref, xl_ref, 0)
    level = [g[:, o * s.ny : (o + 1) * s.ny] for o in range(s.planes)]
    for z in range(s.nz):
        x = prolonged(s, level, z) + own_ref[z]
        if z < R:
            x += low_ref[z]
        if z >= s.nz - R:
            x += high_ref[z - (s.nz - R)]
        out_ref[z] = x


def last_kernel(s, home_ref, *refs):
    *g_refs, out_ref, sum_ref, sems = refs
    level = []
    for o in range(s.planes):
        columns = slice(o * s.ny, (o + 1) * s.ny)
        x = g_refs[0][:, columns]
        for ref in g_refs[1:]:
            x += ref[:, columns]
        level.append(x)
    copies = []
    for first in range(0, s.nz, 4):
        for z in range(first, first + 4):
            sum_ref[z] = home_ref[z] + prolonged(s, level, z)
        planes = slice(first, first + 4)
        copies.append(pltpu.make_async_copy(sum_ref.at[planes], out_ref.at[planes], sems.at[first // 4]))
        copies[-1].start()
    for copy in copies:
        copy.wait()


def call(kernel, name, operands, out_shapes, scalars=(), after=(), scratch=(), flops=0, out_space=pltpu.VMEM):
    operands = list(operands) + list(after)

    def spec(i):
        if i >= len(operands) - len(after):
            return pl.BlockSpec(memory_space=pl.ANY)
        return pl.BlockSpec(memory_space=pltpu.SMEM if i in scalars else pltpu.VMEM)

    moved = sum(x.size * x.dtype.itemsize for x in operands)
    moved += sum(int(np.prod(x.shape)) * x.dtype.itemsize for x in out_shapes)
    return pl.pallas_call(
        kernel,
        name=name,
        out_shape=out_shapes,
        in_specs=[spec(i) for i in range(len(operands))],
        out_specs=[pl.BlockSpec(memory_space=out_space)] * len(out_shapes),
        scratch_shapes=list(scratch),
        compiler_params=pltpu.CompilerParams(vmem_limit_bytes=VMEM_LIMIT),
        cost_estimate=pl.CostEstimate(flops=flops, bytes_accessed=moved, transcendentals=0),
    )(*operands)


def arrays(*shapes, dtype=F32):
    return [jax.ShapeDtypeStruct(shape, dtype) for shape in shapes]


def fetch(x, **shifts):
    names = tuple(shifts)
    sizes = [lax.axis_size(n) for n in names]
    pairs = []
    for here in np.ndindex(*sizes):
        there = [(h + shifts[n]) % size for h, n, size in zip(here, names, sizes)]
        pairs.append((int(np.ravel_multi_index(there, sizes)), int(np.ravel_multi_index(here, sizes))))
    return lax.ppermute(x, names if len(names) > 1 else names[0], pairs)


def two(*shape):
    return arrays(shape, shape, dtype=BF16)


def shards(charges, widths, amplitudes):
    s = Sizes(*charges.shape, lax.axis_size("gz"), lax.axis_size("gx"), lax.axis_size("gy"))
    c = {k: jnp.asarray(v) for k, v in constants(s).items()}
    brick = (s.nz, s.nx, s.ny)
    side = (R, s.nx, s.ny)
    taps, x0, y0 = call(
        functools.partial(tap_kernel, s), "taps", [widths, amplitudes],
        arrays((8, LANES))
        + arrays((TERMS * s.nx, 3 * s.ext), (2 * LANES, 2 * TERMS * s.ny), dtype=BF16),
        flops=6 * 10**8,
    )
    high_rows = fetch(charges, gx=1)
    low_rows = high_rows if s.gx == 2 else fetch(charges, gx=-1)
    strips = (s.fine_tiles, s.ext, LANES)
    share, first_cells, last_cells = call(
        functools.partial(share_kernel, s), "share", [charges, low_rows, high_rows],
        arrays((s.tiles1, s.rows1, LANES), strips, strips), after=[x0], flops=10**9,
    )
    shares = [share] + [fetch(share, gz=b) for b in range(1, s.gz)]
    left, right = fetch(last_cells, gy=-1), fetch(first_cells, gy=1)
    tiles = s.nz + 2 * s.fine_tiles
    halved = pltpu.VMEM((TERMS, s.nz * s.nx, 2 * LANES), BF16)
    near, near_down, near_up = call(
        functools.partial(near_kernel, s), "near",
        [taps, charges, low_rows, high_rows, left, right, x0, y0],
        arrays(brick, side, side), scalars=(0,),
        scratch=[
            pltpu.VMEM((3 * s.ext, tiles * LANES), BF16), pltpu.VMEM((TERMS * s.nx, tiles * LANES), F32),
            halved, halved, pltpu.VMEM((TERMS,) + brick, F32),
        ],
        flops=5 * 10**9,
    )
    size3 = s.tiles3 * s.rows3
    message = (s.base3 + size3, LANES)
    waves, to_low, to_high, level2, coarse = call(
        functools.partial(depth_kernel, s), "depth",
        [taps] + shares + [c[k] for k in ("ry2", "rx2", "ry3", "rx3")],
        arrays((TERMS * s.planes, s.rows1, LANES), message, message, (s.cz[2], s.rows2, LANES), (size3, LANES)),
        scalars=(0,), after=[near], scratch=[pltpu.VMEM((s.cz[1], s.rows1, LANES), F32)], flops=2 * 10**9,
    )
    named = ("px1", "px2", "px3", "px3l", "py2", "py3", "py3l", "pz2", "pz3")
    z_taps, y1, y2h, y2l, xh, xl = call(
        functools.partial(matrix_kernel, s), "matrices",
        [widths, amplitudes] + [c[k] for k in named],
        arrays((2 * TERMS * s.zrows, LANES))
        + arrays((LANES, 2 * TERMS * s.ny), dtype=BF16)
        + two(LANES, 2 * TERMS * s.ny) + two(s.cx[0], s.depth_lanes),
        after=[coarse], flops=2 * 10**9,
    )
    coarses = [coarse]
    for b in range(1, s.gy):
        coarses.append(fetch({1: to_low, s.gy - 1: to_high}.get(b, coarse), gy=b))
    near_low, near_high = fetch(near_up, gz=-1), fetch(near_down, gz=1)
    (terms,) = call(
        functools.partial(along_kernel, s), "along",
        [z_taps, waves, level2] + coarses + [y1, y2h, y2l],
        arrays((s.depth, s.planes * s.ny)), scalars=(0,),
        scratch=[
            pltpu.VMEM((TERMS, s.cz[2], s.rows2, s.ny), F32), pltpu.VMEM((TERMS, s.cz[3], s.rows3, s.ny), F32)
        ], flops=3 * 10**9,
    )
    parts = call(
        functools.partial(away_kernel, s), "away", [terms, xh, xl],
        arrays(*[(s.nx, s.planes * s.ny)] * (s.gx - 1)), flops=10**9,
    )
    parts = [fetch(x, gx=-dx) for dx, x in enumerate(parts, 1)]
    (home,) = call(
        functools.partial(home_kernel, s), "home",
        [terms, xh, xl, near, near_low, near_high], arrays(brick), flops=2 * 10**9,
    )
    (out,) = call(
        functools.partial(last_kernel, s), "last", [home] + parts, arrays(brick), flops=10**9,
        scratch=[pltpu.VMEM(brick, F32), pltpu.SemaphoreType.DMA((s.nz // 4,))], out_space=pl.ANY,
    )
    return out


def solution(mesh):
    placed = (P("gz", "gx", "gy"), P(), P())
    return jax.shard_map(
        shards, mesh=mesh, in_specs=placed, out_specs=P("gz", "gx", "gy"), check_vma=False
    )
```

```python
import functools

import jax
import jax.numpy as jnp
import ml_dtypes
import numpy as np
from jax import lax
from jax.experimental import pallas as pl
from jax.experimental.pallas import tpu as pltpu
from jax.sharding import PartitionSpec as P

R = 8
TERMS = 3
LANES = 128
NEAR = 9.0 / 16.0
FAR = -1.0 / 16.0
F32 = jnp.float32
BF16 = jnp.bfloat16
VMEM_LIMIT = 40 * 1024 * 1024


def up8(n):
    return -(-n // 8) * 8


class Sizes:
    def __init__(self, nz, nx, ny, gz, gx, gy):
        self.nz, self.nx, self.ny = nz, nx, ny
        self.gz, self.gx, self.gy = gz, gx, gy
        self.z1, self.x1, self.y1 = nz // 2, nx // 2, ny // 2
        self.z2, self.x2, self.y2 = nz // 4, nx // 4, ny // 4
        self.cz = [nz * gz >> l for l in range(4)]
        self.cx = [nx * gx >> l for l in range(4)]
        self.cy = [ny * gy >> l for l in range(4)]
        self.planes = self.z1 + 3
        self.zrows = up8(self.planes)
        self.rows1 = self.x1
        self.rows2 = up8(self.x2 + 3)
        self.wide1 = self.y1 + 3
        self.wide2 = self.y2 + 5
        self.tiles1 = -(-self.planes * self.wide1 // LANES)
        self.x3, self.y3 = nx // 8, ny // 8
        self.rows3 = up8(self.x3 + 5)
        self.wide3 = self.y3 + 5
        self.tiles3 = -(-self.cz[3] * self.wide3 // LANES)
        self.strip2 = R + 5
        self.per_tile2 = LANES // self.strip2
        self.tiles_s2 = -(-self.cz[2] // self.per_tile2)
        self.strip = R + 3
        self.per_tile = LANES // self.strip
        self.tiles_s = -(-TERMS * self.planes // self.per_tile)
        self.fine_tiles = -(-nz // (LANES // R))
        self.ext = nx + 2 * R
        self.depth = TERMS * (self.rows1 + self.rows2 + self.rows3)
        self.base2 = self.tiles_s * self.rows1
        self.base3 = self.base2 + self.tiles_s2 * self.rows2
        self.depth_lanes = -(-self.depth // LANES) * LANES


def restrict_circle(n):
    m = np.zeros((n // 2, n))
    for i in range(n // 2):
        for d, w in ((0, 1.0), (1, NEAR), (-1, NEAR), (3, FAR), (-3, FAR)):
            m[i, (2 * i + d) % n] += w
    return m


def prolong_circle(n):
    m = np.zeros((2 * n, n))
    for i in range(n):
        m[2 * i, i] += 1.0
        for d, w in ((0, NEAR), (1, NEAR), (-1, FAR), (2, FAR)):
            m[2 * i + 1, (i + d) % n] += w
    return m


def restrict_open(first_in, n_in, first_out, n_out):
    m = np.zeros((n_out, n_in))
    for i in range(n_out):
        for d, w in ((0, 1.0), (1, NEAR), (-1, NEAR), (3, FAR), (-3, FAR)):
            j = 2 * (first_out + i) + d - first_in
            if 0 <= j < n_in:
                m[i, j] = w
    return m


def padded(m, rows, columns):
    out = np.zeros((rows, columns), np.float32)
    out[: m.shape[0], : m.shape[1]] = m
    return out


def exact(m):
    out = m.astype(ml_dtypes.bfloat16)
    assert np.all(out.astype(np.float64) == m)
    return out


def constants(s):
    c = {}
    c["ry2"] = padded(restrict_open(-1, s.wide1, -2, s.wide2).T, LANES, LANES)
    c["rx2"] = padded(restrict_open(0, s.x1, -1, s.x2 + 3), s.rows2, s.rows1)

    def chain(n):
        p1 = prolong_circle(n[1])
        p2 = p1 @ prolong_circle(n[2])
        return p1, p2, p2 @ prolong_circle(n[3])

    def parts(name, m):
        m = m.astype(np.float32)
        c[name] = m.astype(ml_dtypes.bfloat16)
        c[name + "l"] = (m - c[name].astype(np.float32)).astype(ml_dtypes.bfloat16)

    x1, x2, x3 = chain(s.cx)
    c["px1"], c["px2"] = exact(x1), exact(x2)
    parts("px3", x3)
    _, y2, y3 = chain(s.cy)
    c["py2"] = exact(y2[: s.ny].T)
    parts("py3", y3[: s.ny].T)
    z2 = prolong_circle(s.cz[2])
    z3 = z2 @ prolong_circle(s.cz[3])
    own = [(o - 1) % s.cz[1] for o in range(s.planes)]
    c["pz2"] = exact(padded(z2[own], s.zrows, s.cz[2]))
    c["pz3"] = exact(padded(z3[own], s.zrows, s.cz[3]))
    c["ry3"] = padded(restrict_open(-2, s.wide2, -2, s.wide3).T, LANES, LANES)
    c["rx3"] = padded(restrict_open(-1, s.x2 + 3, -2, s.x3 + 5), s.rows3, s.rows2)
    return c


def halves(x):
    high = x.astype(BF16)
    return high, (x - high.astype(F32)).astype(BF16)


def dot(a, b):
    return jnp.dot(a, b, preferred_element_type=F32)


def dot2(a, b):
    high, low = halves(a)
    return dot(high, b) + dot(low, b)


def dot3(a, b_high, b_low):
    high, low = halves(a)
    return dot(high, b_high) + dot(low, b_high) + dot(high, b_low)


def lanes_of(shape):
    return lax.broadcasted_iota(jnp.int32, shape, len(shape) - 1)


def turn(x, by):
    by = by % x.shape[-1]
    return x if by == 0 else pltpu.roll(x, by, x.ndim - 1)


def packed(planes, wide, tiles):
    out = [None] * tiles

    def add(t, x):
        out[t] = x if out[t] is None else out[t] + x

    for k, x in enumerate(planes):
        t, at = divmod(k * wide, LANES)
        moved = turn(x, at)
        if at + wide <= LANES:
            add(t, moved)
        else:
            lane = lanes_of(x.shape)
            add(t, jnp.where(lane >= at, moved, 0.0))
            add(t + 1, jnp.where(lane < at, moved, 0.0))
    return out


def unpacked(tile, k, wide, shift):
    t, at = divmod(k * wide, LANES)
    x = tile(t)
    lane = lanes_of(x.shape)
    if at + wide > LANES:
        x = jnp.where(lane >= at, x, tile(t + 1))
    x = turn(x, shift - at)
    if shift + wide <= LANES:
        return jnp.where((lane >= shift) & (lane < shift + wide), x, 0.0)
    return jnp.where((lane >= shift) | (lane < shift + wide - LANES), x, 0.0)


def open_restriction(shape, in_dim, first_in, first_out, n_out):
    i = lax.broadcasted_iota(jnp.int32, shape, in_dim) + first_in
    o = lax.broadcasted_iota(jnp.int32, shape, 1 - in_dim)
    d = jnp.abs(i - 2 * (o + first_out))
    w = jnp.where(d == 0, 1.0, jnp.where(d == 1, NEAR, jnp.where(d == 3, FAR, 0.0)))
    return jnp.where(o < n_out, w, 0.0).astype(BF16)


def extended(s, b_ref, lo_ref, hi_ref, z):
    return jnp.concatenate([lo_ref[z, s.nx - R :], b_ref[z], hi_ref[z, 0:R]], axis=0)


def share_kernel(s, b_ref, lo_ref, hi_ref, _, m_ref, first_ref, last_ref):
    b = [extended(s, b_ref, lo_ref, hi_ref, z) for z in range(s.nz)]
    planes = []
    for k in range(-1, s.z1 + 2):
        out = None
        for d, w in ((0, 1.0), (1, NEAR), (-1, NEAR), (3, FAR), (-3, FAR)):
            if 0 <= 2 * k + d < s.nz:
                term = b[2 * k + d] if d == 0 else b[2 * k + d] * w
                out = term if out is None else out + term
        planes.append(out)
    high, low = halves(jnp.concatenate(planes, axis=0))
    ry1 = open_restriction((s.ny, LANES), 0, 0, -1, s.wide1)
    rx1 = open_restriction((s.rows1, s.ext), 1, -R, 0, s.x1)
    along = dot(high, ry1) + dot(low, ry1)
    shares = []
    for k in range(s.planes):
        high, low = halves(along[k * s.ext : (k + 1) * s.ext])
        shares.append(dot(rx1, high) + dot(rx1, low))
    for t, x in enumerate(packed(shares, s.wide1, s.tiles1)):
        m_ref[t] = x
    lane = lanes_of((s.ext, LANES))
    group = LANES // R
    for t in range(s.fine_tiles):
        first = last = jnp.zeros((s.ext, LANES), F32)
        for g in range(min(group, s.nz - t * group)):
            x = b[t * group + g]
            at = R * ((g + 1) % group)
            first = jnp.where((lane >= at) & (lane < at + R), turn(x, at), first)
            at = R * g
            last = jnp.where((lane >= at) & (lane < at + R), turn(x, at + R - s.ny), last)
        first_ref[t] = first
        last_ref[t] = last


def rows_of(shape):
    return lax.broadcasted_iota(jnp.int32, shape, 0)


def bell(c, d):
    d = jnp.abs(d)
    return jnp.where(d <= R, jnp.exp(c * d * d), 0.0)


def one(ref, level, t):
    return ref[level : level + 1, t : t + 1]


def spreads(w_ref, levels):
    out = []
    for l in levels:
        w = [one(w_ref, l, t) for t in range(TERMS)]
        out.append([-0.5 / (x * x) for x in w])
    return out


def units(coef, distance, valid):
    shape = (up8(len(coef)), LANES)
    row = rows_of(shape)
    column = jnp.zeros(shape, F32)
    for r, c in enumerate(coef):
        column = jnp.where(row == r, c, column)
    lane = lanes_of(shape)
    d = distance(row, lane).astype(F32)
    total = jnp.sum(jnp.where(valid(row, lane), jnp.exp(2.0 * column * d * d), 0.0), axis=1, keepdims=True)
    unit = 1.0 / jnp.sqrt(total)
    return [unit[r : r + 1] for r in range(len(coef))]


def near_units(coef):
    flat = [c for level in coef for c in level]
    out = units(flat, lambda row, lane: lane - R, lambda row, lane: lane <= 2 * R)
    return [out[i : i + TERMS] for i in range(0, len(out), TERMS)]


def tap_kernel(s, w_ref, a_ref, tap_ref, x0_ref, y0_ref):
    coef = spreads(w_ref, (0, 1))
    unit = near_units(coef)
    d = lanes_of((1, LANES)).astype(F32)
    for t in range(TERMS):
        tap_ref[t : t + 1] = bell(coef[0][t], d) * (unit[0][t] * one(a_ref, 0, t))
        tap_ref[TERMS + t : TERMS + t + 1] = bell(coef[1][t], d) * (unit[1][t] * one(a_ref, 1, t) * 0.25)
    shape = (s.nx, 3 * s.ext)
    lane = lanes_of(shape)
    part = jnp.where(lane < s.ext, 0, jnp.where(lane < 2 * s.ext, 1, 2))
    d = (lane - part * s.ext - R - rows_of(shape)).astype(F32)
    for t in range(TERMS):
        high, low = halves(bell(coef[0][t], d) * unit[0][t])
        x0_ref[t * s.nx : (t + 1) * s.nx] = jnp.where(part == 1, low.astype(F32), high.astype(F32)).astype(BF16)
    shape = (s.ny + 2 * R, s.ny)
    i = rows_of(shape)
    cell = jnp.where(i < s.ny, i, jnp.where(i < s.ny + R, i - s.ny - R, i - R))
    d = (cell - lanes_of(shape)).astype(F32)
    for t in range(TERMS):
        high, low = halves(bell(coef[0][t], d) * unit[0][t])
        at = 2 * t * s.ny
        y0_ref[s.ny + 2 * R :, at : at + 2 * s.ny] = jnp.zeros((2 * LANES - s.ny - 2 * R, 2 * s.ny), BF16)
        y0_ref[: s.ny + 2 * R, at : at + s.ny] = high
        y0_ref[: s.ny + 2 * R, at + s.ny : at + 2 * s.ny] = low


def matrix_kernel(s, w_ref, a_ref, px1, px2, px3, px3l, py2, py3, py3l, pz2, pz3, _,
                  z_ref, y1_ref, y2h_ref, y2l_ref, xh_ref, xl_ref):
    coef = spreads(w_ref, range(4))
    unit = near_units(coef[:3])
    sizes = [s.cx[3], s.cy[3], s.cz[3]]

    def per_row(row):
        return jnp.where(row < TERMS, sizes[0], jnp.where(row < 2 * TERMS, sizes[1], sizes[2]))

    top = units(
        coef[3] * 3,
        lambda row, lane: jnp.minimum(lane, per_row(row) - lane),
        lambda row, lane: lane < per_row(row),
    )
    top_x, top_y, top_z = top[:TERMS], top[TERMS : 2 * TERMS], top[2 * TERMS :]

    def circle(n, d, c, u):
        d = (d & (n - 1)).astype(F32)
        return (bell(c, d) + bell(c, n - d)) * u

    def full_circle(n, d, c, u):
        d = (d & (n - 1)).astype(F32)
        d = jnp.minimum(d, n - d)
        return jnp.exp(c * d * d) * u

    shape = (LANES, s.ny)
    fine = lanes_of(shape)
    d = (rows_of(shape) - (R + 1) - (fine >> 1)).astype(F32)
    even = (fine & 1) == 0
    known = rows_of(shape) < s.y1 + 3 + 2 * R
    two, three = (LANES, s.cy[2]), (LANES, s.cy[3])
    known2 = rows_of(two) < s.y2 + 5 + 2 * R
    known3 = rows_of(three) < (s.gy - 1) * s.y3 + s.wide3
    for t in range(TERMS):
        c = coef[1][t]
        here = bell(c, d)
        between = NEAR * (here + bell(c, d - 1.0)) + FAR * (bell(c, d + 1.0) + bell(c, d - 2.0))
        high, low = halves(jnp.where(known, jnp.where(even, here, between) * unit[1][t], 0.0))
        y1_ref[:, 2 * t * s.ny : (2 * t + 1) * s.ny] = high
        y1_ref[:, (2 * t + 1) * s.ny : (2 * t + 2) * s.ny] = low
        g = circle(s.cy[2], rows_of(two) - (R + 2) - lanes_of(two), coef[2][t], unit[2][t])
        high, low = halves(dot2(jnp.where(known2, g, 0.0), py2[...]))
        y2h_ref[:, t * s.ny : (t + 1) * s.ny] = high
        y2l_ref[:, t * s.ny : (t + 1) * s.ny] = low
        g = full_circle(s.cy[3], rows_of(three) - 2 - lanes_of(three), coef[3][t], top_y[t])
        high, low = halves(dot3(jnp.where(known3, g, 0.0), py3[...], py3l[...]))
        at = (TERMS + t) * s.ny
        y2h_ref[:, at : at + s.ny] = high
        y2l_ref[:, at : at + s.ny] = low

    def terms(level, first, rows, valid, shift, around, u):
        shape = (s.cx[level], s.depth_lanes)
        lane = lanes_of(shape) - first
        column = lane - jnp.where(lane < rows, 0, jnp.where(lane < 2 * rows, rows, 2 * rows))

        def by_term(v):
            return jnp.where(lane < rows, v[0], jnp.where(lane < 2 * rows, v[1], v[2]))

        g = around(s.cx[level], rows_of(shape) - column + shift, by_term(coef[level]), by_term(u))
        high, low = halves(jnp.where((lane >= 0) & (lane < TERMS * rows) & (column < valid), g, 0.0))
        return high, low

    high, low = terms(1, 0, s.rows1, s.rows1, 0, circle, unit[1])
    x = dot(px1[...], high) + dot(px1[...], low)
    high, low = terms(2, TERMS * s.rows1, s.rows2, s.x2 + 3, 1, circle, unit[2])
    x += dot(px2[...], high) + dot(px2[...], low)
    high, low = terms(3, TERMS * (s.rows1 + s.rows2), s.rows3, s.x3 + 5, 2, full_circle, top_x)
    x += dot(px3[...], high) + dot(px3l[...], high) + dot(px3[...], low)
    xh_ref[...], xl_ref[...] = halves(x)
    for t in range(TERMS):
        shape = (s.cz[2], LANES)
        g = circle(s.cz[2], rows_of(shape) - lanes_of(shape), coef[2][t], unit[2][t])
        high, low = halves(g * (one(a_ref, 2, t) * 0.0625))
        z_ref[t * s.zrows : (t + 1) * s.zrows] = dot(pz2[...], high) + dot(pz2[...], low)
        shape = (s.cz[3], LANES)
        g = full_circle(s.cz[3], rows_of(shape) - lanes_of(shape), coef[3][t], top_z[t])
        high, low = halves(g * (one(a_ref, 3, t) * 0.015625))
        z_ref[(TERMS + t) * s.zrows : (TERMS + t + 1) * s.zrows] = dot(pz3[...], high) + dot(pz3[...], low)


def near_kernel(s, tap_ref, b_ref, lo_ref, hi_ref, left_ref, right_ref, x0_ref, y0_ref,
                own_ref, down_ref, up_ref, e_ref, u_ref, eh_ref, el_ref, v_ref):
    group = LANES // R
    tiles = [extended(s, b_ref, lo_ref, hi_ref, z) for z in range(s.nz)]
    tiles += [left_ref[t] for t in range(s.fine_tiles)] + [right_ref[t] for t in range(s.fine_tiles)]
    for i, x in enumerate(tiles):
        high, low = halves(x)
        columns = slice(i * LANES, (i + 1) * LANES)
        e_ref[0 : s.ext, columns] = high
        e_ref[s.ext : 2 * s.ext, columns] = high
        e_ref[2 * s.ext :, columns] = low
    x0 = x0_ref[...]
    for at in range(0, len(tiles) * LANES, 2 * LANES):
        columns = slice(at, min(at + 2 * LANES, len(tiles) * LANES))
        u_ref[:, columns] = dot(x0, e_ref[:, columns])
    lane = lanes_of((TERMS * s.nx, LANES))
    for z in range(s.nz):
        t, g = divmod(z, group)
        left = u_ref[:, (s.nz + t) * LANES : (s.nz + t + 1) * LANES]
        right = u_ref[:, (s.nz + s.fine_tiles + t) * LANES : (s.nz + s.fine_tiles + t + 1) * LANES]
        strips = turn(jnp.where((lane >= R * g) & (lane < R * g + R), left, right), -R * g)
        for at, x in ((0, u_ref[:, z * LANES : (z + 1) * LANES]), (LANES, strips)):
            high, low = halves(x)
            for t in range(TERMS):
                rows = slice(t * s.nx, (t + 1) * s.nx)
                eh_ref[t, z * s.nx : (z + 1) * s.nx, at : at + LANES] = high[rows]
                el_ref[t, z * s.nx : (z + 1) * s.nx, at : at + LANES] = low[rows]
    step = 4 * s.nx
    for t in range(TERMS):
        at = 2 * t * s.ny
        y0, y0h = y0_ref[:, at : at + 2 * s.ny], y0_ref[:, at : at + s.ny]
        for first in range(0, s.nz * s.nx, step):
            both = dot(eh_ref[t, first : first + step], y0)
            v = both[:, : s.ny] + both[:, s.ny :] + dot(el_ref[t, first : first + step], y0h)
            for q in range(step // s.nx):
                v_ref[t, first // s.nx + q] = v[q * s.nx : (q + 1) * s.nx]

    def depth(r, _):
        rows = pl.ds(pl.multiple_of(r * 8, 8), 8)
        taps = [[tap_ref[t, d] for d in range(R + 1)] for t in range(TERMS)]
        for first in range(-R, s.nz + R, R):
            acc = [None] * R
            for t in range(TERMS):
                for z in range(max(0, first - R), min(s.nz, first + 2 * R)):
                    v = v_ref[t, z, rows]
                    for o in range(R):
                        d = abs(first + o - z)
                        if d <= R:
                            term = v * taps[t][d]
                            acc[o] = term if acc[o] is None else acc[o] + term
            for o in range(R):
                if first < 0:
                    down_ref[o, rows] = acc[o]
                elif first >= s.nz:
                    up_ref[o, rows] = acc[o]
                else:
                    own_ref[first + o, rows] = acc[o]
        return 0

    lax.fori_loop(0, s.nx // 8, depth, 0)


def depth_kernel(s, tap_ref, *refs):
    m_refs = refs[: s.gz]
    ry2_ref, rx2_ref, ry3_ref, rx3_ref, _, w_ref, down_ref, up_ref, c2_ref, c3_ref, c_ref = refs[s.gz :]
    n = s.cz[1]
    parts = [[] for _ in range(n)]
    for b in range(s.gz):
        for k in range(s.planes):
            parts[(b * s.z1 + k - 1) % n].append((b, k))
    for z in range(n):
        out = None
        for b, k in parts[z]:
            x = unpacked(lambda t, b=b: m_refs[b][t], k, s.wide1, 0)
            out = x if out is None else out + x
        c_ref[z] = out
    lane = lanes_of((s.rows1, LANES))
    down = [jnp.zeros((s.rows1, LANES), F32)] * s.tiles_s
    up = list(down)
    for o in range(s.planes):
        sums = [c_ref[(o - 1) % n]]
        sums += [c_ref[(o - 1 + d) % n] + c_ref[(o - 1 - d) % n] for d in range(1, R + 1)]
        for t in range(TERMS):
            x = sums[0] * tap_ref[TERMS + t, 0]
            for d in range(1, R + 1):
                x += sums[d] * tap_ref[TERMS + t, d]
            k = t * s.planes + o
            w_ref[k] = x
            tile, slot = divmod(k, s.per_tile)
            at = slot * s.strip
            here = (lane >= at) & (lane < at + s.strip)
            down[tile] = jnp.where(here, turn(x, at), down[tile])
            up[tile] = jnp.where(here, turn(x, at - (s.wide1 - s.strip)), up[tile])

    def restricted(planes, y_ref, x_ref):
        n, rows = len(planes), planes[0].shape[0]
        coarse = []
        for j in range(n // 2):
            at = lambda d: planes[(2 * j + d) % n]
            coarse.append(at(0) + NEAR * (at(1) + at(-1)) + FAR * (at(3) + at(-3)))
        along = dot2(jnp.concatenate(coarse, axis=0), y_ref[...].astype(BF16))
        x = x_ref[...].astype(BF16)
        out = []
        for j in range(n // 2):
            high, low = halves(along[j * rows : (j + 1) * rows])
            out.append(dot(x, high) + dot(x, low))
        return out

    level2 = restricted([c_ref[z] for z in range(n)], ry2_ref, rx2_ref)
    level3 = restricted(level2, ry3_ref, rx3_ref)
    for t in range(s.tiles_s):
        down_ref[t * s.rows1 : (t + 1) * s.rows1] = down[t]
        up_ref[t * s.rows1 : (t + 1) * s.rows1] = up[t]
    lane = lanes_of((s.rows2, LANES))
    down = [jnp.zeros((s.rows2, LANES), F32)] * s.tiles_s2
    up = list(down)
    for j, x in enumerate(level2):
        c2_ref[j] = x
        tile, slot = divmod(j, s.per_tile2)
        at = slot * s.strip2
        here = (lane >= at) & (lane < at + s.strip2)
        down[tile] = jnp.where(here, turn(x, at), down[tile])
        up[tile] = jnp.where(here, turn(x, at - (s.wide2 - s.strip2)), up[tile])
    for t in range(s.tiles_s2):
        rows = slice(s.base2 + t * s.rows2, s.base2 + (t + 1) * s.rows2)
        down_ref[rows] = down[t]
        up_ref[rows] = up[t]
    for t, x in enumerate(packed(level3, s.wide3, s.tiles3)):
        c3_ref[t * s.rows3 : (t + 1) * s.rows3] = x
        for ref in (down_ref, up_ref):
            ref[s.base3 + t * s.rows3 : s.base3 + (t + 1) * s.rows3] = x


def along_kernel(s, z_ref, w_ref, c2_ref, *refs):
    c3_refs = refs[: s.gy]
    y1_ref, y2h_ref, y2l_ref, xh_ref, xl_ref, d_ref, *g_refs, y2_ref, y3_ref = refs[s.gy :]
    lane = lanes_of((s.rows1, LANES))
    above, below = c3_refs[1], c3_refs[-1]
    end = s.y1 + R
    for t in range(TERMS):
        cells = []
        for o in range(s.planes):
            k = t * s.planes + o
            tile, slot = divmod(k, s.per_tile)
            rows = slice(tile * s.rows1, (tile + 1) * s.rows1)
            at = slot * s.strip
            x = turn(w_ref[k], R)
            x += jnp.where(lane < s.strip, turn(below[rows], -at), 0.0)
            x += jnp.where((lane >= end) & (lane < end + s.strip), turn(above[rows], end - at), 0.0)
            cells.append(x)
        high, low = halves(jnp.concatenate(cells, axis=0))
        at = 2 * t * s.ny
        both = dot(high, y1_ref[:, at : at + 2 * s.ny])
        out = both[:, : s.ny] + both[:, s.ny :] + dot(low, y1_ref[:, at : at + s.ny])
        for o in range(s.planes):
            d_ref[t * s.rows1 : (t + 1) * s.rows1, o * s.ny : (o + 1) * s.ny] = out[o * s.rows1 : (o + 1) * s.rows1]
    lane = lanes_of((s.rows2, LANES))
    end = s.y2 + R
    cells = []
    for j in range(s.cz[2]):
        tile, slot = divmod(j, s.per_tile2)
        rows = slice(s.base2 + tile * s.rows2, s.base2 + (tile + 1) * s.rows2)
        at = slot * s.strip2
        x = turn(c2_ref[j], R)
        x += jnp.where(lane < s.strip2, turn(below[rows], -at), 0.0)
        x += jnp.where((lane >= end) & (lane < end + s.strip2), turn(above[rows], end - at), 0.0)
        cells.append(x)
    cells3 = []
    for j in range(s.cz[3]):
        out = None
        for b in range(s.gy):
            first = s.base3 if c3_refs[b].shape[0] > s.tiles3 * s.rows3 else 0
            tile = lambda t, b=b, f=first: c3_refs[b][f + t * s.rows3 : f + (t + 1) * s.rows3]
            x = unpacked(tile, j, s.wide3, b * s.y3)
            out = x if out is None else out + x
        cells3.append(out)
    at = TERMS * s.rows1
    for q, (x, rows, ref) in enumerate(((cells, s.rows2, y2_ref), (cells3, s.rows3, y3_ref))):
        columns = slice(q * TERMS * s.ny, (q + 1) * TERMS * s.ny)
        y = dot3(jnp.concatenate(x, axis=0), y2h_ref[:, columns], y2l_ref[:, columns])
        for t in range(TERMS):
            for j in range(len(x)):
                ref[t, j] = y[j * rows : (j + 1) * rows, t * s.ny : (t + 1) * s.ny]
        for o in range(s.planes):
            for t in range(TERMS):
                scale = [z_ref[(q * TERMS + t) * s.zrows + o, j] for j in range(len(x))]
                out = ref[t, 0] * scale[0]
                for j in range(1, len(x)):
                    out += ref[t, j] * scale[j]
                d_ref[at + t * rows : at + (t + 1) * rows, o * s.ny : (o + 1) * s.ny] = out
        at += TERMS * rows
    away_kernel(s, d_ref, xh_ref, xl_ref, *g_refs)


def across(s, d_ref, xh_ref, xl_ref, shift):
    rows = slice(shift * s.nx, (shift + 1) * s.nx)
    high, low = halves(d_ref[...])
    xh, xl = xh_ref[rows, : s.depth], xl_ref[rows, : s.depth]
    return dot(xh, high) + dot(xl, high) + dot(xh, low)


def away_kernel(s, d_ref, xh_ref, xl_ref, *g_refs):
    for shift, ref in enumerate(g_refs):
        ref[...] = across(s, d_ref, xh_ref, xl_ref, shift + 1)


def prolonged(s, level, z):
    m = z // 2 + 1
    if z % 2 == 0:
        return level[m]
    return NEAR * (level[m] + level[m + 1]) + FAR * (level[m - 1] + level[m + 2])


def home_kernel(s, d_ref, xh_ref, xl_ref, own_ref, low_ref, high_ref, out_ref):
    g = across(s, d_ref, xh_ref, xl_ref, 0)
    level = [g[:, o * s.ny : (o + 1) * s.ny] for o in range(s.planes)]
    for z in range(s.nz):
        x = prolonged(s, level, z) + own_ref[z]
        if z < R:
            x += low_ref[z]
        if z >= s.nz - R:
            x += high_ref[z - (s.nz - R)]
        out_ref[z] = x


def last_kernel(s, home_ref, *refs):
    *g_refs, out_ref, sum_ref, sems = refs
    level = []
    for o in range(s.planes):
        columns = slice(o * s.ny, (o + 1) * s.ny)
        x = g_refs[0][:, columns]
        for ref in g_refs[1:]:
            x += ref[:, columns]
        level.append(x)
    copies = []
    for first in range(0, s.nz, 4):
        for z in range(first, first + 4):
            sum_ref[z] = home_ref[z] + prolonged(s, level, z)
        planes = slice(first, first + 4)
        copies.append(pltpu.make_async_copy(sum_ref.at[planes], out_ref.at[planes], sems.at[first // 4]))
        copies[-1].start()
    for copy in copies:
        copy.wait()


def call(kernel, name, operands, out_shapes, scalars=(), after=(), scratch=(), flops=0, out_space=pltpu.VMEM):
    operands = list(operands) + list(after)

    def spec(i):
        if i >= len(operands) - len(after):
            return pl.BlockSpec(memory_space=pl.ANY)
        return pl.BlockSpec(memory_space=pltpu.SMEM if i in scalars else pltpu.VMEM)

    moved = sum(x.size * x.dtype.itemsize for x in operands)
    moved += sum(int(np.prod(x.shape)) * x.dtype.itemsize for x in out_shapes)
    return pl.pallas_call(
        kernel,
        name=name,
        out_shape=out_shapes,
        in_specs=[spec(i) for i in range(len(operands))],
        out_specs=[pl.BlockSpec(memory_space=out_space)] * len(out_shapes),
        scratch_shapes=list(scratch),
        compiler_params=pltpu.CompilerParams(vmem_limit_bytes=VMEM_LIMIT),
        cost_estimate=pl.CostEstimate(flops=flops, bytes_accessed=moved, transcendentals=0),
    )(*operands)


def arrays(*shapes, dtype=F32):
    return [jax.ShapeDtypeStruct(shape, dtype) for shape in shapes]


def fetch(x, **shifts):
    names = tuple(shifts)
    sizes = [lax.axis_size(n) for n in names]
    pairs = []
    for here in np.ndindex(*sizes):
        there = [(h + shifts[n]) % size for h, n, size in zip(here, names, sizes)]
        pairs.append((int(np.ravel_multi_index(there, sizes)), int(np.ravel_multi_index(here, sizes))))
    return lax.ppermute(x, names if len(names) > 1 else names[0], pairs)


def two(*shape):
    return arrays(shape, shape, dtype=BF16)


def shards(charges, widths, amplitudes):
    s = Sizes(*charges.shape, lax.axis_size("gz"), lax.axis_size("gx"), lax.axis_size("gy"))
    c = {k: jnp.asarray(v) for k, v in constants(s).items()}
    brick = (s.nz, s.nx, s.ny)
    side = (R, s.nx, s.ny)
    taps, x0, y0 = call(
        functools.partial(tap_kernel, s), "taps", [widths, amplitudes],
        arrays((8, LANES))
        + arrays((TERMS * s.nx, 3 * s.ext), (2 * LANES, 2 * TERMS * s.ny), dtype=BF16),
        flops=6 * 10**8,
    )
    high_rows = fetch(charges, gx=1)
    low_rows = high_rows if s.gx == 2 else fetch(charges, gx=-1)
    strips = (s.fine_tiles, s.ext, LANES)
    share, first_cells, last_cells = call(
        functools.partial(share_kernel, s), "share", [charges, low_rows, high_rows],
        arrays((s.tiles1, s.rows1, LANES), strips, strips), after=[x0], flops=10**9,
    )
    shares = [share] + [fetch(share, gz=b) for b in range(1, s.gz)]
    left, right = fetch(last_cells, gy=-1), fetch(first_cells, gy=1)
    tiles = s.nz + 2 * s.fine_tiles
    halved = pltpu.VMEM((TERMS, s.nz * s.nx, 2 * LANES), BF16)
    near, near_down, near_up = call(
        functools.partial(near_kernel, s), "near",
        [taps, charges, low_rows, high_rows, left, right, x0, y0],
        arrays(brick, side, side), scalars=(0,),
        scratch=[
            pltpu.VMEM((3 * s.ext, tiles * LANES), BF16), pltpu.VMEM((TERMS * s.nx, tiles * LANES), F32),
            halved, halved, pltpu.VMEM((TERMS,) + brick, F32),
        ],
        flops=5 * 10**9,
    )
    size3 = s.tiles3 * s.rows3
    message = (s.base3 + size3, LANES)
    waves, to_low, to_high, level2, coarse = call(
        functools.partial(depth_kernel, s), "depth",
        [taps] + shares + [c[k] for k in ("ry2", "rx2", "ry3", "rx3")],
        arrays((TERMS * s.planes, s.rows1, LANES), message, message, (s.cz[2], s.rows2, LANES), (size3, LANES)),
        scalars=(0,), after=[near], scratch=[pltpu.VMEM((s.cz[1], s.rows1, LANES), F32)], flops=2 * 10**9,
    )
    named = ("px1", "px2", "px3", "px3l", "py2", "py3", "py3l", "pz2", "pz3")
    z_taps, y1, y2h, y2l, xh, xl = call(
        functools.partial(matrix_kernel, s), "matrices",
        [widths, amplitudes] + [c[k] for k in named],
        arrays((2 * TERMS * s.zrows, LANES))
        + arrays((LANES, 2 * TERMS * s.ny), dtype=BF16)
        + two(LANES, 2 * TERMS * s.ny) + two(s.cx[0], s.depth_lanes),
        after=[coarse], flops=2 * 10**9,
    )
    coarses = [coarse]
    for b in range(1, s.gy):
        coarses.append(fetch({1: to_low, s.gy - 1: to_high}.get(b, coarse), gy=b))
    near_low, near_high = fetch(near_up, gz=-1), fetch(near_down, gz=1)
    terms, *parts = call(
        functools.partial(along_kernel, s), "along",
        [z_taps, waves, level2] + coarses + [y1, y2h, y2l, xh, xl],
        arrays((s.depth, s.planes * s.ny), *[(s.nx, s.planes * s.ny)] * (s.gx - 1)), scalars=(0,),
        scratch=[
            pltpu.VMEM((TERMS, s.cz[2], s.rows2, s.ny), F32), pltpu.VMEM((TERMS, s.cz[3], s.rows3, s.ny), F32)
        ], flops=3 * 10**9,
    )
    parts = [fetch(x, gx=-dx) for dx, x in enumerate(parts, 1)]
    (home,) = call(
        functools.partial(home_kernel, s), "home",
        [terms, xh, xl, near, near_low, near_high], arrays(brick), flops=2 * 10**9,
    )
    (out,) = call(
        functools.partial(last_kernel, s), "last", [home] + parts, arrays(brick), flops=10**9,
        scratch=[pltpu.VMEM(brick, F32), pltpu.SemaphoreType.DMA((s.nz // 4,))], out_space=pl.ANY,
    )
    return out


def solution(mesh):
    placed = (P("gz", "gx", "gy"), P(), P())
    return jax.shard_map(
        shards, mesh=mesh, in_specs=placed, out_specs=P("gz", "gx", "gy"), check_vma=False
    )
```
